32 devices in a mesh: fsdp: 4 (over y, core), ctx: 4 (over z), tp: 2 (over x).
Axes of the slice: x: 2, y: 2, z: 4, core: 2. Of those that a mesh axis runs over, the one named last changes fastest.
Arguments:
- tokens: bfloat16 [8, 2048, 960], P('fsdp', ('ctx', 'tp')), may hold values from -6 to 6
- cotangent: bfloat16 [8, 2048, 960], P('fsdp', ('ctx', 'tp')), may hold values from -6 to 6
- input_gain: bfloat16 [960], P('fsdp'), may hold values from 0.099609375 to 1.8984375
- w_query: bfloat16 [960, 960], P('fsdp'), may hold values from -0.1875 to 0.1875
- w_keyval: bfloat16 [960, 640], P('fsdp'), may hold values from -0.1875 to 0.1875
- w_output: bfloat16 [960, 960], P('fsdp'), may hold values from -2 to 2
- middle_gain: bfloat16 [960], P('fsdp'), may hold values from 0.099609375 to 1.8984375
- w_gate: bfloat16 [960, 2560], P('fsdp', 'tp'), may hold values from -0.1875 to 0.1875
- w_up: bfloat16 [960, 2560], P('fsdp', 'tp'), may hold values from -0.1875 to 0.1875
- w_down: bfloat16 [960, 2560], P('fsdp', 'tp'), may hold values from -0.25 to 0.25
Outputs:
- result: bfloat16 [8, 2048, 960], P('fsdp', ('ctx', 'tp'))
- grad_tokens: float32 [8, 2048, 960], P('fsdp', ('ctx', 'tp'))
- grad_input_gain: float32 [960], P('fsdp')
- grad_w_query: float32 [960, 960], P('fsdp')
- grad_w_keyval: float32 [960, 640], P('fsdp')
- grad_w_output: float32 [960, 960], P('fsdp')
- grad_middle_gain: float32 [960], P('fsdp')
- grad_w_gate: float32 [960, 2560], P('fsdp', 'tp')
- grad_w_up: float32 [960, 2560], P('fsdp', 'tp')
- grad_w_down: float32 [960, 2560], P('fsdp', 'tp')
The draws below stay inside these ranges and needn't reach their ends.
All inputs are finite; a program needn't handle non-finite values.
Results may differ from the reference program's by a relative error of at most 0.02.
Values may be sent and summed in bfloat16 or wider, within the bound.
A program may use at most 128 MiB of HBM per device.

```python
import jax
import jax.numpy as jnp
from jax import lax

D = 960
QUERY_HEADS = 15
KEYVAL_HEADS = 5
HEAD_WIDTH = 64
FF = 2560
SEQUENCE_LENGTH = 2048
QW = 960
KEY_WIDTH = 320
SEQS = 8


def with_spikes(array, stream_key, source, target, blocks, factor):
    def block_of(dim):
        return (jnp.arange(array.shape[dim]) // (array.shape[dim] // blocks)).reshape((-1,) + (1,) * (array.ndim - 1 - dim))

    near = jax.random.permutation(stream_key, blocks)[block_of(target)]
    far = (block_of(target) + blocks // 2) % blocks
    return jnp.where((block_of(source) == near) | (block_of(source) == far), factor * array, array)


def block_levels(stream_key, dims, split, low, largest):
    def one(position, parts):
        draws = jax.random.uniform(jax.random.fold_in(jax.random.fold_in(stream_key, 6), position), (parts,), jnp.float32, low / len(split), largest / len(split))
        return jnp.repeat(jnp.exp(draws), dims[position] // parts).reshape((-1,) + (1,) * (len(dims) - position - 1))

    loudness = one(*split[0])
    for cut in split[1:]:
        loudness = loudness * one(*cut)
    return loudness


def normal_values(key, extent, deviation, bound, pieces=(), held_as=jnp.bfloat16):
    array = jax.random.normal(key, extent, jnp.float32) * deviation
    if len(pieces) > 0:
        array = block_levels(key, extent, pieces, -0.22, 0.18) * array
    return jnp.clip(array, min=-bound, max=bound).astype(held_as)


def noise_with(stream_key, shape, scale, reach, shards, heavy, held_as=jnp.bfloat16):
    values = scale * jax.random.normal(stream_key, shape, jnp.float32)
    if shards:
        values = values * block_levels(stream_key, shape, shards, -0.22, 0.18)
    return jnp.clip(with_spikes(values, jax.random.fold_in(stream_key, 3), *heavy), -reach, reach).astype(held_as)


def setup_inputs(seed: int = 0) -> dict:
    key_list = jax.random.split(jax.random.key(seed), 11)
    tokens = noise_with(key_list[0], (SEQS, SEQUENCE_LENGTH, D), 1.0, 6.0, ((0, 4), (1, 8)), (0, 2, 4, 2.0))
    cotangent = noise_with(key_list[1], (SEQS, SEQUENCE_LENGTH, D), 1.0, 6.0, ((0, 4), (1, 8)), (0, 2, 4, 2.0))
    input_gain = jnp.clip(1.0 + 0.18 * jax.random.normal(key_list[2], (D,), jnp.float32), 0.099609375, 1.8984375).astype(jnp.bfloat16)
    w_query = normal_values(key_list[3], (D, QW), D ** -0.5, 0.1875, ((0, 4),))
    w_keyval = normal_values(key_list[4], (D, 2 * KEY_WIDTH), D ** -0.5, 0.1875, ((0, 4),))
    w_output = normal_values(key_list[5], (QW, D), (max(1, QW * 16 // SEQUENCE_LENGTH)) ** -0.5, 2.0, ((0, 4),))
    middle_gain = jnp.clip(1.0 + 0.18 * jax.random.normal(key_list[6], (D,), jnp.float32), 0.099609375, 1.8984375).astype(jnp.bfloat16)
    w_gate = normal_values(key_list[7], (D, FF), D ** -0.5, 0.1875, ((0, 4), (1, 2)))
    w_up = normal_values(key_list[8], (D, FF), D ** -0.5, 0.1875, ((0, 4), (1, 2)))
    w_down = normal_values(key_list[9], (D, FF), (FF // 4) ** -0.5, 0.25, ((0, 4), (1, 2)))
    return {"tokens": tokens, "cotangent": cotangent, "input_gain": input_gain, "w_query": w_query, "w_keyval": w_keyval, "w_output": w_output, "middle_gain": middle_gain, "w_gate": w_gate, "w_up": w_up, "w_down": w_down}


EPS = 1e-05
THETA = 10000.0
precise = lax.Precision.HIGHEST

@jax.custom_vjp
def reduced_precision(v):
    return lax.optimization_barrier(v.astype(jnp.bfloat16)).astype(jnp.float32)

@jax.custom_vjp
def low_back(v):
    return v

def low_keep(v):
    return (reduced_precision(v), None)

def low_pass(kept, grad):
    return (grad,)

def back_keep(v):
    return (v, None)

def back_low(kept, grad):
    return (reduced_precision(grad),)
reduced_precision.defvjp(low_keep, low_pass)
low_back.defvjp(back_keep, back_low)

def normalize(value_rows):
    return value_rows * lax.rsqrt(lax.optimization_barrier(jnp.mean(value_rows * value_rows, -1, keepdims=True)) + EPS)

def apply_rotary(value_rows, cosine_table, sine_table, heads):
    half_width = HEAD_WIDTH // 2
    shaped = value_rows.reshape(value_rows.shape[:-1] + (heads, HEAD_WIDTH))
    leading = shaped[..., :half_width]
    trailing = shaped[..., half_width:]
    cosine_wide = cosine_table[:, None, :]
    sine_wide = sine_table[:, None, :]
    turned = jnp.concatenate([leading * cosine_wide - trailing * sine_wide, trailing * cosine_wide + leading * sine_wide], -1)
    return turned.reshape(value_rows.shape)

def attend(head_items):
    query_rotated, key_rotated, value_reduced = head_items
    group_total = QUERY_HEADS // KEYVAL_HEADS
    query_by_group = query_rotated.reshape(SEQUENCE_LENGTH, KEYVAL_HEADS, group_total, HEAD_WIDTH)
    key_by_group = key_rotated.reshape(SEQUENCE_LENGTH, KEYVAL_HEADS, HEAD_WIDTH)
    value_by_group = value_reduced.reshape(SEQUENCE_LENGTH, KEYVAL_HEADS, HEAD_WIDTH)
    scores = jnp.einsum('qjgd,kjd->jgqk', query_by_group, key_by_group, precision=precise) * HEAD_WIDTH ** (-0.5)
    scores = low_back(scores)
    allowed = jnp.arange(SEQUENCE_LENGTH)[None, :] <= jnp.arange(SEQUENCE_LENGTH)[:, None]
    weights = jax.nn.softmax(jnp.where(allowed, scores, -jnp.inf), axis=-1)
    mixed_heads = jnp.einsum('jgqk,kjd->qjgd', reduced_precision(weights), value_by_group, precision=precise)
    return mixed_heads.reshape(SEQUENCE_LENGTH, QUERY_HEADS * HEAD_WIDTH)

def layer_forward(inputs, weights, cosine_table, sine_table):
    input_gain, w_query, w_keyval, w_output, middle_gain, w_gate, w_up, w_down = weights
    normed_one = reduced_precision(normalize(inputs) * input_gain)
    query_raw = low_back(jnp.dot(normed_one, w_query, precision=precise))
    keyval_unrotated = low_back(jnp.dot(normed_one, w_keyval, precision=precise))
    query_rotated = reduced_precision(apply_rotary(query_raw, cosine_table, sine_table, QUERY_HEADS))
    key_rotated = reduced_precision(apply_rotary(keyval_unrotated[..., :KEY_WIDTH], cosine_table, sine_table, KEYVAL_HEADS))
    value_reduced = reduced_precision(keyval_unrotated[..., KEY_WIDTH:])
    mixed_all = lax.map(jax.checkpoint(attend), (query_rotated, key_rotated, value_reduced))
    mixed_low = reduced_precision(low_back(mixed_all))
    attention_out = low_back(jnp.dot(mixed_low, w_output, precision=precise))
    middle = inputs + attention_out
    normed_two = reduced_precision(normalize(middle) * middle_gain)
    gate_proj = low_back(jnp.dot(normed_two, w_gate, precision=precise))
    up_proj = low_back(jnp.dot(normed_two, w_up, precision=precise))
    hidden = reduced_precision(jax.nn.silu(gate_proj) * up_proj)
    feed_out = low_back(jnp.einsum('bsf,df->bsd', hidden, w_down, precision=precise))
    return middle + feed_out

def reference(tokens, cotangent, input_gain, w_query, w_keyval, w_output, middle_gain, w_gate, w_up, w_down):
    params = tuple((weight.astype(jnp.float32) for weight in (input_gain, w_query, w_keyval, w_output, middle_gain, w_gate, w_up, w_down)))
    half_width = HEAD_WIDTH // 2
    positions = jnp.arange(SEQUENCE_LENGTH).astype(jnp.float32)
    frequency = THETA ** (-(2.0 * jnp.arange(half_width).astype(jnp.float32)) / HEAD_WIDTH)
    angles = positions[:, None] * frequency[None, :]
    cosine_table = jnp.cos(angles)
    sine_table = jnp.sin(angles)
    group_size = 2 if SEQS % 2 == 0 else 1
    group_count = SEQS // group_size
    token_groups = tokens.reshape(group_count, group_size, SEQUENCE_LENGTH, D)
    cotangent_groups = cotangent.reshape(group_count, group_size, SEQUENCE_LENGTH, D)

    def forward(inputs, weights):
        return layer_forward(inputs, weights, cosine_table, sine_table)

    def group_step(totals, group_items):
        inputs = group_items[0].astype(jnp.float32)
        outputs, pullback = jax.vjp(forward, inputs, params)
        back_inputs, back_weights = pullback(group_items[1].astype(jnp.float32))
        totals = jax.tree.map(jnp.add, totals, back_weights)
        return (totals, (outputs.astype(jnp.bfloat16), back_inputs))
    zeros_start = tuple((jnp.zeros_like(weight) for weight in params))
    totals, (results, back_tokens) = lax.scan(group_step, zeros_start, (token_groups, cotangent_groups))
    return (results.reshape(SEQS, SEQUENCE_LENGTH, D), back_tokens.reshape(SEQS, SEQUENCE_LENGTH, D), totals[0], totals[1], totals[2], totals[3], totals[4], totals[5], totals[6], totals[7])
```

```python
import functools

import jax
import jax.numpy as jnp
from jax import lax
from jax.experimental import pallas as pl
from jax.experimental.pallas import tpu as pltpu
from jax.sharding import PartitionSpec as P

QUERY_HEADS = 15
KEYVAL_HEADS = 5
GROUP = QUERY_HEADS // KEYVAL_HEADS
HEAD_WIDTH = 64
HALF = HEAD_WIDTH // 2
KEY_WIDTH = 320
QUERY_WIDTH = QUERY_HEADS * HEAD_WIDTH
SCALE = HEAD_WIDTH ** (-0.5)

EPS = 1e-05
THETA = 10000.0
VMEM_LIMIT = 40 * 1024 * 1024


def dot(left, right, left_dim, right_dim):
    return lax.dot_general(
        left, right, (((left_dim,), (right_dim,)), ((), ())), preferred_element_type=jnp.float32
    )


def rope_tables(token_positions, first_place):
    position = (first_place + lax.iota(jnp.int32, token_positions)).astype(jnp.float32)
    frequency = THETA ** (-(2.0 * lax.iota(jnp.int32, HALF).astype(jnp.float32)) / HEAD_WIDTH)
    angles = frequency[:, None] * position[None, :]
    return (jnp.cos(angles), jnp.sin(angles))


def apply_rotary(rows, cosine, sine):
    shaped = rows.reshape(-1, 2, HALF, rows.shape[-1])
    leading = shaped[:, 0]
    trailing = shaped[:, 1]
    return jnp.stack(
        [leading * cosine - trailing * sine, trailing * cosine + leading * sine], 1
    ).reshape(rows.shape)


def normalize(value_rows):
    inverse_rms = lax.rsqrt(jnp.mean(value_rows * value_rows, -1, keepdims=True) + EPS)
    return (value_rows * inverse_rms, inverse_rms)


def norm_back(back_unit, unit_rows, inverse_rms):
    return inverse_rms * (
        back_unit - unit_rows * jnp.mean(back_unit * unit_rows, -1, keepdims=True)
    )


def causal(scores):
    key_place = lax.broadcasted_iota(jnp.int32, scores.shape, 0)
    query_place = lax.broadcasted_iota(jnp.int32, scores.shape, 1)
    return jnp.where(key_place <= query_place, scores, -jnp.inf)


def forward_kernel(query_ref, key_ref, value_ref, mixed_ref, lse_ref, scaled=False):
    place = lax.axis_index("ctx")
    queries = [
        query_ref[g] if scaled else query_ref[g] * jnp.bfloat16(SCALE) for g in range(GROUP)
    ]

    def scores_of(keys_turned, g, masked):
        scores = dot(keys_turned, queries[g], 1, 0)
        return causal(scores) if masked else scores

    def first():
        keys_turned = key_ref[0, 0, 0].T
        values = value_ref[0, 0, 0]
        carried = []
        for g in range(GROUP):
            scores = scores_of(keys_turned, g, True)
            top = jnp.max(scores, 0, keepdims=True)
            lifted = jnp.exp(scores - top)
            total = jnp.sum(lifted, 0, keepdims=True)
            carried += [top, total, dot(values, lifted.astype(jnp.bfloat16), 1, 0)]
        return tuple(carried)

    def step(block, carried):
        keys_turned = key_ref[block, 0, 0].T
        values = value_ref[block, 0, 0]
        later = []
        for g in range(GROUP):
            top, total, mixed = carried[3 * g : 3 * g + 3]
            scores = scores_of(keys_turned, g, False)
            new_top = jnp.maximum(top, jnp.max(scores, 0, keepdims=True))
            lifted = jnp.exp(scores - new_top)
            shrink = jnp.exp(top - new_top)
            later += [
                new_top,
                total * shrink + jnp.sum(lifted, 0, keepdims=True),
                mixed * shrink + dot(values, lifted.astype(jnp.bfloat16), 1, 0),
            ]
        return tuple(later)

    carried = lax.fori_loop(1, place + 1, step, first())
    for g in range(GROUP):
        top, total, mixed = carried[3 * g : 3 * g + 3]
        mixed_ref[g] = (mixed / total).astype(jnp.bfloat16)
        lse_ref[g] = top + jnp.log(total)


def attend_forward(query, keyval, scaled=False):
    blocks, token_positions = keyval.shape[0], keyval.shape[-1]
    head_block = (GROUP, HEAD_WIDTH, token_positions)
    key_block = (blocks, 1, 1, HEAD_WIDTH, token_positions)
    area = QUERY_HEADS * token_positions * token_positions * blocks
    return pl.pallas_call(
        functools.partial(forward_kernel, scaled=scaled),
        grid=(KEYVAL_HEADS,),
        in_specs=[
            pl.BlockSpec(head_block, lambda j: (j, 0, 0)),
            pl.BlockSpec(key_block, lambda j: (0, 0, j, 0, 0)),
            pl.BlockSpec(key_block, lambda j: (0, 1, j, 0, 0)),
        ],
        out_specs=[
            pl.BlockSpec(head_block, lambda j: (j, 0, 0)),
            pl.BlockSpec((GROUP, 1, token_positions), lambda j: (j, 0, 0)),
        ],
        out_shape=[
            jax.ShapeDtypeStruct(query.shape, jnp.bfloat16),
            jax.ShapeDtypeStruct((QUERY_HEADS, 1, token_positions), jnp.float32),
        ],
        compiler_params=pltpu.CompilerParams(vmem_limit_bytes=VMEM_LIMIT),
        cost_estimate=pl.CostEstimate(
            flops=16 * HEAD_WIDTH * area, bytes_accessed=6 * query.size, transcendentals=area
        ),
        name="attend_forward",
    )(query, keyval, keyval)


def backward_kernel(
    query_ref, key_ref, value_ref, back_ref, mixed_ref, lse_ref, cosine_ref, sine_ref,
    back_query_ref, back_keyval_ref,
):
    place = lax.axis_index("ctx")
    blocks = key_ref.shape[0]
    queries = [query_ref[g] * jnp.bfloat16(SCALE) for g in range(GROUP)]
    backs = [back_ref[g] for g in range(GROUP)]
    tops = [lse_ref[g] for g in range(GROUP)]
    sums = [
        jnp.sum(backs[g].astype(jnp.float32) * mixed_ref[g].astype(jnp.float32), 0, keepdims=True)
        for g in range(GROUP)
    ]

    def step(block, carried, masked=False):
        keys = key_ref[block, 0, 0]
        keys_turned = keys.T
        values_turned = value_ref[block, 0, 0].T
        back_key = jnp.zeros(keys.shape, jnp.float32)
        back_value = jnp.zeros(keys.shape, jnp.float32)
        later = []
        for g in range(GROUP):
            scores = dot(keys_turned, queries[g], 1, 0)
            if masked:
                scores = causal(scores)
            weights = jnp.exp(scores - tops[g])
            back_weights = dot(values_turned, backs[g], 1, 0)
            back_scores = (weights * (back_weights - sums[g])).astype(jnp.bfloat16)
            later.append(carried[g] + dot(keys, back_scores, 1, 0))
            back_key += dot(queries[g], back_scores, 1, 1)
            back_value += dot(backs[g], weights.astype(jnp.bfloat16), 1, 1)
        back_keyval_ref[block, 0, 0] = back_key.astype(jnp.bfloat16)
        back_keyval_ref[block, 1, 0] = back_value.astype(jnp.bfloat16)
        return tuple(later)

    start = tuple(jnp.zeros(query_ref.shape[1:], jnp.float32) for g in range(GROUP))
    carried = lax.fori_loop(1, place + 1, step, step(0, start, True))

    def clear(block, unused):
        zero = jnp.zeros(key_ref.shape[3:], jnp.bfloat16)
        back_keyval_ref[block, 0, 0] = zero
        back_keyval_ref[block, 1, 0] = zero
        return unused

    lax.fori_loop(place + 1, blocks, clear, 0)
    cosine = cosine_ref[...]
    sine = sine_ref[...]
    for g in range(GROUP):
        leading = carried[g][:HALF] * SCALE
        trailing = carried[g][HALF:] * SCALE
        back_query_ref[g, :HALF] = (leading * cosine + trailing * sine).astype(jnp.bfloat16)
        back_query_ref[g, HALF:] = (trailing * cosine - leading * sine).astype(jnp.bfloat16)


def attend_backward(query, keyval, back_mixed, mixed, lse, cosine, sine, first, count):
    blocks, token_positions = keyval.shape[0], keyval.shape[-1]
    head_block = (GROUP, HEAD_WIDTH, token_positions)
    key_block = (blocks, 1, 1, HEAD_WIDTH, token_positions)
    area = count * GROUP * token_positions * token_positions * blocks
    heads = pl.BlockSpec(head_block, lambda j: (j + first, 0, 0))
    table = pl.BlockSpec((HALF, token_positions), lambda j: (0, 0))
    return pl.pallas_call(
        backward_kernel,
        grid=(count,),
        in_specs=[
            heads,
            pl.BlockSpec(key_block, lambda j: (0, 0, j + first, 0, 0)),
            pl.BlockSpec(key_block, lambda j: (0, 1, j + first, 0, 0)),
            heads,
            heads,
            pl.BlockSpec((GROUP, 1, token_positions), lambda j: (j + first, 0, 0)),
            table,
            table,
        ],
        out_specs=[
            pl.BlockSpec(head_block, lambda j: (j, 0, 0)),
            pl.BlockSpec((blocks, 2, 1, HEAD_WIDTH, token_positions), lambda j: (0, 0, j, 0, 0)),
        ],
        out_shape=[
            jax.ShapeDtypeStruct((count * GROUP, HEAD_WIDTH, token_positions), jnp.bfloat16),
            jax.ShapeDtypeStruct(
                (blocks, 2, count, HEAD_WIDTH, token_positions), jnp.bfloat16
            ),
        ],
        compiler_params=pltpu.CompilerParams(vmem_limit_bytes=VMEM_LIMIT),
        cost_estimate=pl.CostEstimate(
            flops=40 * HEAD_WIDTH * area, bytes_accessed=10 * query.size, transcendentals=area
        ),
        name="attend_backward",
    )(query, keyval, keyval, back_mixed, mixed, lse, cosine, sine)


def move_along(value, distance):
    blocks = lax.axis_size("ctx")
    pairs = [(i, i + distance) for i in range(blocks) if 0 <= i + distance < blocks]
    return lax.ppermute(value, "ctx", pairs)


def trade(value, axis, step):
    pairs = [(i, i ^ step) for i in range(lax.axis_size(axis))]
    return lax.ppermute(value, axis, pairs)


def add_low(left, right):
    return (left.astype(jnp.float32) + right.astype(jnp.float32)).astype(jnp.bfloat16)


def scatter_sum(value, axis):
    size = lax.axis_size(axis)
    index = lax.axis_index(axis)
    rows = value.shape[0] // size
    step = 1
    while step < size:
        count = value.shape[0] // (2 * rows)
        split = value.reshape(count, 2, rows, value.shape[-1])
        second = (index // step) % 2 == 1
        kept = jnp.where(second, split[:, 1], split[:, 0])
        sent = jnp.where(second, split[:, 0], split[:, 1])
        value = add_low(kept, trade(sent, axis, step)).reshape(count * rows, value.shape[-1])
        step *= 2
    return value


def whole_sum(value, others):
    half_rows = value.shape[0] // 2
    second = lax.axis_index("ctx") % 2 == 1
    upper, lower = value[:half_rows], value[half_rows:]
    received = trade(jnp.where(second, upper, lower), "ctx", 1)
    total = add_low(jnp.where(second, lower, upper), received)
    for axis, first_step in others:
        step = first_step
        while step < lax.axis_size(axis):
            total = add_low(total, trade(total, axis, step))
            step *= 2
    received = trade(total, "ctx", 1)
    return jnp.concatenate(
        [jnp.where(second, received, total), jnp.where(second, total, received)], 0
    ).astype(jnp.float32)


MESH = pl.DeviceIdType.MESH
KERNEL_VMEM = 58 * 1024 * 1024
CHUNK_ROWS = 80
WIDE = 512


def remote(source, target, send_sem, recv_sem, **place):
    return pltpu.make_async_remote_copy(
        src_ref=source, dst_ref=target, send_sem=send_sem, recv_sem=recv_sem,
        device_id=place, device_id_type=MESH,
    )


def wide(value):
    return value.astype(jnp.float32)


def low(value):
    return value.astype(jnp.bfloat16)


def greet(**place):
    pl.semaphore_signal(
        pltpu.get_barrier_semaphore(), inc=1, device_id=place, device_id_type=MESH
    )


def backward_sum_kernel(
    query_ref, keyval_ref, back_ref, mixed_ref, lse_ref, cosine_ref, sine_ref,
    down_ref, gate_ref, up_ref,
    back_query_ref, back_keyval_ref, share_ref,
    own, mate_in, y_in, up_in, parts, part_out, part_in, back_total, row_sums,
    own_sem, mate_send, mate_recv, y_send, y_recv, up_send, up_recv, down_send, down_recv,
    part_send, part_recv,
):
    place = lax.axis_index("ctx")
    last = lax.axis_size("ctx") - 1
    blocks = last + 1
    rank = lax.axis_index("fsdp")
    core = rank % 2
    y = rank // 2
    mate = rank + 1 - 2 * core
    across = rank + 2 - 4 * y
    gradients = (down_ref, gate_ref, up_ref)
    rows = share_ref.shape[1]
    per = rows // CHUNK_ROWS
    chunks = len(gradients) * per

    for m, gradient in enumerate(gradients):
        for half in range(2):
            pltpu.make_async_copy(
                gradient.at[2 * half + core], own.at[m, half], own_sem.at[m, half]
            ).start()
    greet(fsdp=mate)
    greet(fsdp=across)

    @pl.when(place > 0)
    def _():
        greet(ctx=place - 1)

    @pl.when(place < last)
    def _():
        greet(ctx=place + 1)

    neighbours = (place + last - 1) // last + (2 * last - place - 1) // last
    pl.semaphore_wait(pltpu.get_barrier_semaphore(), 2 + neighbours)

    def chunk_at(ref, m, r, *front):
        return ref.at[(m,) + front + (pl.ds(r * CHUNK_ROWS, CHUNK_ROWS),)]

    def mate_copy(m, r, half):
        gradient = gradients[m]
        return remote(
            gradient.at[2 * half + 1 - core, pl.ds(r * CHUNK_ROWS, CHUNK_ROWS)],
            chunk_at(mate_in, m, r, half),
            mate_send.at[m * per + r, half], mate_recv.at[m * per + r, half], fsdp=mate,
        )

    for m in range(len(gradients)):
        for r in range(per):
            for half in range(2):
                mate_copy(m, r, half).start()
    for m, gradient in enumerate(gradients):
        for half in range(2):
            pltpu.make_async_copy(
                gradient.at[2 * half + core], own.at[m, half], own_sem.at[m, half]
            ).wait()

    def split(k):
        r = lax.rem(k, per)
        return k // per, pl.ds(pl.multiple_of(r * CHUNK_ROWS, CHUNK_ROWS), CHUNK_ROWS)

    def y_copy(k):
        m, at = split(k)
        return remote(
            own.at[m, 1 - y, at], y_in.at[m, at], y_send.at[k], y_recv.at[k], fsdp=across
        )

    def up_copy(k):
        m, at = split(k)
        return remote(
            own.at[m, y, at], up_in.at[m, at], up_send.at[k], up_recv.at[k], ctx=place + 1
        )

    def down_copy(k):
        m, at = split(k)
        return remote(
            share_ref.at[m, at], share_ref.at[m, at], down_send.at[k], down_recv.at[k],
            ctx=place - 1,
        )

    def to_across(k):
        m, at = split(k)
        for half in range(2):
            pltpu.make_async_copy(
                mate_in.at[m, half, at], mate_in.at[m, half, at], mate_recv.at[k, half]
            ).wait()
        own[m, 1 - y, at] = low(wide(own[m, 1 - y, at]) + wide(mate_in[m, 1 - y, at]))
        y_copy(k).start()

    def to_next(k):
        m, at = split(k)
        y_copy(k).wait_recv()
        total = wide(own[m, y, at]) + wide(mate_in[m, y, at]) + wide(y_in[m, at])

        @pl.when(place == 0)
        def _():
            own[m, y, at] = low(total)

        @pl.when(place > 0)
        def _():
            up_copy(k).wait_recv()
            own[m, y, at] = low(total + wide(up_in[m, at]))

        @pl.when(place < last)
        def _():
            up_copy(k).start()

        @pl.when(place == last)
        def _():
            share_ref[m, at] = own[m, y, at]
            down_copy(k).start()

    def to_previous(k):
        down_copy(k).wait_recv()

        @pl.when(place > 0)
        def _():
            down_copy(k).start()

    def tick(t):
        @pl.when(t < chunks)
        def _():
            to_across(t)

        b = t - 3 - 2 * place

        @pl.when((b >= 0) & (b < 2 * chunks) & (lax.rem(b, 2) == 0))
        def _():
            to_next(b // 2)

        c = t - 3 - 2 * last - 2 * (last - place)

        @pl.when((place < last) & (c >= 0) & (c < 2 * chunks) & (lax.rem(c, 2) == 0))
        def _():
            to_previous(c // 2)

    def part_copy(j, s):
        return remote(
            part_out.at[j, s - 1], part_in.at[j, s - 1], part_send.at[j, s - 1],
            part_recv.at[j, s - 1], ctx=place - 1,
        )

    def step(j, s, masked):
        keys = keyval_ref[s, 0, j]
        keys_turned = keys.T
        values_turned = keyval_ref[s, 1, j].T
        back_key = jnp.zeros(keys.shape, jnp.float32)
        back_value = jnp.zeros(keys.shape, jnp.float32)
        for g in range(GROUP):
            head = GROUP * j + g
            query = query_ref[head]
            back = back_ref[head]
            if masked:
                row_sums[g] = jnp.sum(wide(back) * wide(mixed_ref[head]), 0, keepdims=True)
            scores = dot(keys_turned, query, 1, 0)
            if masked:
                scores = causal(scores)
            weights = jnp.exp(scores - lse_ref[head])
            back_weights = dot(values_turned, back, 1, 0)
            back_scores = low(weights * (back_weights - row_sums[g]))
            added = dot(keys, back_scores, 1, 0)
            if masked:
                back_total[g] = added
            else:
                back_total[g] += added
            back_key += dot(query, back_scores, 1, 1)
            back_value += dot(back, low(weights), 1, 1)
        parts[j, s, 0] = back_key
        parts[j, s, 1] = back_value

    def hand_on(j):
        for s in range(blocks):
            @pl.when(s <= place)
            def _(s=s):
                @pl.when(place < last)
                def _():
                    pltpu.make_async_copy(
                        part_in.at[j, s], part_in.at[j, s], part_recv.at[j, s]
                    ).wait()
                    for side in range(2):
                        parts[j, s, side] += wide(part_in[j, s, side])

                if s > 0:
                    for side in range(2):
                        part_out[j, s - 1, side] = low(parts[j, s, side])
                    part_copy(j, s).start()
                else:
                    leading = parts[j, 0, 0, :HALF]
                    trailing = parts[j, 0, 0, HALF:]
                    cosine, sine = cosine_ref[...], sine_ref[...]
                    back_keyval_ref[0, j, :HALF] = low(leading * cosine + trailing * sine)
                    back_keyval_ref[0, j, HALF:] = low(trailing * cosine - leading * sine)
                    back_keyval_ref[1, j] = low(parts[j, 0, 1])

    def head_loop(j, carry):
        @pl.when(j < KEYVAL_HEADS)
        def _():
            step(j, 0, True)

        tick(j * blocks)

        def block_loop(s, inner):
            @pl.when((j < KEYVAL_HEADS) & (s <= place))
            def _():
                step(j, s, False)

            tick(j * blocks + s)
            return inner

        lax.fori_loop(1, blocks, block_loop, 0)

        @pl.when(j < KEYVAL_HEADS)
        def _():
            cosine, sine = cosine_ref[...], sine_ref[...]
            for g in range(GROUP):
                leading = back_total[g, :HALF] * SCALE
                trailing = back_total[g, HALF:] * SCALE
                head = GROUP * j + g
                back_query_ref[head, :HALF] = low(leading * cosine + trailing * sine)
                back_query_ref[head, HALF:] = low(trailing * cosine - leading * sine)

        ready = j - (last - place)

        @pl.when((ready >= 0) & (ready < KEYVAL_HEADS))
        def _():
            hand_on(ready)

        return carry

    assert (KEYVAL_HEADS + last) * blocks >= 4 + 4 * last + 2 * (chunks - 1)
    lax.fori_loop(0, KEYVAL_HEADS + last, head_loop, 0)

    for m in range(len(gradients)):
        for r in range(per):
            for half in range(2):
                mate_copy(m, r, half).wait_send()

    def finish(k, carry):
        y_copy(k).wait_send()

        @pl.when(place < last)
        def _():
            up_copy(k).wait_send()

        @pl.when(place > 0)
        def _():
            down_copy(k).wait_send()

        return carry

    lax.fori_loop(0, chunks, finish, 0)

    def finish_parts(j, carry):
        for s in range(1, blocks):
            @pl.when(s <= place)
            def _(s=s):
                part_copy(j, s).wait_send()
        return carry

    lax.fori_loop(0, KEYVAL_HEADS, finish_parts, 0)


def backward_sum(query, keyval, back_mixed, mixed, lse, cosine, sine, gradients):
    blocks, positions = keyval.shape[0], keyval.shape[-1]
    count, rows, columns = gradients[0].shape
    chunks = len(gradients) * rows // CHUNK_ROWS
    area = QUERY_HEADS * positions * positions * blocks
    vmem = pl.BlockSpec(memory_space=pltpu.VMEM)
    dma = pltpu.SemaphoreType.DMA
    share = (len(gradients), rows, columns)
    head = (2, HEAD_WIDTH, positions)
    return pl.pallas_call(
        backward_sum_kernel,
        in_specs=[vmem] * 7 + [pl.BlockSpec(memory_space=pl.ANY)] * 3,
        out_specs=[vmem] * 3,
        out_shape=[
            jax.ShapeDtypeStruct(query.shape, jnp.bfloat16),
            jax.ShapeDtypeStruct((2, KEYVAL_HEADS, HEAD_WIDTH, positions), jnp.bfloat16),
            jax.ShapeDtypeStruct(share, jnp.bfloat16),
        ],
        scratch_shapes=[
            pltpu.VMEM((len(gradients), 2, rows, columns), jnp.bfloat16),
            pltpu.VMEM((len(gradients), 2, rows, columns), jnp.bfloat16),
            pltpu.VMEM(share, jnp.bfloat16),
            pltpu.VMEM(share, jnp.bfloat16),
            pltpu.VMEM((KEYVAL_HEADS, blocks) + head, jnp.float32),
            pltpu.VMEM((KEYVAL_HEADS, blocks - 1) + head, jnp.bfloat16),
            pltpu.VMEM((KEYVAL_HEADS, blocks - 1) + head, jnp.bfloat16),
            pltpu.VMEM((GROUP, HEAD_WIDTH, positions), jnp.float32),
            pltpu.VMEM((GROUP, 1, positions), jnp.float32),
            dma((len(gradients), 2)),
            dma((chunks, 2)), dma((chunks, 2)),
            dma((chunks,)), dma((chunks,)),
            dma((chunks,)), dma((chunks,)),
            dma((chunks,)), dma((chunks,)),
            dma((KEYVAL_HEADS, blocks - 1)), dma((KEYVAL_HEADS, blocks - 1)),
        ],
        compiler_params=pltpu.CompilerParams(
            vmem_limit_bytes=KERNEL_VMEM, collective_id=0, has_side_effects=True
        ),
        cost_estimate=pl.CostEstimate(
            flops=40 * HEAD_WIDTH * area, bytes_accessed=10 * query.size, transcendentals=area
        ),
        name="backward_sum",
    )(query, keyval, back_mixed, mixed, lse, cosine, sine, *gradients)


def gradient_sum_kernel(
    value_ref, share_ref,
    own, mate_in, y_out, y_in, x_out, x_in, z_out, z_in,
    own_sem, mate_send, mate_recv, y_send, y_recv, x_send, x_recv, z_send, z_recv,
    all_send, all_recv, back_send, back_recv,
):
    place = lax.axis_index("ctx")
    blocks = lax.axis_size("ctx")
    rank = lax.axis_index("fsdp")
    side = lax.axis_index("tp")
    core = rank % 2
    y = rank // 2
    mate = rank + 1 - 2 * core
    across = rank + 2 - 4 * y
    rows, columns = share_ref.shape
    chunks = columns // WIDE
    half_rows = rows // 2
    piece = half_rows // blocks

    own_copies = [
        pltpu.make_async_copy(value_ref.at[2 * half + core], own.at[half], own_sem.at[half])
        for half in range(2)
    ]
    for copy in own_copies:
        copy.start()
    greet(fsdp=mate)
    greet(fsdp=across)
    greet(tp=1 - side)
    for d in range(1, blocks):
        greet(ctx=lax.rem(place + d, blocks))
    pl.semaphore_wait(pltpu.get_barrier_semaphore(), 2 + blocks)

    def mate_copy(n, half):
        return remote(
            value_ref.at[2 * half + 1 - core, :, pl.ds(n * WIDE, WIDE)], mate_in.at[n, half],
            mate_send.at[n, half], mate_recv.at[n, half], fsdp=mate,
        )

    def y_copy(n):
        return remote(y_out.at[n], y_in.at[n], y_send.at[n], y_recv.at[n], fsdp=across)

    def x_copy(n):
        other = pl.ds(pl.multiple_of((1 - side) * half_rows, half_rows), half_rows)
        return remote(
            x_out.at[n, other], x_in.at[n], x_send.at[n], x_recv.at[n], tp=1 - side
        )

    def z_copy(n, d):
        target = lax.rem(place + d, blocks)
        at = pl.ds(pl.multiple_of(target * piece, piece), piece)
        return remote(
            z_out.at[n, at], z_in.at[n, d - 1], z_send.at[n, d - 1], z_recv.at[n, d - 1],
            ctx=target,
        )

    def all_copy(n, d, origin):
        at = pl.ds(pl.multiple_of(side * half_rows + origin * piece, piece), piece)
        spot = share_ref.at[at, pl.ds(n * WIDE, WIDE)]
        return remote(
            spot, spot, all_send.at[n, d - 1], all_recv.at[n, d - 1],
            ctx=lax.rem(place + d, blocks),
        )

    def back_copy(n, half):
        at = pl.ds(pl.multiple_of(half * half_rows, half_rows), half_rows)
        spot = share_ref.at[at, pl.ds(n * WIDE, WIDE)]
        return remote(spot, spot, back_send.at[n], back_recv.at[n], tp=1 - side)

    for n in range(chunks):
        for half in range(2):
            mate_copy(n, half).start()
    for copy in own_copies:
        copy.wait()

    def to_y(n):
        for half in range(2):
            mate_copy(n, half).wait_recv()
        at = pl.ds(n * WIDE, WIDE)
        y_out[n] = low(wide(own[1 - y, :, at]) + wide(mate_in[n, 1 - y]))
        y_copy(n).start()

    def to_x(n):
        y_copy(n).wait_recv()
        at = pl.ds(n * WIDE, WIDE)
        x_out[n] = low(wide(own[y, :, at]) + wide(mate_in[n, y]) + wide(y_in[n]))
        x_copy(n).start()

    def to_z(n):
        x_copy(n).wait_recv()
        at = pl.ds(pl.multiple_of(side * half_rows, half_rows), half_rows)
        z_out[n] = low(wide(x_out[n, at]) + wide(x_in[n]))
        for d in range(1, blocks):
            z_copy(n, d).start()

    def to_all(n):
        at = pl.ds(pl.multiple_of(place * piece, piece), piece)
        total = wide(z_out[n, at])
        for d in range(1, blocks):
            z_copy(n, d).wait_recv()
            total += wide(z_in[n, d - 1])
        at = pl.ds(pl.multiple_of(side * half_rows + place * piece, piece), piece)
        share_ref[at, pl.ds(n * WIDE, WIDE)] = low(total)
        for d in range(1, blocks):
            all_copy(n, d, place).start()

    def to_back(n):
        for d in range(1, blocks):
            all_copy(n, d, lax.rem(place + blocks - d, blocks)).wait_recv()
        back_copy(n, side).start()

    def last_wait(n):
        back_copy(n, 1 - side).wait_recv()

    stages = (to_y, to_x, to_z, to_all, to_back, last_wait)
    for t in range(chunks + len(stages) - 1):
        for index in reversed(range(len(stages))):
            if 0 <= t - index < chunks:
                stages[index](t - index)
    for n in range(chunks):
        for half in range(2):
            mate_copy(n, half).wait_send()
        y_copy(n).wait_send()
        x_copy(n).wait_send()
        for d in range(1, blocks):
            z_copy(n, d).wait_send()
            all_copy(n, d, place).wait_send()
        back_copy(n, side).wait_send()


def gradient_sum(value):
    count, rows, columns = value.shape
    blocks = lax.axis_size("ctx")
    chunks = columns // WIDE
    half_rows = rows // 2
    dma = pltpu.SemaphoreType.DMA
    low_type = jnp.bfloat16
    return pl.pallas_call(
        gradient_sum_kernel,
        in_specs=[pl.BlockSpec(memory_space=pl.ANY)],
        out_specs=pl.BlockSpec(memory_space=pltpu.VMEM),
        out_shape=jax.ShapeDtypeStruct((rows, columns), low_type),
        scratch_shapes=[
            pltpu.VMEM((2, rows, columns), low_type),
            pltpu.VMEM((chunks, 2, rows, WIDE), low_type),
            pltpu.VMEM((chunks, rows, WIDE), low_type),
            pltpu.VMEM((chunks, rows, WIDE), low_type),
            pltpu.VMEM((chunks, rows, WIDE), low_type),
            pltpu.VMEM((chunks, half_rows, WIDE), low_type),
            pltpu.VMEM((chunks, half_rows, WIDE), low_type),
            pltpu.VMEM((chunks, blocks - 1, half_rows // blocks, WIDE), low_type),
            dma((2,)),
            dma((chunks, 2)), dma((chunks, 2)),
            dma((chunks,)), dma((chunks,)),
            dma((chunks,)), dma((chunks,)),
            dma((chunks, blocks - 1)), dma((chunks, blocks - 1)),
            dma((chunks, blocks - 1)), dma((chunks, blocks - 1)),
            dma((chunks,)), dma((chunks,)),
        ],
        compiler_params=pltpu.CompilerParams(
            vmem_limit_bytes=KERNEL_VMEM, collective_id=1, has_side_effects=True
        ),
        cost_estimate=pl.CostEstimate(
            flops=value.size, bytes_accessed=4 * value.size, transcendentals=0
        ),
        name="gradient_sum",
    )(value)


def on_device(
    tokens, cotangent, input_gain, w_query, w_keyval, w_output, middle_gain, w_gate, w_up, w_down
):
    half = lax.axis_index("tp")
    low_half = half == 0
    pair = [(0, 1), (1, 0)]

    def to_partner(value_rows):
        return lax.ppermute(value_rows, "tp", pair)

    def in_order(mine, received):
        return jnp.concatenate(
            [jnp.where(low_half, mine, received), jnp.where(low_half, received, mine)], 0
        )

    def take(value_rows, index):
        return lax.dynamic_index_in_dim(value_rows, index, 0, keepdims=False)

    tokens_own = in_order(take(tokens, half), to_partner(take(tokens, 1 - half)))
    full_gain_one, full_gain_two = (
        lax.all_gather(input_gain, "fsdp", axis=0, tiled=True),
        lax.all_gather(middle_gain, "fsdp", axis=0, tiled=True),
    )
    full_in = lax.all_gather(jnp.concatenate([w_query, w_keyval], 1), "fsdp", axis=0, tiled=True)
    full_output = lax.all_gather(w_output, "fsdp", axis=0, tiled=True)
    full_gate = lax.all_gather(w_gate, "fsdp", axis=0, tiled=True)
    full_up = lax.all_gather(w_up, "fsdp", axis=0, tiled=True)
    full_down = lax.all_gather(w_down, "fsdp", axis=0, tiled=True)
    cotangent_received = to_partner(cotangent)
    cotangent_own = in_order(take(cotangent, half), take(cotangent_received, half))
    cotangent_other = in_order(take(cotangent, 1 - half), take(cotangent_received, 1 - half))

    token_positions = tokens_own.shape[0]
    cosine, sine = rope_tables(token_positions, lax.axis_index("ctx") * token_positions)
    gain_one = full_gain_one.astype(jnp.float32)
    inputs = tokens_own.astype(jnp.float32)
    unit_one, inverse_one = normalize(inputs)
    normed_one = (unit_one * gain_one).astype(jnp.bfloat16)
    keyval_raw = dot(full_in[:, QUERY_WIDTH:], normed_one, 0, 1)
    keyval_low = jnp.concatenate(
        [apply_rotary(keyval_raw[:KEY_WIDTH], cosine, sine), keyval_raw[KEY_WIDTH:]], 0
    ).astype(jnp.bfloat16)
    blocks = lax.axis_size("ctx")
    keyval = jnp.stack([keyval_low] + [move_along(keyval_low, s) for s in range(1, blocks)], 0)
    keyval = keyval.reshape(blocks, 2, KEYVAL_HEADS, HEAD_WIDTH, token_positions)
    query_raw = dot(full_in[:, :QUERY_WIDTH], normed_one, 0, 1)
    query_low = (
        apply_rotary(query_raw, cosine, sine)
        .astype(jnp.bfloat16)
        .reshape(QUERY_HEADS, HEAD_WIDTH, token_positions)
    )
    mixed_heads, lse = attend_forward(query_low, keyval)
    mixed_low = mixed_heads.reshape(QUERY_WIDTH, token_positions)
    middle = inputs + dot(mixed_low, full_output, 0, 0)

    gain_two = full_gain_two.astype(jnp.float32)
    unit_two, inverse_two = normalize(middle)
    normed_two = (unit_two * gain_two).astype(jnp.bfloat16)
    normed_other = to_partner(normed_two)

    def feed(rows, back_rows):
        gate_proj = dot(rows, full_gate, 1, 0)
        up_proj = dot(rows, full_up, 1, 0)
        sigmoid_gate = jax.nn.sigmoid(gate_proj)
        swish_gate = gate_proj * sigmoid_gate
        hidden = (swish_gate * up_proj).astype(jnp.bfloat16)
        back_hidden = dot(back_rows, full_down, 1, 0)
        back_gate = (
            back_hidden * up_proj * sigmoid_gate * (1.0 + gate_proj * (1.0 - sigmoid_gate))
        ).astype(jnp.bfloat16)
        back_up = (back_hidden * swish_gate).astype(jnp.bfloat16)
        return (hidden, back_gate, back_up)

    def feed_input_back(back_gate, back_up):
        return dot(back_gate, full_gate, 1, 1) + dot(back_up, full_up, 1, 1)

    hidden_own, back_gate_own, back_up_own = feed(normed_two, cotangent_own)
    hidden_other, back_gate_other, back_up_other = feed(normed_other, cotangent_other)
    back_two_received = to_partner(
        feed_input_back(back_gate_other, back_up_other).astype(jnp.bfloat16)
    )
    back_two = feed_input_back(back_gate_own, back_up_own) + back_two_received.astype(jnp.float32)
    feed_received = to_partner(dot(hidden_other, full_down, 1, 1).astype(jnp.bfloat16))
    result_own = (
        middle + dot(hidden_own, full_down, 1, 1) + feed_received.astype(jnp.float32)
    ).astype(jnp.bfloat16)

    def feed_gradient(left_own, right_own, left_other, right_other):
        gradient = dot(left_own, right_own, 0, 0) + dot(left_other, right_other, 0, 0)
        shared = scatter_sum(gradient.astype(jnp.bfloat16), "fsdp")
        return whole_sum(shared, (("ctx", 2),))

    share_down = feed_gradient(cotangent_own, hidden_own, cotangent_other, hidden_other)
    share_gate = feed_gradient(normed_two, back_gate_own, normed_other, back_gate_other)
    share_up = feed_gradient(normed_two, back_up_own, normed_other, back_up_other)

    grad_gain_two = jnp.sum(back_two * unit_two, axis=0)
    back_middle = cotangent_own.astype(jnp.float32) + norm_back(
        back_two * gain_two, unit_two, inverse_two
    )
    back_attention = back_middle.astype(jnp.bfloat16)
    back_mixed = dot(full_output, back_attention, 1, 1).astype(jnp.bfloat16)
    back_mixed = back_mixed.reshape(query_low.shape)
    grad_output = dot(mixed_low, back_attention, 1, 0).astype(jnp.bfloat16)
    share_output = whole_sum(scatter_sum(grad_output, "fsdp"), (("tp", 1), ("ctx", 2)))

    back_query = []
    back_key = []
    back_value = []
    for first, count in ((0, 3), (3, 2)):
        part_query, part_keyval = attend_backward(
            query_low, keyval, back_mixed, mixed_heads, lse, cosine, sine, first, count
        )
        part_keyval = part_keyval.reshape(blocks, 2 * count * HEAD_WIDTH, token_positions)
        owned = part_keyval[0].astype(jnp.float32)
        for s in range(1, blocks):
            owned += move_along(part_keyval[s], -s).astype(jnp.float32)
        back_query.append(part_query.reshape(-1, token_positions))
        back_key.append(
            apply_rotary(owned[: count * HEAD_WIDTH], cosine, -sine).astype(jnp.bfloat16)
        )
        back_value.append(owned[count * HEAD_WIDTH :].astype(jnp.bfloat16))
    back_in = jnp.concatenate(back_query + back_key + back_value, 0)
    grad_in = dot(normed_one, back_in, 0, 1)
    back_one = dot(back_in, full_in, 0, 1)
    grad_gain_one = jnp.sum(back_one * unit_one, axis=0)
    back_inputs = back_middle + norm_back(back_one * gain_one, unit_one, inverse_one)

    def to_positions(value_rows):
        split = value_rows.reshape(2, token_positions // 2, value_rows.shape[-1])
        received = to_partner(take(split, 1 - half))
        return in_order(take(split, half)[None], received[None])

    result = to_positions(result_own)
    grad_tokens = to_positions(back_inputs.astype(jnp.bfloat16)).astype(jnp.float32)
    gradients = jnp.concatenate([grad_in, grad_gain_one[:, None], grad_gain_two[:, None]], 1)
    share_in = lax.psum(
        lax.psum_scatter(
            gradients.astype(jnp.bfloat16), "fsdp", scatter_dimension=0, tiled=True
        ),
        ("ctx", "tp"),
    ).astype(jnp.float32)
    width = full_in.shape[1]
    return (
        result,
        grad_tokens,
        share_in[:, width],
        share_in[:, :QUERY_WIDTH],
        share_in[:, QUERY_WIDTH:width],
        share_output,
        share_in[:, width + 1],
        share_gate,
        share_up,
        share_down,
    )


def fast_on_device(
    tokens, cotangent, input_gain, w_query, w_keyval, w_output, middle_gain, w_gate, w_up, w_down
):
    half = lax.axis_index("tp")
    low_half = half == 0
    pair = [(0, 1), (1, 0)]

    def to_partner(value_rows):
        return lax.ppermute(value_rows, "tp", pair)

    def in_order(mine, received):
        return jnp.concatenate(
            [jnp.where(low_half, mine, received), jnp.where(low_half, received, mine)], 0
        )

    def take(value_rows, index):
        return lax.dynamic_index_in_dim(value_rows, index, 0, keepdims=False)

    tokens_own = in_order(take(tokens, half), to_partner(take(tokens, 1 - half)))
    full_gain_one, full_gain_two = (
        lax.all_gather(input_gain, "fsdp", axis=0, tiled=True),
        lax.all_gather(middle_gain, "fsdp", axis=0, tiled=True),
    )
    full_in = lax.all_gather(jnp.concatenate([w_query, w_keyval], 1), "fsdp", axis=0, tiled=True)
    full_output = lax.all_gather(w_output, "fsdp", axis=0, tiled=True)
    full_gate = lax.all_gather(w_gate, "fsdp", axis=0, tiled=True)
    full_up = lax.all_gather(w_up, "fsdp", axis=0, tiled=True)
    full_down = lax.all_gather(w_down, "fsdp", axis=0, tiled=True)
    cotangent_received = to_partner(cotangent)
    cotangent_own = in_order(take(cotangent, half), take(cotangent_received, half))
    cotangent_other = in_order(take(cotangent, 1 - half), take(cotangent_received, 1 - half))

    token_positions = tokens_own.shape[0]
    cosine, sine = rope_tables(token_positions, lax.axis_index("ctx") * token_positions)
    gain_one = full_gain_one.astype(jnp.float32)
    inputs = tokens_own.astype(jnp.float32)
    unit_one, inverse_one = normalize(inputs)
    normed_one = (unit_one * gain_one).astype(jnp.bfloat16)
    keyval_raw = dot(full_in[:, QUERY_WIDTH:], normed_one, 0, 1)
    keyval_low = jnp.concatenate(
        [apply_rotary(keyval_raw[:KEY_WIDTH], cosine, sine), keyval_raw[KEY_WIDTH:]], 0
    ).astype(jnp.bfloat16)
    blocks = lax.axis_size("ctx")
    keyval = jnp.stack([keyval_low] + [move_along(keyval_low, s) for s in range(1, blocks)], 0)
    keyval = keyval.reshape(blocks, 2, KEYVAL_HEADS, HEAD_WIDTH, token_positions)
    query_raw = dot(full_in[:, :QUERY_WIDTH], normed_one, 0, 1)
    query_low = (
        (apply_rotary(query_raw, cosine, sine).astype(jnp.bfloat16) * jnp.bfloat16(SCALE))
        .reshape(QUERY_HEADS, HEAD_WIDTH, token_positions)
    )
    mixed_heads, lse = attend_forward(query_low, keyval, True)
    mixed_low = mixed_heads.reshape(QUERY_WIDTH, token_positions)
    middle = inputs + dot(mixed_low, full_output, 0, 0)

    gain_two = full_gain_two.astype(jnp.float32)
    unit_two, inverse_two = normalize(middle)
    normed_two = (unit_two * gain_two).astype(jnp.bfloat16)
    normed_other = to_partner(normed_two)

    def feed(rows, back_rows):
        gate_proj = dot(rows, full_gate, 1, 0)
        up_proj = dot(rows, full_up, 1, 0)
        sigmoid_gate = jax.nn.sigmoid(gate_proj)
        swish_gate = gate_proj * sigmoid_gate
        hidden = (swish_gate * up_proj).astype(jnp.bfloat16)
        back_hidden = dot(back_rows, full_down, 1, 0)
        back_gate = (
            back_hidden * up_proj * sigmoid_gate * (1.0 + gate_proj * (1.0 - sigmoid_gate))
        ).astype(jnp.bfloat16)
        back_up = (back_hidden * swish_gate).astype(jnp.bfloat16)
        return (hidden, back_gate, back_up)

    def feed_input_back(back_gate, back_up):
        return dot(back_gate, full_gate, 1, 1) + dot(back_up, full_up, 1, 1)

    hidden_own, back_gate_own, back_up_own = feed(normed_two, cotangent_own)
    hidden_other, back_gate_other, back_up_other = feed(normed_other, cotangent_other)
    back_two_received = to_partner(
        feed_input_back(back_gate_other, back_up_other).astype(jnp.bfloat16)
    )
    back_two = feed_input_back(back_gate_own, back_up_own) + back_two_received.astype(jnp.float32)
    feed_received = to_partner(dot(hidden_other, full_down, 1, 1).astype(jnp.bfloat16))
    result_own = (
        middle + dot(hidden_own, full_down, 1, 1) + feed_received.astype(jnp.float32)
    ).astype(jnp.bfloat16)

    def feed_gradient(left_own, right_own, left_other, right_other):
        gradient = dot(left_own, right_own, 0, 0) + dot(left_other, right_other, 0, 0)
        return gradient.astype(jnp.bfloat16).reshape(lax.axis_size("fsdp"), -1, gradient.shape[1])

    gradients = (
        feed_gradient(cotangent_own, hidden_own, cotangent_other, hidden_other),
        feed_gradient(normed_two, back_gate_own, normed_other, back_gate_other),
        feed_gradient(normed_two, back_up_own, normed_other, back_up_other),
    )

    grad_gain_two = jnp.sum(back_two * unit_two, axis=0)
    back_middle = cotangent_own.astype(jnp.float32) + norm_back(
        back_two * gain_two, unit_two, inverse_two
    )
    back_attention = back_middle.astype(jnp.bfloat16)
    back_mixed = dot(full_output, back_attention, 1, 1).astype(jnp.bfloat16)
    back_mixed = back_mixed.reshape(query_low.shape)
    grad_output = dot(mixed_low, back_attention, 1, 0).astype(jnp.bfloat16)
    back_query, back_keyval, share = backward_sum(
        query_low, keyval, back_mixed, mixed_heads, lse, cosine, sine, gradients
    )
    back_in = jnp.concatenate(
        [
            back_query.reshape(QUERY_WIDTH, token_positions),
            back_keyval.reshape(2 * KEY_WIDTH, token_positions),
        ],
        0,
    )
    grad_in = dot(normed_one, back_in, 0, 1)
    back_one = dot(back_in, full_in, 0, 1)
    grad_gain_one = jnp.sum(back_one * unit_one, axis=0)
    back_inputs = back_middle + norm_back(back_one * gain_one, unit_one, inverse_one)

    def to_positions(value_rows):
        split = value_rows.reshape(2, token_positions // 2, value_rows.shape[-1])
        received = to_partner(take(split, 1 - half))
        return in_order(take(split, half)[None], received[None])

    result = to_positions(result_own)
    grad_tokens = to_positions(back_inputs.astype(jnp.bfloat16)).astype(jnp.float32)
    parts = lax.axis_size("fsdp")
    rows = grad_output.shape[0] // parts
    width = QUERY_WIDTH + full_in.shape[1]
    gains = jnp.concatenate(
        [grad_gain_one.reshape(parts, rows), grad_gain_two.reshape(parts, rows)], 1
    )
    gains = jnp.pad(gains[:, None], ((0, 0), (0, 15), (0, width - 2 * rows)))
    summed = jnp.concatenate([grad_output, grad_in.astype(jnp.bfloat16)], 1)
    summed = jnp.concatenate(
        [summed.reshape(parts, rows, width), gains.astype(jnp.bfloat16)], 1
    )
    share_in = gradient_sum(summed).astype(jnp.float32)
    return (
        result,
        grad_tokens,
        share_in[rows, :rows],
        share_in[:rows, QUERY_WIDTH : 2 * QUERY_WIDTH],
        share_in[:rows, 2 * QUERY_WIDTH :],
        share_in[:rows, :QUERY_WIDTH],
        share_in[rows, rows : 2 * rows],
        share[1].astype(jnp.float32),
        share[2].astype(jnp.float32),
        share[0].astype(jnp.float32),
    )


def solution(mesh):
    rows = P("fsdp", ("ctx", "tp"), None)
    specs = (
        P("fsdp"), P("fsdp", None), P("fsdp", None), P("fsdp", None),
        P("fsdp"), P("fsdp", "tp"), P("fsdp", "tp"), P("fsdp", "tp"),
    )
    kernels = mesh.shape["fsdp"] == 4 and mesh.shape["tp"] == 2 and mesh.shape["ctx"] == 4
    return jax.shard_map(
        fast_on_device if kernels else on_device,
        mesh=mesh,
        in_specs=(rows, rows) + specs,
        out_specs=(rows, rows) + specs,
        check_vma=False,
    )
```

```python
import jax
import jax.numpy as jnp
from jax import lax
from jax.experimental import pallas as pl
from jax.experimental.pallas import tpu as pltpu
from jax.sharding import PartitionSpec as P

QUERY_HEADS = 15
KEYVAL_HEADS = 5
GROUP = QUERY_HEADS // KEYVAL_HEADS
HEAD_WIDTH = 64
HALF = HEAD_WIDTH // 2
KEY_WIDTH = 320
QUERY_WIDTH = QUERY_HEADS * HEAD_WIDTH
SCALE = HEAD_WIDTH ** (-0.5)

EPS = 1e-05
THETA = 10000.0
VMEM_LIMIT = 40 * 1024 * 1024


def dot(left, right, left_dim, right_dim):
    return lax.dot_general(
        left, right, (((left_dim,), (right_dim,)), ((), ())), preferred_element_type=jnp.float32
    )


def rope_tables(token_positions, first_place):
    position = (first_place + lax.iota(jnp.int32, token_positions)).astype(jnp.float32)
    frequency = THETA ** (-(2.0 * lax.iota(jnp.int32, HALF).astype(jnp.float32)) / HEAD_WIDTH)
    angles = frequency[:, None] * position[None, :]
    return (jnp.cos(angles), jnp.sin(angles))


def apply_rotary(rows, cosine, sine):
    shaped = rows.reshape(-1, 2, HALF, rows.shape[-1])
    leading = shaped[:, 0]
    trailing = shaped[:, 1]
    return jnp.stack(
        [leading * cosine - trailing * sine, trailing * cosine + leading * sine], 1
    ).reshape(rows.shape)


def normalize(value_rows):
    inverse_rms = lax.rsqrt(jnp.mean(value_rows * value_rows, -1, keepdims=True) + EPS)
    return (value_rows * inverse_rms, inverse_rms)


def norm_back(back_unit, unit_rows, inverse_rms):
    return inverse_rms * (
        back_unit - unit_rows * jnp.mean(back_unit * unit_rows, -1, keepdims=True)
    )


def causal(scores):
    key_place = lax.broadcasted_iota(jnp.int32, scores.shape, 0)
    query_place = lax.broadcasted_iota(jnp.int32, scores.shape, 1)
    return jnp.where(key_place <= query_place, scores, -jnp.inf)


def forward_kernel(query_ref, key_ref, value_ref, mixed_ref, lse_ref):
    place = lax.axis_index("ctx")
    queries = [query_ref[g] * jnp.bfloat16(SCALE) for g in range(GROUP)]

    def scores_of(keys_turned, g, masked):
        scores = dot(keys_turned, queries[g], 1, 0)
        return causal(scores) if masked else scores

    def first():
        keys_turned = key_ref[0, 0, 0].T
        values = value_ref[0, 0, 0]
        carried = []
        for g in range(GROUP):
            scores = scores_of(keys_turned, g, True)
            top = jnp.max(scores, 0, keepdims=True)
            lifted = jnp.exp(scores - top)
            total = jnp.sum(lifted, 0, keepdims=True)
            carried += [top, total, dot(values, lifted.astype(jnp.bfloat16), 1, 0)]
        return tuple(carried)

    def step(block, carried):
        keys_turned = key_ref[block, 0, 0].T
        values = value_ref[block, 0, 0]
        later = []
        for g in range(GROUP):
            top, total, mixed = carried[3 * g : 3 * g + 3]
            scores = scores_of(keys_turned, g, False)
            new_top = jnp.maximum(top, jnp.max(scores, 0, keepdims=True))
            lifted = jnp.exp(scores - new_top)
            shrink = jnp.exp(top - new_top)
            later += [
                new_top,
                total * shrink + jnp.sum(lifted, 0, keepdims=True),
                mixed * shrink + dot(values, lifted.astype(jnp.bfloat16), 1, 0),
            ]
        return tuple(later)

    carried = lax.fori_loop(1, place + 1, step, first())
    for g in range(GROUP):
        top, total, mixed = carried[3 * g : 3 * g + 3]
        mixed_ref[g] = (mixed / total).astype(jnp.bfloat16)
        lse_ref[g] = top + jnp.log(total)


def attend_forward(query, keyval):
    blocks, token_positions = keyval.shape[0], keyval.shape[-1]
    head_block = (GROUP, HEAD_WIDTH, token_positions)
    key_block = (blocks, 1, 1, HEAD_WIDTH, token_positions)
    area = QUERY_HEADS * token_positions * token_positions * blocks
    return pl.pallas_call(
        forward_kernel,
        grid=(KEYVAL_HEADS,),
        in_specs=[
            pl.BlockSpec(head_block, lambda j: (j, 0, 0)),
            pl.BlockSpec(key_block, lambda j: (0, 0, j, 0, 0)),
            pl.BlockSpec(key_block, lambda j: (0, 1, j, 0, 0)),
        ],
        out_specs=[
            pl.BlockSpec(head_block, lambda j: (j, 0, 0)),
            pl.BlockSpec((GROUP, 1, token_positions), lambda j: (j, 0, 0)),
        ],
        out_shape=[
            jax.ShapeDtypeStruct(query.shape, jnp.bfloat16),
            jax.ShapeDtypeStruct((QUERY_HEADS, 1, token_positions), jnp.float32),
        ],
        compiler_params=pltpu.CompilerParams(vmem_limit_bytes=VMEM_LIMIT),
        cost_estimate=pl.CostEstimate(
            flops=16 * HEAD_WIDTH * area, bytes_accessed=6 * query.size, transcendentals=area
        ),
        name="attend_forward",
    )(query, keyval, keyval)


def backward_kernel(
    query_ref, key_ref, value_ref, back_ref, mixed_ref, lse_ref, cosine_ref, sine_ref,
    back_query_ref, back_keyval_ref,
):
    place = lax.axis_index("ctx")
    blocks = key_ref.shape[0]
    queries = [query_ref[g] * jnp.bfloat16(SCALE) for g in range(GROUP)]
    backs = [back_ref[g] for g in range(GROUP)]
    tops = [lse_ref[g] for g in range(GROUP)]
    sums = [
        jnp.sum(backs[g].astype(jnp.float32) * mixed_ref[g].astype(jnp.float32), 0, keepdims=True)
        for g in range(GROUP)
    ]

    def step(block, carried, masked=False):
        keys = key_ref[block, 0, 0]
        keys_turned = keys.T
        values_turned = value_ref[block, 0, 0].T
        back_key = jnp.zeros(keys.shape, jnp.float32)
        back_value = jnp.zeros(keys.shape, jnp.float32)
        later = []
        for g in range(GROUP):
            scores = dot(keys_turned, queries[g], 1, 0)
            if masked:
                scores = causal(scores)
            weights = jnp.exp(scores - tops[g])
            back_weights = dot(values_turned, backs[g], 1, 0)
            back_scores = (weights * (back_weights - sums[g])).astype(jnp.bfloat16)
            later.append(carried[g] + dot(keys, back_scores, 1, 0))
            back_key += dot(queries[g], back_scores, 1, 1)
            back_value += dot(backs[g], weights.astype(jnp.bfloat16), 1, 1)
        back_keyval_ref[block, 0, 0] = back_key.astype(jnp.bfloat16)
        back_keyval_ref[block, 1, 0] = back_value.astype(jnp.bfloat16)
        return tuple(later)

    start = tuple(jnp.zeros(query_ref.shape[1:], jnp.float32) for g in range(GROUP))
    carried = lax.fori_loop(1, place + 1, step, step(0, start, True))

    def clear(block, unused):
        zero = jnp.zeros(key_ref.shape[3:], jnp.bfloat16)
        back_keyval_ref[block, 0, 0] = zero
        back_keyval_ref[block, 1, 0] = zero
        return unused

    lax.fori_loop(place + 1, blocks, clear, 0)
    cosine = cosine_ref[...]
    sine = sine_ref[...]
    for g in range(GROUP):
        leading = carried[g][:HALF] * SCALE
        trailing = carried[g][HALF:] * SCALE
        back_query_ref[g, :HALF] = (leading * cosine + trailing * sine).astype(jnp.bfloat16)
        back_query_ref[g, HALF:] = (trailing * cosine - leading * sine).astype(jnp.bfloat16)


def attend_backward(query, keyval, back_mixed, mixed, lse, cosine, sine, first, count):
    blocks, token_positions = keyval.shape[0], keyval.shape[-1]
    head_block = (GROUP, HEAD_WIDTH, token_positions)
    key_block = (blocks, 1, 1, HEAD_WIDTH, token_positions)
    area = count * GROUP * token_positions * token_positions * blocks
    heads = pl.BlockSpec(head_block, lambda j: (j + first, 0, 0))
    table = pl.BlockSpec((HALF, token_positions), lambda j: (0, 0))
    return pl.pallas_call(
        backward_kernel,
        grid=(count,),
        in_specs=[
            heads,
            pl.BlockSpec(key_block, lambda j: (0, 0, j + first, 0, 0)),
            pl.BlockSpec(key_block, lambda j: (0, 1, j + first, 0, 0)),
            heads,
            heads,
            pl.BlockSpec((GROUP, 1, token_positions), lambda j: (j + first, 0, 0)),
            table,
            table,
        ],
        out_specs=[
            pl.BlockSpec(head_block, lambda j: (j, 0, 0)),
            pl.BlockSpec((blocks, 2, 1, HEAD_WIDTH, token_positions), lambda j: (0, 0, j, 0, 0)),
        ],
        out_shape=[
            jax.ShapeDtypeStruct((count * GROUP, HEAD_WIDTH, token_positions), jnp.bfloat16),
            jax.ShapeDtypeStruct(
                (blocks, 2, count, HEAD_WIDTH, token_positions), jnp.bfloat16
            ),
        ],
        compiler_params=pltpu.CompilerParams(vmem_limit_bytes=VMEM_LIMIT),
        cost_estimate=pl.CostEstimate(
            flops=40 * HEAD_WIDTH * area, bytes_accessed=10 * query.size, transcendentals=area
        ),
        name="attend_backward",
    )(query, keyval, keyval, back_mixed, mixed, lse, cosine, sine)


def move_along(value, distance):
    blocks = lax.axis_size("ctx")
    pairs = [(i, i + distance) for i in range(blocks) if 0 <= i + distance < blocks]
    return lax.ppermute(value, "ctx", pairs)


def trade(value, axis, step):
    pairs = [(i, i ^ step) for i in range(lax.axis_size(axis))]
    return lax.ppermute(value, axis, pairs)


def add_low(left, right):
    return (left.astype(jnp.float32) + right.astype(jnp.float32)).astype(jnp.bfloat16)


def scatter_sum(value, axis):
    size = lax.axis_size(axis)
    index = lax.axis_index(axis)
    rows = value.shape[0] // size
    step = 1
    while step < size:
        count = value.shape[0] // (2 * rows)
        split = value.reshape(count, 2, rows, value.shape[-1])
        second = (index // step) % 2 == 1
        kept = jnp.where(second, split[:, 1], split[:, 0])
        sent = jnp.where(second, split[:, 0], split[:, 1])
        value = add_low(kept, trade(sent, axis, step)).reshape(count * rows, value.shape[-1])
        step *= 2
    return value


def whole_sum(value, others):
    half_rows = value.shape[0] // 2
    second = lax.axis_index("ctx") % 2 == 1
    upper, lower = value[:half_rows], value[half_rows:]
    received = trade(jnp.where(second, upper, lower), "ctx", 1)
    total = add_low(jnp.where(second, lower, upper), received)
    for axis, first_step in others:
        step = first_step
        while step < lax.axis_size(axis):
            total = add_low(total, trade(total, axis, step))
            step *= 2
    received = trade(total, "ctx", 1)
    return jnp.concatenate(
        [jnp.where(second, received, total), jnp.where(second, total, received)], 0
    ).astype(jnp.float32)


MESH = pl.DeviceIdType.MESH
KERNEL_VMEM = 58 * 1024 * 1024
CHUNK_ROWS = 80
WIDE = 512


def remote(source, target, send_sem, recv_sem, **place):
    return pltpu.make_async_remote_copy(
        src_ref=source, dst_ref=target, send_sem=send_sem, recv_sem=recv_sem,
        device_id=place, device_id_type=MESH,
    )


def wide(value):
    return value.astype(jnp.float32)


def low(value):
    return value.astype(jnp.bfloat16)


def greet(**place):
    pl.semaphore_signal(
        pltpu.get_barrier_semaphore(), inc=1, device_id=place, device_id_type=MESH
    )


def backward_sum_kernel(
    query_ref, keyval_ref, back_ref, mixed_ref, lse_ref, cosine_ref, sine_ref,
    down_ref, gate_ref, up_ref,
    back_query_ref, back_keyval_ref, share_ref,
    own, mate_in, y_in, up_in, parts, part_out, part_in, back_total, row_sums,
    own_sem, mate_send, mate_recv, y_send, y_recv, up_send, up_recv, down_send, down_recv,
    part_send, part_recv,
):
    place = lax.axis_index("ctx")
    last = lax.axis_size("ctx") - 1
    blocks = last + 1
    rank = lax.axis_index("fsdp")
    core = rank % 2
    y = rank // 2
    mate = rank + 1 - 2 * core
    across = rank + 2 - 4 * y
    gradients = (down_ref, gate_ref, up_ref)
    rows = share_ref.shape[1]
    per = rows // CHUNK_ROWS
    chunks = len(gradients) * per
    early = per

    for m, gradient in enumerate(gradients):
        for half in range(2):
            pltpu.make_async_copy(
                gradient.at[2 * half + core], own.at[m, half], own_sem.at[m, half]
            ).start()
    greet(fsdp=mate)
    greet(fsdp=across)

    @pl.when(place > 0)
    def _():
        greet(ctx=place - 1)

    @pl.when(place < last)
    def _():
        greet(ctx=place + 1)

    neighbours = (place + last - 1) // last + (2 * last - place - 1) // last
    pl.semaphore_wait(pltpu.get_barrier_semaphore(), 2 + neighbours)

    def chunk_at(ref, m, r, *front):
        return ref.at[(m,) + front + (pl.ds(r * CHUNK_ROWS, CHUNK_ROWS),)]

    def mate_copy(m, r, half):
        gradient = gradients[m]
        return remote(
            gradient.at[2 * half + 1 - core, pl.ds(r * CHUNK_ROWS, CHUNK_ROWS)],
            chunk_at(mate_in, m, r, half),
            mate_send.at[m * per + r, half], mate_recv.at[m * per + r, half], fsdp=mate,
        )

    for m in range(len(gradients)):
        for r in range(per):
            for half in range(2):
                mate_copy(m, r, half).start()
    for m, gradient in enumerate(gradients):
        for half in range(2):
            pltpu.make_async_copy(
                gradient.at[2 * half + core], own.at[m, half], own_sem.at[m, half]
            ).wait()

    def split(k):
        r = lax.rem(k, per)
        return k // per, pl.ds(pl.multiple_of(r * CHUNK_ROWS, CHUNK_ROWS), CHUNK_ROWS)

    def y_copy(k):
        m, at = split(k)
        return remote(
            own.at[m, 1 - y, at], y_in.at[m, at], y_send.at[k], y_recv.at[k], fsdp=across
        )

    def up_copy(k):
        m, at = split(k)
        return remote(
            own.at[m, y, at], up_in.at[m, at], up_send.at[k], up_recv.at[k], ctx=place + 1
        )

    def down_copy(k):
        m, at = split(k)
        return remote(
            share_ref.at[m, at], share_ref.at[m, at], down_send.at[k], down_recv.at[k],
            ctx=place - 1,
        )

    def to_across(k):
        m, at = split(k)
        for half in range(2):
            pltpu.make_async_copy(
                mate_in.at[m, half, at], mate_in.at[m, half, at], mate_recv.at[k, half]
            ).wait()
        own[m, 1 - y, at] = low(wide(own[m, 1 - y, at]) + wide(mate_in[m, 1 - y, at]))
        y_copy(k).start()

    def to_next(k):
        m, at = split(k)
        y_copy(k).wait_recv()
        total = wide(own[m, y, at]) + wide(mate_in[m, y, at]) + wide(y_in[m, at])

        @pl.when(place == 0)
        def _():
            own[m, y, at] = low(total)

        @pl.when(place > 0)
        def _():
            up_copy(k).wait_recv()
            own[m, y, at] = low(total + wide(up_in[m, at]))

        @pl.when(place < last)
        def _():
            up_copy(k).start()

        @pl.when(place == last)
        def _():
            share_ref[m, at] = own[m, y, at]

            @pl.when(k < early)
            def _():
                down_copy(k).start()

    def to_previous(k):
        down_copy(k).wait_recv()

        @pl.when(place > 0)
        def _():
            down_copy(k).start()

    def tick(t):
        @pl.when(t < chunks)
        def _():
            to_across(t)

        b = t - 3 - 2 * place

        @pl.when((b >= 0) & (b < 2 * chunks) & (lax.rem(b, 2) == 0))
        def _():
            to_next(b // 2)

        c = t - 3 - 2 * last - 2 * (last - place)

        @pl.when((place < last) & (c >= 0) & (c < 2 * early) & (lax.rem(c, 2) == 0))
        def _():
            to_previous(c // 2)

    def part_copy(j, s):
        return remote(
            part_out.at[j, s - 1], part_in.at[j, s - 1], part_send.at[j, s - 1],
            part_recv.at[j, s - 1], ctx=place - 1,
        )

    def step(j, s, masked):
        keys = keyval_ref[s, j, 0]
        keys_turned = keys.T
        values_turned = keyval_ref[s, j, 1].T
        back_key = jnp.zeros(keys.shape, jnp.float32)
        back_value = jnp.zeros(keys.shape, jnp.float32)
        for g in range(GROUP):
            head = GROUP * j + g
            query = query_ref[head]
            back = back_ref[head]
            if masked:
                row_sums[g] = jnp.sum(wide(back) * wide(mixed_ref[head]), 0, keepdims=True)
            scores = dot(keys_turned, query, 1, 0)
            if masked:
                scores = causal(scores)
            weights = jnp.exp(scores - lse_ref[head])
            back_weights = dot(values_turned, back, 1, 0)
            back_scores = low(weights * (back_weights - row_sums[g]))
            added = dot(keys, back_scores, 1, 0)
            if masked:
                back_total[g] = added
            else:
                back_total[g] += added
            back_key += dot(query, back_scores, 1, 1)
            back_value += dot(back, low(weights), 1, 1)
        parts[j, s, 0] = back_key
        parts[j, s, 1] = back_value

    def hand_on(j):
        for s in range(blocks):
            @pl.when(s <= place)
            def _(s=s):
                @pl.when(place < last)
                def _():
                    pltpu.make_async_copy(
                        part_in.at[j, s], part_in.at[j, s], part_recv.at[j, s]
                    ).wait()
                    for side in range(2):
                        parts[j, s, side] += wide(part_in[j, s, side])

                if s > 0:
                    for side in range(2):
                        part_out[j, s - 1, side] = low(parts[j, s, side])
                    part_copy(j, s).start()
                else:
                    leading = parts[j, 0, 0, :HALF]
                    trailing = parts[j, 0, 0, HALF:]
                    cosine, sine = cosine_ref[...], sine_ref[...]
                    back_keyval_ref[0, j, :HALF] = low(leading * cosine + trailing * sine)
                    back_keyval_ref[0, j, HALF:] = low(trailing * cosine - leading * sine)
                    back_keyval_ref[1, j] = low(parts[j, 0, 1])

    def head_loop(j, carry):
        @pl.when(j < KEYVAL_HEADS)
        def _():
            step(j, 0, True)

        tick(j * blocks)

        def block_loop(s, inner):
            @pl.when((j < KEYVAL_HEADS) & (s <= place))
            def _():
                step(j, s, False)

            tick(j * blocks + s)
            return inner

        lax.fori_loop(1, blocks, block_loop, 0)

        @pl.when(j < KEYVAL_HEADS)
        def _():
            cosine, sine = cosine_ref[...], sine_ref[...]
            for g in range(GROUP):
                leading = back_total[g, :HALF] * SCALE
                trailing = back_total[g, HALF:] * SCALE
                head = GROUP * j + g
                back_query_ref[head, :HALF] = low(leading * cosine + trailing * sine)
                back_query_ref[head, HALF:] = low(trailing * cosine - leading * sine)

        ready = j - (last - place)

        @pl.when((ready >= 0) & (ready < KEYVAL_HEADS))
        def _():
            hand_on(ready)

        return carry

    assert (KEYVAL_HEADS + last) * blocks >= 4 + 4 * last + 2 * (chunks - 1)
    lax.fori_loop(0, KEYVAL_HEADS + last, head_loop, 0)

    for m in range(len(gradients)):
        for r in range(per):
            for half in range(2):
                mate_copy(m, r, half).wait_send()

    def finish(k, carry):
        y_copy(k).wait_send()

        @pl.when(place < last)
        def _():
            up_copy(k).wait_send()

        @pl.when((place > 0) & (k < early))
        def _():
            down_copy(k).wait_send()

        return carry

    lax.fori_loop(0, chunks, finish, 0)

    def finish_parts(j, carry):
        for s in range(1, blocks):
            @pl.when(s <= place)
            def _(s=s):
                part_copy(j, s).wait_send()
        return carry

    lax.fori_loop(0, KEYVAL_HEADS, finish_parts, 0)


def backward_sum(query, keyval, back_mixed, mixed, lse, cosine, sine, gradients):
    blocks, positions = keyval.shape[0], keyval.shape[-1]
    count, rows, columns = gradients[0].shape
    chunks = len(gradients) * rows // CHUNK_ROWS
    area = QUERY_HEADS * positions * positions * blocks
    vmem = pl.BlockSpec(memory_space=pltpu.VMEM)
    dma = pltpu.SemaphoreType.DMA
    share = (len(gradients), rows, columns)
    head = (2, HEAD_WIDTH, positions)
    return pl.pallas_call(
        backward_sum_kernel,
        in_specs=[vmem] * 7 + [pl.BlockSpec(memory_space=pl.ANY)] * 3,
        out_specs=[vmem] * 3,
        out_shape=[
            jax.ShapeDtypeStruct(query.shape, jnp.bfloat16),
            jax.ShapeDtypeStruct((2, KEYVAL_HEADS, HEAD_WIDTH, positions), jnp.bfloat16),
            jax.ShapeDtypeStruct(share, jnp.bfloat16),
        ],
        scratch_shapes=[
            pltpu.VMEM((len(gradients), 2, rows, columns), jnp.bfloat16),
            pltpu.VMEM((len(gradients), 2, rows, columns), jnp.bfloat16),
            pltpu.VMEM(share, jnp.bfloat16),
            pltpu.VMEM(share, jnp.bfloat16),
            pltpu.VMEM((KEYVAL_HEADS, blocks) + head, jnp.float32),
            pltpu.VMEM((KEYVAL_HEADS, blocks - 1) + head, jnp.bfloat16),
            pltpu.VMEM((KEYVAL_HEADS, blocks - 1) + head, jnp.bfloat16),
            pltpu.VMEM((GROUP, HEAD_WIDTH, positions), jnp.float32),
            pltpu.VMEM((GROUP, 1, positions), jnp.float32),
            dma((len(gradients), 2)),
            dma((chunks, 2)), dma((chunks, 2)),
            dma((chunks,)), dma((chunks,)),
            dma((chunks,)), dma((chunks,)),
            dma((rows // CHUNK_ROWS,)), dma((rows // CHUNK_ROWS,)),
            dma((KEYVAL_HEADS, blocks - 1)), dma((KEYVAL_HEADS, blocks - 1)),
        ],
        compiler_params=pltpu.CompilerParams(
            vmem_limit_bytes=KERNEL_VMEM, collective_id=0, has_side_effects=True
        ),
        cost_estimate=pl.CostEstimate(
            flops=40 * HEAD_WIDTH * area, bytes_accessed=10 * query.size, transcendentals=area
        ),
        name="backward_sum",
    )(query, keyval, back_mixed, mixed, lse, cosine, sine, *gradients)


def gradient_sum_kernel(
    value_ref, feed_ref, share_ref, feed_share_ref,
    own, mate_in, y_out, y_in, x_out, x_in, z_out, z_in,
    own_sem, mate_send, mate_recv, y_send, y_recv, x_send, x_recv, z_send, z_recv,
    all_send, all_recv, back_send, back_recv, down_send, down_recv, feed_sem,
):
    place = lax.axis_index("ctx")
    blocks = lax.axis_size("ctx")
    rank = lax.axis_index("fsdp")
    side = lax.axis_index("tp")
    core = rank % 2
    y = rank // 2
    mate = rank + 1 - 2 * core
    across = rank + 2 - 4 * y
    rows, columns = share_ref.shape
    chunks = columns // WIDE
    half_rows = rows // 2
    piece = half_rows // blocks

    own_copies = [
        pltpu.make_async_copy(value_ref.at[2 * half + core], own.at[half], own_sem.at[half])
        for half in range(2)
    ]
    for copy in own_copies:
        copy.start()
    greet(fsdp=mate)
    greet(fsdp=across)
    greet(tp=1 - side)
    for d in range(1, blocks):
        greet(ctx=lax.rem(place + d, blocks))
    pl.semaphore_wait(pltpu.get_barrier_semaphore(), 2 + blocks)

    def mate_copy(n, half):
        return remote(
            value_ref.at[2 * half + 1 - core, :, pl.ds(n * WIDE, WIDE)], mate_in.at[n, half],
            mate_send.at[n, half], mate_recv.at[n, half], fsdp=mate,
        )

    def y_copy(n):
        return remote(y_out.at[n], y_in.at[n], y_send.at[n], y_recv.at[n], fsdp=across)

    def x_copy(n):
        other = pl.ds(pl.multiple_of((1 - side) * half_rows, half_rows), half_rows)
        return remote(
            x_out.at[n, other], x_in.at[n], x_send.at[n], x_recv.at[n], tp=1 - side
        )

    def z_copy(n, d):
        target = lax.rem(place + d, blocks)
        at = pl.ds(pl.multiple_of(target * piece, piece), piece)
        return remote(
            z_out.at[n, at], z_in.at[n, d - 1], z_send.at[n, d - 1], z_recv.at[n, d - 1],
            ctx=target,
        )

    def all_copy(n, d, origin):
        at = pl.ds(pl.multiple_of(side * half_rows + origin * piece, piece), piece)
        spot = share_ref.at[at, pl.ds(n * WIDE, WIDE)]
        return remote(
            spot, spot, all_send.at[n, d - 1], all_recv.at[n, d - 1],
            ctx=lax.rem(place + d, blocks),
        )

    def back_copy(n, half):
        at = pl.ds(pl.multiple_of(half * half_rows, half_rows), half_rows)
        spot = share_ref.at[at, pl.ds(n * WIDE, WIDE)]
        return remote(spot, spot, back_send.at[n], back_recv.at[n], tp=1 - side)

    last = blocks - 1
    per = feed_ref.shape[1] // CHUNK_ROWS
    returned = feed_share_ref.shape[0] * per

    def feed_at(ref, k, skip):
        return ref.at[k // per + skip, pl.ds(k % per * CHUNK_ROWS, CHUNK_ROWS)]

    def down_copy(k, source):
        return remote(
            source, feed_at(feed_share_ref, k, 0), down_send.at[k], down_recv.at[k],
            ctx=place - 1,
        )

    feed_copy = pltpu.make_async_copy(feed_ref.at[pl.ds(1, 2)], feed_share_ref, feed_sem)

    def to_previous(k):
        down_copy(k, feed_at(feed_share_ref, k, 0)).wait_recv()

        @pl.when(place > 0)
        def _():
            down_copy(k, feed_at(feed_share_ref, k, 0)).start()

    for n in range(chunks):
        for half in range(2):
            mate_copy(n, half).start()

    @pl.when(place == last)
    def _():
        for k in range(returned):
            down_copy(k, feed_at(feed_ref, k, 1)).start()
        feed_copy.start()

    for copy in own_copies:
        copy.wait()

    def to_y(n):
        for half in range(2):
            mate_copy(n, half).wait_recv()
        at = pl.ds(n * WIDE, WIDE)
        y_out[n] = low(wide(own[1 - y, :, at]) + wide(mate_in[n, 1 - y]))
        y_copy(n).start()

    def to_x(n):
        y_copy(n).wait_recv()
        at = pl.ds(n * WIDE, WIDE)
        x_out[n] = low(wide(own[y, :, at]) + wide(mate_in[n, y]) + wide(y_in[n]))
        x_copy(n).start()

    def to_z(n):
        x_copy(n).wait_recv()
        at = pl.ds(pl.multiple_of(side * half_rows, half_rows), half_rows)
        z_out[n] = low(wide(x_out[n, at]) + wide(x_in[n]))
        for d in range(1, blocks):
            z_copy(n, d).start()

    def to_all(n):
        at = pl.ds(pl.multiple_of(place * piece, piece), piece)
        total = wide(z_out[n, at])
        for d in range(1, blocks):
            z_copy(n, d).wait_recv()
            total += wide(z_in[n, d - 1])
        at = pl.ds(pl.multiple_of(side * half_rows + place * piece, piece), piece)
        share_ref[at, pl.ds(n * WIDE, WIDE)] = low(total)
        for d in range(1, blocks):
            all_copy(n, d, place).start()

    def to_back(n):
        for d in range(1, blocks):
            all_copy(n, d, lax.rem(place + blocks - d, blocks)).wait_recv()
        back_copy(n, side).start()

    def last_wait(n):
        back_copy(n, 1 - side).wait_recv()

    stages = (to_y, to_x, to_z, to_all, to_back, last_wait)
    for t in range(max(chunks + len(stages), returned + last) - 1):
        for index in reversed(range(len(stages))):
            if 0 <= t - index < chunks:
                stages[index](t - index)
        for index in range(last):
            if 0 <= t - last + 1 + index < returned:
                @pl.when(place == index)
                def _(k=t - last + 1 + index):
                    to_previous(k)

    @pl.when(place == last)
    def _():
        feed_copy.wait()

    @pl.when(place > 0)
    def _():
        for k in range(returned):
            down_copy(k, feed_at(feed_ref, k, 1)).wait_send()

    for n in range(chunks):
        for half in range(2):
            mate_copy(n, half).wait_send()
        y_copy(n).wait_send()
        x_copy(n).wait_send()
        for d in range(1, blocks):
            z_copy(n, d).wait_send()
            all_copy(n, d, place).wait_send()
        back_copy(n, side).wait_send()


def gradient_sum(value, feed):
    count, rows, columns = value.shape
    returned = (feed.shape[0] - 1) * feed.shape[1] // CHUNK_ROWS
    blocks = lax.axis_size("ctx")
    chunks = columns // WIDE
    half_rows = rows // 2
    dma = pltpu.SemaphoreType.DMA
    low_type = jnp.bfloat16
    return pl.pallas_call(
        gradient_sum_kernel,
        in_specs=[pl.BlockSpec(memory_space=pl.ANY)] * 2,
        out_specs=[pl.BlockSpec(memory_space=pltpu.VMEM)] * 2,
        out_shape=[
            jax.ShapeDtypeStruct((rows, columns), low_type),
            jax.ShapeDtypeStruct((feed.shape[0] - 1,) + feed.shape[1:], low_type),
        ],
        scratch_shapes=[
            pltpu.VMEM((2, rows, columns), low_type),
            pltpu.VMEM((chunks, 2, rows, WIDE), low_type),
            pltpu.VMEM((chunks, rows, WIDE), low_type),
            pltpu.VMEM((chunks, rows, WIDE), low_type),
            pltpu.VMEM((chunks, rows, WIDE), low_type),
            pltpu.VMEM((chunks, half_rows, WIDE), low_type),
            pltpu.VMEM((chunks, half_rows, WIDE), low_type),
            pltpu.VMEM((chunks, blocks - 1, half_rows // blocks, WIDE), low_type),
            dma((2,)),
            dma((chunks, 2)), dma((chunks, 2)),
            dma((chunks,)), dma((chunks,)),
            dma((chunks,)), dma((chunks,)),
            dma((chunks, blocks - 1)), dma((chunks, blocks - 1)),
            dma((chunks, blocks - 1)), dma((chunks, blocks - 1)),
            dma((chunks,)), dma((chunks,)),
            dma((returned,)), dma((returned,)), dma,
        ],
        compiler_params=pltpu.CompilerParams(
            vmem_limit_bytes=KERNEL_VMEM, collective_id=1, has_side_effects=True
        ),
        cost_estimate=pl.CostEstimate(
            flops=value.size, bytes_accessed=4 * value.size, transcendentals=0
        ),
        name="gradient_sum",
    )(value, feed)


def front_kernel(
    tokens_ref, cotangent_ref, gains_ref, cosine_ref, sine_ref, *refs
):
    weights, refs = refs[:6], refs[6:]
    (
        tokens_own, cotangent_own, cotangent_other, gains_out, normed_out, query_out, keyval_ref,
        mixed_out, lse_ref,
    ), refs = refs[:9], refs[9:]
    full, refs = refs[:6], refs[6:]
    (
        gain_in, raw, tops, totals, sums,
        local_sem, gain_send, gain_recv, token_send, token_recv, cot_send, cot_recv,
        y_send, y_recv, mate_send, mate_recv, pass_send, pass_recv, key_send, key_recv,
    ) = refs
    place = lax.axis_index("ctx")
    last = lax.axis_size("ctx") - 1
    rank = lax.axis_index("fsdp")
    side = lax.axis_index("tp")
    core = rank % 2
    mate = rank + 1 - 2 * core
    across = rank + 2 - 4 * (rank // 2)
    part_rows = tokens_ref.shape[1]

    local = [
        pltpu.make_async_copy(tokens_ref.at[side], tokens_own.at[side], local_sem.at[0]),
        pltpu.make_async_copy(cotangent_ref.at[side], cotangent_own.at[side], local_sem.at[1]),
        pltpu.make_async_copy(
            cotangent_ref.at[1 - side], cotangent_other.at[side], local_sem.at[2]
        ),
    ]
    for w in range(len(weights)):
        local.append(pltpu.make_async_copy(weights[w], full[w].at[rank], local_sem.at[3 + w]))
    for copy in local:
        copy.start()

    greet(fsdp=mate)
    greet(fsdp=across)
    greet(tp=1 - side)

    @pl.when(place > 0)
    def _():
        greet(ctx=place - 1)

    @pl.when(place < last)
    def _():
        greet(ctx=place + 1)

    neighbours = (place + last - 1) // last + (2 * last - place - 1) // last
    pl.semaphore_wait(pltpu.get_barrier_semaphore(), 3 + neighbours)

    gain_mate = remote(
        gains_ref, gain_in.at[0], gain_send.at[0], gain_recv.at[0], fsdp=mate
    )
    gain_across = remote(
        gain_in.at[2], gain_in.at[1], gain_send.at[1], gain_recv.at[1], fsdp=across
    )
    token_copy = remote(
        tokens_ref.at[1 - side], tokens_own.at[side], token_send, token_recv, tp=1 - side
    )
    cot_copies = [
        remote(
            cotangent_ref.at[1 - side], cotangent_own.at[side], cot_send.at[0], cot_recv.at[0],
            tp=1 - side,
        ),
        remote(
            cotangent_ref.at[side], cotangent_other.at[side], cot_send.at[1], cot_recv.at[1],
            tp=1 - side,
        ),
    ]

    def y_copy(w):
        return remote(
            weights[w], full[w].at[rank], y_send.at[w], y_recv.at[w], fsdp=across
        )

    def mate_copy(w):
        return remote(
            weights[w], full[w].at[rank], mate_send.at[w], mate_recv.at[w], fsdp=mate
        )

    def pass_copy(w):
        return remote(
            full[w].at[across], full[w].at[across], pass_send.at[w], pass_recv.at[w], fsdp=mate
        )

    gain_mate.start()
    token_copy.start()
    for w in (1, 0):
        y_copy(w).start()
        mate_copy(w).start()
    gain_mate.wait_recv()
    gain_in[2] = gains_ref[...] + gain_in[0]
    gain_across.start()
    gain_across.wait_recv()
    gains = gain_in[1] + gain_in[2]
    gains_out[...] = gains
    gain = wide(gains[:1])

    def norm_rows(slot):
        rows = wide(tokens_own[slot])
        unit, inverse = normalize(rows)
        normed_out[slot] = low(unit * gain)

    local[0].wait()
    norm_rows(side)
    token_copy.wait_recv()
    norm_rows(1 - side)
    for copy in cot_copies:
        copy.start()
    for w in (1, 0):
        y_copy(w).wait_recv()
        pass_copy(w).start()
    for w in range(2, len(weights)):
        y_copy(w).start()
        mate_copy(w).start()
    normed = normed_out[...].reshape(2 * part_rows, -1)
    cosine, sine = cosine_ref[...], sine_ref[...]

    def turned(value, target):
        target[:HALF] = low(value[:HALF] * cosine - value[HALF:] * sine)
        target[HALF:] = low(value[HALF:] * cosine + value[:HALF] * sine)

    def key_copy(s, j):
        return remote(
            keyval_ref.at[s, j], keyval_ref.at[s + 1, j], key_send.at[s, j], key_recv.at[s, j],
            ctx=place + 1,
        )

    def arrived(w):
        local[3 + w].wait()
        mate_copy(w).wait_recv()
        pass_copy(w).wait_recv()

    arrived(1)
    matrix = full[1][...].reshape(-1, 2 * KEY_WIDTH)
    raw[: 2 * KEY_WIDTH] = dot(matrix, normed, 0, 1)
    for j in range(KEYVAL_HEADS):
        turned(raw[j * HEAD_WIDTH : (j + 1) * HEAD_WIDTH], keyval_ref.at[0, j, 0])
        first = KEY_WIDTH + j * HEAD_WIDTH
        keyval_ref[0, j, 1] = low(raw[first : first + HEAD_WIDTH])

        @pl.when(place < last)
        def _(j=j):
            key_copy(0, j).start()

    arrived(0)
    matrix = full[0][...].reshape(-1, QUERY_WIDTH)
    raw[...] = dot(matrix, normed, 0, 1)

    def turn_query(h, carry):
        value = raw[pl.ds(pl.multiple_of(h * HEAD_WIDTH, HEAD_WIDTH), HEAD_WIDTH)]
        first = low(value[:HALF] * cosine - value[HALF:] * sine)
        second = low(value[HALF:] * cosine + value[:HALF] * sine)
        query_out[h, :HALF] = first * jnp.bfloat16(SCALE)
        query_out[h, HALF:] = second * jnp.bfloat16(SCALE)
        return carry

    lax.fori_loop(0, QUERY_HEADS, turn_query, 0)

    def attend(s, j, masked):
        keys_turned = keyval_ref[s, j, 0].T
        values = keyval_ref[s, j, 1]
        for g in range(GROUP):
            head = GROUP * j + g
            scores = dot(keys_turned, query_out[head], 1, 0)
            if masked:
                scores = causal(scores)
                top = jnp.max(scores, 0, keepdims=True)
                lifted = jnp.exp(scores - top)
                tops[head] = top
                totals[head] = jnp.sum(lifted, 0, keepdims=True)
                sums[head] = dot(values, low(lifted), 1, 0)
            else:
                old = tops[head]
                top = jnp.maximum(old, jnp.max(scores, 0, keepdims=True))
                lifted = jnp.exp(scores - top)
                shrink = jnp.exp(old - top)
                tops[head] = top
                totals[head] = totals[head] * shrink + jnp.sum(lifted, 0, keepdims=True)
                sums[head] = sums[head] * shrink + dot(values, low(lifted), 1, 0)

    def hand_on(s, j):
        @pl.when(s < place)
        def _():
            pltpu.make_async_copy(
                keyval_ref.at[s + 1, j], keyval_ref.at[s + 1, j], key_recv.at[s, j]
            ).wait()

            @pl.when(place < last)
            def _():
                key_copy(s + 1, j).start()

    def first_block(j, carry):
        attend(0, j, True)
        hand_on(0, j)
        return carry

    lax.fori_loop(0, KEYVAL_HEADS, first_block, 0)
    passed = 2

    def later_block(i, carry):
        s = 1 + i // KEYVAL_HEADS
        j = lax.rem(i, KEYVAL_HEADS)
        attend(s, j, False)
        hand_on(s, j)
        return carry

    lax.fori_loop(0, place * KEYVAL_HEADS, later_block, 0)

    def divide(h, carry):
        total = totals[h]
        mixed_out[h] = low(sums[h] / total)
        lse_ref[h] = tops[h] + jnp.log(total)
        return carry

    lax.fori_loop(0, QUERY_HEADS, divide, 0)

    for w in range(passed, len(weights)):
        y_copy(w).wait_recv()
        pass_copy(w).start()
    local[1].wait()
    local[2].wait()
    gain_mate.wait_send()
    gain_across.wait_send()
    token_copy.wait_send()
    for copy in cot_copies:
        copy.wait()
    for w in range(passed, len(weights)):
        arrived(w)
    for w in range(len(weights)):
        y_copy(w).wait_send()
        mate_copy(w).wait_send()
        pass_copy(w).wait_send()

    @pl.when(place < last)
    def _():
        def sent(i, carry):
            key_copy(i // KEYVAL_HEADS, lax.rem(i, KEYVAL_HEADS)).wait_send()
            return carry

        lax.fori_loop(0, (place + 1) * KEYVAL_HEADS, sent, 0)


def front(tokens, cotangent, gains, cosine, sine, weights):
    blocks = lax.axis_size("ctx")
    parts = lax.axis_size("fsdp")
    positions = cosine.shape[-1]
    vmem = pl.BlockSpec(memory_space=pltpu.VMEM)
    anywhere = pl.BlockSpec(memory_space=pl.ANY)
    dma = pltpu.SemaphoreType.DMA
    shape = lambda *dims: jax.ShapeDtypeStruct(dims, jnp.bfloat16)
    count = len(weights)
    area = QUERY_HEADS * positions * positions * blocks
    return pl.pallas_call(
        front_kernel,
        in_specs=[anywhere, anywhere, vmem, vmem, vmem] + [anywhere] * count,
        out_specs=[vmem, anywhere, anywhere] + [vmem] * 6 + [vmem] * 2 + [anywhere] * 4,
        out_shape=[
            shape(*tokens.shape), shape(*tokens.shape), shape(*tokens.shape),
            shape(*gains.shape), shape(*tokens.shape),
            shape(QUERY_HEADS, HEAD_WIDTH, positions),
            shape(blocks, KEYVAL_HEADS, 2, HEAD_WIDTH, positions),
            shape(QUERY_HEADS, HEAD_WIDTH, positions),
            jax.ShapeDtypeStruct((QUERY_HEADS, 1, positions), jnp.float32),
        ] + [shape(parts, *w.shape) for w in weights],
        scratch_shapes=[
            pltpu.VMEM((3,) + gains.shape, jnp.bfloat16),
            pltpu.VMEM((QUERY_WIDTH, positions), jnp.float32),
            pltpu.VMEM((QUERY_HEADS, 1, positions), jnp.float32),
            pltpu.VMEM((QUERY_HEADS, 1, positions), jnp.float32),
            pltpu.VMEM((QUERY_HEADS, HEAD_WIDTH, positions), jnp.float32),
            dma((3 + count,)),
            dma((2,)), dma((2,)),
            dma, dma,
            dma((2,)), dma((2,)),
            dma((count,)), dma((count,)),
            dma((count,)), dma((count,)),
            dma((count,)), dma((count,)),
            dma((blocks, KEYVAL_HEADS)), dma((blocks, KEYVAL_HEADS)),
        ],
        compiler_params=pltpu.CompilerParams(
            vmem_limit_bytes=KERNEL_VMEM, collective_id=2, has_side_effects=True
        ),
        cost_estimate=pl.CostEstimate(
            flops=16 * HEAD_WIDTH * area, bytes_accessed=10 * tokens.size, transcendentals=area
        ),
        name="front",
    )(tokens, cotangent, gains, cosine, sine, *weights)


def on_device(
    tokens, cotangent, input_gain, w_query, w_keyval, w_output, middle_gain, w_gate, w_up, w_down
):
    half = lax.axis_index("tp")
    low_half = half == 0
    pair = [(0, 1), (1, 0)]

    def to_partner(value_rows):
        return lax.ppermute(value_rows, "tp", pair)

    def in_order(mine, received):
        return jnp.concatenate(
            [jnp.where(low_half, mine, received), jnp.where(low_half, received, mine)], 0
        )

    def take(value_rows, index):
        return lax.dynamic_index_in_dim(value_rows, index, 0, keepdims=False)

    tokens_own = in_order(take(tokens, half), to_partner(take(tokens, 1 - half)))
    full_gain_one, full_gain_two = (
        lax.all_gather(input_gain, "fsdp", axis=0, tiled=True),
        lax.all_gather(middle_gain, "fsdp", axis=0, tiled=True),
    )
    full_in = lax.all_gather(jnp.concatenate([w_query, w_keyval], 1), "fsdp", axis=0, tiled=True)
    full_output = lax.all_gather(w_output, "fsdp", axis=0, tiled=True)
    full_gate = lax.all_gather(w_gate, "fsdp", axis=0, tiled=True)
    full_up = lax.all_gather(w_up, "fsdp", axis=0, tiled=True)
    full_down = lax.all_gather(w_down, "fsdp", axis=0, tiled=True)
    cotangent_received = to_partner(cotangent)
    cotangent_own = in_order(take(cotangent, half), take(cotangent_received, half))
    cotangent_other = in_order(take(cotangent, 1 - half), take(cotangent_received, 1 - half))

    token_positions = tokens_own.shape[0]
    cosine, sine = rope_tables(token_positions, lax.axis_index("ctx") * token_positions)
    gain_one = full_gain_one.astype(jnp.float32)
    inputs = tokens_own.astype(jnp.float32)
    unit_one, inverse_one = normalize(inputs)
    normed_one = (unit_one * gain_one).astype(jnp.bfloat16)
    keyval_raw = dot(full_in[:, QUERY_WIDTH:], normed_one, 0, 1)
    keyval_low = jnp.concatenate(
        [apply_rotary(keyval_raw[:KEY_WIDTH], cosine, sine), keyval_raw[KEY_WIDTH:]], 0
    ).astype(jnp.bfloat16)
    blocks = lax.axis_size("ctx")
    keyval = jnp.stack([keyval_low] + [move_along(keyval_low, s) for s in range(1, blocks)], 0)
    keyval = keyval.reshape(blocks, 2, KEYVAL_HEADS, HEAD_WIDTH, token_positions)
    query_raw = dot(full_in[:, :QUERY_WIDTH], normed_one, 0, 1)
    query_low = (
        apply_rotary(query_raw, cosine, sine)
        .astype(jnp.bfloat16)
        .reshape(QUERY_HEADS, HEAD_WIDTH, token_positions)
    )
    mixed_heads, lse = attend_forward(query_low, keyval)
    mixed_low = mixed_heads.reshape(QUERY_WIDTH, token_positions)
    middle = inputs + dot(mixed_low, full_output, 0, 0)

    gain_two = full_gain_two.astype(jnp.float32)
    unit_two, inverse_two = normalize(middle)
    normed_two = (unit_two * gain_two).astype(jnp.bfloat16)
    normed_other = to_partner(normed_two)

    def feed(rows, back_rows):
        gate_proj = dot(rows, full_gate, 1, 0)
        up_proj = dot(rows, full_up, 1, 0)
        sigmoid_gate = jax.nn.sigmoid(gate_proj)
        swish_gate = gate_proj * sigmoid_gate
        hidden = (swish_gate * up_proj).astype(jnp.bfloat16)
        back_hidden = dot(back_rows, full_down, 1, 0)
        back_gate = (
            back_hidden * up_proj * sigmoid_gate * (1.0 + gate_proj * (1.0 - sigmoid_gate))
        ).astype(jnp.bfloat16)
        back_up = (back_hidden * swish_gate).astype(jnp.bfloat16)
        return (hidden, back_gate, back_up)

    def feed_input_back(back_gate, back_up):
        return dot(back_gate, full_gate, 1, 1) + dot(back_up, full_up, 1, 1)

    hidden_own, back_gate_own, back_up_own = feed(normed_two, cotangent_own)
    hidden_other, back_gate_other, back_up_other = feed(normed_other, cotangent_other)
    back_two_received = to_partner(
        feed_input_back(back_gate_other, back_up_other).astype(jnp.bfloat16)
    )
    back_two = feed_input_back(back_gate_own, back_up_own) + back_two_received.astype(jnp.float32)
    feed_received = to_partner(dot(hidden_other, full_down, 1, 1).astype(jnp.bfloat16))
    result_own = (
        middle + dot(hidden_own, full_down, 1, 1) + feed_received.astype(jnp.float32)
    ).astype(jnp.bfloat16)

    def feed_gradient(left_own, right_own, left_other, right_other):
        gradient = dot(left_own, right_own, 0, 0) + dot(left_other, right_other, 0, 0)
        shared = scatter_sum(gradient.astype(jnp.bfloat16), "fsdp")
        return whole_sum(shared, (("ctx", 2),))

    share_down = feed_gradient(cotangent_own, hidden_own, cotangent_other, hidden_other)
    share_gate = feed_gradient(normed_two, back_gate_own, normed_other, back_gate_other)
    share_up = feed_gradient(normed_two, back_up_own, normed_other, back_up_other)

    grad_gain_two = jnp.sum(back_two * unit_two, axis=0)
    back_middle = cotangent_own.astype(jnp.float32) + norm_back(
        back_two * gain_two, unit_two, inverse_two
    )
    back_attention = back_middle.astype(jnp.bfloat16)
    back_mixed = dot(full_output, back_attention, 1, 1).astype(jnp.bfloat16)
    back_mixed = back_mixed.reshape(query_low.shape)
    grad_output = dot(mixed_low, back_attention, 1, 0).astype(jnp.bfloat16)
    share_output = whole_sum(scatter_sum(grad_output, "fsdp"), (("tp", 1), ("ctx", 2)))

    back_query = []
    back_key = []
    back_value = []
    for first, count in ((0, 3), (3, 2)):
        part_query, part_keyval = attend_backward(
            query_low, keyval, back_mixed, mixed_heads, lse, cosine, sine, first, count
        )
        part_keyval = part_keyval.reshape(blocks, 2 * count * HEAD_WIDTH, token_positions)
        owned = part_keyval[0].astype(jnp.float32)
        for s in range(1, blocks):
            owned += move_along(part_keyval[s], -s).astype(jnp.float32)
        back_query.append(part_query.reshape(-1, token_positions))
        back_key.append(
            apply_rotary(owned[: count * HEAD_WIDTH], cosine, -sine).astype(jnp.bfloat16)
        )
        back_value.append(owned[count * HEAD_WIDTH :].astype(jnp.bfloat16))
    back_in = jnp.concatenate(back_query + back_key + back_value, 0)
    grad_in = dot(normed_one, back_in, 0, 1)
    back_one = dot(back_in, full_in, 0, 1)
    grad_gain_one = jnp.sum(back_one * unit_one, axis=0)
    back_inputs = back_middle + norm_back(back_one * gain_one, unit_one, inverse_one)

    def to_positions(value_rows):
        split = value_rows.reshape(2, token_positions // 2, value_rows.shape[-1])
        received = to_partner(take(split, 1 - half))
        return in_order(take(split, half)[None], received[None])

    result = to_positions(result_own)
    grad_tokens = to_positions(back_inputs.astype(jnp.bfloat16)).astype(jnp.float32)
    gradients = jnp.concatenate([grad_in, grad_gain_one[:, None], grad_gain_two[:, None]], 1)
    share_in = lax.psum(
        lax.psum_scatter(
            gradients.astype(jnp.bfloat16), "fsdp", scatter_dimension=0, tiled=True
        ),
        ("ctx", "tp"),
    ).astype(jnp.float32)
    width = full_in.shape[1]
    return (
        result,
        grad_tokens,
        share_in[:, width],
        share_in[:, :QUERY_WIDTH],
        share_in[:, QUERY_WIDTH:width],
        share_output,
        share_in[:, width + 1],
        share_gate,
        share_up,
        share_down,
    )


def fast_on_device(
    tokens, cotangent, input_gain, w_query, w_keyval, w_output, middle_gain, w_gate, w_up, w_down
):
    half = lax.axis_index("tp")
    low_half = half == 0
    pair = [(0, 1), (1, 0)]

    def to_partner(value_rows):
        return lax.ppermute(value_rows, "tp", pair)

    def in_order(mine, received):
        return jnp.concatenate(
            [jnp.where(low_half, mine, received), jnp.where(low_half, received, mine)], 0
        )

    def take(value_rows, index):
        return lax.dynamic_index_in_dim(value_rows, index, 0, keepdims=False)

    parts = lax.axis_size("fsdp")
    width_in = tokens.shape[-1]
    rows = width_in // parts
    token_positions = 2 * tokens.shape[1]
    cosine, sine = rope_tables(token_positions, lax.axis_index("ctx") * token_positions)
    gains = lax.dynamic_update_slice(
        jnp.zeros((16, width_in), jnp.bfloat16), jnp.stack([input_gain, middle_gain]),
        (0, lax.axis_index("fsdp") * rows),
    )
    (
        tokens_own, cotangent_own, cotangent_other, gains, normed_one, query_low, keyval,
        mixed_heads, lse, *full,
    ) = front(
        tokens, cotangent, gains, cosine, sine,
        (w_query, w_keyval, w_output, w_gate, w_up, w_down),
    )
    full_query, full_keyval, full_output, full_gate, full_up, full_down = [
        w.reshape(width_in, -1) for w in full
    ]
    tokens_own, cotangent_own, cotangent_other, normed_one = [
        v.reshape(token_positions, width_in)
        for v in (tokens_own, cotangent_own, cotangent_other, normed_one)
    ]
    gain_one = gains[0].astype(jnp.float32)
    full_gain_two = gains[1]
    inputs = tokens_own.astype(jnp.float32)
    unit_one, inverse_one = normalize(inputs)
    mixed_low = mixed_heads.reshape(QUERY_WIDTH, token_positions)
    middle = inputs + dot(mixed_low, full_output, 0, 0)

    gain_two = full_gain_two.astype(jnp.float32)
    unit_two, inverse_two = normalize(middle)
    normed_two = (unit_two * gain_two).astype(jnp.bfloat16)
    normed_other = to_partner(normed_two)

    def feed(rows, back_rows):
        gate_proj = dot(rows, full_gate, 1, 0)
        up_proj = dot(rows, full_up, 1, 0)
        sigmoid_gate = jax.nn.sigmoid(gate_proj)
        swish_gate = gate_proj * sigmoid_gate
        hidden = (swish_gate * up_proj).astype(jnp.bfloat16)
        back_hidden = dot(back_rows, full_down, 1, 0)
        back_gate = (
            back_hidden * up_proj * sigmoid_gate * (1.0 + gate_proj * (1.0 - sigmoid_gate))
        ).astype(jnp.bfloat16)
        back_up = (back_hidden * swish_gate).astype(jnp.bfloat16)
        return (hidden, back_gate, back_up)

    def feed_input_back(back_gate, back_up):
        return dot(back_gate, full_gate, 1, 1) + dot(back_up, full_up, 1, 1)

    hidden_own, back_gate_own, back_up_own = feed(normed_two, cotangent_own)
    hidden_other, back_gate_other, back_up_other = feed(normed_other, cotangent_other)
    back_two_received = to_partner(
        feed_input_back(back_gate_other, back_up_other).astype(jnp.bfloat16)
    )
    back_two = feed_input_back(back_gate_own, back_up_own) + back_two_received.astype(jnp.float32)
    feed_received = to_partner(dot(hidden_other, full_down, 1, 1).astype(jnp.bfloat16))
    result_own = (
        middle + dot(hidden_own, full_down, 1, 1) + feed_received.astype(jnp.float32)
    ).astype(jnp.bfloat16)

    def feed_gradient(left_own, right_own, left_other, right_other):
        gradient = dot(left_own, right_own, 0, 0) + dot(left_other, right_other, 0, 0)
        return gradient.astype(jnp.bfloat16).reshape(lax.axis_size("fsdp"), -1, gradient.shape[1])

    gradients = (
        feed_gradient(cotangent_own, hidden_own, cotangent_other, hidden_other),
        feed_gradient(normed_two, back_gate_own, normed_other, back_gate_other),
        feed_gradient(normed_two, back_up_own, normed_other, back_up_other),
    )

    grad_gain_two = jnp.sum(back_two * unit_two, axis=0)
    back_middle = cotangent_own.astype(jnp.float32) + norm_back(
        back_two * gain_two, unit_two, inverse_two
    )
    back_attention = back_middle.astype(jnp.bfloat16)
    back_mixed = dot(full_output, back_attention, 1, 1).astype(jnp.bfloat16)
    back_mixed = back_mixed.reshape(query_low.shape)
    grad_output = dot(mixed_low, back_attention, 1, 0).astype(jnp.bfloat16)
    back_query, back_keyval, share = backward_sum(
        query_low, keyval, back_mixed, mixed_heads, lse, cosine, sine, gradients
    )
    back_query = back_query.reshape(QUERY_WIDTH, token_positions)
    back_keyval = back_keyval.reshape(2 * KEY_WIDTH, token_positions)
    grad_query = dot(normed_one, back_query, 0, 1).astype(jnp.bfloat16)
    grad_keyval = dot(normed_one, back_keyval, 0, 1).astype(jnp.bfloat16)
    back_one = dot(back_query, full_query, 0, 1) + dot(back_keyval, full_keyval, 0, 1)
    grad_gain_one = jnp.sum(back_one * unit_one, axis=0)
    back_inputs = back_middle + norm_back(back_one * gain_one, unit_one, inverse_one)

    def to_positions(value_rows):
        split = value_rows.reshape(2, token_positions // 2, value_rows.shape[-1])
        received = to_partner(take(split, 1 - half))
        return in_order(take(split, half)[None], received[None])

    result = to_positions(result_own)
    grad_tokens = to_positions(back_inputs.astype(jnp.bfloat16)).astype(jnp.float32)
    width = 2 * QUERY_WIDTH + 2 * KEY_WIDTH
    gains = jnp.concatenate(
        [grad_gain_one.reshape(parts, rows), grad_gain_two.reshape(parts, rows)], 1
    )
    gains = jnp.pad(gains[:, None], ((0, 0), (0, 15), (0, width - 2 * rows)))
    summed = jnp.concatenate([grad_output, grad_query, grad_keyval], 1)
    summed = jnp.concatenate(
        [summed.reshape(parts, rows, width), gains.astype(jnp.bfloat16)], 1
    )
    share_in, share_rest = gradient_sum(summed, share)
    share_in = share_in.astype(jnp.float32)
    return (
        result,
        grad_tokens,
        share_in[rows, :rows],
        share_in[:rows, QUERY_WIDTH : 2 * QUERY_WIDTH],
        share_in[:rows, 2 * QUERY_WIDTH :],
        share_in[:rows, :QUERY_WIDTH],
        share_in[rows, rows : 2 * rows],
        share_rest[0].astype(jnp.float32),
        share_rest[1].astype(jnp.float32),
        share[0].astype(jnp.float32),
    )


def solution(mesh):
    rows = P("fsdp", ("ctx", "tp"), None)
    specs = (
        P("fsdp"), P("fsdp", None), P("fsdp", None), P("fsdp", None),
        P("fsdp"), P("fsdp", "tp"), P("fsdp", "tp"), P("fsdp", "tp"),
    )
    kernels = mesh.shape["fsdp"] == 4 and mesh.shape["tp"] == 2 and mesh.shape["ctx"] == 4
    return jax.shard_map(
        fast_on_device if kernels else on_device,
        mesh=mesh,
        in_specs=(rows, rows) + specs,
        out_specs=(rows, rows) + specs,
        check_vma=False,
    )
```

```python
import jax
import jax.numpy as jnp
from jax import lax
from jax.experimental import pallas as pl
from jax.experimental.pallas import tpu as pltpu
from jax.sharding import PartitionSpec as P

QUERY_HEADS = 15
KEYVAL_HEADS = 5
GROUP = QUERY_HEADS // KEYVAL_HEADS
HEAD_WIDTH = 64
HALF = HEAD_WIDTH // 2
KEY_WIDTH = 320
QUERY_WIDTH = QUERY_HEADS * HEAD_WIDTH
SCALE = HEAD_WIDTH ** (-0.5)

EPS = 1e-05
THETA = 10000.0
VMEM_LIMIT = 40 * 1024 * 1024


def dot(left, right, left_dim, right_dim):
    return lax.dot_general(
        left, right, (((left_dim,), (right_dim,)), ((), ())), preferred_element_type=jnp.float32
    )


def rope_tables(token_positions, first_place):
    position = (first_place + lax.iota(jnp.int32, token_positions)).astype(jnp.float32)
    frequency = THETA ** (-(2.0 * lax.iota(jnp.int32, HALF).astype(jnp.float32)) / HEAD_WIDTH)
    angles = frequency[:, None] * position[None, :]
    return (jnp.cos(angles), jnp.sin(angles))


def apply_rotary(rows, cosine, sine):
    shaped = rows.reshape(-1, 2, HALF, rows.shape[-1])
    leading = shaped[:, 0]
    trailing = shaped[:, 1]
    return jnp.stack(
        [leading * cosine - trailing * sine, trailing * cosine + leading * sine], 1
    ).reshape(rows.shape)


def normalize(value_rows):
    inverse_rms = lax.rsqrt(jnp.mean(value_rows * value_rows, -1, keepdims=True) + EPS)
    return (value_rows * inverse_rms, inverse_rms)


def norm_back(back_unit, unit_rows, inverse_rms):
    return inverse_rms * (
        back_unit - unit_rows * jnp.mean(back_unit * unit_rows, -1, keepdims=True)
    )


def causal(scores):
    key_place = lax.broadcasted_iota(jnp.int32, scores.shape, 0)
    query_place = lax.broadcasted_iota(jnp.int32, scores.shape, 1)
    return jnp.where(key_place <= query_place, scores, -jnp.inf)


def forward_kernel(query_ref, key_ref, value_ref, mixed_ref, lse_ref):
    place = lax.axis_index("ctx")
    queries = [query_ref[g] * jnp.bfloat16(SCALE) for g in range(GROUP)]

    def scores_of(keys_turned, g, masked):
        scores = dot(keys_turned, queries[g], 1, 0)
        return causal(scores) if masked else scores

    def first():
        keys_turned = key_ref[0, 0, 0].T
        values = value_ref[0, 0, 0]
        carried = []
        for g in range(GROUP):
            scores = scores_of(keys_turned, g, True)
            top = jnp.max(scores, 0, keepdims=True)
            lifted = jnp.exp(scores - top)
            total = jnp.sum(lifted, 0, keepdims=True)
            carried += [top, total, dot(values, lifted.astype(jnp.bfloat16), 1, 0)]
        return tuple(carried)

    def step(block, carried):
        keys_turned = key_ref[block, 0, 0].T
        values = value_ref[block, 0, 0]
        later = []
        for g in range(GROUP):
            top, total, mixed = carried[3 * g : 3 * g + 3]
            scores = scores_of(keys_turned, g, False)
            new_top = jnp.maximum(top, jnp.max(scores, 0, keepdims=True))
            lifted = jnp.exp(scores - new_top)
            shrink = jnp.exp(top - new_top)
            later += [
                new_top,
                total * shrink + jnp.sum(lifted, 0, keepdims=True),
                mixed * shrink + dot(values, lifted.astype(jnp.bfloat16), 1, 0),
            ]
        return tuple(later)

    carried = lax.fori_loop(1, place + 1, step, first())
    for g in range(GROUP):
        top, total, mixed = carried[3 * g : 3 * g + 3]
        mixed_ref[g] = (mixed / total).astype(jnp.bfloat16)
        lse_ref[g] = top + jnp.log(total)


def attend_forward(query, keyval):
    blocks, token_positions = keyval.shape[0], keyval.shape[-1]
    head_block = (GROUP, HEAD_WIDTH, token_positions)
    key_block = (blocks, 1, 1, HEAD_WIDTH, token_positions)
    area = QUERY_HEADS * token_positions * token_positions * blocks
    return pl.pallas_call(
        forward_kernel,
        grid=(KEYVAL_HEADS,),
        in_specs=[
            pl.BlockSpec(head_block, lambda j: (j, 0, 0)),
            pl.BlockSpec(key_block, lambda j: (0, 0, j, 0, 0)),
            pl.BlockSpec(key_block, lambda j: (0, 1, j, 0, 0)),
        ],
        out_specs=[
            pl.BlockSpec(head_block, lambda j: (j, 0, 0)),
            pl.BlockSpec((GROUP, 1, token_positions), lambda j: (j, 0, 0)),
        ],
        out_shape=[
            jax.ShapeDtypeStruct(query.shape, jnp.bfloat16),
            jax.ShapeDtypeStruct((QUERY_HEADS, 1, token_positions), jnp.float32),
        ],
        compiler_params=pltpu.CompilerParams(vmem_limit_bytes=VMEM_LIMIT),
        cost_estimate=pl.CostEstimate(
            flops=16 * HEAD_WIDTH * area, bytes_accessed=6 * query.size, transcendentals=area
        ),
        name="attend_forward",
    )(query, keyval, keyval)


def backward_kernel(
    query_ref, key_ref, value_ref, back_ref, mixed_ref, lse_ref, cosine_ref, sine_ref,
    back_query_ref, back_keyval_ref,
):
    place = lax.axis_index("ctx")
    blocks = key_ref.shape[0]
    queries = [query_ref[g] * jnp.bfloat16(SCALE) for g in range(GROUP)]
    backs = [back_ref[g] for g in range(GROUP)]
    tops = [lse_ref[g] for g in range(GROUP)]
    sums = [
        jnp.sum(backs[g].astype(jnp.float32) * mixed_ref[g].astype(jnp.float32), 0, keepdims=True)
        for g in range(GROUP)
    ]

    def step(block, carried, masked=False):
        keys = key_ref[block, 0, 0]
        keys_turned = keys.T
        values_turned = value_ref[block, 0, 0].T
        back_key = jnp.zeros(keys.shape, jnp.float32)
        back_value = jnp.zeros(keys.shape, jnp.float32)
        later = []
        for g in range(GROUP):
            scores = dot(keys_turned, queries[g], 1, 0)
            if masked:
                scores = causal(scores)
            weights = jnp.exp(scores - tops[g])
            back_weights = dot(values_turned, backs[g], 1, 0)
            back_scores = (weights * (back_weights - sums[g])).astype(jnp.bfloat16)
            later.append(carried[g] + dot(keys, back_scores, 1, 0))
            back_key += dot(queries[g], back_scores, 1, 1)
            back_value += dot(backs[g], weights.astype(jnp.bfloat16), 1, 1)
        back_keyval_ref[block, 0, 0] = back_key.astype(jnp.bfloat16)
        back_keyval_ref[block, 1, 0] = back_value.astype(jnp.bfloat16)
        return tuple(later)

    start = tuple(jnp.zeros(query_ref.shape[1:], jnp.float32) for g in range(GROUP))
    carried = lax.fori_loop(1, place + 1, step, step(0, start, True))

    def clear(block, unused):
        zero = jnp.zeros(key_ref.shape[3:], jnp.bfloat16)
        back_keyval_ref[block, 0, 0] = zero
        back_keyval_ref[block, 1, 0] = zero
        return unused

    lax.fori_loop(place + 1, blocks, clear, 0)
    cosine = cosine_ref[...]
    sine = sine_ref[...]
    for g in range(GROUP):
        leading = carried[g][:HALF] * SCALE
        trailing = carried[g][HALF:] * SCALE
        back_query_ref[g, :HALF] = (leading * cosine + trailing * sine).astype(jnp.bfloat16)
        back_query_ref[g, HALF:] = (trailing * cosine - leading * sine).astype(jnp.bfloat16)


def attend_backward(query, keyval, back_mixed, mixed, lse, cosine, sine, first, count):
    blocks, token_positions = keyval.shape[0], keyval.shape[-1]
    head_block = (GROUP, HEAD_WIDTH, token_positions)
    key_block = (blocks, 1, 1, HEAD_WIDTH, token_positions)
    area = count * GROUP * token_positions * token_positions * blocks
    heads = pl.BlockSpec(head_block, lambda j: (j + first, 0, 0))
    table = pl.BlockSpec((HALF, token_positions), lambda j: (0, 0))
    return pl.pallas_call(
        backward_kernel,
        grid=(count,),
        in_specs=[
            heads,
            pl.BlockSpec(key_block, lambda j: (0, 0, j + first, 0, 0)),
            pl.BlockSpec(key_block, lambda j: (0, 1, j + first, 0, 0)),
            heads,
            heads,
            pl.BlockSpec((GROUP, 1, token_positions), lambda j: (j + first, 0, 0)),
            table,
            table,
        ],
        out_specs=[
            pl.BlockSpec(head_block, lambda j: (j, 0, 0)),
            pl.BlockSpec((blocks, 2, 1, HEAD_WIDTH, token_positions), lambda j: (0, 0, j, 0, 0)),
        ],
        out_shape=[
            jax.ShapeDtypeStruct((count * GROUP, HEAD_WIDTH, token_positions), jnp.bfloat16),
            jax.ShapeDtypeStruct(
                (blocks, 2, count, HEAD_WIDTH, token_positions), jnp.bfloat16
            ),
        ],
        compiler_params=pltpu.CompilerParams(vmem_limit_bytes=VMEM_LIMIT),
        cost_estimate=pl.CostEstimate(
            flops=40 * HEAD_WIDTH * area, bytes_accessed=10 * query.size, transcendentals=area
        ),
        name="attend_backward",
    )(query, keyval, keyval, back_mixed, mixed, lse, cosine, sine)


def move_along(value, distance):
    blocks = lax.axis_size("ctx")
    pairs = [(i, i + distance) for i in range(blocks) if 0 <= i + distance < blocks]
    return lax.ppermute(value, "ctx", pairs)


def trade(value, axis, step):
    pairs = [(i, i ^ step) for i in range(lax.axis_size(axis))]
    return lax.ppermute(value, axis, pairs)


def add_low(left, right):
    return (left.astype(jnp.float32) + right.astype(jnp.float32)).astype(jnp.bfloat16)


def scatter_sum(value, axis):
    size = lax.axis_size(axis)
    index = lax.axis_index(axis)
    rows = value.shape[0] // size
    step = 1
    while step < size:
        count = value.shape[0] // (2 * rows)
        split = value.reshape(count, 2, rows, value.shape[-1])
        second = (index // step) % 2 == 1
        kept = jnp.where(second, split[:, 1], split[:, 0])
        sent = jnp.where(second, split[:, 0], split[:, 1])
        value = add_low(kept, trade(sent, axis, step)).reshape(count * rows, value.shape[-1])
        step *= 2
    return value


def whole_sum(value, others):
    half_rows = value.shape[0] // 2
    second = lax.axis_index("ctx") % 2 == 1
    upper, lower = value[:half_rows], value[half_rows:]
    received = trade(jnp.where(second, upper, lower), "ctx", 1)
    total = add_low(jnp.where(second, lower, upper), received)
    for axis, first_step in others:
        step = first_step
        while step < lax.axis_size(axis):
            total = add_low(total, trade(total, axis, step))
            step *= 2
    received = trade(total, "ctx", 1)
    return jnp.concatenate(
        [jnp.where(second, received, total), jnp.where(second, total, received)], 0
    ).astype(jnp.float32)


MESH = pl.DeviceIdType.MESH
KERNEL_VMEM = 58 * 1024 * 1024
CHUNK_ROWS = 80
WIDE = 512


def remote(source, target, send_sem, recv_sem, **place):
    return pltpu.make_async_remote_copy(
        src_ref=source, dst_ref=target, send_sem=send_sem, recv_sem=recv_sem,
        device_id=place, device_id_type=MESH,
    )


def wide(value):
    return value.astype(jnp.float32)


def low(value):
    return value.astype(jnp.bfloat16)


def greet(**place):
    pl.semaphore_signal(
        pltpu.get_barrier_semaphore(), inc=1, device_id=place, device_id_type=MESH
    )


def backward_sum_kernel(
    query_ref, keyval_ref, back_ref, mixed_ref, lse_ref, cosine_ref, sine_ref,
    base_ref, feed_ref, down_ref, gate_ref, up_ref,
    back_query_ref, back_keyval_ref, share_ref, result_ref,
    own, mate_in, y_in, up_in, parts, part_out, part_in, back_total, row_sums,
    own_sem, mate_send, mate_recv, y_send, y_recv, up_send, up_recv, down_send, down_recv,
    part_send, part_recv, feed_in, traded, feed_send, feed_recv, trade_send, trade_recv,
):
    place = lax.axis_index("ctx")
    last = lax.axis_size("ctx") - 1
    blocks = last + 1
    rank = lax.axis_index("fsdp")
    core = rank % 2
    y = rank // 2
    side = lax.axis_index("tp")
    mate = rank + 1 - 2 * core
    across = rank + 2 - 4 * y
    gradients = (down_ref, gate_ref, up_ref)
    rows = share_ref.shape[1]
    per = rows // CHUNK_ROWS
    chunks = len(gradients) * per
    early = per

    for m, gradient in enumerate(gradients):
        for half in range(2):
            pltpu.make_async_copy(
                gradient.at[2 * half + core], own.at[m, half], own_sem.at[m, half]
            ).start()
    greet(fsdp=mate)
    greet(fsdp=across)
    greet(tp=1 - side)

    @pl.when(place > 0)
    def _():
        greet(ctx=place - 1)

    @pl.when(place < last)
    def _():
        greet(ctx=place + 1)

    neighbours = (place + last - 1) // last + (2 * last - place - 1) // last
    pl.semaphore_wait(pltpu.get_barrier_semaphore(), 3 + neighbours)

    feed_copy = remote(feed_ref, feed_in, feed_send, feed_recv, tp=1 - side)
    trade_copy = remote(traded, result_ref.at[side], trade_send, trade_recv, tp=1 - side)
    feed_copy.start()
    width = traded.shape[-1]
    step_rows = traded.shape[0] // 4

    def finish_result():
        feed_copy.wait_recv()

        def some_rows(i, carry):
            at = pl.ds(pl.multiple_of(i * step_rows, step_rows), step_rows)
            for target, slot in ((result_ref.at[side], side), (traded, 1 - side)):
                columns = pl.ds(pl.multiple_of(slot * width, width), width)
                target[at] = low(base_ref[at, columns] + wide(feed_in[at, columns]))
            return carry

        lax.fori_loop(0, 4, some_rows, 0)
        trade_copy.start()

    def chunk_at(ref, m, r, *front):
        return ref.at[(m,) + front + (pl.ds(r * CHUNK_ROWS, CHUNK_ROWS),)]

    def mate_copy(m, r, half):
        gradient = gradients[m]
        return remote(
            gradient.at[2 * half + 1 - core, pl.ds(r * CHUNK_ROWS, CHUNK_ROWS)],
            chunk_at(mate_in, m, r, half),
            mate_send.at[m * per + r, half], mate_recv.at[m * per + r, half], fsdp=mate,
        )

    for m in range(len(gradients)):
        for r in range(per):
            for half in range(2):
                mate_copy(m, r, half).start()
    for m, gradient in enumerate(gradients):
        for half in range(2):
            pltpu.make_async_copy(
                gradient.at[2 * half + core], own.at[m, half], own_sem.at[m, half]
            ).wait()

    def split(k):
        r = lax.rem(k, per)
        return k // per, pl.ds(pl.multiple_of(r * CHUNK_ROWS, CHUNK_ROWS), CHUNK_ROWS)

    def y_copy(k):
        m, at = split(k)
        return remote(
            own.at[m, 1 - y, at], y_in.at[m, at], y_send.at[k], y_recv.at[k], fsdp=across
        )

    def up_copy(k):
        m, at = split(k)
        return remote(
            own.at[m, y, at], up_in.at[m, at], up_send.at[k], up_recv.at[k], ctx=place + 1
        )

    def down_copy(k):
        m, at = split(k)
        return remote(
            share_ref.at[m, at], share_ref.at[m, at], down_send.at[k], down_recv.at[k],
            ctx=place - 1,
        )

    def to_across(k):
        m, at = split(k)
        for half in range(2):
            pltpu.make_async_copy(
                mate_in.at[m, half, at], mate_in.at[m, half, at], mate_recv.at[k, half]
            ).wait()
        own[m, 1 - y, at] = low(wide(own[m, 1 - y, at]) + wide(mate_in[m, 1 - y, at]))
        y_copy(k).start()

    def to_next(k):
        m, at = split(k)
        y_copy(k).wait_recv()
        total = wide(own[m, y, at]) + wide(mate_in[m, y, at]) + wide(y_in[m, at])

        @pl.when(place == 0)
        def _():
            own[m, y, at] = low(total)

        @pl.when(place > 0)
        def _():
            up_copy(k).wait_recv()
            own[m, y, at] = low(total + wide(up_in[m, at]))

        @pl.when(place < last)
        def _():
            up_copy(k).start()

        @pl.when(place == last)
        def _():
            share_ref[m, at] = own[m, y, at]

            @pl.when(k < early)
            def _():
                down_copy(k).start()

    def to_previous(k):
        down_copy(k).wait_recv()

        @pl.when(place > 0)
        def _():
            down_copy(k).start()

    def tick(t):
        @pl.when(t < chunks)
        def _():
            to_across(t)

        @pl.when(t == chunks)
        def _():
            finish_result()

        b = t - 3 - 2 * place

        @pl.when((b >= 0) & (b < 2 * chunks) & (lax.rem(b, 2) == 0))
        def _():
            to_next(b // 2)

        c = t - 3 - 2 * last - 2 * (last - place)

        @pl.when((place < last) & (c >= 0) & (c < 2 * early) & (lax.rem(c, 2) == 0))
        def _():
            to_previous(c // 2)

    def part_copy(j, s):
        return remote(
            part_out.at[j, s - 1], part_in.at[j, s - 1], part_send.at[j, s - 1],
            part_recv.at[j, s - 1], ctx=place - 1,
        )

    def step(j, s, masked):
        keys = keyval_ref[s, j, 0]
        keys_turned = keys.T
        values_turned = keyval_ref[s, j, 1].T
        back_key = jnp.zeros(keys.shape, jnp.float32)
        back_value = jnp.zeros(keys.shape, jnp.float32)
        for g in range(GROUP):
            head = GROUP * j + g
            query = query_ref[head]
            back = back_ref[head]
            if masked:
                row_sums[g] = jnp.sum(wide(back) * wide(mixed_ref[head]), 0, keepdims=True)
            scores = dot(keys_turned, query, 1, 0)
            if masked:
                scores = causal(scores)
            weights = jnp.exp(scores - lse_ref[head])
            back_weights = dot(values_turned, back, 1, 0)
            back_scores = low(weights * (back_weights - row_sums[g]))
            added = dot(keys, back_scores, 1, 0)
            if masked:
                back_total[g] = added
            else:
                back_total[g] += added
            back_key += dot(query, back_scores, 1, 1)
            back_value += dot(back, low(weights), 1, 1)
        parts[j, s, 0] = back_key
        parts[j, s, 1] = back_value

    def hand_on(j):
        for s in range(blocks):
            @pl.when(s <= place)
            def _(s=s):
                @pl.when(place < last)
                def _():
                    pltpu.make_async_copy(
                        part_in.at[j, s], part_in.at[j, s], part_recv.at[j, s]
                    ).wait()
                    for side in range(2):
                        parts[j, s, side] += wide(part_in[j, s, side])

                if s > 0:
                    for side in range(2):
                        part_out[j, s - 1, side] = low(parts[j, s, side])
                    part_copy(j, s).start()
                else:
                    leading = parts[j, 0, 0, :HALF]
                    trailing = parts[j, 0, 0, HALF:]
                    cosine, sine = cosine_ref[...], sine_ref[...]
                    back_keyval_ref[0, j, :HALF] = low(leading * cosine + trailing * sine)
                    back_keyval_ref[0, j, HALF:] = low(trailing * cosine - leading * sine)
                    back_keyval_ref[1, j] = low(parts[j, 0, 1])

    def head_loop(j, carry):
        @pl.when(j < KEYVAL_HEADS)
        def _():
            step(j, 0, True)

        tick(j * blocks)

        def block_loop(s, inner):
            @pl.when((j < KEYVAL_HEADS) & (s <= place))
            def _():
                step(j, s, False)

            tick(j * blocks + s)
            return inner

        lax.fori_loop(1, blocks, block_loop, 0)

        @pl.when(j < KEYVAL_HEADS)
        def _():
            cosine, sine = cosine_ref[...], sine_ref[...]
            for g in range(GROUP):
                leading = back_total[g, :HALF] * SCALE
                trailing = back_total[g, HALF:] * SCALE
                head = GROUP * j + g
                back_query_ref[head, :HALF] = low(leading * cosine + trailing * sine)
                back_query_ref[head, HALF:] = low(trailing * cosine - leading * sine)

        ready = j - (last - place)

        @pl.when((ready >= 0) & (ready < KEYVAL_HEADS))
        def _():
            hand_on(ready)

        return carry

    assert (KEYVAL_HEADS + last) * blocks >= 4 + 4 * last + 2 * (chunks - 1)
    lax.fori_loop(0, KEYVAL_HEADS + last, head_loop, 0)

    for m in range(len(gradients)):
        for r in range(per):
            for half in range(2):
                mate_copy(m, r, half).wait_send()

    def finish(k, carry):
        y_copy(k).wait_send()

        @pl.when(place < last)
        def _():
            up_copy(k).wait_send()

        @pl.when((place > 0) & (k < early))
        def _():
            down_copy(k).wait_send()

        return carry

    lax.fori_loop(0, chunks, finish, 0)

    def finish_parts(j, carry):
        for s in range(1, blocks):
            @pl.when(s <= place)
            def _(s=s):
                part_copy(j, s).wait_send()
        return carry

    lax.fori_loop(0, KEYVAL_HEADS, finish_parts, 0)
    feed_copy.wait_send()
    trade_copy.wait()


def backward_sum(query, keyval, back_mixed, mixed, lse, cosine, sine, base, feed, gradients):
    blocks, positions = keyval.shape[0], keyval.shape[-1]
    count, rows, columns = gradients[0].shape
    chunks = len(gradients) * rows // CHUNK_ROWS
    area = QUERY_HEADS * positions * positions * blocks
    vmem = pl.BlockSpec(memory_space=pltpu.VMEM)
    dma = pltpu.SemaphoreType.DMA
    share = (len(gradients), rows, columns)
    head = (2, HEAD_WIDTH, positions)
    return pl.pallas_call(
        backward_sum_kernel,
        in_specs=[vmem] * 9 + [pl.BlockSpec(memory_space=pl.ANY)] * 3,
        out_specs=[vmem] * 4,
        out_shape=[
            jax.ShapeDtypeStruct(query.shape, jnp.bfloat16),
            jax.ShapeDtypeStruct((2, KEYVAL_HEADS, HEAD_WIDTH, positions), jnp.bfloat16),
            jax.ShapeDtypeStruct(share, jnp.bfloat16),
            jax.ShapeDtypeStruct((2, feed.shape[0], positions // 2), jnp.bfloat16),
        ],
        scratch_shapes=[
            pltpu.VMEM((len(gradients), 2, rows, columns), jnp.bfloat16),
            pltpu.VMEM((len(gradients), 2, rows, columns), jnp.bfloat16),
            pltpu.VMEM(share, jnp.bfloat16),
            pltpu.VMEM(share, jnp.bfloat16),
            pltpu.VMEM((KEYVAL_HEADS, blocks) + head, jnp.float32),
            pltpu.VMEM((KEYVAL_HEADS, blocks - 1) + head, jnp.bfloat16),
            pltpu.VMEM((KEYVAL_HEADS, blocks - 1) + head, jnp.bfloat16),
            pltpu.VMEM((GROUP, HEAD_WIDTH, positions), jnp.float32),
            pltpu.VMEM((GROUP, 1, positions), jnp.float32),
            dma((len(gradients), 2)),
            dma((chunks, 2)), dma((chunks, 2)),
            dma((chunks,)), dma((chunks,)),
            dma((chunks,)), dma((chunks,)),
            dma((rows // CHUNK_ROWS,)), dma((rows // CHUNK_ROWS,)),
            dma((KEYVAL_HEADS, blocks - 1)), dma((KEYVAL_HEADS, blocks - 1)),
            pltpu.VMEM(feed.shape, jnp.bfloat16),
            pltpu.VMEM((feed.shape[0], positions // 2), jnp.bfloat16),
            dma, dma, dma, dma,
        ],
        compiler_params=pltpu.CompilerParams(
            vmem_limit_bytes=KERNEL_VMEM, collective_id=0, has_side_effects=True
        ),
        cost_estimate=pl.CostEstimate(
            flops=40 * HEAD_WIDTH * area, bytes_accessed=10 * query.size, transcendentals=area
        ),
        name="backward_sum",
    )(query, keyval, back_mixed, mixed, lse, cosine, sine, base, feed, *gradients)


def gradient_sum_kernel(out_ref, query_ref, keyval_ref, gains_ref, feed_ref, back_ref, *refs):
    values = (out_ref, query_ref, keyval_ref)
    chunks = len(values)
    shares, (feed_share_ref, tokens_ref), refs = refs[:chunks], refs[chunks : chunks + 2], refs[chunks + 2 :]
    own, mate_in, y_out, y_in, x_out, x_in, z_out, z_in = [
        refs[i * chunks : (i + 1) * chunks] for i in range(8)
    ]
    (
        own_sem, mate_send, mate_recv, y_send, y_recv, x_send, x_recv, z_send, z_recv,
        all_send, all_recv, back_send, back_recv, down_send, down_recv, feed_sem,
        token_send, token_recv, token_sem,
    ) = refs[8 * chunks :]
    place = lax.axis_index("ctx")
    blocks = lax.axis_size("ctx")
    last = blocks - 1
    rank = lax.axis_index("fsdp")
    side = lax.axis_index("tp")
    core = rank % 2
    y = rank // 2
    mate = rank + 1 - 2 * core
    across = rank + 2 - 4 * y
    rows = shares[0].shape[0]
    filled = values[0].shape[1]
    half_rows = rows // 2
    piece = half_rows // blocks
    width = tokens_ref.shape[-1]

    def columns(slot):
        return back_ref.at[:, pl.ds(pl.multiple_of(slot * width, width), width)]

    def own_copy(n, half):
        return pltpu.make_async_copy(
            values[n].at[2 * half + core], own[n].at[half, pl.ds(0, filled)], own_sem.at[n, half]
        )

    def own_gains(half):
        return pltpu.make_async_copy(
            gains_ref.at[2 * half + core], own[-1].at[half, pl.ds(filled, rows - filled)],
            own_sem.at[chunks, half],
        )

    for half in range(2):
        for n in range(chunks):
            own_copy(n, half).start()
        own_gains(half).start()
    for n in range(chunks - 1):
        tail = (2, rows - filled, own[n].shape[-1])
        own[n][:, filled:] = jnp.zeros(tail, jnp.bfloat16)
        mate_in[n][:, filled:] = jnp.zeros(tail, jnp.bfloat16)

    greet(fsdp=mate)
    greet(fsdp=across)
    greet(tp=1 - side)
    for d in range(1, blocks):
        greet(ctx=lax.rem(place + d, blocks))
    pl.semaphore_wait(pltpu.get_barrier_semaphore(), 2 + blocks)

    def mate_copy(n, half):
        return remote(
            values[n].at[2 * half + 1 - core], mate_in[n].at[half, pl.ds(0, filled)],
            mate_send.at[n, half], mate_recv.at[n, half], fsdp=mate,
        )

    def mate_gains(half):
        return remote(
            gains_ref.at[2 * half + 1 - core], mate_in[-1].at[half, pl.ds(filled, rows - filled)],
            mate_send.at[chunks, half], mate_recv.at[chunks, half], fsdp=mate,
        )

    def y_copy(n):
        return remote(y_out[n], y_in[n], y_send.at[n], y_recv.at[n], fsdp=across)

    def x_copy(n):
        other = pl.ds(pl.multiple_of((1 - side) * half_rows, half_rows), half_rows)
        return remote(x_out[n].at[other], x_in[n], x_send.at[n], x_recv.at[n], tp=1 - side)

    def z_copy(n, d):
        target = lax.rem(place + d, blocks)
        at = pl.ds(pl.multiple_of(target * piece, piece), piece)
        return remote(
            z_out[n].at[at], z_in[n].at[d - 1], z_send.at[n, d - 1], z_recv.at[n, d - 1],
            ctx=target,
        )

    def all_copy(n, d, origin):
        spot = shares[n].at[
            pl.ds(pl.multiple_of(side * half_rows + origin * piece, piece), piece)
        ]
        return remote(
            spot, spot, all_send.at[n, d - 1], all_recv.at[n, d - 1],
            ctx=lax.rem(place + d, blocks),
        )

    def back_copy(n, half):
        spot = shares[n].at[pl.ds(pl.multiple_of(half * half_rows, half_rows), half_rows)]
        return remote(spot, spot, back_send.at[n], back_recv.at[n], tp=1 - side)

    per = feed_ref.shape[1] // CHUNK_ROWS
    returned = feed_share_ref.shape[0] * per

    def feed_at(ref, k, skip):
        return ref.at[k // per + skip, pl.ds(k % per * CHUNK_ROWS, CHUNK_ROWS)]

    def down_copy(k, source):
        return remote(
            source, feed_at(feed_share_ref, k, 0), down_send.at[k], down_recv.at[k],
            ctx=place - 1,
        )

    feed_copy = pltpu.make_async_copy(feed_ref.at[pl.ds(1, 2)], feed_share_ref, feed_sem)

    def to_previous(k):
        down_copy(k, feed_at(feed_share_ref, k, 0)).wait_recv()

        @pl.when(place > 0)
        def _():
            down_copy(k, feed_at(feed_share_ref, k, 0)).start()

    token_copy = remote(
        columns(1 - side), tokens_ref.at[side], token_send, token_recv, tp=1 - side
    )
    token_own = pltpu.make_async_copy(columns(side), tokens_ref.at[side], token_sem)

    for n in range(chunks):
        for half in range(2):
            mate_copy(n, half).start()
    for half in range(2):
        mate_gains(half).start()
    token_own.start()

    @pl.when(place == last)
    def _():
        for k in range(returned):
            down_copy(k, feed_at(feed_ref, k, 1)).start()
        feed_copy.start()

    for half in range(2):
        for n in range(chunks):
            own_copy(n, half).wait()
        own_gains(half).wait()

    def to_y(n):
        for half in range(2):
            mate_copy(n, half).wait_recv()
            if n == chunks - 1:
                mate_gains(half).wait_recv()
        y_out[n][...] = low(wide(own[n][1 - y]) + wide(mate_in[n][1 - y]))
        y_copy(n).start()
        if n == chunks - 1:
            token_copy.start()

    def to_x(n):
        y_copy(n).wait_recv()
        x_out[n][...] = low(wide(own[n][y]) + wide(mate_in[n][y]) + wide(y_in[n][...]))
        x_copy(n).start()

    def to_z(n):
        x_copy(n).wait_recv()
        at = pl.ds(pl.multiple_of(side * half_rows, half_rows), half_rows)
        z_out[n][...] = low(wide(x_out[n][at]) + wide(x_in[n][...]))
        for d in range(1, blocks):
            z_copy(n, d).start()

    def to_all(n):
        total = wide(z_out[n][pl.ds(pl.multiple_of(place * piece, piece), piece)])
        for d in range(1, blocks):
            z_copy(n, d).wait_recv()
            total += wide(z_in[n][d - 1])
        at = pl.ds(pl.multiple_of(side * half_rows + place * piece, piece), piece)
        shares[n][at] = low(total)
        for d in range(1, blocks):
            all_copy(n, d, place).start()

    def to_back(n):
        for d in range(1, blocks):
            all_copy(n, d, lax.rem(place + blocks - d, blocks)).wait_recv()
        back_copy(n, side).start()

    def last_wait(n):
        back_copy(n, 1 - side).wait_recv()

    stages = (to_y, to_x, to_z, to_all, to_back, last_wait)
    for t in range(max(chunks + len(stages), returned + last) - 1):
        for index in reversed(range(len(stages))):
            if 0 <= t - index < chunks:
                stages[index](t - index)
        for index in range(last):
            if 0 <= t - last + 1 + index < returned:
                @pl.when(place == index)
                def _(k=t - last + 1 + index):
                    to_previous(k)

    @pl.when(place == last)
    def _():
        feed_copy.wait()

    @pl.when(place > 0)
    def _():
        for k in range(returned):
            down_copy(k, feed_at(feed_ref, k, 1)).wait_send()

    for n in range(chunks):
        for half in range(2):
            mate_copy(n, half).wait_send()
        y_copy(n).wait_send()
        x_copy(n).wait_send()
        for d in range(1, blocks):
            z_copy(n, d).wait_send()
            all_copy(n, d, place).wait_send()
        back_copy(n, side).wait_send()
    for half in range(2):
        mate_gains(half).wait_send()
    token_own.wait()
    token_copy.wait()


def gradient_sum(values, gains, feed, back):
    filled = values[0].shape[1]
    rows = filled + gains.shape[1]
    widths = [value.shape[-1] for value in values]
    chunks = len(values)
    returned = (feed.shape[0] - 1) * feed.shape[1] // CHUNK_ROWS
    blocks = lax.axis_size("ctx")
    half_rows = rows // 2
    dma = pltpu.SemaphoreType.DMA
    anywhere = pl.BlockSpec(memory_space=pl.ANY)
    vmem = pl.BlockSpec(memory_space=pltpu.VMEM)
    scratch = []
    for front in ((2, rows), (2, rows), (rows,), (rows,), (rows,), (half_rows,), (half_rows,),
                  (blocks - 1, half_rows // blocks)):
        scratch += [pltpu.VMEM(front + (w,), jnp.bfloat16) for w in widths]
    return pl.pallas_call(
        gradient_sum_kernel,
        in_specs=[anywhere] * (chunks + 2) + [vmem],
        out_specs=[vmem] * (chunks + 2),
        out_shape=[jax.ShapeDtypeStruct((rows, w), jnp.bfloat16) for w in widths] + [
            jax.ShapeDtypeStruct((feed.shape[0] - 1,) + feed.shape[1:], jnp.bfloat16),
            jax.ShapeDtypeStruct((2, back.shape[0], back.shape[1] // 2), jnp.bfloat16),
        ],
        scratch_shapes=scratch + [
            dma((chunks + 1, 2)),
            dma((chunks + 1, 2)), dma((chunks + 1, 2)),
            dma((chunks,)), dma((chunks,)),
            dma((chunks,)), dma((chunks,)),
            dma((chunks, blocks - 1)), dma((chunks, blocks - 1)),
            dma((chunks, blocks - 1)), dma((chunks, blocks - 1)),
            dma((chunks,)), dma((chunks,)),
            dma((returned,)), dma((returned,)), dma,
            dma, dma, dma,
        ],
        compiler_params=pltpu.CompilerParams(
            vmem_limit_bytes=KERNEL_VMEM, collective_id=1, has_side_effects=True
        ),
        cost_estimate=pl.CostEstimate(
            flops=back.size, bytes_accessed=20 * back.size, transcendentals=0
        ),
        name="gradient_sum",
    )(*values, gains, feed, back)


def front_kernel(
    tokens_ref, cotangent_ref, cosine_ref, sine_ref, *refs
):
    weights, refs = refs[:7], refs[7:]
    (
        tokens_own, cotangent_own, cotangent_other, normed_out, query_out, keyval_ref,
        mixed_out, lse_ref,
    ), refs = refs[:8], refs[8:]
    full, refs = refs[:7], refs[7:]
    (
        raw, tops, totals, sums,
        local_sem, token_send, token_recv, cot_send, cot_recv,
        y_send, y_recv, mate_send, mate_recv, pass_send, pass_recv, key_send, key_recv,
    ) = refs
    place = lax.axis_index("ctx")
    last = lax.axis_size("ctx") - 1
    rank = lax.axis_index("fsdp")
    side = lax.axis_index("tp")
    core = rank % 2
    mate = rank + 1 - 2 * core
    across = rank + 2 - 4 * (rank // 2)
    width = tokens_ref.shape[-1]

    def columns(ref, slot):
        return ref.at[:, pl.ds(pl.multiple_of(slot * width, width), width)]

    local = [
        pltpu.make_async_copy(tokens_ref.at[side], columns(tokens_own, side), local_sem.at[0]),
        pltpu.make_async_copy(
            cotangent_ref.at[side], columns(cotangent_own, side), local_sem.at[1]
        ),
        pltpu.make_async_copy(
            cotangent_ref.at[1 - side], columns(cotangent_other, side), local_sem.at[2]
        ),
    ]
    for w in range(len(weights)):
        local.append(pltpu.make_async_copy(weights[w], full[w].at[rank], local_sem.at[3 + w]))
    for copy in local:
        copy.start()

    greet(fsdp=mate)
    greet(fsdp=across)
    greet(tp=1 - side)

    @pl.when(place > 0)
    def _():
        greet(ctx=place - 1)

    @pl.when(place < last)
    def _():
        greet(ctx=place + 1)

    neighbours = (place + last - 1) // last + (2 * last - place - 1) // last
    pl.semaphore_wait(pltpu.get_barrier_semaphore(), 3 + neighbours)

    token_copy = remote(
        tokens_ref.at[1 - side], columns(tokens_own, side), token_send, token_recv, tp=1 - side
    )
    cot_copies = [
        remote(
            cotangent_ref.at[1 - side], columns(cotangent_own, side), cot_send.at[0],
            cot_recv.at[0], tp=1 - side,
        ),
        remote(
            cotangent_ref.at[side], columns(cotangent_other, side), cot_send.at[1],
            cot_recv.at[1], tp=1 - side,
        ),
    ]

    def y_copy(w):
        return remote(
            weights[w], full[w].at[rank], y_send.at[w], y_recv.at[w], fsdp=across
        )

    def mate_copy(w):
        return remote(
            weights[w], full[w].at[rank], mate_send.at[w], mate_recv.at[w], fsdp=mate
        )

    def pass_copy(w):
        return remote(
            full[w].at[across], full[w].at[across], pass_send.at[w], pass_recv.at[w], fsdp=mate
        )

    def arrived(w):
        local[3 + w].wait()
        mate_copy(w).wait_recv()
        pass_copy(w).wait_recv()

    for w in (6, 1):
        y_copy(w).start()
        mate_copy(w).start()
    token_copy.start()
    y_copy(0).start()
    mate_copy(0).start()
    y_copy(6).wait_recv()
    pass_copy(6).start()
    arrived(6)
    gain = wide(full[6][...].reshape(-1, full[6].shape[-1])[:, :1])

    def norm_rows(slot):
        at = pl.ds(pl.multiple_of(slot * width, width), width)
        rows = wide(tokens_own[:, at])
        inverse = lax.rsqrt(jnp.mean(rows * rows, 0, keepdims=True) + EPS)
        normed_out[:, at] = low(rows * inverse * gain)

    local[0].wait()
    norm_rows(side)
    token_copy.wait_recv()
    norm_rows(1 - side)
    for copy in cot_copies:
        copy.start()
    for w in (1, 0):
        y_copy(w).wait_recv()
        pass_copy(w).start()
    for w in range(2, 6):
        y_copy(w).start()
        mate_copy(w).start()
    normed = normed_out[...]
    cosine, sine = cosine_ref[...], sine_ref[...]

    def turned(value, target):
        target[:HALF] = low(value[:HALF] * cosine - value[HALF:] * sine)
        target[HALF:] = low(value[HALF:] * cosine + value[:HALF] * sine)

    def key_copy(s, j):
        return remote(
            keyval_ref.at[s, j], keyval_ref.at[s + 1, j], key_send.at[s, j], key_recv.at[s, j],
            ctx=place + 1,
        )

    arrived(1)
    matrix = full[1][...].reshape(-1, 2 * KEY_WIDTH)
    raw[: 2 * KEY_WIDTH] = dot(matrix, normed, 0, 0)
    for j in range(KEYVAL_HEADS):
        turned(raw[j * HEAD_WIDTH : (j + 1) * HEAD_WIDTH], keyval_ref.at[0, j, 0])
        first = KEY_WIDTH + j * HEAD_WIDTH
        keyval_ref[0, j, 1] = low(raw[first : first + HEAD_WIDTH])

        @pl.when(place < last)
        def _(j=j):
            key_copy(0, j).start()

    arrived(0)
    matrix = full[0][...].reshape(-1, QUERY_WIDTH)
    raw[...] = dot(matrix, normed, 0, 0)

    def turn_query(h, carry):
        value = raw[pl.ds(pl.multiple_of(h * HEAD_WIDTH, HEAD_WIDTH), HEAD_WIDTH)]
        first = low(value[:HALF] * cosine - value[HALF:] * sine)
        second = low(value[HALF:] * cosine + value[:HALF] * sine)
        query_out[h, :HALF] = first * jnp.bfloat16(SCALE)
        query_out[h, HALF:] = second * jnp.bfloat16(SCALE)
        return carry

    lax.fori_loop(0, QUERY_HEADS, turn_query, 0)

    def attend(s, j, masked):
        keys_turned = keyval_ref[s, j, 0].T
        values = keyval_ref[s, j, 1]
        for g in range(GROUP):
            head = GROUP * j + g
            scores = dot(keys_turned, query_out[head], 1, 0)
            if masked:
                scores = causal(scores)
                top = jnp.max(scores, 0, keepdims=True)
                lifted = jnp.exp(scores - top)
                tops[head] = top
                totals[head] = jnp.sum(lifted, 0, keepdims=True)
                sums[head] = dot(values, low(lifted), 1, 0)
            else:
                old = tops[head]
                top = jnp.maximum(old, jnp.max(scores, 0, keepdims=True))
                lifted = jnp.exp(scores - top)
                shrink = jnp.exp(old - top)
                tops[head] = top
                totals[head] = totals[head] * shrink + jnp.sum(lifted, 0, keepdims=True)
                sums[head] = sums[head] * shrink + dot(values, low(lifted), 1, 0)

    def hand_on(s, j):
        @pl.when(s < place)
        def _():
            pltpu.make_async_copy(
                keyval_ref.at[s + 1, j], keyval_ref.at[s + 1, j], key_recv.at[s, j]
            ).wait()

            @pl.when(place < last)
            def _():
                key_copy(s + 1, j).start()

    def first_block(j, carry):
        attend(0, j, True)
        hand_on(0, j)
        return carry

    lax.fori_loop(0, KEYVAL_HEADS, first_block, 0)
    passed = 2

    def later_block(i, carry):
        s = 1 + i // KEYVAL_HEADS
        j = lax.rem(i, KEYVAL_HEADS)
        attend(s, j, False)
        hand_on(s, j)
        return carry

    lax.fori_loop(0, place * KEYVAL_HEADS, later_block, 0)

    def divide(h, carry):
        total = totals[h]
        mixed_out[h] = low(sums[h] / total)
        lse_ref[h] = tops[h] + jnp.log(total)
        return carry

    lax.fori_loop(0, QUERY_HEADS, divide, 0)

    for w in range(passed, 6):
        y_copy(w).wait_recv()
        pass_copy(w).start()
    local[1].wait()
    local[2].wait()
    token_copy.wait_send()
    for copy in cot_copies:
        copy.wait()
    for w in range(passed, 6):
        arrived(w)
    for w in range(len(weights)):
        y_copy(w).wait_send()
        mate_copy(w).wait_send()
        pass_copy(w).wait_send()

    @pl.when(place < last)
    def _():
        def sent(i, carry):
            key_copy(i // KEYVAL_HEADS, lax.rem(i, KEYVAL_HEADS)).wait_send()
            return carry

        lax.fori_loop(0, (place + 1) * KEYVAL_HEADS, sent, 0)


def front(tokens, cotangent, cosine, sine, weights):
    blocks = lax.axis_size("ctx")
    parts = lax.axis_size("fsdp")
    positions = cosine.shape[-1]
    vmem = pl.BlockSpec(memory_space=pltpu.VMEM)
    anywhere = pl.BlockSpec(memory_space=pl.ANY)
    dma = pltpu.SemaphoreType.DMA
    shape = lambda *dims: jax.ShapeDtypeStruct(dims, jnp.bfloat16)
    count = len(weights)
    features = tokens.shape[1]
    area = QUERY_HEADS * positions * positions * blocks
    return pl.pallas_call(
        front_kernel,
        in_specs=[vmem] * (4 + count),
        out_specs=[vmem] * 8 + [vmem] * 2 + [anywhere] * 4 + [vmem],
        out_shape=[
            shape(features, positions), shape(features, positions), shape(features, positions),
            shape(features, positions),
            shape(QUERY_HEADS, HEAD_WIDTH, positions),
            shape(blocks, KEYVAL_HEADS, 2, HEAD_WIDTH, positions),
            shape(QUERY_HEADS, HEAD_WIDTH, positions),
            jax.ShapeDtypeStruct((QUERY_HEADS, 1, positions), jnp.float32),
        ] + [shape(parts, *w.shape) for w in weights],
        scratch_shapes=[
            pltpu.VMEM((QUERY_WIDTH, positions), jnp.float32),
            pltpu.VMEM((QUERY_HEADS, 1, positions), jnp.float32),
            pltpu.VMEM((QUERY_HEADS, 1, positions), jnp.float32),
            pltpu.VMEM((QUERY_HEADS, HEAD_WIDTH, positions), jnp.float32),
            dma((3 + count,)),
            dma, dma,
            dma((2,)), dma((2,)),
            dma((count,)), dma((count,)),
            dma((count,)), dma((count,)),
            dma((count,)), dma((count,)),
            dma((blocks, KEYVAL_HEADS)), dma((blocks, KEYVAL_HEADS)),
        ],
        compiler_params=pltpu.CompilerParams(
            vmem_limit_bytes=KERNEL_VMEM, collective_id=2, has_side_effects=True
        ),
        cost_estimate=pl.CostEstimate(
            flops=16 * HEAD_WIDTH * area, bytes_accessed=10 * tokens.size, transcendentals=area
        ),
        name="front",
    )(tokens, cotangent, cosine, sine, *weights)


def on_device(
    tokens, cotangent, input_gain, w_query, w_keyval, w_output, middle_gain, w_gate, w_up, w_down
):
    half = lax.axis_index("tp")
    low_half = half == 0
    pair = [(0, 1), (1, 0)]

    def to_partner(value_rows):
        return lax.ppermute(value_rows, "tp", pair)

    def in_order(mine, received):
        return jnp.concatenate(
            [jnp.where(low_half, mine, received), jnp.where(low_half, received, mine)], 0
        )

    def take(value_rows, index):
        return lax.dynamic_index_in_dim(value_rows, index, 0, keepdims=False)

    tokens_own = in_order(take(tokens, half), to_partner(take(tokens, 1 - half)))
    full_gain_one, full_gain_two = (
        lax.all_gather(input_gain, "fsdp", axis=0, tiled=True),
        lax.all_gather(middle_gain, "fsdp", axis=0, tiled=True),
    )
    full_in = lax.all_gather(jnp.concatenate([w_query, w_keyval], 1), "fsdp", axis=0, tiled=True)
    full_output = lax.all_gather(w_output, "fsdp", axis=0, tiled=True)
    full_gate = lax.all_gather(w_gate, "fsdp", axis=0, tiled=True)
    full_up = lax.all_gather(w_up, "fsdp", axis=0, tiled=True)
    full_down = lax.all_gather(w_down, "fsdp", axis=0, tiled=True)
    cotangent_received = to_partner(cotangent)
    cotangent_own = in_order(take(cotangent, half), take(cotangent_received, half))
    cotangent_other = in_order(take(cotangent, 1 - half), take(cotangent_received, 1 - half))

    token_positions = tokens_own.shape[0]
    cosine, sine = rope_tables(token_positions, lax.axis_index("ctx") * token_positions)
    gain_one = full_gain_one.astype(jnp.float32)
    inputs = tokens_own.astype(jnp.float32)
    unit_one, inverse_one = normalize(inputs)
    normed_one = (unit_one * gain_one).astype(jnp.bfloat16)
    keyval_raw = dot(full_in[:, QUERY_WIDTH:], normed_one, 0, 1)
    keyval_low = jnp.concatenate(
        [apply_rotary(keyval_raw[:KEY_WIDTH], cosine, sine), keyval_raw[KEY_WIDTH:]], 0
    ).astype(jnp.bfloat16)
    blocks = lax.axis_size("ctx")
    keyval = jnp.stack([keyval_low] + [move_along(keyval_low, s) for s in range(1, blocks)], 0)
    keyval = keyval.reshape(blocks, 2, KEYVAL_HEADS, HEAD_WIDTH, token_positions)
    query_raw = dot(full_in[:, :QUERY_WIDTH], normed_one, 0, 1)
    query_low = (
        apply_rotary(query_raw, cosine, sine)
        .astype(jnp.bfloat16)
        .reshape(QUERY_HEADS, HEAD_WIDTH, token_positions)
    )
    mixed_heads, lse = attend_forward(query_low, keyval)
    mixed_low = mixed_heads.reshape(QUERY_WIDTH, token_positions)
    middle = inputs + dot(mixed_low, full_output, 0, 0)

    gain_two = full_gain_two.astype(jnp.float32)
    unit_two, inverse_two = normalize(middle)
    normed_two = (unit_two * gain_two).astype(jnp.bfloat16)
    normed_other = to_partner(normed_two)

    def feed(rows, back_rows):
        gate_proj = dot(rows, full_gate, 1, 0)
        up_proj = dot(rows, full_up, 1, 0)
        sigmoid_gate = jax.nn.sigmoid(gate_proj)
        swish_gate = gate_proj * sigmoid_gate
        hidden = (swish_gate * up_proj).astype(jnp.bfloat16)
        back_hidden = dot(back_rows, full_down, 1, 0)
        back_gate = (
            back_hidden * up_proj * sigmoid_gate * (1.0 + gate_proj * (1.0 - sigmoid_gate))
        ).astype(jnp.bfloat16)
        back_up = (back_hidden * swish_gate).astype(jnp.bfloat16)
        return (hidden, back_gate, back_up)

    def feed_input_back(back_gate, back_up):
        return dot(back_gate, full_gate, 1, 1) + dot(back_up, full_up, 1, 1)

    hidden_own, back_gate_own, back_up_own = feed(normed_two, cotangent_own)
    hidden_other, back_gate_other, back_up_other = feed(normed_other, cotangent_other)
    back_two_received = to_partner(
        feed_input_back(back_gate_other, back_up_other).astype(jnp.bfloat16)
    )
    back_two = feed_input_back(back_gate_own, back_up_own) + back_two_received.astype(jnp.float32)
    feed_received = to_partner(dot(hidden_other, full_down, 1, 1).astype(jnp.bfloat16))
    result_own = (
        middle + dot(hidden_own, full_down, 1, 1) + feed_received.astype(jnp.float32)
    ).astype(jnp.bfloat16)

    def feed_gradient(left_own, right_own, left_other, right_other):
        gradient = dot(left_own, right_own, 0, 0) + dot(left_other, right_other, 0, 0)
        shared = scatter_sum(gradient.astype(jnp.bfloat16), "fsdp")
        return whole_sum(shared, (("ctx", 2),))

    share_down = feed_gradient(cotangent_own, hidden_own, cotangent_other, hidden_other)
    share_gate = feed_gradient(normed_two, back_gate_own, normed_other, back_gate_other)
    share_up = feed_gradient(normed_two, back_up_own, normed_other, back_up_other)

    grad_gain_two = jnp.sum(back_two * unit_two, axis=0)
    back_middle = cotangent_own.astype(jnp.float32) + norm_back(
        back_two * gain_two, unit_two, inverse_two
    )
    back_attention = back_middle.astype(jnp.bfloat16)
    back_mixed = dot(full_output, back_attention, 1, 1).astype(jnp.bfloat16)
    back_mixed = back_mixed.reshape(query_low.shape)
    grad_output = dot(mixed_low, back_attention, 1, 0).astype(jnp.bfloat16)
    share_output = whole_sum(scatter_sum(grad_output, "fsdp"), (("tp", 1), ("ctx", 2)))

    back_query = []
    back_key = []
    back_value = []
    for first, count in ((0, 3), (3, 2)):
        part_query, part_keyval = attend_backward(
            query_low, keyval, back_mixed, mixed_heads, lse, cosine, sine, first, count
        )
        part_keyval = part_keyval.reshape(blocks, 2 * count * HEAD_WIDTH, token_positions)
        owned = part_keyval[0].astype(jnp.float32)
        for s in range(1, blocks):
            owned += move_along(part_keyval[s], -s).astype(jnp.float32)
        back_query.append(part_query.reshape(-1, token_positions))
        back_key.append(
            apply_rotary(owned[: count * HEAD_WIDTH], cosine, -sine).astype(jnp.bfloat16)
        )
        back_value.append(owned[count * HEAD_WIDTH :].astype(jnp.bfloat16))
    back_in = jnp.concatenate(back_query + back_key + back_value, 0)
    grad_in = dot(normed_one, back_in, 0, 1)
    back_one = dot(back_in, full_in, 0, 1)
    grad_gain_one = jnp.sum(back_one * unit_one, axis=0)
    back_inputs = back_middle + norm_back(back_one * gain_one, unit_one, inverse_one)

    def to_positions(value_rows):
        split = value_rows.reshape(2, token_positions // 2, value_rows.shape[-1])
        received = to_partner(take(split, 1 - half))
        return in_order(take(split, half)[None], received[None])

    result = to_positions(result_own)
    grad_tokens = to_positions(back_inputs.astype(jnp.bfloat16)).astype(jnp.float32)
    gradients = jnp.concatenate([grad_in, grad_gain_one[:, None], grad_gain_two[:, None]], 1)
    share_in = lax.psum(
        lax.psum_scatter(
            gradients.astype(jnp.bfloat16), "fsdp", scatter_dimension=0, tiled=True
        ),
        ("ctx", "tp"),
    ).astype(jnp.float32)
    width = full_in.shape[1]
    return (
        result,
        grad_tokens,
        share_in[:, width],
        share_in[:, :QUERY_WIDTH],
        share_in[:, QUERY_WIDTH:width],
        share_output,
        share_in[:, width + 1],
        share_gate,
        share_up,
        share_down,
    )


def fast_on_device(
    tokens, cotangent, input_gain, w_query, w_keyval, w_output, middle_gain, w_gate, w_up, w_down
):
    pair = [(0, 1), (1, 0)]

    def to_partner(value_rows):
        return lax.ppermute(value_rows, "tp", pair)

    parts = lax.axis_size("fsdp")
    width_in = tokens.shape[-1]
    rows = width_in // parts
    token_positions = 2 * tokens.shape[1]
    cosine, sine = rope_tables(token_positions, lax.axis_index("ctx") * token_positions)
    gains = jnp.pad(jnp.stack([input_gain, middle_gain], 1), ((0, 0), (0, 126)))
    (
        tokens_own, cotangent_own, cotangent_other, normed_one, query_low, keyval,
        mixed_heads, lse, *full,
    ) = front(
        tokens.swapaxes(1, 2), cotangent.swapaxes(1, 2), cosine, sine,
        (w_query, w_keyval, w_output, w_gate, w_up, w_down, gains),
    )
    full_query, full_keyval, full_output, full_gate, full_up, full_down, gains = [
        w.reshape(width_in, -1) for w in full
    ]
    tokens_own, cotangent_own, cotangent_other, normed_one = [
        v.T for v in (tokens_own, cotangent_own, cotangent_other, normed_one)
    ]
    gain_one = gains[:, 0].astype(jnp.float32)
    full_gain_two = gains[:, 1]
    inputs = tokens_own.astype(jnp.float32)
    unit_one, inverse_one = normalize(inputs)
    mixed_low = mixed_heads.reshape(QUERY_WIDTH, token_positions)
    middle = inputs + dot(mixed_low, full_output, 0, 0)

    gain_two = full_gain_two.astype(jnp.float32)
    unit_two, inverse_two = normalize(middle)
    normed_two = (unit_two * gain_two).astype(jnp.bfloat16)
    normed_other = to_partner(normed_two)

    def feed(rows, back_rows):
        gate_proj = dot(rows, full_gate, 1, 0)
        up_proj = dot(rows, full_up, 1, 0)
        sigmoid_gate = jax.nn.sigmoid(gate_proj)
        swish_gate = gate_proj * sigmoid_gate
        hidden = (swish_gate * up_proj).astype(jnp.bfloat16)
        back_hidden = dot(back_rows, full_down, 1, 0)
        back_gate = (
            back_hidden * up_proj * sigmoid_gate * (1.0 + gate_proj * (1.0 - sigmoid_gate))
        ).astype(jnp.bfloat16)
        back_up = (back_hidden * swish_gate).astype(jnp.bfloat16)
        return (hidden, back_gate, back_up)

    def feed_input_back(back_gate, back_up):
        return dot(back_gate, full_gate, 1, 1) + dot(back_up, full_up, 1, 1)

    hidden_own, back_gate_own, back_up_own = feed(normed_two, cotangent_own)
    hidden_other, back_gate_other, back_up_other = feed(normed_other, cotangent_other)
    back_two_received = to_partner(
        feed_input_back(back_gate_other, back_up_other).astype(jnp.bfloat16)
    )
    back_two = feed_input_back(back_gate_own, back_up_own) + back_two_received.astype(jnp.float32)
    feed_other = dot(hidden_other, full_down, 1, 1).astype(jnp.bfloat16)
    base = middle + dot(hidden_own, full_down, 1, 1)

    def feed_gradient(left_own, right_own, left_other, right_other):
        gradient = dot(left_own, right_own, 0, 0) + dot(left_other, right_other, 0, 0)
        return gradient.astype(jnp.bfloat16).reshape(lax.axis_size("fsdp"), -1, gradient.shape[1])

    gradients = (
        feed_gradient(cotangent_own, hidden_own, cotangent_other, hidden_other),
        feed_gradient(normed_two, back_gate_own, normed_other, back_gate_other),
        feed_gradient(normed_two, back_up_own, normed_other, back_up_other),
    )

    grad_gain_two = jnp.sum(back_two * unit_two, axis=0)
    back_middle = cotangent_own.astype(jnp.float32) + norm_back(
        back_two * gain_two, unit_two, inverse_two
    )
    back_attention = back_middle.astype(jnp.bfloat16)
    back_mixed = dot(full_output, back_attention, 1, 1).astype(jnp.bfloat16)
    back_mixed = back_mixed.reshape(query_low.shape)
    grad_output = dot(mixed_low, back_attention, 1, 0).astype(jnp.bfloat16)
    back_query, back_keyval, share, result = backward_sum(
        query_low, keyval, back_mixed, mixed_heads, lse, cosine, sine, base.T, feed_other.T,
        gradients,
    )
    back_query = back_query.reshape(QUERY_WIDTH, token_positions)
    back_keyval = back_keyval.reshape(2 * KEY_WIDTH, token_positions)
    grad_query = dot(normed_one, back_query, 0, 1).astype(jnp.bfloat16)
    grad_keyval = dot(normed_one, back_keyval, 0, 1).astype(jnp.bfloat16)
    back_one = dot(back_query, full_query, 0, 1) + dot(back_keyval, full_keyval, 0, 1)
    grad_gain_one = jnp.sum(back_one * unit_one, axis=0)
    back_inputs = back_middle + norm_back(back_one * gain_one, unit_one, inverse_one)

    gains = jnp.pad(
        jnp.stack([grad_gain_one.reshape(parts, rows), grad_gain_two.reshape(parts, rows)], 1),
        ((0, 0), (0, 14), (0, 2 * KEY_WIDTH - rows)),
    )
    share_output, share_query, share_keyval, share_rest, grad_tokens = gradient_sum(
        [v.reshape(parts, rows, -1) for v in (grad_output, grad_query, grad_keyval)],
        gains.astype(jnp.bfloat16), share, back_inputs.astype(jnp.bfloat16).T,
    )
    return (
        result.swapaxes(1, 2),
        grad_tokens.swapaxes(1, 2).astype(jnp.float32),
        share_keyval[rows, :rows].astype(jnp.float32),
        share_query[:rows].astype(jnp.float32),
        share_keyval[:rows].astype(jnp.float32),
        share_output[:rows].astype(jnp.float32),
        share_keyval[rows + 1, :rows].astype(jnp.float32),
        share_rest[0].astype(jnp.float32),
        share_rest[1].astype(jnp.float32),
        share[0].astype(jnp.float32),
    )


def solution(mesh):
    rows = P("fsdp", ("ctx", "tp"), None)
    specs = (
        P("fsdp"), P("fsdp", None), P("fsdp", None), P("fsdp", None),
        P("fsdp"), P("fsdp", "tp"), P("fsdp", "tp"), P("fsdp", "tp"),
    )
    kernels = mesh.shape["fsdp"] == 4 and mesh.shape["tp"] == 2 and mesh.shape["ctx"] == 4
    return jax.shard_map(
        fast_on_device if kernels else on_device,
        mesh=mesh,
        in_specs=(rows, rows) + specs,
        out_specs=(rows, rows) + specs,
        check_vma=False,
    )
```

```python
import jax
import jax.numpy as jnp
from jax import lax
from jax.experimental import pallas as pl
from jax.experimental.pallas import tpu as pltpu
from jax.sharding import PartitionSpec as P

QUERY_HEADS = 15
KEYVAL_HEADS = 5
GROUP = QUERY_HEADS // KEYVAL_HEADS
HEAD_WIDTH = 64
HALF = HEAD_WIDTH // 2
KEY_WIDTH = 320
QUERY_WIDTH = QUERY_HEADS * HEAD_WIDTH
SCALE = HEAD_WIDTH ** (-0.5)

EPS = 1e-05
THETA = 10000.0
VMEM_LIMIT = 40 * 1024 * 1024


def dot(left, right, left_dim, right_dim):
    return lax.dot_general(
        left, right, (((left_dim,), (right_dim,)), ((), ())), preferred_element_type=jnp.float32
    )


def rope_tables(token_positions, first_place):
    position = (first_place + lax.iota(jnp.int32, token_positions)).astype(jnp.float32)
    frequency = THETA ** (-(2.0 * lax.iota(jnp.int32, HALF).astype(jnp.float32)) / HEAD_WIDTH)
    angles = frequency[:, None] * position[None, :]
    return (jnp.cos(angles), jnp.sin(angles))


def apply_rotary(rows, cosine, sine):
    shaped = rows.reshape(-1, 2, HALF, rows.shape[-1])
    leading = shaped[:, 0]
    trailing = shaped[:, 1]
    return jnp.stack(
        [leading * cosine - trailing * sine, trailing * cosine + leading * sine], 1
    ).reshape(rows.shape)


def normalize(value_rows):
    inverse_rms = lax.rsqrt(jnp.mean(value_rows * value_rows, -1, keepdims=True) + EPS)
    return (value_rows * inverse_rms, inverse_rms)


def norm_back(back_unit, unit_rows, inverse_rms):
    return inverse_rms * (
        back_unit - unit_rows * jnp.mean(back_unit * unit_rows, -1, keepdims=True)
    )


def causal(scores):
    key_place = lax.broadcasted_iota(jnp.int32, scores.shape, 0)
    query_place = lax.broadcasted_iota(jnp.int32, scores.shape, 1)
    return jnp.where(key_place <= query_place, scores, -jnp.inf)


def forward_kernel(query_ref, key_ref, value_ref, mixed_ref, lse_ref):
    place = lax.axis_index("ctx")
    queries = [query_ref[g] * jnp.bfloat16(SCALE) for g in range(GROUP)]

    def scores_of(keys_turned, g, masked):
        scores = dot(keys_turned, queries[g], 1, 0)
        return causal(scores) if masked else scores

    def first():
        keys_turned = key_ref[0, 0, 0].T
        values = value_ref[0, 0, 0]
        carried = []
        for g in range(GROUP):
            scores = scores_of(keys_turned, g, True)
            top = jnp.max(scores, 0, keepdims=True)
            lifted = jnp.exp(scores - top)
            total = jnp.sum(lifted, 0, keepdims=True)
            carried += [top, total, dot(values, lifted.astype(jnp.bfloat16), 1, 0)]
        return tuple(carried)

    def step(block, carried):
        keys_turned = key_ref[block, 0, 0].T
        values = value_ref[block, 0, 0]
        later = []
        for g in range(GROUP):
            top, total, mixed = carried[3 * g : 3 * g + 3]
            scores = scores_of(keys_turned, g, False)
            new_top = jnp.maximum(top, jnp.max(scores, 0, keepdims=True))
            lifted = jnp.exp(scores - new_top)
            shrink = jnp.exp(top - new_top)
            later += [
                new_top,
                total * shrink + jnp.sum(lifted, 0, keepdims=True),
                mixed * shrink + dot(values, lifted.astype(jnp.bfloat16), 1, 0),
            ]
        return tuple(later)

    carried = lax.fori_loop(1, place + 1, step, first())
    for g in range(GROUP):
        top, total, mixed = carried[3 * g : 3 * g + 3]
        mixed_ref[g] = (mixed / total).astype(jnp.bfloat16)
        lse_ref[g] = top + jnp.log(total)


def attend_forward(query, keyval):
    blocks, token_positions = keyval.shape[0], keyval.shape[-1]
    head_block = (GROUP, HEAD_WIDTH, token_positions)
    key_block = (blocks, 1, 1, HEAD_WIDTH, token_positions)
    area = QUERY_HEADS * token_positions * token_positions * blocks
    return pl.pallas_call(
        forward_kernel,
        grid=(KEYVAL_HEADS,),
        in_specs=[
            pl.BlockSpec(head_block, lambda j: (j, 0, 0)),
            pl.BlockSpec(key_block, lambda j: (0, 0, j, 0, 0)),
            pl.BlockSpec(key_block, lambda j: (0, 1, j, 0, 0)),
        ],
        out_specs=[
            pl.BlockSpec(head_block, lambda j: (j, 0, 0)),
            pl.BlockSpec((GROUP, 1, token_positions), lambda j: (j, 0, 0)),
        ],
        out_shape=[
            jax.ShapeDtypeStruct(query.shape, jnp.bfloat16),
            jax.ShapeDtypeStruct((QUERY_HEADS, 1, token_positions), jnp.float32),
        ],
        compiler_params=pltpu.CompilerParams(vmem_limit_bytes=VMEM_LIMIT),
        cost_estimate=pl.CostEstimate(
            flops=16 * HEAD_WIDTH * area, bytes_accessed=6 * query.size, transcendentals=area
        ),
        name="attend_forward",
    )(query, keyval, keyval)


def backward_kernel(
    query_ref, key_ref, value_ref, back_ref, mixed_ref, lse_ref, cosine_ref, sine_ref,
    back_query_ref, back_keyval_ref,
):
    place = lax.axis_index("ctx")
    blocks = key_ref.shape[0]
    queries = [query_ref[g] * jnp.bfloat16(SCALE) for g in range(GROUP)]
    backs = [back_ref[g] for g in range(GROUP)]
    tops = [lse_ref[g] for g in range(GROUP)]
    sums = [
        jnp.sum(backs[g].astype(jnp.float32) * mixed_ref[g].astype(jnp.float32), 0, keepdims=True)
        for g in range(GROUP)
    ]

    def step(block, carried, masked=False):
        keys = key_ref[block, 0, 0]
        keys_turned = keys.T
        values_turned = value_ref[block, 0, 0].T
        back_key = jnp.zeros(keys.shape, jnp.float32)
        back_value = jnp.zeros(keys.shape, jnp.float32)
        later = []
        for g in range(GROUP):
            scores = dot(keys_turned, queries[g], 1, 0)
            if masked:
                scores = causal(scores)
            weights = jnp.exp(scores - tops[g])
            back_weights = dot(values_turned, backs[g], 1, 0)
            back_scores = (weights * (back_weights - sums[g])).astype(jnp.bfloat16)
            later.append(carried[g] + dot(keys, back_scores, 1, 0))
            back_key += dot(queries[g], back_scores, 1, 1)
            back_value += dot(backs[g], weights.astype(jnp.bfloat16), 1, 1)
        back_keyval_ref[block, 0, 0] = back_key.astype(jnp.bfloat16)
        back_keyval_ref[block, 1, 0] = back_value.astype(jnp.bfloat16)
        return tuple(later)

    start = tuple(jnp.zeros(query_ref.shape[1:], jnp.float32) for g in range(GROUP))
    carried = lax.fori_loop(1, place + 1, step, step(0, start, True))

    def clear(block, unused):
        zero = jnp.zeros(key_ref.shape[3:], jnp.bfloat16)
        back_keyval_ref[block, 0, 0] = zero
        back_keyval_ref[block, 1, 0] = zero
        return unused

    lax.fori_loop(place + 1, blocks, clear, 0)
    cosine = cosine_ref[...]
    sine = sine_ref[...]
    for g in range(GROUP):
        leading = carried[g][:HALF] * SCALE
        trailing = carried[g][HALF:] * SCALE
        back_query_ref[g, :HALF] = (leading * cosine + trailing * sine).astype(jnp.bfloat16)
        back_query_ref[g, HALF:] = (trailing * cosine - leading * sine).astype(jnp.bfloat16)


def attend_backward(query, keyval, back_mixed, mixed, lse, cosine, sine, first, count):
    blocks, token_positions = keyval.shape[0], keyval.shape[-1]
    head_block = (GROUP, HEAD_WIDTH, token_positions)
    key_block = (blocks, 1, 1, HEAD_WIDTH, token_positions)
    area = count * GROUP * token_positions * token_positions * blocks
    heads = pl.BlockSpec(head_block, lambda j: (j + first, 0, 0))
    table = pl.BlockSpec((HALF, token_positions), lambda j: (0, 0))
    return pl.pallas_call(
        backward_kernel,
        grid=(count,),
        in_specs=[
            heads,
            pl.BlockSpec(key_block, lambda j: (0, 0, j + first, 0, 0)),
            pl.BlockSpec(key_block, lambda j: (0, 1, j + first, 0, 0)),
            heads,
            heads,
            pl.BlockSpec((GROUP, 1, token_positions), lambda j: (j + first, 0, 0)),
            table,
            table,
        ],
        out_specs=[
            pl.BlockSpec(head_block, lambda j: (j, 0, 0)),
            pl.BlockSpec((blocks, 2, 1, HEAD_WIDTH, token_positions), lambda j: (0, 0, j, 0, 0)),
        ],
        out_shape=[
            jax.ShapeDtypeStruct((count * GROUP, HEAD_WIDTH, token_positions), jnp.bfloat16),
            jax.ShapeDtypeStruct(
                (blocks, 2, count, HEAD_WIDTH, token_positions), jnp.bfloat16
            ),
        ],
        compiler_params=pltpu.CompilerParams(vmem_limit_bytes=VMEM_LIMIT),
        cost_estimate=pl.CostEstimate(
            flops=40 * HEAD_WIDTH * area, bytes_accessed=10 * query.size, transcendentals=area
        ),
        name="attend_backward",
    )(query, keyval, keyval, back_mixed, mixed, lse, cosine, sine)


def move_along(value, distance):
    blocks = lax.axis_size("ctx")
    pairs = [(i, i + distance) for i in range(blocks) if 0 <= i + distance < blocks]
    return lax.ppermute(value, "ctx", pairs)


def trade(value, axis, step):
    pairs = [(i, i ^ step) for i in range(lax.axis_size(axis))]
    return lax.ppermute(value, axis, pairs)


def add_low(left, right):
    return (left.astype(jnp.float32) + right.astype(jnp.float32)).astype(jnp.bfloat16)


def scatter_sum(value, axis):
    size = lax.axis_size(axis)
    index = lax.axis_index(axis)
    rows = value.shape[0] // size
    step = 1
    while step < size:
        count = value.shape[0] // (2 * rows)
        split = value.reshape(count, 2, rows, value.shape[-1])
        second = (index // step) % 2 == 1
        kept = jnp.where(second, split[:, 1], split[:, 0])
        sent = jnp.where(second, split[:, 0], split[:, 1])
        value = add_low(kept, trade(sent, axis, step)).reshape(count * rows, value.shape[-1])
        step *= 2
    return value


def whole_sum(value, others):
    half_rows = value.shape[0] // 2
    second = lax.axis_index("ctx") % 2 == 1
    upper, lower = value[:half_rows], value[half_rows:]
    received = trade(jnp.where(second, upper, lower), "ctx", 1)
    total = add_low(jnp.where(second, lower, upper), received)
    for axis, first_step in others:
        step = first_step
        while step < lax.axis_size(axis):
            total = add_low(total, trade(total, axis, step))
            step *= 2
    received = trade(total, "ctx", 1)
    return jnp.concatenate(
        [jnp.where(second, received, total), jnp.where(second, total, received)], 0
    ).astype(jnp.float32)


MESH = pl.DeviceIdType.MESH
KERNEL_VMEM = 60 * 1024 * 1024
CHUNK_ROWS = 80


def remote(source, target, send_sem, recv_sem, **place):
    return pltpu.make_async_remote_copy(
        src_ref=source, dst_ref=target, send_sem=send_sem, recv_sem=recv_sem,
        device_id=place, device_id_type=MESH,
    )


def wide(value):
    return value.astype(jnp.float32)


def low(value):
    return value.astype(jnp.bfloat16)


def greet(**place):
    pl.semaphore_signal(
        pltpu.get_barrier_semaphore(), inc=1, device_id=place, device_id_type=MESH
    )


def backward_sum_kernel(
    query_ref, keyval_ref, back_ref, mixed_ref, lse_ref, cosine_ref, sine_ref,
    base_ref, feed_ref, tokens_ref, normed_ref, middle_ref, gains_ref, gain_two_ref,
    full_query, full_keyval, down_ref, gate_ref, up_ref, out_ref,
    share_ref, result_ref, back_tokens_ref, *refs,
):
    chunks_in = 4
    shares, refs = refs[:chunks_in], refs[chunks_in:]
    whole, mate_part, y_part, x_part, z_part = [
        refs[i * chunks_in : (i + 1) * chunks_in] for i in range(5)
    ]
    (
    own, mate_in, y_in, up_in, parts, part_in, back_total, row_sums,
    own_sem, mate_send, mate_recv, y_send, y_recv, up_send, up_recv, down_send, down_recv,
    part_send, part_recv, feed_in, traded, feed_send, feed_recv, trade_send, trade_recv,
    back_query_ref, back_keyval_ref, back_one, token_traded,
    whole_sem, sum_mate_send, sum_mate_recv, sum_y_send, sum_y_recv, sum_x_send, sum_x_recv,
    sum_z_send, sum_z_recv, all_send, all_recv, back_send, back_recv, token_send, token_recv,
    ) = refs[5 * chunks_in :]
    place = lax.axis_index("ctx")
    last = lax.axis_size("ctx") - 1
    blocks = last + 1
    rank = lax.axis_index("fsdp")
    core = rank % 2
    y = rank // 2
    side = lax.axis_index("tp")
    mate = rank + 1 - 2 * core
    across = rank + 2 - 4 * y
    gradients = (down_ref, gate_ref, up_ref)
    rows = share_ref.shape[1]
    per = rows // CHUNK_ROWS
    chunks = len(gradients) * per
    early = per

    for m, gradient in enumerate(gradients):
        for half in range(2):
            pltpu.make_async_copy(
                gradient.at[2 * half + core], own.at[m, half], own_sem.at[m, half]
            ).start()
    greet(fsdp=mate)
    greet(fsdp=across)
    greet(tp=1 - side)
    for d in range(1, blocks):
        greet(ctx=lax.rem(place + d, blocks))
    filled = out_ref.shape[1]
    tail = whole[0].shape[1] - filled
    for n in range(chunks_in):
        width = whole[n].shape[-1]
        whole[n][:, filled:] = jnp.zeros((whole[n].shape[0], tail, width), jnp.bfloat16)
        mate_part[n][:, filled:] = jnp.zeros((2, tail, width), jnp.bfloat16)
    for f in range(whole[0].shape[0]):
        pltpu.make_async_copy(
            out_ref.at[f], whole[0].at[f, pl.ds(0, filled)], whole_sem.at[f]
        ).start()
    pl.semaphore_wait(pltpu.get_barrier_semaphore(), 3 + last)

    feed_copy = remote(feed_ref, feed_in, feed_send, feed_recv, tp=1 - side)
    trade_copy = remote(traded, result_ref.at[side], trade_send, trade_recv, tp=1 - side)
    feed_copy.start()
    pair_width = traded.shape[-1]
    step_rows = traded.shape[0] // 4

    def finish_result():
        feed_copy.wait_recv()

        def some_rows(i, carry):
            at = pl.ds(pl.multiple_of(i * step_rows, step_rows), step_rows)
            for target, slot in ((result_ref.at[side], side), (traded, 1 - side)):
                columns = pl.ds(pl.multiple_of(slot * pair_width, pair_width), pair_width)
                target[at] = low(base_ref[at, columns] + wide(feed_in[at, columns]))
            return carry

        lax.fori_loop(0, 4, some_rows, 0)
        trade_copy.start()

    half_rows = whole[0].shape[1] // 2
    piece = half_rows // blocks
    kept = 2 * y + core

    def sum_mate(n, half):
        return remote(
            whole[n].at[2 * half + 1 - core, pl.ds(0, filled)],
            mate_part[n].at[half, pl.ds(0, filled)],
            sum_mate_send.at[n, half], sum_mate_recv.at[n, half], fsdp=mate,
        )

    def sum_y(n):
        return remote(
            mate_part[n].at[1 - y], y_part[n], sum_y_send.at[n], sum_y_recv.at[n], fsdp=across
        )

    def sum_x(n):
        other = pl.ds(pl.multiple_of((1 - side) * half_rows, half_rows), half_rows)
        return remote(
            whole[n].at[kept, other], x_part[n], sum_x_send.at[n], sum_x_recv.at[n],
            tp=1 - side,
        )

    def sum_z(n, d):
        target = lax.rem(place + d, blocks)
        at = pl.ds(pl.multiple_of(side * half_rows + target * piece, piece), piece)
        return remote(
            whole[n].at[kept, at], z_part[n].at[d - 1], sum_z_send.at[n, d - 1],
            sum_z_recv.at[n, d - 1], ctx=target,
        )

    def all_copy(n, d, origin):
        spot = shares[n].at[
            pl.ds(pl.multiple_of(side * half_rows + origin * piece, piece), piece)
        ]
        return remote(
            spot, spot, all_send.at[n, d - 1], all_recv.at[n, d - 1],
            ctx=lax.rem(place + d, blocks),
        )

    def back_copy(n, half):
        spot = shares[n].at[pl.ds(pl.multiple_of(half * half_rows, half_rows), half_rows)]
        return remote(spot, spot, back_send.at[n], back_recv.at[n], tp=1 - side)

    def to_mate(n):
        for half in range(2):
            sum_mate(n, half).start()

    def to_y(n):
        for half in range(2):
            sum_mate(n, half).wait_recv()
        quarter = 2 * (1 - y) + core
        mate_part[n][1 - y] = low(wide(whole[n][quarter]) + wide(mate_part[n][1 - y]))
        sum_y(n).start()

    def to_x(n):
        sum_y(n).wait_recv()
        whole[n][kept] = low(
            wide(whole[n][kept]) + wide(mate_part[n][y]) + wide(y_part[n][...])
        )
        sum_x(n).start()

    def to_z(n):
        sum_x(n).wait_recv()
        at = pl.ds(pl.multiple_of(side * half_rows, half_rows), half_rows)
        whole[n][kept, at] = low(wide(whole[n][kept, at]) + wide(x_part[n][...]))
        for d in range(1, blocks):
            sum_z(n, d).start()

    def to_all(n):
        at = pl.ds(pl.multiple_of(side * half_rows + place * piece, piece), piece)
        total = wide(whole[n][kept, at])
        for d in range(1, blocks):
            sum_z(n, d).wait_recv()
            total += wide(z_part[n][d - 1])
        shares[n][at] = low(total)
        for d in range(1, blocks):
            all_copy(n, d, place).start()

    def to_back(n):
        for d in range(1, blocks):
            all_copy(n, d, lax.rem(place + blocks - d, blocks)).wait_recv()
        back_copy(n, side).start()

    def finish_sum(n):
        back_copy(n, 1 - side).wait_recv()
        for half in range(2):
            sum_mate(n, half).wait_send()
        sum_y(n).wait_send()
        sum_x(n).wait_send()
        for d in range(1, blocks):
            sum_z(n, d).wait_send()
            all_copy(n, d, place).wait_send()
        back_copy(n, side).wait_send()

    def weight_gradient(n, back_ref):
        def quarter(f, carry):
            rows_of = normed_ref[pl.ds(pl.multiple_of(f * filled, filled), filled)]
            whole[n][f, :filled] = low(dot(rows_of, back_ref[...], 1, 1))
            return carry

        lax.fori_loop(0, whole[n].shape[0], quarter, 0)

    token_copy = remote(
        token_traded, back_tokens_ref.at[side], token_send, token_recv, tp=1 - side
    )

    def input_gradient():
        tokens = wide(tokens_ref[...])
        inverse = lax.rsqrt(jnp.mean(tokens * tokens, 0, keepdims=True) + EPS)

        def quarter(f, total):
            at = pl.ds(pl.multiple_of(f * filled, filled), filled)
            unit = wide(tokens_ref[at]) * inverse
            back = dot(full_query[at], back_query_ref[...], 1, 0) + dot(
                full_keyval[at], back_keyval_ref[...], 1, 0
            )
            gain_sum = jnp.sum(back * unit, 1, keepdims=True)
            lane = lax.broadcasted_iota(jnp.int32, (filled, whole[3].shape[-1]), 1)
            whole[3][f, :filled] = low(
                jnp.where(lane == 0, gain_sum, jnp.where(lane == 1, gain_two_ref[at], 0.0))
            )
            back = back * wide(gains_ref[at])[:, :1]
            back_one[at] = back
            return total + jnp.sum(back * unit, 0, keepdims=True)

        total = lax.fori_loop(
            0, whole[0].shape[0], quarter, jnp.zeros((1, tokens_ref.shape[-1]), jnp.float32)
        )
        to_mate(3)
        mean = total / tokens_ref.shape[0]

        def rows_back(f, carry):
            at = pl.ds(pl.multiple_of(f * filled, filled), filled)
            unit = wide(tokens_ref[at]) * inverse
            back_one[at] = middle_ref[at] + inverse * (back_one[at] - unit * mean)
            for target, slot in ((back_tokens_ref.at[side], side), (token_traded, 1 - side)):
                columns = pl.ds(pl.multiple_of(slot * pair_width, pair_width), pair_width)
                target[at] = low(back_one[at, columns])
            return carry

        lax.fori_loop(0, whole[0].shape[0], rows_back, 0)
        token_copy.start()

    def chunk_at(ref, m, r, *front):
        return ref.at[(m,) + front + (pl.ds(r * CHUNK_ROWS, CHUNK_ROWS),)]

    def mate_copy(m, r, half):
        gradient = gradients[m]
        return remote(
            gradient.at[2 * half + 1 - core, pl.ds(r * CHUNK_ROWS, CHUNK_ROWS)],
            chunk_at(mate_in, m, r, half),
            mate_send.at[m * per + r, half], mate_recv.at[m * per + r, half], fsdp=mate,
        )

    for m in range(len(gradients)):
        for r in range(per):
            for half in range(2):
                mate_copy(m, r, half).start()
    for f in range(whole[0].shape[0]):
        pltpu.make_async_copy(
            out_ref.at[f], whole[0].at[f, pl.ds(0, filled)], whole_sem.at[f]
        ).wait()
    to_mate(0)
    for m, gradient in enumerate(gradients):
        for half in range(2):
            pltpu.make_async_copy(
                gradient.at[2 * half + core], own.at[m, half], own_sem.at[m, half]
            ).wait()

    def split(k):
        r = lax.rem(k, per)
        return k // per, pl.ds(pl.multiple_of(r * CHUNK_ROWS, CHUNK_ROWS), CHUNK_ROWS)

    def y_copy(k):
        m, at = split(k)
        return remote(
            own.at[m, 1 - y, at], y_in.at[m, at], y_send.at[k], y_recv.at[k], fsdp=across
        )

    def up_copy(k):
        m, at = split(k)
        return remote(
            own.at[m, y, at], up_in.at[m, at], up_send.at[k], up_recv.at[k], ctx=place + 1
        )

    def down_copy(k):
        m, at = split(k)
        return remote(
            share_ref.at[m, at], share_ref.at[m, at], down_send.at[k], down_recv.at[k],
            ctx=place - 1,
        )

    def to_across(k):
        m, at = split(k)
        for half in range(2):
            pltpu.make_async_copy(
                mate_in.at[m, half, at], mate_in.at[m, half, at], mate_recv.at[k, half]
            ).wait()
        own[m, 1 - y, at] = low(wide(own[m, 1 - y, at]) + wide(mate_in[m, 1 - y, at]))
        y_copy(k).start()

    def to_next(k):
        m, at = split(k)
        y_copy(k).wait_recv()
        total = wide(own[m, y, at]) + wide(mate_in[m, y, at]) + wide(y_in[m, at])

        @pl.when(place == 0)
        def _():
            own[m, y, at] = low(total)

        @pl.when(place > 0)
        def _():
            up_copy(k).wait_recv()
            own[m, y, at] = low(total + wide(up_in[m, at]))

        @pl.when(place < last)
        def _():
            up_copy(k).start()

        @pl.when(place == last)
        def _():
            share_ref[m, at] = own[m, y, at]

    def to_previous(k):
        down_copy(k).wait_recv()

        @pl.when(place > 0)
        def _():
            down_copy(k).start()

    def query_gradient(n):
        weight_gradient(n, back_query_ref)
        to_mate(n)

    def tick(t):
        @pl.when(t < chunks)
        def _():
            to_across(t)

        @pl.when(t == chunks)
        def _():
            finish_result()

        b = t - 3 - 2 * place

        @pl.when((b >= 0) & (b < 2 * chunks) & (lax.rem(b, 2) == 0))
        def _():
            to_next(b // 2)

        c = t - KEYVAL_HEADS * blocks - (last - place)

        @pl.when((place == last) & (c >= 0) & (c < chunks))
        def _():
            down_copy(c).start()

        @pl.when((place < last) & (c >= 0) & (c < early))
        def _():
            to_previous(c)

        for at, stage, n in (
            (chunks + 1, to_y, 0), (20, query_gradient, 1), (20, to_x, 0), (21, to_y, 1),
            (22, to_z, 0), (24, to_all, 0), (26, to_x, 1), (26, to_back, 0), (28, to_z, 1),
            (30, to_all, 1),
        ):
            @pl.when(t == at)
            def _(stage=stage, n=n):
                stage(n)

    def part_copy(j, s):
        return remote(
            parts.at[j, s], part_in.at[j, s - 1], part_send.at[j, s - 1],
            part_recv.at[j, s - 1], ctx=place - 1,
        )

    def step(j, s, masked):
        keys = keyval_ref[s, j, 0]
        keys_turned = keys.T
        values_turned = keyval_ref[s, j, 1].T
        back_key = jnp.zeros(keys.shape, jnp.float32)
        back_value = jnp.zeros(keys.shape, jnp.float32)
        for g in range(GROUP):
            head = GROUP * j + g
            query = query_ref[head]
            back = back_ref[head]
            if masked:
                row_sums[g] = jnp.sum(wide(back) * wide(mixed_ref[head]), 0, keepdims=True)
            scores = dot(keys_turned, query, 1, 0)
            if masked:
                scores = causal(scores)
            weights = jnp.exp(scores - lse_ref[head])
            back_weights = dot(values_turned, back, 1, 0)
            back_scores = low(weights * (back_weights - row_sums[g]))
            added = dot(keys, back_scores, 1, 0)
            if masked:
                back_total[g] = added
            else:
                back_total[g] += added
            back_key += dot(query, back_scores, 1, 1)
            back_value += dot(back, low(weights), 1, 1)
        parts[j, s, 0] = low(back_key)
        parts[j, s, 1] = low(back_value)

    def hand_on(j):
        for s in range(blocks):
            @pl.when(s <= place)
            def _(s=s):
                @pl.when(place < last)
                def _():
                    pltpu.make_async_copy(
                        part_in.at[j, s], part_in.at[j, s], part_recv.at[j, s]
                    ).wait()
                    for kind in range(2):
                        total = wide(parts[j, s, kind]) + wide(part_in[j, s, kind])
                        parts[j, s, kind] = low(total)

                if s > 0:
                    part_copy(j, s).start()
                else:
                    leading = wide(parts[j, 0, 0, :HALF])
                    trailing = wide(parts[j, 0, 0, HALF:])
                    cosine, sine = cosine_ref[...], sine_ref[...]
                    at = j * HEAD_WIDTH
                    back_keyval_ref[pl.ds(pl.multiple_of(at, HALF), HALF)] = low(
                        leading * cosine + trailing * sine
                    )
                    back_keyval_ref[pl.ds(pl.multiple_of(at + HALF, HALF), HALF)] = low(
                        trailing * cosine - leading * sine
                    )
                    at = pl.ds(pl.multiple_of(KEY_WIDTH + at, HEAD_WIDTH), HEAD_WIDTH)
                    back_keyval_ref[at] = low(wide(parts[j, 0, 1]))

    def head_loop(j, carry):
        @pl.when(j < KEYVAL_HEADS)
        def _():
            step(j, 0, True)

        tick(j * blocks)

        def block_loop(s, inner):
            @pl.when((j < KEYVAL_HEADS) & (s <= place))
            def _():
                step(j, s, False)

            tick(j * blocks + s)
            return inner

        lax.fori_loop(1, blocks, block_loop, 0)

        @pl.when(j < KEYVAL_HEADS)
        def _():
            cosine, sine = cosine_ref[...], sine_ref[...]
            for g in range(GROUP):
                leading = back_total[g, :HALF] * SCALE
                trailing = back_total[g, HALF:] * SCALE
                at = (GROUP * j + g) * HEAD_WIDTH
                back_query_ref[pl.ds(pl.multiple_of(at, HALF), HALF)] = low(
                    leading * cosine + trailing * sine
                )
                back_query_ref[pl.ds(pl.multiple_of(at + HALF, HALF), HALF)] = low(
                    trailing * cosine - leading * sine
                )

        ready = j - (last - place)

        @pl.when((ready >= 0) & (ready < KEYVAL_HEADS))
        def _():
            hand_on(ready)

        return carry

    assert (KEYVAL_HEADS + last) * blocks >= 4 + 4 * last + 2 * (chunks - 1)
    lax.fori_loop(0, KEYVAL_HEADS + last, head_loop, 0)

    def keyval_gradient(n):
        weight_gradient(n, back_keyval_ref)
        to_mate(n)

    later = (
        ((keyval_gradient, 2), (to_back, 1)), ((to_y, 2),), ((lambda n: input_gradient(), 3),),
        ((to_x, 2),), ((to_y, 3),), ((to_z, 2), (to_x, 3)), ((to_all, 2), (to_z, 3)),
        ((to_back, 2), (to_all, 3)), ((to_back, 3),),
    )
    for slot, stages in enumerate(later):
        for stage, n in stages:
            stage(n)
        for index in range(last):
            if early <= early + slot - last + 1 + index < chunks:
                @pl.when(place == index)
                def _(k=early + slot - last + 1 + index):
                    to_previous(k)

    assert len(later) >= chunks - early + last - 1
    for n in range(chunks_in):
        finish_sum(n)
    token_copy.wait()

    for m in range(len(gradients)):
        for r in range(per):
            for half in range(2):
                mate_copy(m, r, half).wait_send()

    def finish(k, carry):
        y_copy(k).wait_send()

        @pl.when(place < last)
        def _():
            up_copy(k).wait_send()

        @pl.when(place > 0)
        def _():
            down_copy(k).wait_send()

        return carry

    lax.fori_loop(0, chunks, finish, 0)

    def finish_parts(j, carry):
        for s in range(1, blocks):
            @pl.when(s <= place)
            def _(s=s):
                part_copy(j, s).wait_send()
        return carry

    lax.fori_loop(0, KEYVAL_HEADS, finish_parts, 0)
    feed_copy.wait_send()
    trade_copy.wait()


def backward_sum(
    query, keyval, back_mixed, mixed, lse, cosine, sine, base, feed, tokens, normed, middle,
    gains, gain_two, full_query, full_keyval, gradients, gradient_out,
):
    blocks, positions = keyval.shape[0], keyval.shape[-1]
    count, rows, columns = gradients[0].shape
    chunks = len(gradients) * rows // CHUNK_ROWS
    area = QUERY_HEADS * positions * positions * blocks
    vmem = pl.BlockSpec(memory_space=pltpu.VMEM)
    anywhere = pl.BlockSpec(memory_space=pl.ANY)
    dma = pltpu.SemaphoreType.DMA
    share = (len(gradients), rows, columns)
    head = (2, HEAD_WIDTH, positions)
    features = feed.shape[0]
    widths = (QUERY_WIDTH, QUERY_WIDTH, 2 * KEY_WIDTH, gains.shape[-1])
    padded = rows + 16
    half_rows = padded // 2
    low_type = jnp.bfloat16
    scratch = []
    for first in ((count, padded), (2, padded), (padded,), (half_rows,),
                  (blocks - 1, half_rows // blocks)):
        scratch += [pltpu.VMEM(first + (w,), low_type) for w in widths]
    each = len(widths)
    pairs = jax.ShapeDtypeStruct((2, features, positions // 2), low_type)
    return pl.pallas_call(
        backward_sum_kernel,
        in_specs=[vmem] * 16 + [anywhere] * 4,
        out_specs=[vmem] * (3 + each),
        out_shape=[jax.ShapeDtypeStruct(share, low_type), pairs, pairs] + [
            jax.ShapeDtypeStruct((padded, w), low_type) for w in widths
        ],
        scratch_shapes=scratch + [
            pltpu.VMEM((len(gradients), 2, rows, columns), low_type),
            pltpu.VMEM((len(gradients), 2, rows, columns), low_type),
            pltpu.VMEM(share, low_type),
            pltpu.VMEM(share, low_type),
            pltpu.VMEM((KEYVAL_HEADS, blocks) + head, low_type),
            pltpu.VMEM((KEYVAL_HEADS, blocks - 1) + head, low_type),
            pltpu.VMEM((GROUP, HEAD_WIDTH, positions), jnp.float32),
            pltpu.VMEM((GROUP, 1, positions), jnp.float32),
            dma((len(gradients), 2)),
            dma((chunks, 2)), dma((chunks, 2)),
            dma((chunks,)), dma((chunks,)),
            dma((chunks,)), dma((chunks,)),
            dma((chunks,)), dma((chunks,)),
            dma((KEYVAL_HEADS, blocks - 1)), dma((KEYVAL_HEADS, blocks - 1)),
            pltpu.VMEM(feed.shape, low_type),
            pltpu.VMEM((features, positions // 2), low_type),
            dma, dma, dma, dma,
            pltpu.VMEM((QUERY_WIDTH, positions), low_type),
            pltpu.VMEM((2 * KEY_WIDTH, positions), low_type),
            pltpu.VMEM((features, positions), jnp.float32),
            pltpu.VMEM((features, positions // 2), low_type),
            dma((count,)),
            dma((each, 2)), dma((each, 2)),
            dma((each,)), dma((each,)),
            dma((each,)), dma((each,)),
            dma((each, blocks - 1)), dma((each, blocks - 1)),
            dma((each, blocks - 1)), dma((each, blocks - 1)),
            dma((each,)), dma((each,)),
            dma, dma,
        ],
        compiler_params=pltpu.CompilerParams(
            vmem_limit_bytes=KERNEL_VMEM, collective_id=0, has_side_effects=True
        ),
        cost_estimate=pl.CostEstimate(
            flops=40 * HEAD_WIDTH * area, bytes_accessed=10 * query.size, transcendentals=area
        ),
        name="backward_sum",
    )(
        query, keyval, back_mixed, mixed, lse, cosine, sine, base, feed, tokens, normed, middle,
        gains, gain_two, full_query, full_keyval, *gradients, gradient_out,
    )


def front_kernel(
    tokens_ref, cotangent_ref, cosine_ref, sine_ref, *refs
):
    weights, refs = refs[:7], refs[7:]
    (
        tokens_own, cotangent_own, cotangent_other, normed_out, query_out, keyval_ref,
        mixed_out, lse_ref,
    ), refs = refs[:8], refs[8:]
    full, refs = refs[:7], refs[7:]
    (
        raw, tops, totals, sums,
        local_sem, token_send, token_recv, cot_send, cot_recv,
        y_send, y_recv, mate_send, mate_recv, pass_send, pass_recv, key_send, key_recv,
    ) = refs
    place = lax.axis_index("ctx")
    last = lax.axis_size("ctx") - 1
    rank = lax.axis_index("fsdp")
    side = lax.axis_index("tp")
    core = rank % 2
    mate = rank + 1 - 2 * core
    across = rank + 2 - 4 * (rank // 2)
    width = tokens_ref.shape[-1]

    def columns(ref, slot):
        return ref.at[:, pl.ds(pl.multiple_of(slot * width, width), width)]

    local = [
        pltpu.make_async_copy(tokens_ref.at[side], columns(tokens_own, side), local_sem.at[0]),
        pltpu.make_async_copy(
            cotangent_ref.at[side], columns(cotangent_own, side), local_sem.at[1]
        ),
        pltpu.make_async_copy(
            cotangent_ref.at[1 - side], columns(cotangent_other, side), local_sem.at[2]
        ),
    ]
    for w in range(len(weights)):
        local.append(pltpu.make_async_copy(weights[w], full[w].at[rank], local_sem.at[3 + w]))
    for copy in local:
        copy.start()

    greet(fsdp=mate)
    greet(fsdp=across)
    greet(tp=1 - side)

    @pl.when(place > 0)
    def _():
        greet(ctx=place - 1)

    @pl.when(place < last)
    def _():
        greet(ctx=place + 1)

    neighbours = (place + last - 1) // last + (2 * last - place - 1) // last
    pl.semaphore_wait(pltpu.get_barrier_semaphore(), 3 + neighbours)

    token_copy = remote(
        tokens_ref.at[1 - side], columns(tokens_own, side), token_send, token_recv, tp=1 - side
    )
    cot_copies = [
        remote(
            cotangent_ref.at[1 - side], columns(cotangent_own, side), cot_send.at[0],
            cot_recv.at[0], tp=1 - side,
        ),
        remote(
            cotangent_ref.at[side], columns(cotangent_other, side), cot_send.at[1],
            cot_recv.at[1], tp=1 - side,
        ),
    ]

    def y_copy(w):
        return remote(
            weights[w], full[w].at[rank], y_send.at[w], y_recv.at[w], fsdp=across
        )

    def mate_copy(w):
        return remote(
            weights[w], full[w].at[rank], mate_send.at[w], mate_recv.at[w], fsdp=mate
        )

    def pass_copy(w):
        return remote(
            full[w].at[across], full[w].at[across], pass_send.at[w], pass_recv.at[w], fsdp=mate
        )

    def arrived(w):
        local[3 + w].wait()
        mate_copy(w).wait_recv()
        pass_copy(w).wait_recv()

    for w in (6, 1):
        y_copy(w).start()
        mate_copy(w).start()
    token_copy.start()
    y_copy(0).start()
    mate_copy(0).start()
    y_copy(6).wait_recv()
    pass_copy(6).start()
    arrived(6)
    gain = wide(full[6][...].reshape(-1, full[6].shape[-1])[:, :1])

    def norm_rows(slot):
        at = pl.ds(pl.multiple_of(slot * width, width), width)
        rows = wide(tokens_own[:, at])
        inverse = lax.rsqrt(jnp.mean(rows * rows, 0, keepdims=True) + EPS)
        normed_out[:, at] = low(rows * inverse * gain)

    local[0].wait()
    norm_rows(side)
    token_copy.wait_recv()
    norm_rows(1 - side)
    for copy in cot_copies:
        copy.start()
    for w in (1, 0):
        y_copy(w).wait_recv()
        pass_copy(w).start()
    for w in range(2, 6):
        y_copy(w).start()
        mate_copy(w).start()
    normed = normed_out[...]
    cosine, sine = cosine_ref[...], sine_ref[...]

    def turned(value, target):
        target[:HALF] = low(value[:HALF] * cosine - value[HALF:] * sine)
        target[HALF:] = low(value[HALF:] * cosine + value[:HALF] * sine)

    def key_copy(s, j):
        return remote(
            keyval_ref.at[s, j], keyval_ref.at[s + 1, j], key_send.at[s, j], key_recv.at[s, j],
            ctx=place + 1,
        )

    arrived(1)
    matrix = full[1][...].reshape(-1, 2 * KEY_WIDTH)
    raw[: 2 * KEY_WIDTH] = dot(matrix, normed, 0, 0)
    for j in range(KEYVAL_HEADS):
        turned(raw[j * HEAD_WIDTH : (j + 1) * HEAD_WIDTH], keyval_ref.at[0, j, 0])
        first = KEY_WIDTH + j * HEAD_WIDTH
        keyval_ref[0, j, 1] = low(raw[first : first + HEAD_WIDTH])

        @pl.when(place < last)
        def _(j=j):
            key_copy(0, j).start()

    arrived(0)
    matrix = full[0][...].reshape(-1, QUERY_WIDTH)
    raw[...] = dot(matrix, normed, 0, 0)

    def turn_query(h, carry):
        value = raw[pl.ds(pl.multiple_of(h * HEAD_WIDTH, HEAD_WIDTH), HEAD_WIDTH)]
        first = low(value[:HALF] * cosine - value[HALF:] * sine)
        second = low(value[HALF:] * cosine + value[:HALF] * sine)
        query_out[h, :HALF] = first * jnp.bfloat16(SCALE)
        query_out[h, HALF:] = second * jnp.bfloat16(SCALE)
        return carry

    lax.fori_loop(0, QUERY_HEADS, turn_query, 0)

    def attend(s, j, masked):
        keys_turned = keyval_ref[s, j, 0].T
        values = keyval_ref[s, j, 1]
        for g in range(GROUP):
            head = GROUP * j + g
            scores = dot(keys_turned, query_out[head], 1, 0)
            if masked:
                scores = causal(scores)
                top = jnp.max(scores, 0, keepdims=True)
                lifted = jnp.exp(scores - top)
                tops[head] = top
                totals[head] = jnp.sum(lifted, 0, keepdims=True)
                sums[head] = dot(values, low(lifted), 1, 0)
            else:
                old = tops[head]
                top = jnp.maximum(old, jnp.max(scores, 0, keepdims=True))
                lifted = jnp.exp(scores - top)
                shrink = jnp.exp(old - top)
                tops[head] = top
                totals[head] = totals[head] * shrink + jnp.sum(lifted, 0, keepdims=True)
                sums[head] = sums[head] * shrink + dot(values, low(lifted), 1, 0)

    def hand_on(s, j):
        @pl.when(s < place)
        def _():
            pltpu.make_async_copy(
                keyval_ref.at[s + 1, j], keyval_ref.at[s + 1, j], key_recv.at[s, j]
            ).wait()

            @pl.when(place < last)
            def _():
                key_copy(s + 1, j).start()

    def first_block(j, carry):
        attend(0, j, True)
        hand_on(0, j)
        return carry

    lax.fori_loop(0, KEYVAL_HEADS, first_block, 0)
    passed = 2

    def later_block(i, carry):
        s = 1 + i // KEYVAL_HEADS
        j = lax.rem(i, KEYVAL_HEADS)
        attend(s, j, False)
        hand_on(s, j)
        return carry

    lax.fori_loop(0, place * KEYVAL_HEADS, later_block, 0)

    def divide(h, carry):
        total = totals[h]
        mixed_out[h] = low(sums[h] / total)
        lse_ref[h] = tops[h] + jnp.log(total)
        return carry

    lax.fori_loop(0, QUERY_HEADS, divide, 0)

    for w in range(passed, 6):
        y_copy(w).wait_recv()
        pass_copy(w).start()
    local[1].wait()
    local[2].wait()
    token_copy.wait_send()
    for copy in cot_copies:
        copy.wait()
    for w in range(passed, 6):
        arrived(w)
    for w in range(len(weights)):
        y_copy(w).wait_send()
        mate_copy(w).wait_send()
        pass_copy(w).wait_send()

    @pl.when(place < last)
    def _():
        def sent(i, carry):
            key_copy(i // KEYVAL_HEADS, lax.rem(i, KEYVAL_HEADS)).wait_send()
            return carry

        lax.fori_loop(0, (place + 1) * KEYVAL_HEADS, sent, 0)


def front(tokens, cotangent, cosine, sine, weights):
    blocks = lax.axis_size("ctx")
    parts = lax.axis_size("fsdp")
    positions = cosine.shape[-1]
    vmem = pl.BlockSpec(memory_space=pltpu.VMEM)
    anywhere = pl.BlockSpec(memory_space=pl.ANY)
    dma = pltpu.SemaphoreType.DMA
    shape = lambda *dims: jax.ShapeDtypeStruct(dims, jnp.bfloat16)
    count = len(weights)
    features = tokens.shape[1]
    area = QUERY_HEADS * positions * positions * blocks
    return pl.pallas_call(
        front_kernel,
        in_specs=[vmem] * (4 + count),
        out_specs=[vmem] * 8 + [vmem] * 2 + [anywhere] * 4 + [vmem],
        out_shape=[
            shape(features, positions), shape(features, positions), shape(features, positions),
            shape(features, positions),
            shape(QUERY_HEADS, HEAD_WIDTH, positions),
            shape(blocks, KEYVAL_HEADS, 2, HEAD_WIDTH, positions),
            shape(QUERY_HEADS, HEAD_WIDTH, positions),
            jax.ShapeDtypeStruct((QUERY_HEADS, 1, positions), jnp.float32),
        ] + [shape(parts, *w.shape) for w in weights],
        scratch_shapes=[
            pltpu.VMEM((QUERY_WIDTH, positions), jnp.float32),
            pltpu.VMEM((QUERY_HEADS, 1, positions), jnp.float32),
            pltpu.VMEM((QUERY_HEADS, 1, positions), jnp.float32),
            pltpu.VMEM((QUERY_HEADS, HEAD_WIDTH, positions), jnp.float32),
            dma((3 + count,)),
            dma, dma,
            dma((2,)), dma((2,)),
            dma((count,)), dma((count,)),
            dma((count,)), dma((count,)),
            dma((count,)), dma((count,)),
            dma((blocks, KEYVAL_HEADS)), dma((blocks, KEYVAL_HEADS)),
        ],
        compiler_params=pltpu.CompilerParams(
            vmem_limit_bytes=KERNEL_VMEM, collective_id=1, has_side_effects=True
        ),
        cost_estimate=pl.CostEstimate(
            flops=16 * HEAD_WIDTH * area, bytes_accessed=10 * tokens.size, transcendentals=area
        ),
        name="front",
    )(tokens, cotangent, cosine, sine, *weights)


def on_device(
    tokens, cotangent, input_gain, w_query, w_keyval, w_output, middle_gain, w_gate, w_up, w_down
):
    half = lax.axis_index("tp")
    low_half = half == 0
    pair = [(0, 1), (1, 0)]

    def to_partner(value_rows):
        return lax.ppermute(value_rows, "tp", pair)

    def in_order(mine, received):
        return jnp.concatenate(
            [jnp.where(low_half, mine, received), jnp.where(low_half, received, mine)], 0
        )

    def take(value_rows, index):
        return lax.dynamic_index_in_dim(value_rows, index, 0, keepdims=False)

    tokens_own = in_order(take(tokens, half), to_partner(take(tokens, 1 - half)))
    full_gain_one, full_gain_two = (
        lax.all_gather(input_gain, "fsdp", axis=0, tiled=True),
        lax.all_gather(middle_gain, "fsdp", axis=0, tiled=True),
    )
    full_in = lax.all_gather(jnp.concatenate([w_query, w_keyval], 1), "fsdp", axis=0, tiled=True)
    full_output = lax.all_gather(w_output, "fsdp", axis=0, tiled=True)
    full_gate = lax.all_gather(w_gate, "fsdp", axis=0, tiled=True)
    full_up = lax.all_gather(w_up, "fsdp", axis=0, tiled=True)
    full_down = lax.all_gather(w_down, "fsdp", axis=0, tiled=True)
    cotangent_received = to_partner(cotangent)
    cotangent_own = in_order(take(cotangent, half), take(cotangent_received, half))
    cotangent_other = in_order(take(cotangent, 1 - half), take(cotangent_received, 1 - half))

    token_positions = tokens_own.shape[0]
    cosine, sine = rope_tables(token_positions, lax.axis_index("ctx") * token_positions)
    gain_one = full_gain_one.astype(jnp.float32)
    inputs = tokens_own.astype(jnp.float32)
    unit_one, inverse_one = normalize(inputs)
    normed_one = (unit_one * gain_one).astype(jnp.bfloat16)
    keyval_raw = dot(full_in[:, QUERY_WIDTH:], normed_one, 0, 1)
    keyval_low = jnp.concatenate(
        [apply_rotary(keyval_raw[:KEY_WIDTH], cosine, sine), keyval_raw[KEY_WIDTH:]], 0
    ).astype(jnp.bfloat16)
    blocks = lax.axis_size("ctx")
    keyval = jnp.stack([keyval_low] + [move_along(keyval_low, s) for s in range(1, blocks)], 0)
    keyval = keyval.reshape(blocks, 2, KEYVAL_HEADS, HEAD_WIDTH, token_positions)
    query_raw = dot(full_in[:, :QUERY_WIDTH], normed_one, 0, 1)
    query_low = (
        apply_rotary(query_raw, cosine, sine)
        .astype(jnp.bfloat16)
        .reshape(QUERY_HEADS, HEAD_WIDTH, token_positions)
    )
    mixed_heads, lse = attend_forward(query_low, keyval)
    mixed_low = mixed_heads.reshape(QUERY_WIDTH, token_positions)
    middle = inputs + dot(mixed_low, full_output, 0, 0)

    gain_two = full_gain_two.astype(jnp.float32)
    unit_two, inverse_two = normalize(middle)
    normed_two = (unit_two * gain_two).astype(jnp.bfloat16)
    normed_other = to_partner(normed_two)

    def feed(rows, back_rows):
        gate_proj = dot(rows, full_gate, 1, 0)
        up_proj = dot(rows, full_up, 1, 0)
        sigmoid_gate = jax.nn.sigmoid(gate_proj)
        swish_gate = gate_proj * sigmoid_gate
        hidden = (swish_gate * up_proj).astype(jnp.bfloat16)
        back_hidden = dot(back_rows, full_down, 1, 0)
        back_gate = (
            back_hidden * up_proj * sigmoid_gate * (1.0 + gate_proj * (1.0 - sigmoid_gate))
        ).astype(jnp.bfloat16)
        back_up = (back_hidden * swish_gate).astype(jnp.bfloat16)
        return (hidden, back_gate, back_up)

    def feed_input_back(back_gate, back_up):
        return dot(back_gate, full_gate, 1, 1) + dot(back_up, full_up, 1, 1)

    hidden_own, back_gate_own, back_up_own = feed(normed_two, cotangent_own)
    hidden_other, back_gate_other, back_up_other = feed(normed_other, cotangent_other)
    back_two_received = to_partner(
        feed_input_back(back_gate_other, back_up_other).astype(jnp.bfloat16)
    )
    back_two = feed_input_back(back_gate_own, back_up_own) + back_two_received.astype(jnp.float32)
    feed_received = to_partner(dot(hidden_other, full_down, 1, 1).astype(jnp.bfloat16))
    result_own = (
        middle + dot(hidden_own, full_down, 1, 1) + feed_received.astype(jnp.float32)
    ).astype(jnp.bfloat16)

    def feed_gradient(left_own, right_own, left_other, right_other):
        gradient = dot(left_own, right_own, 0, 0) + dot(left_other, right_other, 0, 0)
        shared = scatter_sum(gradient.astype(jnp.bfloat16), "fsdp")
        return whole_sum(shared, (("ctx", 2),))

    share_down = feed_gradient(cotangent_own, hidden_own, cotangent_other, hidden_other)
    share_gate = feed_gradient(normed_two, back_gate_own, normed_other, back_gate_other)
    share_up = feed_gradient(normed_two, back_up_own, normed_other, back_up_other)

    grad_gain_two = jnp.sum(back_two * unit_two, axis=0)
    back_middle = cotangent_own.astype(jnp.float32) + norm_back(
        back_two * gain_two, unit_two, inverse_two
    )
    back_attention = back_middle.astype(jnp.bfloat16)
    back_mixed = dot(full_output, back_attention, 1, 1).astype(jnp.bfloat16)
    back_mixed = back_mixed.reshape(query_low.shape)
    grad_output = dot(mixed_low, back_attention, 1, 0).astype(jnp.bfloat16)
    share_output = whole_sum(scatter_sum(grad_output, "fsdp"), (("tp", 1), ("ctx", 2)))

    back_query = []
    back_key = []
    back_value = []
    for first, count in ((0, 3), (3, 2)):
        part_query, part_keyval = attend_backward(
            query_low, keyval, back_mixed, mixed_heads, lse, cosine, sine, first, count
        )
        part_keyval = part_keyval.reshape(blocks, 2 * count * HEAD_WIDTH, token_positions)
        owned = part_keyval[0].astype(jnp.float32)
        for s in range(1, blocks):
            owned += move_along(part_keyval[s], -s).astype(jnp.float32)
        back_query.append(part_query.reshape(-1, token_positions))
        back_key.append(
            apply_rotary(owned[: count * HEAD_WIDTH], cosine, -sine).astype(jnp.bfloat16)
        )
        back_value.append(owned[count * HEAD_WIDTH :].astype(jnp.bfloat16))
    back_in = jnp.concatenate(back_query + back_key + back_value, 0)
    grad_in = dot(normed_one, back_in, 0, 1)
    back_one = dot(back_in, full_in, 0, 1)
    grad_gain_one = jnp.sum(back_one * unit_one, axis=0)
    back_inputs = back_middle + norm_back(back_one * gain_one, unit_one, inverse_one)

    def to_positions(value_rows):
        split = value_rows.reshape(2, token_positions // 2, value_rows.shape[-1])
        received = to_partner(take(split, 1 - half))
        return in_order(take(split, half)[None], received[None])

    result = to_positions(result_own)
    grad_tokens = to_positions(back_inputs.astype(jnp.bfloat16)).astype(jnp.float32)
    gradients = jnp.concatenate([grad_in, grad_gain_one[:, None], grad_gain_two[:, None]], 1)
    share_in = lax.psum(
        lax.psum_scatter(
            gradients.astype(jnp.bfloat16), "fsdp", scatter_dimension=0, tiled=True
        ),
        ("ctx", "tp"),
    ).astype(jnp.float32)
    width = full_in.shape[1]
    return (
        result,
        grad_tokens,
        share_in[:, width],
        share_in[:, :QUERY_WIDTH],
        share_in[:, QUERY_WIDTH:width],
        share_output,
        share_in[:, width + 1],
        share_gate,
        share_up,
        share_down,
    )


def fast_on_device(
    tokens, cotangent, input_gain, w_query, w_keyval, w_output, middle_gain, w_gate, w_up, w_down
):
    pair = [(0, 1), (1, 0)]

    def to_partner(value_rows):
        return lax.ppermute(value_rows, "tp", pair)

    parts = lax.axis_size("fsdp")
    width_in = tokens.shape[-1]
    rows = width_in // parts
    token_positions = 2 * tokens.shape[1]
    cosine, sine = rope_tables(token_positions, lax.axis_index("ctx") * token_positions)
    gains = jnp.pad(jnp.stack([input_gain, middle_gain], 1), ((0, 0), (0, 126)))
    (
        tokens_own, cotangent_own, cotangent_other, normed_one, query_low, keyval,
        mixed_heads, lse, *full,
    ) = front(
        tokens.swapaxes(1, 2), cotangent.swapaxes(1, 2), cosine, sine,
        (w_query, w_keyval, w_output, w_gate, w_up, w_down, gains),
    )
    full_query, full_keyval, full_output, full_gate, full_up, full_down, gains = [
        w.reshape(width_in, -1) for w in full
    ]
    tokens_own, cotangent_own, cotangent_other, normed_one = [
        v.T for v in (tokens_own, cotangent_own, cotangent_other, normed_one)
    ]
    full_gain_two = gains[:, 1]
    inputs = tokens_own.astype(jnp.float32)
    mixed_low = mixed_heads.reshape(QUERY_WIDTH, token_positions)
    middle = inputs + dot(mixed_low, full_output, 0, 0)

    gain_two = full_gain_two.astype(jnp.float32)
    unit_two, inverse_two = normalize(middle)
    normed_two = (unit_two * gain_two).astype(jnp.bfloat16)
    normed_other = to_partner(normed_two)

    def feed(rows, back_rows):
        gate_proj = dot(rows, full_gate, 1, 0)
        up_proj = dot(rows, full_up, 1, 0)
        sigmoid_gate = jax.nn.sigmoid(gate_proj)
        swish_gate = gate_proj * sigmoid_gate
        hidden = (swish_gate * up_proj).astype(jnp.bfloat16)
        back_hidden = dot(back_rows, full_down, 1, 0)
        back_gate = (
            back_hidden * up_proj * sigmoid_gate * (1.0 + gate_proj * (1.0 - sigmoid_gate))
        ).astype(jnp.bfloat16)
        back_up = (back_hidden * swish_gate).astype(jnp.bfloat16)
        return (hidden, back_gate, back_up)

    def feed_input_back(back_gate, back_up):
        return dot(back_gate, full_gate, 1, 1) + dot(back_up, full_up, 1, 1)

    hidden_own, back_gate_own, back_up_own = feed(normed_two, cotangent_own)
    hidden_other, back_gate_other, back_up_other = feed(normed_other, cotangent_other)
    back_two_received = to_partner(
        feed_input_back(back_gate_other, back_up_other).astype(jnp.bfloat16)
    )
    back_two = feed_input_back(back_gate_own, back_up_own) + back_two_received.astype(jnp.float32)
    feed_other = dot(hidden_other, full_down, 1, 1).astype(jnp.bfloat16)
    base = middle + dot(hidden_own, full_down, 1, 1)

    def feed_gradient(left_own, right_own, left_other, right_other):
        gradient = dot(left_own, right_own, 0, 0) + dot(left_other, right_other, 0, 0)
        return gradient.astype(jnp.bfloat16).reshape(lax.axis_size("fsdp"), -1, gradient.shape[1])

    gradients = (
        feed_gradient(cotangent_own, hidden_own, cotangent_other, hidden_other),
        feed_gradient(normed_two, back_gate_own, normed_other, back_gate_other),
        feed_gradient(normed_two, back_up_own, normed_other, back_up_other),
    )

    grad_gain_two = jnp.sum(back_two * unit_two, axis=0)
    back_middle = cotangent_own.astype(jnp.float32) + norm_back(
        back_two * gain_two, unit_two, inverse_two
    )
    back_attention = back_middle.astype(jnp.bfloat16)
    back_mixed = dot(full_output, back_attention, 1, 1).astype(jnp.bfloat16)
    back_mixed = back_mixed.reshape(query_low.shape)
    grad_output = dot(mixed_low, back_attention, 1, 0).astype(jnp.bfloat16)
    share, result, grad_tokens, share_output, share_query, share_keyval, share_gains = backward_sum(
        query_low, keyval, back_mixed, mixed_heads, lse, cosine, sine, base.T, feed_other.T,
        tokens_own.T, normed_one.T, back_middle.T, gains, grad_gain_two[:, None],
        full_query, full_keyval, gradients, grad_output.reshape(parts, rows, -1),
    )
    return (
        result.swapaxes(1, 2),
        grad_tokens.swapaxes(1, 2).astype(jnp.float32),
        share_gains[:rows, 0].astype(jnp.float32),
        share_query[:rows].astype(jnp.float32),
        share_keyval[:rows].astype(jnp.float32),
        share_output[:rows].astype(jnp.float32),
        share_gains[:rows, 1].astype(jnp.float32),
        share[1].astype(jnp.float32),
        share[2].astype(jnp.float32),
        share[0].astype(jnp.float32),
    )


def solution(mesh):
    rows = P("fsdp", ("ctx", "tp"), None)
    specs = (
        P("fsdp"), P("fsdp", None), P("fsdp", None), P("fsdp", None),
        P("fsdp"), P("fsdp", "tp"), P("fsdp", "tp"), P("fsdp", "tp"),
    )
    kernels = mesh.shape["fsdp"] == 4 and mesh.shape["tp"] == 2 and mesh.shape["ctx"] == 4
    return jax.shard_map(
        fast_on_device if kernels else on_device,
        mesh=mesh,
        in_specs=(rows, rows) + specs,
        out_specs=(rows, rows) + specs,
        check_vma=False,
    )
```

```python
import jax
import jax.numpy as jnp
from jax import lax
from jax.experimental import pallas as pl
from jax.experimental.pallas import tpu as pltpu
from jax.sharding import PartitionSpec as P

QUERY_HEADS = 15
KEYVAL_HEADS = 5
GROUP = QUERY_HEADS // KEYVAL_HEADS
HEAD_WIDTH = 64
HALF = HEAD_WIDTH // 2
KEY_WIDTH = 320
QUERY_WIDTH = QUERY_HEADS * HEAD_WIDTH
SCALE = HEAD_WIDTH ** (-0.5)

EPS = 1e-05
THETA = 10000.0
VMEM_LIMIT = 40 * 1024 * 1024


def dot(left, right, left_dim, right_dim):
    return lax.dot_general(
        left, right, (((left_dim,), (right_dim,)), ((), ())), preferred_element_type=jnp.float32
    )


def rope_tables(token_positions, first_place):
    position = (first_place + lax.iota(jnp.int32, token_positions)).astype(jnp.float32)
    frequency = THETA ** (-(2.0 * lax.iota(jnp.int32, HALF).astype(jnp.float32)) / HEAD_WIDTH)
    angles = frequency[:, None] * position[None, :]
    return (jnp.cos(angles), jnp.sin(angles))


def apply_rotary(rows, cosine, sine):
    shaped = rows.reshape(-1, 2, HALF, rows.shape[-1])
    leading = shaped[:, 0]
    trailing = shaped[:, 1]
    return jnp.stack(
        [leading * cosine - trailing * sine, trailing * cosine + leading * sine], 1
    ).reshape(rows.shape)


def normalize(value_rows):
    inverse_rms = lax.rsqrt(jnp.mean(value_rows * value_rows, -1, keepdims=True) + EPS)
    return (value_rows * inverse_rms, inverse_rms)


def norm_back(back_unit, unit_rows, inverse_rms):
    return inverse_rms * (
        back_unit - unit_rows * jnp.mean(back_unit * unit_rows, -1, keepdims=True)
    )


def causal(scores):
    key_place = lax.broadcasted_iota(jnp.int32, scores.shape, 0)
    query_place = lax.broadcasted_iota(jnp.int32, scores.shape, 1)
    return jnp.where(key_place <= query_place, scores, -jnp.inf)


def forward_kernel(query_ref, key_ref, value_ref, mixed_ref, lse_ref):
    place = lax.axis_index("ctx")
    queries = [query_ref[g] * jnp.bfloat16(SCALE) for g in range(GROUP)]

    def scores_of(keys_turned, g, masked):
        scores = dot(keys_turned, queries[g], 1, 0)
        return causal(scores) if masked else scores

    def first():
        keys_turned = key_ref[0, 0, 0].T
        values = value_ref[0, 0, 0]
        carried = []
        for g in range(GROUP):
            scores = scores_of(keys_turned, g, True)
            top = jnp.max(scores, 0, keepdims=True)
            lifted = jnp.exp(scores - top)
            total = jnp.sum(lifted, 0, keepdims=True)
            carried += [top, total, dot(values, lifted.astype(jnp.bfloat16), 1, 0)]
        return tuple(carried)

    def step(block, carried):
        keys_turned = key_ref[block, 0, 0].T
        values = value_ref[block, 0, 0]
        later = []
        for g in range(GROUP):
            top, total, mixed = carried[3 * g : 3 * g + 3]
            scores = scores_of(keys_turned, g, False)
            new_top = jnp.maximum(top, jnp.max(scores, 0, keepdims=True))
            lifted = jnp.exp(scores - new_top)
            shrink = jnp.exp(top - new_top)
            later += [
                new_top,
                total * shrink + jnp.sum(lifted, 0, keepdims=True),
                mixed * shrink + dot(values, lifted.astype(jnp.bfloat16), 1, 0),
            ]
        return tuple(later)

    carried = lax.fori_loop(1, place + 1, step, first())
    for g in range(GROUP):
        top, total, mixed = carried[3 * g : 3 * g + 3]
        mixed_ref[g] = (mixed / total).astype(jnp.bfloat16)
        lse_ref[g] = top + jnp.log(total)


def attend_forward(query, keyval):
    blocks, token_positions = keyval.shape[0], keyval.shape[-1]
    head_block = (GROUP, HEAD_WIDTH, token_positions)
    key_block = (blocks, 1, 1, HEAD_WIDTH, token_positions)
    area = QUERY_HEADS * token_positions * token_positions * blocks
    return pl.pallas_call(
        forward_kernel,
        grid=(KEYVAL_HEADS,),
        in_specs=[
            pl.BlockSpec(head_block, lambda j: (j, 0, 0)),
            pl.BlockSpec(key_block, lambda j: (0, 0, j, 0, 0)),
            pl.BlockSpec(key_block, lambda j: (0, 1, j, 0, 0)),
        ],
        out_specs=[
            pl.BlockSpec(head_block, lambda j: (j, 0, 0)),
            pl.BlockSpec((GROUP, 1, token_positions), lambda j: (j, 0, 0)),
        ],
        out_shape=[
            jax.ShapeDtypeStruct(query.shape, jnp.bfloat16),
            jax.ShapeDtypeStruct((QUERY_HEADS, 1, token_positions), jnp.float32),
        ],
        compiler_params=pltpu.CompilerParams(vmem_limit_bytes=VMEM_LIMIT),
        cost_estimate=pl.CostEstimate(
            flops=16 * HEAD_WIDTH * area, bytes_accessed=6 * query.size, transcendentals=area
        ),
        name="attend_forward",
    )(query, keyval, keyval)


def backward_kernel(
    query_ref, key_ref, value_ref, back_ref, mixed_ref, lse_ref, cosine_ref, sine_ref,
    back_query_ref, back_keyval_ref,
):
    place = lax.axis_index("ctx")
    blocks = key_ref.shape[0]
    queries = [query_ref[g] * jnp.bfloat16(SCALE) for g in range(GROUP)]
    backs = [back_ref[g] for g in range(GROUP)]
    tops = [lse_ref[g] for g in range(GROUP)]
    sums = [
        jnp.sum(backs[g].astype(jnp.float32) * mixed_ref[g].astype(jnp.float32), 0, keepdims=True)
        for g in range(GROUP)
    ]

    def step(block, carried, masked=False):
        keys = key_ref[block, 0, 0]
        keys_turned = keys.T
        values_turned = value_ref[block, 0, 0].T
        back_key = jnp.zeros(keys.shape, jnp.float32)
        back_value = jnp.zeros(keys.shape, jnp.float32)
        later = []
        for g in range(GROUP):
            scores = dot(keys_turned, queries[g], 1, 0)
            if masked:
                scores = causal(scores)
            weights = jnp.exp(scores - tops[g])
            back_weights = dot(values_turned, backs[g], 1, 0)
            back_scores = (weights * (back_weights - sums[g])).astype(jnp.bfloat16)
            later.append(carried[g] + dot(keys, back_scores, 1, 0))
            back_key += dot(queries[g], back_scores, 1, 1)
            back_value += dot(backs[g], weights.astype(jnp.bfloat16), 1, 1)
        back_keyval_ref[block, 0, 0] = back_key.astype(jnp.bfloat16)
        back_keyval_ref[block, 1, 0] = back_value.astype(jnp.bfloat16)
        return tuple(later)

    start = tuple(jnp.zeros(query_ref.shape[1:], jnp.float32) for g in range(GROUP))
    carried = lax.fori_loop(1, place + 1, step, step(0, start, True))

    def clear(block, unused):
        zero = jnp.zeros(key_ref.shape[3:], jnp.bfloat16)
        back_keyval_ref[block, 0, 0] = zero
        back_keyval_ref[block, 1, 0] = zero
        return unused

    lax.fori_loop(place + 1, blocks, clear, 0)
    cosine = cosine_ref[...]
    sine = sine_ref[...]
    for g in range(GROUP):
        leading = carried[g][:HALF] * SCALE
        trailing = carried[g][HALF:] * SCALE
        back_query_ref[g, :HALF] = (leading * cosine + trailing * sine).astype(jnp.bfloat16)
        back_query_ref[g, HALF:] = (trailing * cosine - leading * sine).astype(jnp.bfloat16)


def attend_backward(query, keyval, back_mixed, mixed, lse, cosine, sine, first, count):
    blocks, token_positions = keyval.shape[0], keyval.shape[-1]
    head_block = (GROUP, HEAD_WIDTH, token_positions)
    key_block = (blocks, 1, 1, HEAD_WIDTH, token_positions)
    area = count * GROUP * token_positions * token_positions * blocks
    heads = pl.BlockSpec(head_block, lambda j: (j + first, 0, 0))
    table = pl.BlockSpec((HALF, token_positions), lambda j: (0, 0))
    return pl.pallas_call(
        backward_kernel,
        grid=(count,),
        in_specs=[
            heads,
            pl.BlockSpec(key_block, lambda j: (0, 0, j + first, 0, 0)),
            pl.BlockSpec(key_block, lambda j: (0, 1, j + first, 0, 0)),
            heads,
            heads,
            pl.BlockSpec((GROUP, 1, token_positions), lambda j: (j + first, 0, 0)),
            table,
            table,
        ],
        out_specs=[
            pl.BlockSpec(head_block, lambda j: (j, 0, 0)),
            pl.BlockSpec((blocks, 2, 1, HEAD_WIDTH, token_positions), lambda j: (0, 0, j, 0, 0)),
        ],
        out_shape=[
            jax.ShapeDtypeStruct((count * GROUP, HEAD_WIDTH, token_positions), jnp.bfloat16),
            jax.ShapeDtypeStruct(
                (blocks, 2, count, HEAD_WIDTH, token_positions), jnp.bfloat16
            ),
        ],
        compiler_params=pltpu.CompilerParams(vmem_limit_bytes=VMEM_LIMIT),
        cost_estimate=pl.CostEstimate(
            flops=40 * HEAD_WIDTH * area, bytes_accessed=10 * query.size, transcendentals=area
        ),
        name="attend_backward",
    )(query, keyval, keyval, back_mixed, mixed, lse, cosine, sine)


def move_along(value, distance):
    blocks = lax.axis_size("ctx")
    pairs = [(i, i + distance) for i in range(blocks) if 0 <= i + distance < blocks]
    return lax.ppermute(value, "ctx", pairs)


def trade(value, axis, step):
    pairs = [(i, i ^ step) for i in range(lax.axis_size(axis))]
    return lax.ppermute(value, axis, pairs)


def add_low(left, right):
    return (left.astype(jnp.float32) + right.astype(jnp.float32)).astype(jnp.bfloat16)


def scatter_sum(value, axis):
    size = lax.axis_size(axis)
    index = lax.axis_index(axis)
    rows = value.shape[0] // size
    step = 1
    while step < size:
        count = value.shape[0] // (2 * rows)
        split = value.reshape(count, 2, rows, value.shape[-1])
        second = (index // step) % 2 == 1
        kept = jnp.where(second, split[:, 1], split[:, 0])
        sent = jnp.where(second, split[:, 0], split[:, 1])
        value = add_low(kept, trade(sent, axis, step)).reshape(count * rows, value.shape[-1])
        step *= 2
    return value


def whole_sum(value, others):
    half_rows = value.shape[0] // 2
    second = lax.axis_index("ctx") % 2 == 1
    upper, lower = value[:half_rows], value[half_rows:]
    received = trade(jnp.where(second, upper, lower), "ctx", 1)
    total = add_low(jnp.where(second, lower, upper), received)
    for axis, first_step in others:
        step = first_step
        while step < lax.axis_size(axis):
            total = add_low(total, trade(total, axis, step))
            step *= 2
    received = trade(total, "ctx", 1)
    return jnp.concatenate(
        [jnp.where(second, received, total), jnp.where(second, total, received)], 0
    ).astype(jnp.float32)


MESH = pl.DeviceIdType.MESH
KERNEL_VMEM = 60 * 1024 * 1024
CHUNK_ROWS = 80


def remote(source, target, send_sem, recv_sem, **place):
    return pltpu.make_async_remote_copy(
        src_ref=source, dst_ref=target, send_sem=send_sem, recv_sem=recv_sem,
        device_id=place, device_id_type=MESH,
    )


def wide(value):
    return value.astype(jnp.float32)


def low(value):
    return value.astype(jnp.bfloat16)


def greet(**place):
    pl.semaphore_signal(
        pltpu.get_barrier_semaphore(), inc=1, device_id=place, device_id_type=MESH
    )


def backward_sum_kernel(
    query_ref, keyval_ref, back_ref, mixed_ref, lse_ref, cosine_ref, sine_ref,
    base_ref, feed_ref, tokens_ref, normed_ref, middle_ref, gains_ref, gain_two_ref,
    full_query, full_keyval, down_ref, gate_ref, up_ref, out_ref,
    share_ref, result_ref, back_tokens_ref, *refs,
):
    chunks_in = 4
    shares, refs = refs[:chunks_in], refs[chunks_in:]
    whole, mate_part, y_part, x_part, z_part = [
        refs[i * chunks_in : (i + 1) * chunks_in] for i in range(5)
    ]
    (
    own, mate_in, y_in, up_in, parts, part_in, back_total, row_sums,
    own_sem, mate_send, mate_recv, y_send, y_recv, up_send, up_recv, down_send, down_recv,
    part_send, part_recv, feed_in, traded, feed_send, feed_recv, trade_send, trade_recv,
    back_query_ref, back_keyval_ref, back_one, token_traded,
    whole_sem, sum_mate_send, sum_mate_recv, sum_y_send, sum_y_recv, sum_x_send, sum_x_recv,
    sum_z_send, sum_z_recv, all_send, all_recv, back_send, back_recv, token_send, token_recv,
    ) = refs[5 * chunks_in :]
    place = lax.axis_index("ctx")
    last = lax.axis_size("ctx") - 1
    blocks = last + 1
    rank = lax.axis_index("fsdp")
    core = rank % 2
    y = rank // 2
    side = lax.axis_index("tp")
    mate = rank + 1 - 2 * core
    across = rank + 2 - 4 * y
    gradients = (down_ref, gate_ref, up_ref)
    rows = share_ref.shape[1]
    per = rows // CHUNK_ROWS
    chunks = len(gradients) * per
    early = per

    for m, gradient in enumerate(gradients):
        for half in range(2):
            pltpu.make_async_copy(
                gradient.at[2 * half + core], own.at[m, half], own_sem.at[m, half]
            ).start()
    greet(fsdp=mate)
    greet(fsdp=across)
    greet(tp=1 - side)
    for d in range(1, blocks):
        greet(ctx=lax.rem(place + d, blocks))
    filled = out_ref.shape[1]
    tail = whole[0].shape[1] - filled
    for n in range(chunks_in):
        width = whole[n].shape[-1]
        whole[n][:, filled:] = jnp.zeros((whole[n].shape[0], tail, width), jnp.bfloat16)
        mate_part[n][:, filled:] = jnp.zeros((2, tail, width), jnp.bfloat16)
    for f in range(whole[0].shape[0]):
        pltpu.make_async_copy(
            out_ref.at[f], whole[0].at[f, pl.ds(0, filled)], whole_sem.at[f]
        ).start()
    pl.semaphore_wait(pltpu.get_barrier_semaphore(), 3 + last)

    feed_copy = remote(feed_ref, feed_in, feed_send, feed_recv, tp=1 - side)
    trade_copy = remote(traded, result_ref.at[side], trade_send, trade_recv, tp=1 - side)
    feed_copy.start()
    pair_width = traded.shape[-1]
    step_rows = traded.shape[0] // 4

    def finish_result():
        feed_copy.wait_recv()

        def some_rows(i, carry):
            at = pl.ds(pl.multiple_of(i * step_rows, step_rows), step_rows)
            for target, slot in ((result_ref.at[side], side), (traded, 1 - side)):
                columns = pl.ds(pl.multiple_of(slot * pair_width, pair_width), pair_width)
                target[at] = low(base_ref[at, columns] + wide(feed_in[at, columns]))
            return carry

        lax.fori_loop(0, 4, some_rows, 0)
        trade_copy.start()

    half_rows = whole[0].shape[1] // 2
    piece = half_rows // blocks
    kept = 2 * y + core

    def sum_mate(n, half):
        return remote(
            whole[n].at[2 * half + 1 - core, pl.ds(0, filled)],
            mate_part[n].at[half, pl.ds(0, filled)],
            sum_mate_send.at[n, half], sum_mate_recv.at[n, half], fsdp=mate,
        )

    def sum_y(n):
        return remote(
            mate_part[n].at[1 - y], y_part[n], sum_y_send.at[n], sum_y_recv.at[n], fsdp=across
        )

    def sum_x(n):
        other = pl.ds(pl.multiple_of((1 - side) * half_rows, half_rows), half_rows)
        return remote(
            whole[n].at[kept, other], x_part[n], sum_x_send.at[n], sum_x_recv.at[n],
            tp=1 - side,
        )

    def sum_z(n, d):
        target = lax.rem(place + d, blocks)
        at = pl.ds(pl.multiple_of(side * half_rows + target * piece, piece), piece)
        return remote(
            whole[n].at[kept, at], z_part[n].at[d - 1], sum_z_send.at[n, d - 1],
            sum_z_recv.at[n, d - 1], ctx=target,
        )

    def all_copy(n, d, origin):
        spot = shares[n].at[
            pl.ds(pl.multiple_of(side * half_rows + origin * piece, piece), piece)
        ]
        return remote(
            spot, spot, all_send.at[n, d - 1], all_recv.at[n, d - 1],
            ctx=lax.rem(place + d, blocks),
        )

    def back_copy(n, half):
        spot = shares[n].at[pl.ds(pl.multiple_of(half * half_rows, half_rows), half_rows)]
        return remote(spot, spot, back_send.at[n], back_recv.at[n], tp=1 - side)

    def to_mate(n):
        for half in range(2):
            sum_mate(n, half).start()

    def to_y(n):
        for half in range(2):
            sum_mate(n, half).wait_recv()
        quarter = 2 * (1 - y) + core
        mate_part[n][1 - y] = low(wide(whole[n][quarter]) + wide(mate_part[n][1 - y]))
        sum_y(n).start()

    def to_x(n):
        sum_y(n).wait_recv()
        whole[n][kept] = low(
            wide(whole[n][kept]) + wide(mate_part[n][y]) + wide(y_part[n][...])
        )
        sum_x(n).start()

    def to_z(n):
        sum_x(n).wait_recv()
        at = pl.ds(pl.multiple_of(side * half_rows, half_rows), half_rows)
        whole[n][kept, at] = low(wide(whole[n][kept, at]) + wide(x_part[n][...]))
        for d in range(1, blocks):
            sum_z(n, d).start()

    def to_all(n):
        at = pl.ds(pl.multiple_of(side * half_rows + place * piece, piece), piece)
        total = wide(whole[n][kept, at])
        for d in range(1, blocks):
            sum_z(n, d).wait_recv()
            total += wide(z_part[n][d - 1])
        shares[n][at] = low(total)
        for d in range(1, blocks):
            all_copy(n, d, place).start()

    def to_back(n):
        for d in range(1, blocks):
            all_copy(n, d, lax.rem(place + blocks - d, blocks)).wait_recv()
        back_copy(n, side).start()

    def finish_sum(n):
        back_copy(n, 1 - side).wait_recv()
        for half in range(2):
            sum_mate(n, half).wait_send()
        sum_y(n).wait_send()
        sum_x(n).wait_send()
        for d in range(1, blocks):
            sum_z(n, d).wait_send()
            all_copy(n, d, place).wait_send()
        back_copy(n, side).wait_send()

    def weight_gradient(n, back_ref):
        def quarter(f, carry):
            rows_of = normed_ref[pl.ds(pl.multiple_of(f * filled, filled), filled)]
            whole[n][f, :filled] = low(dot(rows_of, back_ref[...], 1, 1))
            return carry

        lax.fori_loop(0, whole[n].shape[0], quarter, 0)

    token_copy = remote(
        token_traded, back_tokens_ref.at[side], token_send, token_recv, tp=1 - side
    )

    def input_gradient():
        tokens = wide(tokens_ref[...])
        inverse = lax.rsqrt(jnp.mean(tokens * tokens, 0, keepdims=True) + EPS)

        def quarter(f, total):
            at = pl.ds(pl.multiple_of(f * filled, filled), filled)
            unit = wide(tokens_ref[at]) * inverse
            back = dot(full_query[at], back_query_ref[...], 1, 0) + dot(
                full_keyval[at], back_keyval_ref[...], 1, 0
            )
            gain_sum = jnp.sum(back * unit, 1, keepdims=True)
            lane = lax.broadcasted_iota(jnp.int32, (filled, whole[3].shape[-1]), 1)
            whole[3][f, :filled] = low(
                jnp.where(lane == 0, gain_sum, jnp.where(lane == 1, gain_two_ref[at], 0.0))
            )
            back = back * wide(gains_ref[at])[:, :1]
            back_one[at] = back
            return total + jnp.sum(back * unit, 0, keepdims=True)

        total = lax.fori_loop(
            0, whole[0].shape[0], quarter, jnp.zeros((1, tokens_ref.shape[-1]), jnp.float32)
        )
        to_mate(3)
        mean = total / tokens_ref.shape[0]

        def rows_back(f, carry):
            at = pl.ds(pl.multiple_of(f * filled, filled), filled)
            unit = wide(tokens_ref[at]) * inverse
            back_one[at] = middle_ref[at] + inverse * (back_one[at] - unit * mean)
            for target, slot in ((back_tokens_ref.at[side], side), (token_traded, 1 - side)):
                columns = pl.ds(pl.multiple_of(slot * pair_width, pair_width), pair_width)
                target[at] = low(back_one[at, columns])
            return carry

        lax.fori_loop(0, whole[0].shape[0], rows_back, 0)
        token_copy.start()

    def chunk_at(ref, m, r, *front):
        return ref.at[(m,) + front + (pl.ds(r * CHUNK_ROWS, CHUNK_ROWS),)]

    def mate_copy(m, r, half):
        gradient = gradients[m]
        return remote(
            gradient.at[2 * half + 1 - core, pl.ds(r * CHUNK_ROWS, CHUNK_ROWS)],
            chunk_at(mate_in, m, r, half),
            mate_send.at[m * per + r, half], mate_recv.at[m * per + r, half], fsdp=mate,
        )

    for m in range(len(gradients)):
        for r in range(per):
            for half in range(2):
                mate_copy(m, r, half).start()
    for f in range(whole[0].shape[0]):
        pltpu.make_async_copy(
            out_ref.at[f], whole[0].at[f, pl.ds(0, filled)], whole_sem.at[f]
        ).wait()
    to_mate(0)
    for m, gradient in enumerate(gradients):
        for half in range(2):
            pltpu.make_async_copy(
                gradient.at[2 * half + core], own.at[m, half], own_sem.at[m, half]
            ).wait()

    def split(k):
        r = lax.rem(k, per)
        return k // per, pl.ds(pl.multiple_of(r * CHUNK_ROWS, CHUNK_ROWS), CHUNK_ROWS)

    def y_copy(k):
        m, at = split(k)
        return remote(
            own.at[m, 1 - y, at], y_in.at[m, at], y_send.at[k], y_recv.at[k], fsdp=across
        )

    def up_copy(k):
        m, at = split(k)
        return remote(
            own.at[m, y, at], up_in.at[m, at], up_send.at[k], up_recv.at[k], ctx=place + 1
        )

    def down_copy(k):
        m, at = split(k)
        return remote(
            share_ref.at[m, at], share_ref.at[m, at], down_send.at[k], down_recv.at[k],
            ctx=place - 1,
        )

    def to_across(k):
        m, at = split(k)
        for half in range(2):
            pltpu.make_async_copy(
                mate_in.at[m, half, at], mate_in.at[m, half, at], mate_recv.at[k, half]
            ).wait()
        own[m, 1 - y, at] = low(wide(own[m, 1 - y, at]) + wide(mate_in[m, 1 - y, at]))
        y_copy(k).start()

    def to_next(k):
        m, at = split(k)
        y_copy(k).wait_recv()
        total = wide(own[m, y, at]) + wide(mate_in[m, y, at]) + wide(y_in[m, at])

        @pl.when(place == 0)
        def _():
            own[m, y, at] = low(total)

        @pl.when(place > 0)
        def _():
            up_copy(k).wait_recv()
            own[m, y, at] = low(total + wide(up_in[m, at]))

        @pl.when(place < last)
        def _():
            up_copy(k).start()

        @pl.when(place == last)
        def _():
            share_ref[m, at] = own[m, y, at]

    def give_back(k):
        @pl.when(place < last)
        def _():
            down_copy(k).wait_recv()

        @pl.when(place > 0)
        def _():
            down_copy(k).start()

    def query_gradient(n):
        weight_gradient(n, back_query_ref)
        to_mate(n)

    def tick(t):
        @pl.when(t < chunks)
        def _():
            to_across(t)

        @pl.when(t == chunks)
        def _():
            finish_result()

        b = t - 3 - 2 * place

        @pl.when((b >= 0) & (b < 2 * chunks) & (lax.rem(b, 2) == 0))
        def _():
            to_next(b // 2)

        c = t - KEYVAL_HEADS * blocks - 2 * (last - place)

        @pl.when((c >= 0) & (c < 2 * early) & (lax.rem(c, 2) == 0))
        def _():
            give_back(c // 2)

        for at, stage, n in (
            (chunks + 1, to_y, 0), (20, query_gradient, 1), (20, to_x, 0), (21, to_y, 1),
            (22, to_z, 0), (24, to_all, 0), (26, to_x, 1), (26, to_back, 0), (28, to_z, 1),
            (30, to_all, 1),
        ):
            @pl.when(t == at)
            def _(stage=stage, n=n):
                stage(n)

    def part_copy(j, s):
        return remote(
            parts.at[j, s], part_in.at[j, s - 1], part_send.at[j, s - 1],
            part_recv.at[j, s - 1], ctx=place - 1,
        )

    def step(j, s, masked):
        keys = keyval_ref[s, j, 0]
        keys_turned = keys.T
        values_turned = keyval_ref[s, j, 1].T
        back_key = jnp.zeros(keys.shape, jnp.float32)
        back_value = jnp.zeros(keys.shape, jnp.float32)
        for g in range(GROUP):
            head = GROUP * j + g
            query = query_ref[head]
            back = back_ref[head]
            if masked:
                row_sums[g] = jnp.sum(wide(back) * wide(mixed_ref[head]), 0, keepdims=True)
            scores = dot(keys_turned, query, 1, 0)
            if masked:
                scores = causal(scores)
            weights = jnp.exp(scores - lse_ref[head])
            back_weights = dot(values_turned, back, 1, 0)
            back_scores = low(weights * (back_weights - row_sums[g]))
            added = dot(keys, back_scores, 1, 0)
            if masked:
                back_total[g] = added
            else:
                back_total[g] += added
            back_key += dot(query, back_scores, 1, 1)
            back_value += dot(back, low(weights), 1, 1)
        parts[j, s, 0] = low(back_key)
        parts[j, s, 1] = low(back_value)

    def hand_on(j):
        for s in range(blocks):
            @pl.when(s <= place)
            def _(s=s):
                @pl.when(place < last)
                def _():
                    pltpu.make_async_copy(
                        part_in.at[j, s], part_in.at[j, s], part_recv.at[j, s]
                    ).wait()
                    for kind in range(2):
                        total = wide(parts[j, s, kind]) + wide(part_in[j, s, kind])
                        parts[j, s, kind] = low(total)

                if s > 0:
                    part_copy(j, s).start()
                else:
                    leading = wide(parts[j, 0, 0, :HALF])
                    trailing = wide(parts[j, 0, 0, HALF:])
                    cosine, sine = cosine_ref[...], sine_ref[...]
                    at = j * HEAD_WIDTH
                    back_keyval_ref[pl.ds(pl.multiple_of(at, HALF), HALF)] = low(
                        leading * cosine + trailing * sine
                    )
                    back_keyval_ref[pl.ds(pl.multiple_of(at + HALF, HALF), HALF)] = low(
                        trailing * cosine - leading * sine
                    )
                    at = pl.ds(pl.multiple_of(KEY_WIDTH + at, HEAD_WIDTH), HEAD_WIDTH)
                    back_keyval_ref[at] = low(wide(parts[j, 0, 1]))

    def head_loop(j, carry):
        @pl.when(j < KEYVAL_HEADS)
        def _():
            step(j, 0, True)

        tick(j * blocks)

        def block_loop(s, inner):
            @pl.when((j < KEYVAL_HEADS) & (s <= place))
            def _():
                step(j, s, False)

            tick(j * blocks + s)
            return inner

        lax.fori_loop(1, blocks, block_loop, 0)

        @pl.when(j < KEYVAL_HEADS)
        def _():
            cosine, sine = cosine_ref[...], sine_ref[...]
            for g in range(GROUP):
                leading = back_total[g, :HALF] * SCALE
                trailing = back_total[g, HALF:] * SCALE
                at = (GROUP * j + g) * HEAD_WIDTH
                back_query_ref[pl.ds(pl.multiple_of(at, HALF), HALF)] = low(
                    leading * cosine + trailing * sine
                )
                back_query_ref[pl.ds(pl.multiple_of(at + HALF, HALF), HALF)] = low(
                    trailing * cosine - leading * sine
                )

        ready = j - (last - place)

        @pl.when((ready >= 0) & (ready < KEYVAL_HEADS))
        def _():
            hand_on(ready)

        return carry

    assert (KEYVAL_HEADS + last) * blocks >= 4 + 4 * last + 2 * (chunks - 1)
    lax.fori_loop(0, KEYVAL_HEADS + last, head_loop, 0)

    def keyval_gradient(n):
        weight_gradient(n, back_keyval_ref)
        to_mate(n)

    later = (
        ((keyval_gradient, 2), (to_back, 1)), ((to_y, 2),), ((lambda n: input_gradient(), 3),),
        ((to_x, 2),), ((to_y, 3),), ((to_z, 2), (to_x, 3)), ((to_all, 2), (to_z, 3)),
        ((to_back, 2), (to_all, 3)), ((to_back, 3),),
    )
    for slot, stages in enumerate(later):
        for stage, n in stages:
            stage(n)
        for index in range(blocks):
            if early <= early + slot - last + index < chunks:
                @pl.when(place == index)
                def _(k=early + slot - last + index):
                    give_back(k)

    assert len(later) >= chunks - early + last
    for n in range(chunks_in):
        finish_sum(n)
    token_copy.wait()

    for m in range(len(gradients)):
        for r in range(per):
            for half in range(2):
                mate_copy(m, r, half).wait_send()

    def finish(k, carry):
        y_copy(k).wait_send()

        @pl.when(place < last)
        def _():
            up_copy(k).wait_send()

        @pl.when(place > 0)
        def _():
            down_copy(k).wait_send()

        return carry

    lax.fori_loop(0, chunks, finish, 0)

    def finish_parts(j, carry):
        for s in range(1, blocks):
            @pl.when(s <= place)
            def _(s=s):
                part_copy(j, s).wait_send()
        return carry

    lax.fori_loop(0, KEYVAL_HEADS, finish_parts, 0)
    feed_copy.wait_send()
    trade_copy.wait()


def backward_sum(
    query, keyval, back_mixed, mixed, lse, cosine, sine, base, feed, tokens, normed, middle,
    gains, gain_two, full_query, full_keyval, gradients, gradient_out,
):
    blocks, positions = keyval.shape[0], keyval.shape[-1]
    count, rows, columns = gradients[0].shape
    chunks = len(gradients) * rows // CHUNK_ROWS
    area = QUERY_HEADS * positions * positions * blocks
    vmem = pl.BlockSpec(memory_space=pltpu.VMEM)
    anywhere = pl.BlockSpec(memory_space=pl.ANY)
    dma = pltpu.SemaphoreType.DMA
    share = (len(gradients), rows, columns)
    head = (2, HEAD_WIDTH, positions)
    features = feed.shape[0]
    widths = (QUERY_WIDTH, QUERY_WIDTH, 2 * KEY_WIDTH, gains.shape[-1])
    padded = rows + 16
    half_rows = padded // 2
    low_type = jnp.bfloat16
    scratch = []
    for first in ((count, padded), (2, padded), (padded,), (half_rows,),
                  (blocks - 1, half_rows // blocks)):
        scratch += [pltpu.VMEM(first + (w,), low_type) for w in widths]
    each = len(widths)
    pairs = jax.ShapeDtypeStruct((2, features, positions // 2), low_type)
    return pl.pallas_call(
        backward_sum_kernel,
        in_specs=[vmem] * 16 + [anywhere] * 4,
        out_specs=[vmem] * (3 + each),
        out_shape=[jax.ShapeDtypeStruct(share, low_type), pairs, pairs] + [
            jax.ShapeDtypeStruct((padded, w), low_type) for w in widths
        ],
        scratch_shapes=scratch + [
            pltpu.VMEM((len(gradients), 2, rows, columns), low_type),
            pltpu.VMEM((len(gradients), 2, rows, columns), low_type),
            pltpu.VMEM(share, low_type),
            pltpu.VMEM(share, low_type),
            pltpu.VMEM((KEYVAL_HEADS, blocks) + head, low_type),
            pltpu.VMEM((KEYVAL_HEADS, blocks - 1) + head, low_type),
            pltpu.VMEM((GROUP, HEAD_WIDTH, positions), jnp.float32),
            pltpu.VMEM((GROUP, 1, positions), jnp.float32),
            dma((len(gradients), 2)),
            dma((chunks, 2)), dma((chunks, 2)),
            dma((chunks,)), dma((chunks,)),
            dma((chunks,)), dma((chunks,)),
            dma((chunks,)), dma((chunks,)),
            dma((KEYVAL_HEADS, blocks - 1)), dma((KEYVAL_HEADS, blocks - 1)),
            pltpu.VMEM(feed.shape, low_type),
            pltpu.VMEM((features, positions // 2), low_type),
            dma, dma, dma, dma,
            pltpu.VMEM((QUERY_WIDTH, positions), low_type),
            pltpu.VMEM((2 * KEY_WIDTH, positions), low_type),
            pltpu.VMEM((features, positions), jnp.float32),
            pltpu.VMEM((features, positions // 2), low_type),
            dma((count,)),
            dma((each, 2)), dma((each, 2)),
            dma((each,)), dma((each,)),
            dma((each,)), dma((each,)),
            dma((each, blocks - 1)), dma((each, blocks - 1)),
            dma((each, blocks - 1)), dma((each, blocks - 1)),
            dma((each,)), dma((each,)),
            dma, dma,
        ],
        compiler_params=pltpu.CompilerParams(
            vmem_limit_bytes=KERNEL_VMEM, collective_id=0, has_side_effects=True
        ),
        cost_estimate=pl.CostEstimate(
            flops=40 * HEAD_WIDTH * area, bytes_accessed=10 * query.size, transcendentals=area
        ),
        name="backward_sum",
    )(
        query, keyval, back_mixed, mixed, lse, cosine, sine, base, feed, tokens, normed, middle,
        gains, gain_two, full_query, full_keyval, *gradients, gradient_out,
    )


def front_kernel(
    tokens_ref, cotangent_ref, cosine_ref, sine_ref, *refs
):
    weights, refs = refs[:7], refs[7:]
    (
        tokens_own, cotangent_own, cotangent_other, normed_out, query_out, keyval_ref,
        mixed_out, lse_ref, tokens_other, mixed_other,
    ), refs = refs[:10], refs[10:]
    full, refs = refs[:7], refs[7:]
    (
        raw, tops, totals, sums,
        local_sem, token_send, token_recv, cot_send, cot_recv,
        y_send, y_recv, mate_send, mate_recv, pass_send, pass_recv, key_send, key_recv,
        mixed_send, mixed_recv,
    ) = refs
    place = lax.axis_index("ctx")
    last = lax.axis_size("ctx") - 1
    rank = lax.axis_index("fsdp")
    side = lax.axis_index("tp")
    core = rank % 2
    mate = rank + 1 - 2 * core
    across = rank + 2 - 4 * (rank // 2)
    width = tokens_ref.shape[-1]

    def columns(ref, slot):
        return ref.at[:, pl.ds(pl.multiple_of(slot * width, width), width)]

    local = [
        pltpu.make_async_copy(tokens_ref.at[side], columns(tokens_own, side), local_sem.at[0]),
        pltpu.make_async_copy(
            cotangent_ref.at[side], columns(cotangent_own, side), local_sem.at[1]
        ),
        pltpu.make_async_copy(
            cotangent_ref.at[1 - side], columns(cotangent_other, side), local_sem.at[2]
        ),
        pltpu.make_async_copy(
            tokens_ref.at[1 - side], columns(tokens_other, side), local_sem.at[3]
        ),
    ]
    for w in range(len(weights)):
        local.append(pltpu.make_async_copy(weights[w], full[w].at[rank], local_sem.at[4 + w]))
    for copy in local:
        copy.start()

    greet(fsdp=mate)
    greet(fsdp=across)
    greet(tp=1 - side)

    @pl.when(place > 0)
    def _():
        greet(ctx=place - 1)

    @pl.when(place < last)
    def _():
        greet(ctx=place + 1)

    neighbours = (place + last - 1) // last + (2 * last - place - 1) // last
    pl.semaphore_wait(pltpu.get_barrier_semaphore(), 3 + neighbours)

    token_copy = remote(
        tokens_ref.at[1 - side], columns(tokens_own, side), token_send, token_recv, tp=1 - side
    )
    cot_copies = [
        remote(
            cotangent_ref.at[1 - side], columns(cotangent_own, side), cot_send.at[0],
            cot_recv.at[0], tp=1 - side,
        ),
        remote(
            cotangent_ref.at[side], columns(cotangent_other, side), cot_send.at[1],
            cot_recv.at[1], tp=1 - side,
        ),
        remote(
            tokens_ref.at[side], columns(tokens_other, side), cot_send.at[2], cot_recv.at[2],
            tp=1 - side,
        ),
    ]

    def mixed_copy(j):
        heads = pl.ds(GROUP * j, GROUP)
        return remote(
            mixed_out.at[heads], mixed_other.at[heads], mixed_send.at[j], mixed_recv.at[j],
            tp=1 - side,
        )


    def y_copy(w):
        return remote(
            weights[w], full[w].at[rank], y_send.at[w], y_recv.at[w], fsdp=across
        )

    def mate_copy(w):
        return remote(
            weights[w], full[w].at[rank], mate_send.at[w], mate_recv.at[w], fsdp=mate
        )

    def pass_copy(w):
        return remote(
            full[w].at[across], full[w].at[across], pass_send.at[w], pass_recv.at[w], fsdp=mate
        )

    def arrived(w):
        local[4 + w].wait()
        mate_copy(w).wait_recv()
        pass_copy(w).wait_recv()

    for w in (6, 1):
        y_copy(w).start()
        mate_copy(w).start()
    token_copy.start()
    y_copy(0).start()
    mate_copy(0).start()
    y_copy(6).wait_recv()
    pass_copy(6).start()
    arrived(6)
    gain = wide(full[6][...].reshape(-1, full[6].shape[-1])[:, :1])

    def norm_rows(slot):
        at = pl.ds(pl.multiple_of(slot * width, width), width)
        rows = wide(tokens_own[:, at])
        inverse = lax.rsqrt(jnp.mean(rows * rows, 0, keepdims=True) + EPS)
        normed_out[:, at] = low(rows * inverse * gain)

    local[0].wait()
    norm_rows(side)
    token_copy.wait_recv()
    norm_rows(1 - side)
    for copy in cot_copies:
        copy.start()
    for w in (1, 0):
        y_copy(w).wait_recv()
        pass_copy(w).start()
    for w in range(2, 6):
        y_copy(w).start()
        mate_copy(w).start()
    normed = normed_out[...]
    cosine, sine = cosine_ref[...], sine_ref[...]

    def turned(value, target):
        target[:HALF] = low(value[:HALF] * cosine - value[HALF:] * sine)
        target[HALF:] = low(value[HALF:] * cosine + value[:HALF] * sine)

    def key_copy(s, j):
        return remote(
            keyval_ref.at[s, j], keyval_ref.at[s + 1, j], key_send.at[s, j], key_recv.at[s, j],
            ctx=place + 1,
        )

    arrived(1)
    matrix = full[1][...].reshape(-1, 2 * KEY_WIDTH)
    raw[: 2 * KEY_WIDTH] = dot(matrix, normed, 0, 0)
    for j in range(KEYVAL_HEADS):
        turned(raw[j * HEAD_WIDTH : (j + 1) * HEAD_WIDTH], keyval_ref.at[0, j, 0])
        first = KEY_WIDTH + j * HEAD_WIDTH
        keyval_ref[0, j, 1] = low(raw[first : first + HEAD_WIDTH])

        @pl.when(place < last)
        def _(j=j):
            key_copy(0, j).start()

    arrived(0)
    matrix = full[0][...].reshape(-1, QUERY_WIDTH)
    raw[...] = dot(matrix, normed, 0, 0)

    def turn_query(h, carry):
        value = raw[pl.ds(pl.multiple_of(h * HEAD_WIDTH, HEAD_WIDTH), HEAD_WIDTH)]
        first = low(value[:HALF] * cosine - value[HALF:] * sine)
        second = low(value[HALF:] * cosine + value[:HALF] * sine)
        query_out[h, :HALF] = first * jnp.bfloat16(SCALE)
        query_out[h, HALF:] = second * jnp.bfloat16(SCALE)
        return carry

    lax.fori_loop(0, QUERY_HEADS, turn_query, 0)

    def attend(s, j, masked):
        keys_turned = keyval_ref[s, j, 0].T
        values = keyval_ref[s, j, 1]
        for g in range(GROUP):
            head = GROUP * j + g
            scores = dot(keys_turned, query_out[head], 1, 0)
            if masked:
                scores = causal(scores)
                top = jnp.max(scores, 0, keepdims=True)
                lifted = jnp.exp(scores - top)
                tops[head] = top
                totals[head] = jnp.sum(lifted, 0, keepdims=True)
                sums[head] = dot(values, low(lifted), 1, 0)
            else:
                old = tops[head]
                top = jnp.maximum(old, jnp.max(scores, 0, keepdims=True))
                lifted = jnp.exp(scores - top)
                shrink = jnp.exp(old - top)
                tops[head] = top
                totals[head] = totals[head] * shrink + jnp.sum(lifted, 0, keepdims=True)
                sums[head] = sums[head] * shrink + dot(values, low(lifted), 1, 0)

    def hand_on(s, j):
        @pl.when(s < place)
        def _():
            pltpu.make_async_copy(
                keyval_ref.at[s + 1, j], keyval_ref.at[s + 1, j], key_recv.at[s, j]
            ).wait()

            @pl.when(place < last)
            def _():
                key_copy(s + 1, j).start()

    def finish_heads(j):
        for g in range(GROUP):
            head = GROUP * j + g
            total = totals[head]
            mixed_out[head] = low(sums[head] / total)
            lse_ref[head] = tops[head] + jnp.log(total)
        mixed_copy(j).start()

    def first_block(j, carry):
        attend(0, j, True)

        @pl.when(place == 0)
        def _():
            finish_heads(j)

        hand_on(0, j)
        return carry

    lax.fori_loop(0, KEYVAL_HEADS, first_block, 0)
    passed = 2

    def later_block(i, carry):
        s = 1 + i // KEYVAL_HEADS
        j = lax.rem(i, KEYVAL_HEADS)
        attend(s, j, False)

        @pl.when(s == place)
        def _():
            finish_heads(j)

        hand_on(s, j)
        return carry

    lax.fori_loop(0, place * KEYVAL_HEADS, later_block, 0)

    for w in range(passed, 6):
        y_copy(w).wait_recv()
        pass_copy(w).start()
    for copy in local[1:4]:
        copy.wait()
    for j in range(KEYVAL_HEADS):
        mixed_copy(j).wait()
    token_copy.wait_send()
    for copy in cot_copies:
        copy.wait()
    for w in range(passed, 6):
        arrived(w)
    for w in range(len(weights)):
        y_copy(w).wait_send()
        mate_copy(w).wait_send()
        pass_copy(w).wait_send()

    @pl.when(place < last)
    def _():
        def sent(i, carry):
            key_copy(i // KEYVAL_HEADS, lax.rem(i, KEYVAL_HEADS)).wait_send()
            return carry

        lax.fori_loop(0, (place + 1) * KEYVAL_HEADS, sent, 0)


def front(tokens, cotangent, cosine, sine, weights):
    blocks = lax.axis_size("ctx")
    parts = lax.axis_size("fsdp")
    positions = cosine.shape[-1]
    vmem = pl.BlockSpec(memory_space=pltpu.VMEM)
    anywhere = pl.BlockSpec(memory_space=pl.ANY)
    dma = pltpu.SemaphoreType.DMA
    shape = lambda *dims: jax.ShapeDtypeStruct(dims, jnp.bfloat16)
    count = len(weights)
    features = tokens.shape[1]
    area = QUERY_HEADS * positions * positions * blocks
    return pl.pallas_call(
        front_kernel,
        in_specs=[vmem] * (4 + count),
        out_specs=[vmem] * 12 + [anywhere] * 4 + [vmem],
        out_shape=[
            shape(features, positions), shape(features, positions), shape(features, positions),
            shape(features, positions),
            shape(QUERY_HEADS, HEAD_WIDTH, positions),
            shape(blocks, KEYVAL_HEADS, 2, HEAD_WIDTH, positions),
            shape(QUERY_HEADS, HEAD_WIDTH, positions),
            jax.ShapeDtypeStruct((QUERY_HEADS, 1, positions), jnp.float32),
            shape(features, positions),
            shape(QUERY_HEADS, HEAD_WIDTH, positions),
        ] + [shape(parts, *w.shape) for w in weights],
        scratch_shapes=[
            pltpu.VMEM((QUERY_WIDTH, positions), jnp.float32),
            pltpu.VMEM((QUERY_HEADS, 1, positions), jnp.float32),
            pltpu.VMEM((QUERY_HEADS, 1, positions), jnp.float32),
            pltpu.VMEM((QUERY_HEADS, HEAD_WIDTH, positions), jnp.float32),
            dma((4 + count,)),
            dma, dma,
            dma((3,)), dma((3,)),
            dma((count,)), dma((count,)),
            dma((count,)), dma((count,)),
            dma((count,)), dma((count,)),
            dma((blocks, KEYVAL_HEADS)), dma((blocks, KEYVAL_HEADS)),
            dma((KEYVAL_HEADS,)), dma((KEYVAL_HEADS,)),
        ],
        compiler_params=pltpu.CompilerParams(
            vmem_limit_bytes=KERNEL_VMEM, collective_id=1, has_side_effects=True
        ),
        cost_estimate=pl.CostEstimate(
            flops=16 * HEAD_WIDTH * area, bytes_accessed=10 * tokens.size, transcendentals=area
        ),
        name="front",
    )(tokens, cotangent, cosine, sine, *weights)


def on_device(
    tokens, cotangent, input_gain, w_query, w_keyval, w_output, middle_gain, w_gate, w_up, w_down
):
    half = lax.axis_index("tp")
    low_half = half == 0
    pair = [(0, 1), (1, 0)]

    def to_partner(value_rows):
        return lax.ppermute(value_rows, "tp", pair)

    def in_order(mine, received):
        return jnp.concatenate(
            [jnp.where(low_half, mine, received), jnp.where(low_half, received, mine)], 0
        )

    def take(value_rows, index):
        return lax.dynamic_index_in_dim(value_rows, index, 0, keepdims=False)

    tokens_own = in_order(take(tokens, half), to_partner(take(tokens, 1 - half)))
    full_gain_one, full_gain_two = (
        lax.all_gather(input_gain, "fsdp", axis=0, tiled=True),
        lax.all_gather(middle_gain, "fsdp", axis=0, tiled=True),
    )
    full_in = lax.all_gather(jnp.concatenate([w_query, w_keyval], 1), "fsdp", axis=0, tiled=True)
    full_output = lax.all_gather(w_output, "fsdp", axis=0, tiled=True)
    full_gate = lax.all_gather(w_gate, "fsdp", axis=0, tiled=True)
    full_up = lax.all_gather(w_up, "fsdp", axis=0, tiled=True)
    full_down = lax.all_gather(w_down, "fsdp", axis=0, tiled=True)
    cotangent_received = to_partner(cotangent)
    cotangent_own = in_order(take(cotangent, half), take(cotangent_received, half))
    cotangent_other = in_order(take(cotangent, 1 - half), take(cotangent_received, 1 - half))

    token_positions = tokens_own.shape[0]
    cosine, sine = rope_tables(token_positions, lax.axis_index("ctx") * token_positions)
    gain_one = full_gain_one.astype(jnp.float32)
    inputs = tokens_own.astype(jnp.float32)
    unit_one, inverse_one = normalize(inputs)
    normed_one = (unit_one * gain_one).astype(jnp.bfloat16)
    keyval_raw = dot(full_in[:, QUERY_WIDTH:], normed_one, 0, 1)
    keyval_low = jnp.concatenate(
        [apply_rotary(keyval_raw[:KEY_WIDTH], cosine, sine), keyval_raw[KEY_WIDTH:]], 0
    ).astype(jnp.bfloat16)
    blocks = lax.axis_size("ctx")
    keyval = jnp.stack([keyval_low] + [move_along(keyval_low, s) for s in range(1, blocks)], 0)
    keyval = keyval.reshape(blocks, 2, KEYVAL_HEADS, HEAD_WIDTH, token_positions)
    query_raw = dot(full_in[:, :QUERY_WIDTH], normed_one, 0, 1)
    query_low = (
        apply_rotary(query_raw, cosine, sine)
        .astype(jnp.bfloat16)
        .reshape(QUERY_HEADS, HEAD_WIDTH, token_positions)
    )
    mixed_heads, lse = attend_forward(query_low, keyval)
    mixed_low = mixed_heads.reshape(QUERY_WIDTH, token_positions)
    middle = inputs + dot(mixed_low, full_output, 0, 0)

    gain_two = full_gain_two.astype(jnp.float32)
    unit_two, inverse_two = normalize(middle)
    normed_two = (unit_two * gain_two).astype(jnp.bfloat16)
    normed_other = to_partner(normed_two)

    def feed(rows, back_rows):
        gate_proj = dot(rows, full_gate, 1, 0)
        up_proj = dot(rows, full_up, 1, 0)
        sigmoid_gate = jax.nn.sigmoid(gate_proj)
        swish_gate = gate_proj * sigmoid_gate
        hidden = (swish_gate * up_proj).astype(jnp.bfloat16)
        back_hidden = dot(back_rows, full_down, 1, 0)
        back_gate = (
            back_hidden * up_proj * sigmoid_gate * (1.0 + gate_proj * (1.0 - sigmoid_gate))
        ).astype(jnp.bfloat16)
        back_up = (back_hidden * swish_gate).astype(jnp.bfloat16)
        return (hidden, back_gate, back_up)

    def feed_input_back(back_gate, back_up):
        return dot(back_gate, full_gate, 1, 1) + dot(back_up, full_up, 1, 1)

    hidden_own, back_gate_own, back_up_own = feed(normed_two, cotangent_own)
    hidden_other, back_gate_other, back_up_other = feed(normed_other, cotangent_other)
    back_two_received = to_partner(
        feed_input_back(back_gate_other, back_up_other).astype(jnp.bfloat16)
    )
    back_two = feed_input_back(back_gate_own, back_up_own) + back_two_received.astype(jnp.float32)
    feed_received = to_partner(dot(hidden_other, full_down, 1, 1).astype(jnp.bfloat16))
    result_own = (
        middle + dot(hidden_own, full_down, 1, 1) + feed_received.astype(jnp.float32)
    ).astype(jnp.bfloat16)

    def feed_gradient(left_own, right_own, left_other, right_other):
        gradient = dot(left_own, right_own, 0, 0) + dot(left_other, right_other, 0, 0)
        shared = scatter_sum(gradient.astype(jnp.bfloat16), "fsdp")
        return whole_sum(shared, (("ctx", 2),))

    share_down = feed_gradient(cotangent_own, hidden_own, cotangent_other, hidden_other)
    share_gate = feed_gradient(normed_two, back_gate_own, normed_other, back_gate_other)
    share_up = feed_gradient(normed_two, back_up_own, normed_other, back_up_other)

    grad_gain_two = jnp.sum(back_two * unit_two, axis=0)
    back_middle = cotangent_own.astype(jnp.float32) + norm_back(
        back_two * gain_two, unit_two, inverse_two
    )
    back_attention = back_middle.astype(jnp.bfloat16)
    back_mixed = dot(full_output, back_attention, 1, 1).astype(jnp.bfloat16)
    back_mixed = back_mixed.reshape(query_low.shape)
    grad_output = dot(mixed_low, back_attention, 1, 0).astype(jnp.bfloat16)
    share_output = whole_sum(scatter_sum(grad_output, "fsdp"), (("tp", 1), ("ctx", 2)))

    back_query = []
    back_key = []
    back_value = []
    for first, count in ((0, 3), (3, 2)):
        part_query, part_keyval = attend_backward(
            query_low, keyval, back_mixed, mixed_heads, lse, cosine, sine, first, count
        )
        part_keyval = part_keyval.reshape(blocks, 2 * count * HEAD_WIDTH, token_positions)
        owned = part_keyval[0].astype(jnp.float32)
        for s in range(1, blocks):
            owned += move_along(part_keyval[s], -s).astype(jnp.float32)
        back_query.append(part_query.reshape(-1, token_positions))
        back_key.append(
            apply_rotary(owned[: count * HEAD_WIDTH], cosine, -sine).astype(jnp.bfloat16)
        )
        back_value.append(owned[count * HEAD_WIDTH :].astype(jnp.bfloat16))
    back_in = jnp.concatenate(back_query + back_key + back_value, 0)
    grad_in = dot(normed_one, back_in, 0, 1)
    back_one = dot(back_in, full_in, 0, 1)
    grad_gain_one = jnp.sum(back_one * unit_one, axis=0)
    back_inputs = back_middle + norm_back(back_one * gain_one, unit_one, inverse_one)

    def to_positions(value_rows):
        split = value_rows.reshape(2, token_positions // 2, value_rows.shape[-1])
        received = to_partner(take(split, 1 - half))
        return in_order(take(split, half)[None], received[None])

    result = to_positions(result_own)
    grad_tokens = to_positions(back_inputs.astype(jnp.bfloat16)).astype(jnp.float32)
    gradients = jnp.concatenate([grad_in, grad_gain_one[:, None], grad_gain_two[:, None]], 1)
    share_in = lax.psum(
        lax.psum_scatter(
            gradients.astype(jnp.bfloat16), "fsdp", scatter_dimension=0, tiled=True
        ),
        ("ctx", "tp"),
    ).astype(jnp.float32)
    width = full_in.shape[1]
    return (
        result,
        grad_tokens,
        share_in[:, width],
        share_in[:, :QUERY_WIDTH],
        share_in[:, QUERY_WIDTH:width],
        share_output,
        share_in[:, width + 1],
        share_gate,
        share_up,
        share_down,
    )


def fast_on_device(
    tokens, cotangent, input_gain, w_query, w_keyval, w_output, middle_gain, w_gate, w_up, w_down
):
    pair = [(0, 1), (1, 0)]

    def to_partner(value_rows):
        return lax.ppermute(value_rows, "tp", pair)

    parts = lax.axis_size("fsdp")
    width_in = tokens.shape[-1]
    rows = width_in // parts
    token_positions = 2 * tokens.shape[1]
    cosine, sine = rope_tables(token_positions, lax.axis_index("ctx") * token_positions)
    gains = jnp.pad(jnp.stack([input_gain, middle_gain], 1), ((0, 0), (0, 126)))
    (
        tokens_own, cotangent_own, cotangent_other, normed_one, query_low, keyval,
        mixed_heads, lse, tokens_other, mixed_other, *full,
    ) = front(
        tokens.swapaxes(1, 2), cotangent.swapaxes(1, 2), cosine, sine,
        (w_query, w_keyval, w_output, w_gate, w_up, w_down, gains),
    )
    full_query, full_keyval, full_output, full_gate, full_up, full_down, gains = [
        w.reshape(width_in, -1) for w in full
    ]
    tokens_own, cotangent_own, cotangent_other, normed_one, tokens_other = [
        v.T for v in (tokens_own, cotangent_own, cotangent_other, normed_one, tokens_other)
    ]
    full_gain_two = gains[:, 1]
    inputs = tokens_own.astype(jnp.float32)
    mixed_low = mixed_heads.reshape(QUERY_WIDTH, token_positions)
    middle = inputs + dot(mixed_low, full_output, 0, 0)

    gain_two = full_gain_two.astype(jnp.float32)
    unit_two, inverse_two = normalize(middle)
    normed_two = (unit_two * gain_two).astype(jnp.bfloat16)
    mixed_other = mixed_other.reshape(QUERY_WIDTH, token_positions)
    middle_other = tokens_other.astype(jnp.float32) + dot(mixed_other, full_output, 0, 0)
    normed_other = (normalize(middle_other)[0] * gain_two).astype(jnp.bfloat16)

    def feed(rows, back_rows):
        gate_proj = dot(rows, full_gate, 1, 0)
        up_proj = dot(rows, full_up, 1, 0)
        sigmoid_gate = jax.nn.sigmoid(gate_proj)
        swish_gate = gate_proj * sigmoid_gate
        hidden = (swish_gate * up_proj).astype(jnp.bfloat16)
        back_hidden = dot(back_rows, full_down, 1, 0)
        back_gate = (
            back_hidden * up_proj * sigmoid_gate * (1.0 + gate_proj * (1.0 - sigmoid_gate))
        ).astype(jnp.bfloat16)
        back_up = (back_hidden * swish_gate).astype(jnp.bfloat16)
        return (hidden, back_gate, back_up)

    def feed_input_back(back_gate, back_up):
        return dot(back_gate, full_gate, 1, 1) + dot(back_up, full_up, 1, 1)

    hidden_other, back_gate_other, back_up_other = feed(normed_other, cotangent_other)
    back_two_received = to_partner(
        feed_input_back(back_gate_other, back_up_other).astype(jnp.bfloat16)
    )
    hidden_own, back_gate_own, back_up_own = feed(normed_two, cotangent_own)
    back_two = feed_input_back(back_gate_own, back_up_own) + back_two_received.astype(jnp.float32)
    feed_other = dot(hidden_other, full_down, 1, 1).astype(jnp.bfloat16)
    base = middle + dot(hidden_own, full_down, 1, 1)

    def feed_gradient(left_own, right_own, left_other, right_other):
        gradient = dot(left_own, right_own, 0, 0) + dot(left_other, right_other, 0, 0)
        return gradient.astype(jnp.bfloat16).reshape(lax.axis_size("fsdp"), -1, gradient.shape[1])

    gradients = (
        feed_gradient(cotangent_own, hidden_own, cotangent_other, hidden_other),
        feed_gradient(normed_two, back_gate_own, normed_other, back_gate_other),
        feed_gradient(normed_two, back_up_own, normed_other, back_up_other),
    )

    grad_gain_two = jnp.sum(back_two * unit_two, axis=0)
    back_middle = cotangent_own.astype(jnp.float32) + norm_back(
        back_two * gain_two, unit_two, inverse_two
    )
    back_attention = back_middle.astype(jnp.bfloat16)
    back_mixed = dot(full_output, back_attention, 1, 1).astype(jnp.bfloat16)
    back_mixed = back_mixed.reshape(query_low.shape)
    grad_output = dot(mixed_low, back_attention, 1, 0).astype(jnp.bfloat16)
    share, result, grad_tokens, share_output, share_query, share_keyval, share_gains = backward_sum(
        query_low, keyval, back_mixed, mixed_heads, lse, cosine, sine, base.T, feed_other.T,
        tokens_own.T, normed_one.T, back_middle.T, gains, grad_gain_two[:, None],
        full_query, full_keyval, gradients, grad_output.reshape(parts, rows, -1),
    )
    return (
        result.swapaxes(1, 2),
        grad_tokens.swapaxes(1, 2).astype(jnp.float32),
        share_gains[:rows, 0].astype(jnp.float32),
        share_query[:rows].astype(jnp.float32),
        share_keyval[:rows].astype(jnp.float32),
        share_output[:rows].astype(jnp.float32),
        share_gains[:rows, 1].astype(jnp.float32),
        share[1].astype(jnp.float32),
        share[2].astype(jnp.float32),
        share[0].astype(jnp.float32),
    )


def solution(mesh):
    rows = P("fsdp", ("ctx", "tp"), None)
    specs = (
        P("fsdp"), P("fsdp", None), P("fsdp", None), P("fsdp", None),
        P("fsdp"), P("fsdp", "tp"), P("fsdp", "tp"), P("fsdp", "tp"),
    )
    kernels = mesh.shape["fsdp"] == 4 and mesh.shape["tp"] == 2 and mesh.shape["ctx"] == 4
    return jax.shard_map(
        fast_on_device if kernels else on_device,
        mesh=mesh,
        in_specs=(rows, rows) + specs,
        out_specs=(rows, rows) + specs,
        check_vma=False,
    )
```

```python
import jax
import jax.numpy as jnp
from jax import lax
from jax.experimental import pallas as pl
from jax.experimental.pallas import tpu as pltpu
from jax.sharding import PartitionSpec as P

QUERY_HEADS = 15
KEYVAL_HEADS = 5
GROUP = QUERY_HEADS // KEYVAL_HEADS
HEAD_WIDTH = 64
HALF = HEAD_WIDTH // 2
KEY_WIDTH = 320
QUERY_WIDTH = QUERY_HEADS * HEAD_WIDTH
SCALE = HEAD_WIDTH ** (-0.5)

EPS = 1e-05
THETA = 10000.0
VMEM_LIMIT = 40 * 1024 * 1024


def dot(left, right, left_dim, right_dim):
    return lax.dot_general(
        left, right, (((left_dim,), (right_dim,)), ((), ())), preferred_element_type=jnp.float32
    )


def rope_tables(token_positions, first_place):
    position = (first_place + lax.iota(jnp.int32, token_positions)).astype(jnp.float32)
    frequency = THETA ** (-(2.0 * lax.iota(jnp.int32, HALF).astype(jnp.float32)) / HEAD_WIDTH)
    angles = frequency[:, None] * position[None, :]
    return (jnp.cos(angles), jnp.sin(angles))


def apply_rotary(rows, cosine, sine):
    shaped = rows.reshape(-1, 2, HALF, rows.shape[-1])
    leading = shaped[:, 0]
    trailing = shaped[:, 1]
    return jnp.stack(
        [leading * cosine - trailing * sine, trailing * cosine + leading * sine], 1
    ).reshape(rows.shape)


def normalize(value_rows):
    inverse_rms = lax.rsqrt(jnp.mean(value_rows * value_rows, -1, keepdims=True) + EPS)
    return (value_rows * inverse_rms, inverse_rms)


def norm_back(back_unit, unit_rows, inverse_rms):
    return inverse_rms * (
        back_unit - unit_rows * jnp.mean(back_unit * unit_rows, -1, keepdims=True)
    )


def causal(scores):
    key_place = lax.broadcasted_iota(jnp.int32, scores.shape, 0)
    query_place = lax.broadcasted_iota(jnp.int32, scores.shape, 1)
    return jnp.where(key_place <= query_place, scores, -jnp.inf)


def forward_kernel(query_ref, key_ref, value_ref, mixed_ref, lse_ref):
    place = lax.axis_index("ctx")
    queries = [query_ref[g] * jnp.bfloat16(SCALE) for g in range(GROUP)]

    def scores_of(keys_turned, g, masked):
        scores = dot(keys_turned, queries[g], 1, 0)
        return causal(scores) if masked else scores

    def first():
        keys_turned = key_ref[0, 0, 0].T
        values = value_ref[0, 0, 0]
        carried = []
        for g in range(GROUP):
            scores = scores_of(keys_turned, g, True)
            top = jnp.max(scores, 0, keepdims=True)
            lifted = jnp.exp(scores - top)
            total = jnp.sum(lifted, 0, keepdims=True)
            carried += [top, total, dot(values, lifted.astype(jnp.bfloat16), 1, 0)]
        return tuple(carried)

    def step(block, carried):
        keys_turned = key_ref[block, 0, 0].T
        values = value_ref[block, 0, 0]
        later = []
        for g in range(GROUP):
            top, total, mixed = carried[3 * g : 3 * g + 3]
            scores = scores_of(keys_turned, g, False)
            new_top = jnp.maximum(top, jnp.max(scores, 0, keepdims=True))
            lifted = jnp.exp(scores - new_top)
            shrink = jnp.exp(top - new_top)
            later += [
                new_top,
                total * shrink + jnp.sum(lifted, 0, keepdims=True),
                mixed * shrink + dot(values, lifted.astype(jnp.bfloat16), 1, 0),
            ]
        return tuple(later)

    carried = lax.fori_loop(1, place + 1, step, first())
    for g in range(GROUP):
        top, total, mixed = carried[3 * g : 3 * g + 3]
        mixed_ref[g] = (mixed / total).astype(jnp.bfloat16)
        lse_ref[g] = top + jnp.log(total)


def attend_forward(query, keyval):
    blocks, token_positions = keyval.shape[0], keyval.shape[-1]
    head_block = (GROUP, HEAD_WIDTH, token_positions)
    key_block = (blocks, 1, 1, HEAD_WIDTH, token_positions)
    area = QUERY_HEADS * token_positions * token_positions * blocks
    return pl.pallas_call(
        forward_kernel,
        grid=(KEYVAL_HEADS,),
        in_specs=[
            pl.BlockSpec(head_block, lambda j: (j, 0, 0)),
            pl.BlockSpec(key_block, lambda j: (0, 0, j, 0, 0)),
            pl.BlockSpec(key_block, lambda j: (0, 1, j, 0, 0)),
        ],
        out_specs=[
            pl.BlockSpec(head_block, lambda j: (j, 0, 0)),
            pl.BlockSpec((GROUP, 1, token_positions), lambda j: (j, 0, 0)),
        ],
        out_shape=[
            jax.ShapeDtypeStruct(query.shape, jnp.bfloat16),
            jax.ShapeDtypeStruct((QUERY_HEADS, 1, token_positions), jnp.float32),
        ],
        compiler_params=pltpu.CompilerParams(vmem_limit_bytes=VMEM_LIMIT),
        cost_estimate=pl.CostEstimate(
            flops=16 * HEAD_WIDTH * area, bytes_accessed=6 * query.size, transcendentals=area
        ),
        name="attend_forward",
    )(query, keyval, keyval)


def backward_kernel(
    query_ref, key_ref, value_ref, back_ref, mixed_ref, lse_ref, cosine_ref, sine_ref,
    back_query_ref, back_keyval_ref,
):
    place = lax.axis_index("ctx")
    blocks = key_ref.shape[0]
    queries = [query_ref[g] * jnp.bfloat16(SCALE) for g in range(GROUP)]
    backs = [back_ref[g] for g in range(GROUP)]
    tops = [lse_ref[g] for g in range(GROUP)]
    sums = [
        jnp.sum(backs[g].astype(jnp.float32) * mixed_ref[g].astype(jnp.float32), 0, keepdims=True)
        for g in range(GROUP)
    ]

    def step(block, carried, masked=False):
        keys = key_ref[block, 0, 0]
        keys_turned = keys.T
        values_turned = value_ref[block, 0, 0].T
        back_key = jnp.zeros(keys.shape, jnp.float32)
        back_value = jnp.zeros(keys.shape, jnp.float32)
        later = []
        for g in range(GROUP):
            scores = dot(keys_turned, queries[g], 1, 0)
            if masked:
                scores = causal(scores)
            weights = jnp.exp(scores - tops[g])
            back_weights = dot(values_turned, backs[g], 1, 0)
            back_scores = (weights * (back_weights - sums[g])).astype(jnp.bfloat16)
            later.append(carried[g] + dot(keys, back_scores, 1, 0))
            back_key += dot(queries[g], back_scores, 1, 1)
            back_value += dot(backs[g], weights.astype(jnp.bfloat16), 1, 1)
        back_keyval_ref[block, 0, 0] = back_key.astype(jnp.bfloat16)
        back_keyval_ref[block, 1, 0] = back_value.astype(jnp.bfloat16)
        return tuple(later)

    start = tuple(jnp.zeros(query_ref.shape[1:], jnp.float32) for g in range(GROUP))
    carried = lax.fori_loop(1, place + 1, step, step(0, start, True))

    def clear(block, unused):
        zero = jnp.zeros(key_ref.shape[3:], jnp.bfloat16)
        back_keyval_ref[block, 0, 0] = zero
        back_keyval_ref[block, 1, 0] = zero
        return unused

    lax.fori_loop(place + 1, blocks, clear, 0)
    cosine = cosine_ref[...]
    sine = sine_ref[...]
    for g in range(GROUP):
        leading = carried[g][:HALF] * SCALE
        trailing = carried[g][HALF:] * SCALE
        back_query_ref[g, :HALF] = (leading * cosine + trailing * sine).astype(jnp.bfloat16)
        back_query_ref[g, HALF:] = (trailing * cosine - leading * sine).astype(jnp.bfloat16)


def attend_backward(query, keyval, back_mixed, mixed, lse, cosine, sine, first, count):
    blocks, token_positions = keyval.shape[0], keyval.shape[-1]
    head_block = (GROUP, HEAD_WIDTH, token_positions)
    key_block = (blocks, 1, 1, HEAD_WIDTH, token_positions)
    area = count * GROUP * token_positions * token_positions * blocks
    heads = pl.BlockSpec(head_block, lambda j: (j + first, 0, 0))
    table = pl.BlockSpec((HALF, token_positions), lambda j: (0, 0))
    return pl.pallas_call(
        backward_kernel,
        grid=(count,),
        in_specs=[
            heads,
            pl.BlockSpec(key_block, lambda j: (0, 0, j + first, 0, 0)),
            pl.BlockSpec(key_block, lambda j: (0, 1, j + first, 0, 0)),
            heads,
            heads,
            pl.BlockSpec((GROUP, 1, token_positions), lambda j: (j + first, 0, 0)),
            table,
            table,
        ],
        out_specs=[
            pl.BlockSpec(head_block, lambda j: (j, 0, 0)),
            pl.BlockSpec((blocks, 2, 1, HEAD_WIDTH, token_positions), lambda j: (0, 0, j, 0, 0)),
        ],
        out_shape=[
            jax.ShapeDtypeStruct((count * GROUP, HEAD_WIDTH, token_positions), jnp.bfloat16),
            jax.ShapeDtypeStruct(
                (blocks, 2, count, HEAD_WIDTH, token_positions), jnp.bfloat16
            ),
        ],
        compiler_params=pltpu.CompilerParams(vmem_limit_bytes=VMEM_LIMIT),
        cost_estimate=pl.CostEstimate(
            flops=40 * HEAD_WIDTH * area, bytes_accessed=10 * query.size, transcendentals=area
        ),
        name="attend_backward",
    )(query, keyval, keyval, back_mixed, mixed, lse, cosine, sine)


def move_along(value, distance):
    blocks = lax.axis_size("ctx")
    pairs = [(i, i + distance) for i in range(blocks) if 0 <= i + distance < blocks]
    return lax.ppermute(value, "ctx", pairs)


def trade(value, axis, step):
    pairs = [(i, i ^ step) for i in range(lax.axis_size(axis))]
    return lax.ppermute(value, axis, pairs)


def add_low(left, right):
    return (left.astype(jnp.float32) + right.astype(jnp.float32)).astype(jnp.bfloat16)


def scatter_sum(value, axis):
    size = lax.axis_size(axis)
    index = lax.axis_index(axis)
    rows = value.shape[0] // size
    step = 1
    while step < size:
        count = value.shape[0] // (2 * rows)
        split = value.reshape(count, 2, rows, value.shape[-1])
        second = (index // step) % 2 == 1
        kept = jnp.where(second, split[:, 1], split[:, 0])
        sent = jnp.where(second, split[:, 0], split[:, 1])
        value = add_low(kept, trade(sent, axis, step)).reshape(count * rows, value.shape[-1])
        step *= 2
    return value


def whole_sum(value, others):
    half_rows = value.shape[0] // 2
    second = lax.axis_index("ctx") % 2 == 1
    upper, lower = value[:half_rows], value[half_rows:]
    received = trade(jnp.where(second, upper, lower), "ctx", 1)
    total = add_low(jnp.where(second, lower, upper), received)
    for axis, first_step in others:
        step = first_step
        while step < lax.axis_size(axis):
            total = add_low(total, trade(total, axis, step))
            step *= 2
    received = trade(total, "ctx", 1)
    return jnp.concatenate(
        [jnp.where(second, received, total), jnp.where(second, total, received)], 0
    ).astype(jnp.float32)


MESH = pl.DeviceIdType.MESH
KERNEL_VMEM = 60 * 1024 * 1024
CHUNK_ROWS = 80


def remote(source, target, send_sem, recv_sem, **place):
    return pltpu.make_async_remote_copy(
        src_ref=source, dst_ref=target, send_sem=send_sem, recv_sem=recv_sem,
        device_id=place, device_id_type=MESH,
    )


def wide(value):
    return value.astype(jnp.float32)


def low(value):
    return value.astype(jnp.bfloat16)


def greet(**place):
    pl.semaphore_signal(
        pltpu.get_barrier_semaphore(), inc=1, device_id=place, device_id_type=MESH
    )


def backward_sum_kernel(
    query_ref, keyval_ref, back_ref, mixed_ref, lse_ref, cosine_ref, sine_ref,
    base_ref, feed_ref, tokens_ref, normed_ref, middle_ref, gains_ref, gain_two_ref,
    full_query, full_keyval, down_ref, gate_ref, up_ref, out_ref,
    share_ref, result_ref, back_tokens_ref, *refs,
):
    chunks_in = 4
    shares, refs = refs[:chunks_in], refs[chunks_in:]
    whole, mate_part, y_part, x_part, z_part = [
        refs[i * chunks_in : (i + 1) * chunks_in] for i in range(5)
    ]
    (
    own, mate_in, y_in, up_in, parts, part_in, back_total, row_sums,
    own_sem, mate_send, mate_recv, y_send, y_recv, up_send, up_recv, down_send, down_recv,
    part_send, part_recv, feed_in, traded, feed_send, feed_recv, trade_send, trade_recv,
    back_query_ref, back_keyval_ref, back_one, token_traded,
    whole_sem, sum_mate_send, sum_mate_recv, sum_y_send, sum_y_recv, sum_x_send, sum_x_recv,
    sum_z_send, sum_z_recv, all_send, all_recv, back_send, back_recv, token_send, token_recv,
    ) = refs[5 * chunks_in :]
    place = lax.axis_index("ctx")
    last = lax.axis_size("ctx") - 1
    blocks = last + 1
    rank = lax.axis_index("fsdp")
    core = rank % 2
    y = rank // 2
    side = lax.axis_index("tp")
    mate = rank + 1 - 2 * core
    across = rank + 2 - 4 * y
    gradients = (down_ref, gate_ref, up_ref)
    rows = share_ref.shape[1]
    per = rows // CHUNK_ROWS
    chunks = len(gradients) * per
    early = 2 * per

    for m, gradient in enumerate(gradients):
        for half in range(2):
            pltpu.make_async_copy(
                gradient.at[2 * half + core], own.at[m, half], own_sem.at[m, half]
            ).start()
    greet(fsdp=mate)
    greet(fsdp=across)
    greet(tp=1 - side)
    for d in range(1, blocks):
        greet(ctx=lax.rem(place + d, blocks))
    filled = out_ref.shape[1]
    tail = whole[0].shape[1] - filled
    for n in range(chunks_in):
        width = whole[n].shape[-1]
        whole[n][:, filled:] = jnp.zeros((whole[n].shape[0], tail, width), jnp.bfloat16)
        mate_part[n][:, filled:] = jnp.zeros((2, tail, width), jnp.bfloat16)
    for f in range(whole[0].shape[0]):
        pltpu.make_async_copy(
            out_ref.at[f], whole[0].at[f, pl.ds(0, filled)], whole_sem.at[f]
        ).start()
    pl.semaphore_wait(pltpu.get_barrier_semaphore(), 3 + last)

    feed_copy = remote(feed_ref, feed_in, feed_send, feed_recv, tp=1 - side)
    trade_copy = remote(traded, result_ref.at[side], trade_send, trade_recv, tp=1 - side)
    feed_copy.start()
    pair_width = traded.shape[-1]
    step_rows = traded.shape[0] // 4

    def finish_result():
        feed_copy.wait_recv()

        def some_rows(i, carry):
            at = pl.ds(pl.multiple_of(i * step_rows, step_rows), step_rows)
            for target, slot in ((result_ref.at[side], side), (traded, 1 - side)):
                columns = pl.ds(pl.multiple_of(slot * pair_width, pair_width), pair_width)
                target[at] = low(base_ref[at, columns] + wide(feed_in[at, columns]))
            return carry

        lax.fori_loop(0, 4, some_rows, 0)
        trade_copy.start()

    half_rows = whole[0].shape[1] // 2
    piece = half_rows // blocks
    kept = 2 * y + core

    def sum_mate(n, half):
        return remote(
            whole[n].at[2 * half + 1 - core, pl.ds(0, filled)],
            mate_part[n].at[half, pl.ds(0, filled)],
            sum_mate_send.at[n, half], sum_mate_recv.at[n, half], fsdp=mate,
        )

    def sum_y(n):
        return remote(
            mate_part[n].at[1 - y], y_part[n], sum_y_send.at[n], sum_y_recv.at[n], fsdp=across
        )

    def sum_x(n):
        other = pl.ds(pl.multiple_of((1 - side) * half_rows, half_rows), half_rows)
        return remote(
            whole[n].at[kept, other], x_part[n], sum_x_send.at[n], sum_x_recv.at[n],
            tp=1 - side,
        )

    def sum_z(n, d):
        target = lax.rem(place + d, blocks)
        at = pl.ds(pl.multiple_of(side * half_rows + target * piece, piece), piece)
        return remote(
            whole[n].at[kept, at], z_part[n].at[d - 1], sum_z_send.at[n, d - 1],
            sum_z_recv.at[n, d - 1], ctx=target,
        )

    def all_copy(n, d, origin):
        spot = shares[n].at[
            pl.ds(pl.multiple_of(side * half_rows + origin * piece, piece), piece)
        ]
        return remote(
            spot, spot, all_send.at[n, d - 1], all_recv.at[n, d - 1],
            ctx=lax.rem(place + d, blocks),
        )

    def back_copy(n, half):
        spot = shares[n].at[pl.ds(pl.multiple_of(half * half_rows, half_rows), half_rows)]
        return remote(spot, spot, back_send.at[n], back_recv.at[n], tp=1 - side)

    def to_mate(n):
        for half in range(2):
            sum_mate(n, half).start()

    def to_y(n):
        for half in range(2):
            sum_mate(n, half).wait_recv()
        quarter = 2 * (1 - y) + core
        mate_part[n][1 - y] = low(wide(whole[n][quarter]) + wide(mate_part[n][1 - y]))
        sum_y(n).start()

    def to_x(n):
        sum_y(n).wait_recv()
        whole[n][kept] = low(
            wide(whole[n][kept]) + wide(mate_part[n][y]) + wide(y_part[n][...])
        )
        sum_x(n).start()

    def to_z(n):
        sum_x(n).wait_recv()
        at = pl.ds(pl.multiple_of(side * half_rows, half_rows), half_rows)
        whole[n][kept, at] = low(wide(whole[n][kept, at]) + wide(x_part[n][...]))
        for d in range(1, blocks):
            sum_z(n, d).start()

    def to_all(n):
        at = pl.ds(pl.multiple_of(side * half_rows + place * piece, piece), piece)
        total = wide(whole[n][kept, at])
        for d in range(1, blocks):
            sum_z(n, d).wait_recv()
            total += wide(z_part[n][d - 1])
        shares[n][at] = low(total)
        for d in range(1, blocks):
            all_copy(n, d, place).start()

    def to_back(n):
        for d in range(1, blocks):
            all_copy(n, d, lax.rem(place + blocks - d, blocks)).wait_recv()
        back_copy(n, side).start()

    def finish_sum(n):
        back_copy(n, 1 - side).wait_recv()
        for half in range(2):
            sum_mate(n, half).wait_send()
        sum_y(n).wait_send()
        sum_x(n).wait_send()
        for d in range(1, blocks):
            sum_z(n, d).wait_send()
            all_copy(n, d, place).wait_send()
        back_copy(n, side).wait_send()

    def weight_gradient(n, back_ref):
        def quarter(f, carry):
            rows_of = normed_ref[pl.ds(pl.multiple_of(f * filled, filled), filled)]
            whole[n][f, :filled] = low(dot(rows_of, back_ref[...], 1, 1))
            return carry

        lax.fori_loop(0, whole[n].shape[0], quarter, 0)

    token_copy = remote(
        token_traded, back_tokens_ref.at[side], token_send, token_recv, tp=1 - side
    )

    def input_gradient():
        tokens = wide(tokens_ref[...])
        inverse = lax.rsqrt(jnp.mean(tokens * tokens, 0, keepdims=True) + EPS)

        def quarter(f, total):
            at = pl.ds(pl.multiple_of(f * filled, filled), filled)
            unit = wide(tokens_ref[at]) * inverse
            back = dot(full_query[at], back_query_ref[...], 1, 0) + dot(
                full_keyval[at], back_keyval_ref[...], 1, 0
            )
            gain_sum = jnp.sum(back * unit, 1, keepdims=True)
            lane = lax.broadcasted_iota(jnp.int32, (filled, whole[3].shape[-1]), 1)
            whole[3][f, :filled] = low(
                jnp.where(lane == 0, gain_sum, jnp.where(lane == 1, gain_two_ref[at], 0.0))
            )
            back = back * wide(gains_ref[at])[:, :1]
            back_one[at] = back
            return total + jnp.sum(back * unit, 0, keepdims=True)

        total = lax.fori_loop(
            0, whole[0].shape[0], quarter, jnp.zeros((1, tokens_ref.shape[-1]), jnp.float32)
        )
        to_mate(3)
        mean = total / tokens_ref.shape[0]

        def rows_back(f, carry):
            at = pl.ds(pl.multiple_of(f * filled, filled), filled)
            unit = wide(tokens_ref[at]) * inverse
            back_one[at] = middle_ref[at] + inverse * (back_one[at] - unit * mean)
            for target, slot in ((back_tokens_ref.at[side], side), (token_traded, 1 - side)):
                columns = pl.ds(pl.multiple_of(slot * pair_width, pair_width), pair_width)
                target[at] = low(back_one[at, columns])
            return carry

        lax.fori_loop(0, whole[0].shape[0], rows_back, 0)
        token_copy.start()

    def chunk_at(ref, m, r, *front):
        return ref.at[(m,) + front + (pl.ds(r * CHUNK_ROWS, CHUNK_ROWS),)]

    def mate_copy(m, r, half):
        gradient = gradients[m]
        return remote(
            gradient.at[2 * half + 1 - core, pl.ds(r * CHUNK_ROWS, CHUNK_ROWS)],
            chunk_at(mate_in, m, r, half),
            mate_send.at[m * per + r, half], mate_recv.at[m * per + r, half], fsdp=mate,
        )

    for m in range(len(gradients)):
        for r in range(per):
            for half in range(2):
                mate_copy(m, r, half).start()
    for f in range(whole[0].shape[0]):
        pltpu.make_async_copy(
            out_ref.at[f], whole[0].at[f, pl.ds(0, filled)], whole_sem.at[f]
        ).wait()
    to_mate(0)
    for m, gradient in enumerate(gradients):
        for half in range(2):
            pltpu.make_async_copy(
                gradient.at[2 * half + core], own.at[m, half], own_sem.at[m, half]
            ).wait()

    def split(k):
        r = lax.rem(k, per)
        return k // per, pl.ds(pl.multiple_of(r * CHUNK_ROWS, CHUNK_ROWS), CHUNK_ROWS)

    def y_copy(k):
        m, at = split(k)
        return remote(
            own.at[m, 1 - y, at], y_in.at[m, at], y_send.at[k], y_recv.at[k], fsdp=across
        )

    def up_copy(k):
        m, at = split(k)
        return remote(
            own.at[m, y, at], up_in.at[m, at], up_send.at[k], up_recv.at[k], ctx=place + 1
        )

    def down_copy(k):
        m, at = split(k)
        return remote(
            share_ref.at[m, at], share_ref.at[m, at], down_send.at[k], down_recv.at[k],
            ctx=place - 1,
        )

    def to_across(k):
        m, at = split(k)
        for half in range(2):
            pltpu.make_async_copy(
                mate_in.at[m, half, at], mate_in.at[m, half, at], mate_recv.at[k, half]
            ).wait()
        own[m, 1 - y, at] = low(wide(own[m, 1 - y, at]) + wide(mate_in[m, 1 - y, at]))
        y_copy(k).start()

    def to_next(k):
        m, at = split(k)
        y_copy(k).wait_recv()
        total = wide(own[m, y, at]) + wide(mate_in[m, y, at]) + wide(y_in[m, at])

        @pl.when(place == 0)
        def _():
            own[m, y, at] = low(total)

        @pl.when(place > 0)
        def _():
            up_copy(k).wait_recv()
            own[m, y, at] = low(total + wide(up_in[m, at]))

        @pl.when(place < last)
        def _():
            up_copy(k).start()

        @pl.when(place == last)
        def _():
            share_ref[m, at] = own[m, y, at]

    def give_back(k):
        @pl.when(place < last)
        def _():
            down_copy(k).wait_recv()

        @pl.when(place > 0)
        def _():
            down_copy(k).start()

    def query_gradient(n):
        weight_gradient(n, back_query_ref)
        to_mate(n)

    def tick(t):
        @pl.when(t < chunks)
        def _():
            to_across(t)

        @pl.when(t == chunks + 1)
        def _():
            finish_result()

        b = t - 4 - 2 * place

        @pl.when((b >= 0) & (b < 2 * chunks) & (lax.rem(b, 2) == 0))
        def _():
            to_next(b // 2)

        c = t - 6 - 3 * last - 2 * (last - place)

        @pl.when((c >= 0) & (c < 2 * early) & (lax.rem(c, 2) == 0))
        def _():
            give_back(c // 2)

        for at, stage, n in (
            (4, to_y, 0), (15, to_x, 0), (18, to_z, 0), (20, query_gradient, 1),
            (20, to_all, 0), (21, to_y, 1), (23, to_back, 0), (25, to_x, 1), (27, to_z, 1),
            (29, to_all, 1),
        ):
            @pl.when(t == at)
            def _(stage=stage, n=n):
                stage(n)

    def part_copy(j, s):
        return remote(
            parts.at[j, s], part_in.at[j, s - 1], part_send.at[j, s - 1],
            part_recv.at[j, s - 1], ctx=place - 1,
        )

    def step(j, s, masked):
        keys = keyval_ref[s, j, 0]
        keys_turned = keys.T
        values_turned = keyval_ref[s, j, 1].T
        back_key = jnp.zeros(keys.shape, jnp.float32)
        back_value = jnp.zeros(keys.shape, jnp.float32)
        for g in range(GROUP):
            head = GROUP * j + g
            query = query_ref[head]
            back = back_ref[head]
            if masked:
                row_sums[g] = jnp.sum(wide(back) * wide(mixed_ref[head]), 0, keepdims=True)
            scores = dot(keys_turned, query, 1, 0)
            if masked:
                scores = causal(scores)
            weights = jnp.exp(scores - lse_ref[head])
            back_weights = dot(values_turned, back, 1, 0)
            back_scores = low(weights * (back_weights - row_sums[g]))
            added = dot(keys, back_scores, 1, 0)
            if masked:
                back_total[g] = added
            else:
                back_total[g] += added
            back_key += dot(query, back_scores, 1, 1)
            back_value += dot(back, low(weights), 1, 1)
        parts[j, s, 0] = low(back_key)
        parts[j, s, 1] = low(back_value)

    def hand_on(j):
        for s in range(blocks):
            @pl.when(s <= place)
            def _(s=s):
                @pl.when(place < last)
                def _():
                    pltpu.make_async_copy(
                        part_in.at[j, s], part_in.at[j, s], part_recv.at[j, s]
                    ).wait()
                    for kind in range(2):
                        total = wide(parts[j, s, kind]) + wide(part_in[j, s, kind])
                        parts[j, s, kind] = low(total)

                if s > 0:
                    part_copy(j, s).start()
                else:
                    leading = wide(parts[j, 0, 0, :HALF])
                    trailing = wide(parts[j, 0, 0, HALF:])
                    cosine, sine = cosine_ref[...], sine_ref[...]
                    at = j * HEAD_WIDTH
                    back_keyval_ref[pl.ds(pl.multiple_of(at, HALF), HALF)] = low(
                        leading * cosine + trailing * sine
                    )
                    back_keyval_ref[pl.ds(pl.multiple_of(at + HALF, HALF), HALF)] = low(
                        trailing * cosine - leading * sine
                    )
                    at = pl.ds(pl.multiple_of(KEY_WIDTH + at, HEAD_WIDTH), HEAD_WIDTH)
                    back_keyval_ref[at] = low(wide(parts[j, 0, 1]))

    def head_loop(j, carry):
        @pl.when(j < KEYVAL_HEADS)
        def _():
            step(j, 0, True)

        tick(j * blocks)

        def block_loop(s, inner):
            @pl.when((j < KEYVAL_HEADS) & (s <= place))
            def _():
                step(j, s, False)

            tick(j * blocks + s)
            return inner

        lax.fori_loop(1, blocks, block_loop, 0)

        @pl.when(j < KEYVAL_HEADS)
        def _():
            cosine, sine = cosine_ref[...], sine_ref[...]
            for g in range(GROUP):
                leading = back_total[g, :HALF] * SCALE
                trailing = back_total[g, HALF:] * SCALE
                at = (GROUP * j + g) * HEAD_WIDTH
                back_query_ref[pl.ds(pl.multiple_of(at, HALF), HALF)] = low(
                    leading * cosine + trailing * sine
                )
                back_query_ref[pl.ds(pl.multiple_of(at + HALF, HALF), HALF)] = low(
                    trailing * cosine - leading * sine
                )

        ready = j - (last - place)

        @pl.when((ready >= 0) & (ready < KEYVAL_HEADS))
        def _():
            hand_on(ready)

        return carry

    assert (KEYVAL_HEADS + last) * blocks >= 4 + 4 * last + 2 * (chunks - 1)
    lax.fori_loop(0, KEYVAL_HEADS + last, head_loop, 0)

    def keyval_gradient(n):
        weight_gradient(n, back_keyval_ref)
        to_mate(n)

    later = (
        ((keyval_gradient, 2), (to_back, 1)), ((to_y, 2),), ((lambda n: input_gradient(), 3),),
        ((to_x, 2),), ((to_y, 3),), ((to_z, 2), (to_x, 3)), ((to_all, 2), (to_z, 3)),
        ((to_back, 2), (to_all, 3)), ((to_back, 3),),
    )
    for slot, stages in enumerate(later):
        for stage, n in stages:
            stage(n)
        for index in range(blocks):
            if early <= early + slot - last + index < chunks:
                @pl.when(place == index)
                def _(k=early + slot - last + index):
                    give_back(k)

    assert len(later) >= chunks - early + last
    for n in range(chunks_in):
        finish_sum(n)
    token_copy.wait()

    for m in range(len(gradients)):
        for r in range(per):
            for half in range(2):
                mate_copy(m, r, half).wait_send()

    def finish(k, carry):
        y_copy(k).wait_send()

        @pl.when(place < last)
        def _():
            up_copy(k).wait_send()

        @pl.when(place > 0)
        def _():
            down_copy(k).wait_send()

        return carry

    lax.fori_loop(0, chunks, finish, 0)

    def finish_parts(j, carry):
        for s in range(1, blocks):
            @pl.when(s <= place)
            def _(s=s):
                part_copy(j, s).wait_send()
        return carry

    lax.fori_loop(0, KEYVAL_HEADS, finish_parts, 0)
    feed_copy.wait_send()
    trade_copy.wait()


def backward_sum(
    query, keyval, back_mixed, mixed, lse, cosine, sine, base, feed, tokens, normed, middle,
    gains, gain_two, full_query, full_keyval, gradients, gradient_out,
):
    blocks, positions = keyval.shape[0], keyval.shape[-1]
    count, rows, columns = gradients[0].shape
    chunks = len(gradients) * rows // CHUNK_ROWS
    area = QUERY_HEADS * positions * positions * blocks
    vmem = pl.BlockSpec(memory_space=pltpu.VMEM)
    anywhere = pl.BlockSpec(memory_space=pl.ANY)
    dma = pltpu.SemaphoreType.DMA
    share = (len(gradients), rows, columns)
    head = (2, HEAD_WIDTH, positions)
    features = feed.shape[0]
    widths = (QUERY_WIDTH, QUERY_WIDTH, 2 * KEY_WIDTH, gains.shape[-1])
    padded = rows + 16
    half_rows = padded // 2
    low_type = jnp.bfloat16
    scratch = []
    for first in ((count, padded), (2, padded), (padded,), (half_rows,),
                  (blocks - 1, half_rows // blocks)):
        scratch += [pltpu.VMEM(first + (w,), low_type) for w in widths]
    each = len(widths)
    pairs = jax.ShapeDtypeStruct((2, features, positions // 2), low_type)
    return pl.pallas_call(
        backward_sum_kernel,
        in_specs=[vmem] * 16 + [anywhere] * 4,
        out_specs=[vmem] * (3 + each),
        out_shape=[jax.ShapeDtypeStruct(share, low_type), pairs, pairs] + [
            jax.ShapeDtypeStruct((padded, w), low_type) for w in widths
        ],
        scratch_shapes=scratch + [
            pltpu.VMEM((len(gradients), 2, rows, columns), low_type),
            pltpu.VMEM((len(gradients), 2, rows, columns), low_type),
            pltpu.VMEM(share, low_type),
            pltpu.VMEM(share, low_type),
            pltpu.VMEM((KEYVAL_HEADS, blocks) + head, low_type),
            pltpu.VMEM((KEYVAL_HEADS, blocks - 1) + head, low_type),
            pltpu.VMEM((GROUP, HEAD_WIDTH, positions), jnp.float32),
            pltpu.VMEM((GROUP, 1, positions), jnp.float32),
            dma((len(gradients), 2)),
            dma((chunks, 2)), dma((chunks, 2)),
            dma((chunks,)), dma((chunks,)),
            dma((chunks,)), dma((chunks,)),
            dma((chunks,)), dma((chunks,)),
            dma((KEYVAL_HEADS, blocks - 1)), dma((KEYVAL_HEADS, blocks - 1)),
            pltpu.VMEM(feed.shape, low_type),
            pltpu.VMEM((features, positions // 2), low_type),
            dma, dma, dma, dma,
            pltpu.VMEM((QUERY_WIDTH, positions), low_type),
            pltpu.VMEM((2 * KEY_WIDTH, positions), low_type),
            pltpu.VMEM((features, positions), jnp.float32),
            pltpu.VMEM((features, positions // 2), low_type),
            dma((count,)),
            dma((each, 2)), dma((each, 2)),
            dma((each,)), dma((each,)),
            dma((each,)), dma((each,)),
            dma((each, blocks - 1)), dma((each, blocks - 1)),
            dma((each, blocks - 1)), dma((each, blocks - 1)),
            dma((each,)), dma((each,)),
            dma, dma,
        ],
        compiler_params=pltpu.CompilerParams(
            vmem_limit_bytes=KERNEL_VMEM, collective_id=0, has_side_effects=True
        ),
        cost_estimate=pl.CostEstimate(
            flops=40 * HEAD_WIDTH * area, bytes_accessed=10 * query.size, transcendentals=area
        ),
        name="backward_sum",
    )(
        query, keyval, back_mixed, mixed, lse, cosine, sine, base, feed, tokens, normed, middle,
        gains, gain_two, full_query, full_keyval, *gradients, gradient_out,
    )


def front_kernel(
    tokens_ref, cotangent_ref, cosine_ref, sine_ref, *refs
):
    weights, refs = refs[:7], refs[7:]
    (
        tokens_own, cotangent_own, cotangent_other, normed_out, query_out, keyval_ref,
        mixed_out, lse_ref, tokens_other, mixed_other,
    ), refs = refs[:10], refs[10:]
    full, refs = refs[:7], refs[7:]
    (
        raw, tops, totals, sums,
        local_sem, token_send, token_recv, cot_send, cot_recv,
        y_send, y_recv, mate_send, mate_recv, pass_send, pass_recv, key_send, key_recv,
        mixed_send, mixed_recv,
    ) = refs
    place = lax.axis_index("ctx")
    last = lax.axis_size("ctx") - 1
    rank = lax.axis_index("fsdp")
    side = lax.axis_index("tp")
    core = rank % 2
    mate = rank + 1 - 2 * core
    across = rank + 2 - 4 * (rank // 2)
    width = tokens_ref.shape[-1]

    def columns(ref, slot):
        return ref.at[:, pl.ds(pl.multiple_of(slot * width, width), width)]

    local = [
        pltpu.make_async_copy(tokens_ref.at[side], columns(tokens_own, side), local_sem.at[0]),
        pltpu.make_async_copy(
            cotangent_ref.at[side], columns(cotangent_own, side), local_sem.at[1]
        ),
        pltpu.make_async_copy(
            cotangent_ref.at[1 - side], columns(cotangent_other, side), local_sem.at[2]
        ),
        pltpu.make_async_copy(
            tokens_ref.at[1 - side], columns(tokens_other, side), local_sem.at[3]
        ),
    ]
    for w in range(len(weights)):
        local.append(pltpu.make_async_copy(weights[w], full[w].at[rank], local_sem.at[4 + w]))
    for copy in local:
        copy.start()

    greet(fsdp=mate)
    greet(fsdp=across)
    greet(tp=1 - side)

    @pl.when(place > 0)
    def _():
        greet(ctx=place - 1)

    @pl.when(place < last)
    def _():
        greet(ctx=place + 1)

    neighbours = (place + last - 1) // last + (2 * last - place - 1) // last
    pl.semaphore_wait(pltpu.get_barrier_semaphore(), 3 + neighbours)

    token_copy = remote(
        tokens_ref.at[1 - side], columns(tokens_own, side), token_send, token_recv, tp=1 - side
    )
    cot_copies = [
        remote(
            cotangent_ref.at[1 - side], columns(cotangent_own, side), cot_send.at[0],
            cot_recv.at[0], tp=1 - side,
        ),
        remote(
            cotangent_ref.at[side], columns(cotangent_other, side), cot_send.at[1],
            cot_recv.at[1], tp=1 - side,
        ),
        remote(
            tokens_ref.at[side], columns(tokens_other, side), cot_send.at[2], cot_recv.at[2],
            tp=1 - side,
        ),
    ]

    def mixed_copy(j):
        heads = pl.ds(GROUP * j, GROUP)
        return remote(
            mixed_out.at[heads], mixed_other.at[heads], mixed_send.at[j], mixed_recv.at[j],
            tp=1 - side,
        )


    def y_copy(w):
        return remote(
            weights[w], full[w].at[rank], y_send.at[w], y_recv.at[w], fsdp=across
        )

    def mate_copy(w):
        return remote(
            weights[w], full[w].at[rank], mate_send.at[w], mate_recv.at[w], fsdp=mate
        )

    def pass_copy(w):
        return remote(
            full[w].at[across], full[w].at[across], pass_send.at[w], pass_recv.at[w], fsdp=mate
        )

    def arrived(w):
        local[4 + w].wait()
        mate_copy(w).wait_recv()
        pass_copy(w).wait_recv()

    for w in (6, 1):
        y_copy(w).start()
        mate_copy(w).start()
    token_copy.start()
    y_copy(0).start()
    mate_copy(0).start()
    y_copy(6).wait_recv()
    pass_copy(6).start()
    arrived(6)
    gain = wide(full[6][...].reshape(-1, full[6].shape[-1])[:, :1])

    def norm_rows(slot):
        at = pl.ds(pl.multiple_of(slot * width, width), width)
        rows = wide(tokens_own[:, at])
        inverse = lax.rsqrt(jnp.mean(rows * rows, 0, keepdims=True) + EPS)
        normed_out[:, at] = low(rows * inverse * gain)

    local[0].wait()
    norm_rows(side)
    token_copy.wait_recv()
    norm_rows(1 - side)
    for copy in cot_copies:
        copy.start()
    for w in (1, 0):
        y_copy(w).wait_recv()
        pass_copy(w).start()
    for w in range(2, 6):
        y_copy(w).start()
        mate_copy(w).start()
    normed = normed_out[...]
    cosine, sine = cosine_ref[...], sine_ref[...]

    def turned(value, target):
        target[:HALF] = low(value[:HALF] * cosine - value[HALF:] * sine)
        target[HALF:] = low(value[HALF:] * cosine + value[:HALF] * sine)

    def key_copy(s, j):
        return remote(
            keyval_ref.at[s, j], keyval_ref.at[s + 1, j], key_send.at[s, j], key_recv.at[s, j],
            ctx=place + 1,
        )

    arrived(1)
    matrix = full[1][...].reshape(-1, 2 * KEY_WIDTH)
    raw[: 2 * KEY_WIDTH] = dot(matrix, normed, 0, 0)
    for j in range(KEYVAL_HEADS):
        turned(raw[j * HEAD_WIDTH : (j + 1) * HEAD_WIDTH], keyval_ref.at[0, j, 0])
        first = KEY_WIDTH + j * HEAD_WIDTH
        keyval_ref[0, j, 1] = low(raw[first : first + HEAD_WIDTH])

        if j == 0:
            @pl.when(place < last)
            def _():
                key_copy(0, 0).start()

    arrived(0)
    matrix = full[0][...].reshape(-1, QUERY_WIDTH)
    raw[...] = dot(matrix, normed, 0, 0)

    def turn_query(h, carry):
        value = raw[pl.ds(pl.multiple_of(h * HEAD_WIDTH, HEAD_WIDTH), HEAD_WIDTH)]
        first = low(value[:HALF] * cosine - value[HALF:] * sine)
        second = low(value[HALF:] * cosine + value[:HALF] * sine)
        query_out[h, :HALF] = first * jnp.bfloat16(SCALE)
        query_out[h, HALF:] = second * jnp.bfloat16(SCALE)
        return carry

    lax.fori_loop(0, QUERY_HEADS, turn_query, 0)

    def attend(s, j, masked):
        keys_turned = keyval_ref[s, j, 0].T
        values = keyval_ref[s, j, 1]
        for g in range(GROUP):
            head = GROUP * j + g
            scores = dot(keys_turned, query_out[head], 1, 0)
            if masked:
                scores = causal(scores)
                top = jnp.max(scores, 0, keepdims=True)
                lifted = jnp.exp(scores - top)
                tops[head] = top
                totals[head] = jnp.sum(lifted, 0, keepdims=True)
                sums[head] = dot(values, low(lifted), 1, 0)
            else:
                old = tops[head]
                top = jnp.maximum(old, jnp.max(scores, 0, keepdims=True))
                lifted = jnp.exp(scores - top)
                shrink = jnp.exp(old - top)
                tops[head] = top
                totals[head] = totals[head] * shrink + jnp.sum(lifted, 0, keepdims=True)
                sums[head] = sums[head] * shrink + dot(values, low(lifted), 1, 0)

    def hand_on(s, j):
        @pl.when(s < place)
        def _():
            pltpu.make_async_copy(
                keyval_ref.at[s + 1, j], keyval_ref.at[s + 1, j], key_recv.at[s, j]
            ).wait()

            @pl.when(place < last)
            def _():
                key_copy(s + 1, j).start()

    def finish_heads(j):
        for g in range(GROUP):
            head = GROUP * j + g
            total = totals[head]
            mixed_out[head] = low(sums[head] / total)
            lse_ref[head] = tops[head] + jnp.log(total)
        mixed_copy(j).start()

    def one_head(j, carry):
        @pl.when((place < last) & (j + 1 < KEYVAL_HEADS))
        def _():
            key_copy(0, j + 1).start()

        attend(0, j, True)
        hand_on(0, j)

        def later_block(s, inner):
            attend(s, j, False)
            hand_on(s, j)
            return inner

        lax.fori_loop(1, place + 1, later_block, 0)
        finish_heads(j)
        return carry

    lax.fori_loop(0, KEYVAL_HEADS, one_head, 0)
    passed = 2

    for w in range(passed, 6):
        y_copy(w).wait_recv()
        pass_copy(w).start()
    for copy in local[1:4]:
        copy.wait()
    for j in range(KEYVAL_HEADS):
        mixed_copy(j).wait()
    token_copy.wait_send()
    for copy in cot_copies:
        copy.wait()
    for w in range(passed, 6):
        arrived(w)
    for w in range(len(weights)):
        y_copy(w).wait_send()
        mate_copy(w).wait_send()
        pass_copy(w).wait_send()

    @pl.when(place < last)
    def _():
        def sent(i, carry):
            key_copy(i // KEYVAL_HEADS, lax.rem(i, KEYVAL_HEADS)).wait_send()
            return carry

        lax.fori_loop(0, (place + 1) * KEYVAL_HEADS, sent, 0)


def front(tokens, cotangent, cosine, sine, weights):
    blocks = lax.axis_size("ctx")
    parts = lax.axis_size("fsdp")
    positions = cosine.shape[-1]
    vmem = pl.BlockSpec(memory_space=pltpu.VMEM)
    anywhere = pl.BlockSpec(memory_space=pl.ANY)
    dma = pltpu.SemaphoreType.DMA
    shape = lambda *dims: jax.ShapeDtypeStruct(dims, jnp.bfloat16)
    count = len(weights)
    features = tokens.shape[1]
    area = QUERY_HEADS * positions * positions * blocks
    return pl.pallas_call(
        front_kernel,
        in_specs=[vmem] * (4 + count),
        out_specs=[vmem] * 12 + [anywhere] * 4 + [vmem],
        out_shape=[
            shape(features, positions), shape(features, positions), shape(features, positions),
            shape(features, positions),
            shape(QUERY_HEADS, HEAD_WIDTH, positions),
            shape(blocks, KEYVAL_HEADS, 2, HEAD_WIDTH, positions),
            shape(QUERY_HEADS, HEAD_WIDTH, positions),
            jax.ShapeDtypeStruct((QUERY_HEADS, 1, positions), jnp.float32),
            shape(features, positions),
            shape(QUERY_HEADS, HEAD_WIDTH, positions),
        ] + [shape(parts, *w.shape) for w in weights],
        scratch_shapes=[
            pltpu.VMEM((QUERY_WIDTH, positions), jnp.float32),
            pltpu.VMEM((QUERY_HEADS, 1, positions), jnp.float32),
            pltpu.VMEM((QUERY_HEADS, 1, positions), jnp.float32),
            pltpu.VMEM((QUERY_HEADS, HEAD_WIDTH, positions), jnp.float32),
            dma((4 + count,)),
            dma, dma,
            dma((3,)), dma((3,)),
            dma((count,)), dma((count,)),
            dma((count,)), dma((count,)),
            dma((count,)), dma((count,)),
            dma((blocks, KEYVAL_HEADS)), dma((blocks, KEYVAL_HEADS)),
            dma((KEYVAL_HEADS,)), dma((KEYVAL_HEADS,)),
        ],
        compiler_params=pltpu.CompilerParams(
            vmem_limit_bytes=KERNEL_VMEM, collective_id=1, has_side_effects=True
        ),
        cost_estimate=pl.CostEstimate(
            flops=16 * HEAD_WIDTH * area, bytes_accessed=10 * tokens.size, transcendentals=area
        ),
        name="front",
    )(tokens, cotangent, cosine, sine, *weights)


def on_device(
    tokens, cotangent, input_gain, w_query, w_keyval, w_output, middle_gain, w_gate, w_up, w_down
):
    half = lax.axis_index("tp")
    low_half = half == 0
    pair = [(0, 1), (1, 0)]

    def to_partner(value_rows):
        return lax.ppermute(value_rows, "tp", pair)

    def in_order(mine, received):
        return jnp.concatenate(
            [jnp.where(low_half, mine, received), jnp.where(low_half, received, mine)], 0
        )

    def take(value_rows, index):
        return lax.dynamic_index_in_dim(value_rows, index, 0, keepdims=False)

    tokens_own = in_order(take(tokens, half), to_partner(take(tokens, 1 - half)))
    full_gain_one, full_gain_two = (
        lax.all_gather(input_gain, "fsdp", axis=0, tiled=True),
        lax.all_gather(middle_gain, "fsdp", axis=0, tiled=True),
    )
    full_in = lax.all_gather(jnp.concatenate([w_query, w_keyval], 1), "fsdp", axis=0, tiled=True)
    full_output = lax.all_gather(w_output, "fsdp", axis=0, tiled=True)
    full_gate = lax.all_gather(w_gate, "fsdp", axis=0, tiled=True)
    full_up = lax.all_gather(w_up, "fsdp", axis=0, tiled=True)
    full_down = lax.all_gather(w_down, "fsdp", axis=0, tiled=True)
    cotangent_received = to_partner(cotangent)
    cotangent_own = in_order(take(cotangent, half), take(cotangent_received, half))
    cotangent_other = in_order(take(cotangent, 1 - half), take(cotangent_received, 1 - half))

    token_positions = tokens_own.shape[0]
    cosine, sine = rope_tables(token_positions, lax.axis_index("ctx") * token_positions)
    gain_one = full_gain_one.astype(jnp.float32)
    inputs = tokens_own.astype(jnp.float32)
    unit_one, inverse_one = normalize(inputs)
    normed_one = (unit_one * gain_one).astype(jnp.bfloat16)
    keyval_raw = dot(full_in[:, QUERY_WIDTH:], normed_one, 0, 1)
    keyval_low = jnp.concatenate(
        [apply_rotary(keyval_raw[:KEY_WIDTH], cosine, sine), keyval_raw[KEY_WIDTH:]], 0
    ).astype(jnp.bfloat16)
    blocks = lax.axis_size("ctx")
    keyval = jnp.stack([keyval_low] + [move_along(keyval_low, s) for s in range(1, blocks)], 0)
    keyval = keyval.reshape(blocks, 2, KEYVAL_HEADS, HEAD_WIDTH, token_positions)
    query_raw = dot(full_in[:, :QUERY_WIDTH], normed_one, 0, 1)
    query_low = (
        apply_rotary(query_raw, cosine, sine)
        .astype(jnp.bfloat16)
        .reshape(QUERY_HEADS, HEAD_WIDTH, token_positions)
    )
    mixed_heads, lse = attend_forward(query_low, keyval)
    mixed_low = mixed_heads.reshape(QUERY_WIDTH, token_positions)
    middle = inputs + dot(mixed_low, full_output, 0, 0)

    gain_two = full_gain_two.astype(jnp.float32)
    unit_two, inverse_two = normalize(middle)
    normed_two = (unit_two * gain_two).astype(jnp.bfloat16)
    normed_other = to_partner(normed_two)

    def feed(rows, back_rows):
        gate_proj = dot(rows, full_gate, 1, 0)
        up_proj = dot(rows, full_up, 1, 0)
        sigmoid_gate = jax.nn.sigmoid(gate_proj)
        swish_gate = gate_proj * sigmoid_gate
        hidden = (swish_gate * up_proj).astype(jnp.bfloat16)
        back_hidden = dot(back_rows, full_down, 1, 0)
        back_gate = (
            back_hidden * up_proj * sigmoid_gate * (1.0 + gate_proj * (1.0 - sigmoid_gate))
        ).astype(jnp.bfloat16)
        back_up = (back_hidden * swish_gate).astype(jnp.bfloat16)
        return (hidden, back_gate, back_up)

    def feed_input_back(back_gate, back_up):
        return dot(back_gate, full_gate, 1, 1) + dot(back_up, full_up, 1, 1)

    hidden_own, back_gate_own, back_up_own = feed(normed_two, cotangent_own)
    hidden_other, back_gate_other, back_up_other = feed(normed_other, cotangent_other)
    back_two_received = to_partner(
        feed_input_back(back_gate_other, back_up_other).astype(jnp.bfloat16)
    )
    back_two = feed_input_back(back_gate_own, back_up_own) + back_two_received.astype(jnp.float32)
    feed_received = to_partner(dot(hidden_other, full_down, 1, 1).astype(jnp.bfloat16))
    result_own = (
        middle + dot(hidden_own, full_down, 1, 1) + feed_received.astype(jnp.float32)
    ).astype(jnp.bfloat16)

    def feed_gradient(left_own, right_own, left_other, right_other):
        gradient = dot(left_own, right_own, 0, 0) + dot(left_other, right_other, 0, 0)
        shared = scatter_sum(gradient.astype(jnp.bfloat16), "fsdp")
        return whole_sum(shared, (("ctx", 2),))

    share_down = feed_gradient(cotangent_own, hidden_own, cotangent_other, hidden_other)
    share_gate = feed_gradient(normed_two, back_gate_own, normed_other, back_gate_other)
    share_up = feed_gradient(normed_two, back_up_own, normed_other, back_up_other)

    grad_gain_two = jnp.sum(back_two * unit_two, axis=0)
    back_middle = cotangent_own.astype(jnp.float32) + norm_back(
        back_two * gain_two, unit_two, inverse_two
    )
    back_attention = back_middle.astype(jnp.bfloat16)
    back_mixed = dot(full_output, back_attention, 1, 1).astype(jnp.bfloat16)
    back_mixed = back_mixed.reshape(query_low.shape)
    grad_output = dot(mixed_low, back_attention, 1, 0).astype(jnp.bfloat16)
    share_output = whole_sum(scatter_sum(grad_output, "fsdp"), (("tp", 1), ("ctx", 2)))

    back_query = []
    back_key = []
    back_value = []
    for first, count in ((0, 3), (3, 2)):
        part_query, part_keyval = attend_backward(
            query_low, keyval, back_mixed, mixed_heads, lse, cosine, sine, first, count
        )
        part_keyval = part_keyval.reshape(blocks, 2 * count * HEAD_WIDTH, token_positions)
        owned = part_keyval[0].astype(jnp.float32)
        for s in range(1, blocks):
            owned += move_along(part_keyval[s], -s).astype(jnp.float32)
        back_query.append(part_query.reshape(-1, token_positions))
        back_key.append(
            apply_rotary(owned[: count * HEAD_WIDTH], cosine, -sine).astype(jnp.bfloat16)
        )
        back_value.append(owned[count * HEAD_WIDTH :].astype(jnp.bfloat16))
    back_in = jnp.concatenate(back_query + back_key + back_value, 0)
    grad_in = dot(normed_one, back_in, 0, 1)
    back_one = dot(back_in, full_in, 0, 1)
    grad_gain_one = jnp.sum(back_one * unit_one, axis=0)
    back_inputs = back_middle + norm_back(back_one * gain_one, unit_one, inverse_one)

    def to_positions(value_rows):
        split = value_rows.reshape(2, token_positions // 2, value_rows.shape[-1])
        received = to_partner(take(split, 1 - half))
        return in_order(take(split, half)[None], received[None])

    result = to_positions(result_own)
    grad_tokens = to_positions(back_inputs.astype(jnp.bfloat16)).astype(jnp.float32)
    gradients = jnp.concatenate([grad_in, grad_gain_one[:, None], grad_gain_two[:, None]], 1)
    share_in = lax.psum(
        lax.psum_scatter(
            gradients.astype(jnp.bfloat16), "fsdp", scatter_dimension=0, tiled=True
        ),
        ("ctx", "tp"),
    ).astype(jnp.float32)
    width = full_in.shape[1]
    return (
        result,
        grad_tokens,
        share_in[:, width],
        share_in[:, :QUERY_WIDTH],
        share_in[:, QUERY_WIDTH:width],
        share_output,
        share_in[:, width + 1],
        share_gate,
        share_up,
        share_down,
    )


def fast_on_device(
    tokens, cotangent, input_gain, w_query, w_keyval, w_output, middle_gain, w_gate, w_up, w_down
):
    pair = [(0, 1), (1, 0)]

    def to_partner(value_rows):
        return lax.ppermute(value_rows, "tp", pair)

    parts = lax.axis_size("fsdp")
    width_in = tokens.shape[-1]
    rows = width_in // parts
    token_positions = 2 * tokens.shape[1]
    cosine, sine = rope_tables(token_positions, lax.axis_index("ctx") * token_positions)
    gains = jnp.pad(jnp.stack([input_gain, middle_gain], 1), ((0, 0), (0, 126)))
    (
        tokens_own, cotangent_own, cotangent_other, normed_one, query_low, keyval,
        mixed_heads, lse, tokens_other, mixed_other, *full,
    ) = front(
        tokens.swapaxes(1, 2), cotangent.swapaxes(1, 2), cosine, sine,
        (w_query, w_keyval, w_output, w_gate, w_up, w_down, gains),
    )
    full_query, full_keyval, full_output, full_gate, full_up, full_down, gains = [
        w.reshape(width_in, -1) for w in full
    ]
    tokens_own, cotangent_own, cotangent_other, normed_one, tokens_other = [
        v.T for v in (tokens_own, cotangent_own, cotangent_other, normed_one, tokens_other)
    ]
    full_gain_two = gains[:, 1]
    inputs = tokens_own.astype(jnp.float32)
    mixed_low = mixed_heads.reshape(QUERY_WIDTH, token_positions)
    middle = inputs + dot(mixed_low, full_output, 0, 0)

    gain_two = full_gain_two.astype(jnp.float32)
    unit_two, inverse_two = normalize(middle)
    normed_two = (unit_two * gain_two).astype(jnp.bfloat16)
    mixed_other = mixed_other.reshape(QUERY_WIDTH, token_positions)
    middle_other = tokens_other.astype(jnp.float32) + dot(mixed_other, full_output, 0, 0)
    normed_other = (normalize(middle_other)[0] * gain_two).astype(jnp.bfloat16)

    def feed(rows, back_rows):
        gate_proj = dot(rows, full_gate, 1, 0)
        up_proj = dot(rows, full_up, 1, 0)
        sigmoid_gate = jax.nn.sigmoid(gate_proj)
        swish_gate = gate_proj * sigmoid_gate
        hidden = (swish_gate * up_proj).astype(jnp.bfloat16)
        back_hidden = dot(back_rows, full_down, 1, 0)
        back_gate = (
            back_hidden * up_proj * sigmoid_gate * (1.0 + gate_proj * (1.0 - sigmoid_gate))
        ).astype(jnp.bfloat16)
        back_up = (back_hidden * swish_gate).astype(jnp.bfloat16)
        return (hidden, back_gate, back_up)

    def feed_input_back(back_gate, back_up):
        return dot(back_gate, full_gate, 1, 1) + dot(back_up, full_up, 1, 1)

    hidden_other, back_gate_other, back_up_other = feed(normed_other, cotangent_other)
    back_two_received = to_partner(
        feed_input_back(back_gate_other, back_up_other).astype(jnp.bfloat16)
    )
    hidden_own, back_gate_own, back_up_own = feed(normed_two, cotangent_own)
    back_two = feed_input_back(back_gate_own, back_up_own) + back_two_received.astype(jnp.float32)
    feed_other = dot(hidden_other, full_down, 1, 1).astype(jnp.bfloat16)
    base = middle + dot(hidden_own, full_down, 1, 1)

    def feed_gradient(left_own, right_own, left_other, right_other):
        gradient = dot(left_own, right_own, 0, 0) + dot(left_other, right_other, 0, 0)
        return gradient.astype(jnp.bfloat16).reshape(lax.axis_size("fsdp"), -1, gradient.shape[1])

    gradients = (
        feed_gradient(cotangent_own, hidden_own, cotangent_other, hidden_other),
        feed_gradient(normed_two, back_gate_own, normed_other, back_gate_other),
        feed_gradient(normed_two, back_up_own, normed_other, back_up_other),
    )

    grad_gain_two = jnp.sum(back_two * unit_two, axis=0)
    back_middle = cotangent_own.astype(jnp.float32) + norm_back(
        back_two * gain_two, unit_two, inverse_two
    )
    back_attention = back_middle.astype(jnp.bfloat16)
    back_mixed = dot(full_output, back_attention, 1, 1).astype(jnp.bfloat16)
    back_mixed = back_mixed.reshape(query_low.shape)
    grad_output = dot(mixed_low, back_attention, 1, 0).astype(jnp.bfloat16)
    share, result, grad_tokens, share_output, share_query, share_keyval, share_gains = backward_sum(
        query_low, keyval, back_mixed, mixed_heads, lse, cosine, sine, base.T, feed_other.T,
        tokens_own.T, normed_one.T, back_middle.T, gains, grad_gain_two[:, None],
        full_query, full_keyval, gradients, grad_output.reshape(parts, rows, -1),
    )
    return (
        result.swapaxes(1, 2),
        grad_tokens.swapaxes(1, 2).astype(jnp.float32),
        share_gains[:rows, 0].astype(jnp.float32),
        share_query[:rows].astype(jnp.float32),
        share_keyval[:rows].astype(jnp.float32),
        share_output[:rows].astype(jnp.float32),
        share_gains[:rows, 1].astype(jnp.float32),
        share[1].astype(jnp.float32),
        share[2].astype(jnp.float32),
        share[0].astype(jnp.float32),
    )


def solution(mesh):
    rows = P("fsdp", ("ctx", "tp"), None)
    specs = (
        P("fsdp"), P("fsdp", None), P("fsdp", None), P("fsdp", None),
        P("fsdp"), P("fsdp", "tp"), P("fsdp", "tp"), P("fsdp", "tp"),
    )
    kernels = mesh.shape["fsdp"] == 4 and mesh.shape["tp"] == 2 and mesh.shape["ctx"] == 4
    return jax.shard_map(
        fast_on_device if kernels else on_device,
        mesh=mesh,
        in_specs=(rows, rows) + specs,
        out_specs=(rows, rows) + specs,
        check_vma=False,
    )
```

```python
import jax
import jax.numpy as jnp
from jax import lax
from jax.experimental import pallas as pl
from jax.experimental.pallas import tpu as pltpu
from jax.sharding import PartitionSpec as P

QUERY_HEADS = 15
KEYVAL_HEADS = 5
GROUP = QUERY_HEADS // KEYVAL_HEADS
HEAD_WIDTH = 64
HALF = HEAD_WIDTH // 2
KEY_WIDTH = 320
QUERY_WIDTH = QUERY_HEADS * HEAD_WIDTH
SCALE = HEAD_WIDTH ** (-0.5)

EPS = 1e-05
THETA = 10000.0
VMEM_LIMIT = 40 * 1024 * 1024


def dot(left, right, left_dim, right_dim):
    return lax.dot_general(
        left, right, (((left_dim,), (right_dim,)), ((), ())), preferred_element_type=jnp.float32
    )


def rope_tables(token_positions, first_place):
    position = (first_place + lax.iota(jnp.int32, token_positions)).astype(jnp.float32)
    frequency = THETA ** (-(2.0 * lax.iota(jnp.int32, HALF).astype(jnp.float32)) / HEAD_WIDTH)
    angles = frequency[:, None] * position[None, :]
    return (jnp.cos(angles), jnp.sin(angles))


def apply_rotary(rows, cosine, sine):
    shaped = rows.reshape(-1, 2, HALF, rows.shape[-1])
    leading = shaped[:, 0]
    trailing = shaped[:, 1]
    return jnp.stack(
        [leading * cosine - trailing * sine, trailing * cosine + leading * sine], 1
    ).reshape(rows.shape)


def normalize(value_rows):
    inverse_rms = lax.rsqrt(jnp.mean(value_rows * value_rows, -1, keepdims=True) + EPS)
    return (value_rows * inverse_rms, inverse_rms)


def norm_back(back_unit, unit_rows, inverse_rms):
    return inverse_rms * (
        back_unit - unit_rows * jnp.mean(back_unit * unit_rows, -1, keepdims=True)
    )


def causal(scores):
    key_place = lax.broadcasted_iota(jnp.int32, scores.shape, 0)
    query_place = lax.broadcasted_iota(jnp.int32, scores.shape, 1)
    return jnp.where(key_place <= query_place, scores, -jnp.inf)


def forward_kernel(query_ref, key_ref, value_ref, mixed_ref, lse_ref):
    place = lax.axis_index("ctx")
    queries = [query_ref[g] * jnp.bfloat16(SCALE) for g in range(GROUP)]

    def scores_of(keys_turned, g, masked):
        scores = dot(keys_turned, queries[g], 1, 0)
        return causal(scores) if masked else scores

    def first():
        keys_turned = key_ref[0, 0, 0].T
        values = value_ref[0, 0, 0]
        carried = []
        for g in range(GROUP):
            scores = scores_of(keys_turned, g, True)
            top = jnp.max(scores, 0, keepdims=True)
            lifted = jnp.exp(scores - top)
            total = jnp.sum(lifted, 0, keepdims=True)
            carried += [top, total, dot(values, lifted.astype(jnp.bfloat16), 1, 0)]
        return tuple(carried)

    def step(block, carried):
        keys_turned = key_ref[block, 0, 0].T
        values = value_ref[block, 0, 0]
        later = []
        for g in range(GROUP):
            top, total, mixed = carried[3 * g : 3 * g + 3]
            scores = scores_of(keys_turned, g, False)
            new_top = jnp.maximum(top, jnp.max(scores, 0, keepdims=True))
            lifted = jnp.exp(scores - new_top)
            shrink = jnp.exp(top - new_top)
            later += [
                new_top,
                total * shrink + jnp.sum(lifted, 0, keepdims=True),
                mixed * shrink + dot(values, lifted.astype(jnp.bfloat16), 1, 0),
            ]
        return tuple(later)

    carried = lax.fori_loop(1, place + 1, step, first())
    for g in range(GROUP):
        top, total, mixed = carried[3 * g : 3 * g + 3]
        mixed_ref[g] = (mixed / total).astype(jnp.bfloat16)
        lse_ref[g] = top + jnp.log(total)


def attend_forward(query, keyval):
    blocks, token_positions = keyval.shape[0], keyval.shape[-1]
    head_block = (GROUP, HEAD_WIDTH, token_positions)
    key_block = (blocks, 1, 1, HEAD_WIDTH, token_positions)
    area = QUERY_HEADS * token_positions * token_positions * blocks
    return pl.pallas_call(
        forward_kernel,
        grid=(KEYVAL_HEADS,),
        in_specs=[
            pl.BlockSpec(head_block, lambda j: (j, 0, 0)),
            pl.BlockSpec(key_block, lambda j: (0, 0, j, 0, 0)),
            pl.BlockSpec(key_block, lambda j: (0, 1, j, 0, 0)),
        ],
        out_specs=[
            pl.BlockSpec(head_block, lambda j: (j, 0, 0)),
            pl.BlockSpec((GROUP, 1, token_positions), lambda j: (j, 0, 0)),
        ],
        out_shape=[
            jax.ShapeDtypeStruct(query.shape, jnp.bfloat16),
            jax.ShapeDtypeStruct((QUERY_HEADS, 1, token_positions), jnp.float32),
        ],
        compiler_params=pltpu.CompilerParams(vmem_limit_bytes=VMEM_LIMIT),
        cost_estimate=pl.CostEstimate(
            flops=16 * HEAD_WIDTH * area, bytes_accessed=6 * query.size, transcendentals=area
        ),
        name="attend_forward",
    )(query, keyval, keyval)


def backward_kernel(
    query_ref, key_ref, value_ref, back_ref, mixed_ref, lse_ref, cosine_ref, sine_ref,
    back_query_ref, back_keyval_ref,
):
    place = lax.axis_index("ctx")
    blocks = key_ref.shape[0]
    queries = [query_ref[g] * jnp.bfloat16(SCALE) for g in range(GROUP)]
    backs = [back_ref[g] for g in range(GROUP)]
    tops = [lse_ref[g] for g in range(GROUP)]
    sums = [
        jnp.sum(backs[g].astype(jnp.float32) * mixed_ref[g].astype(jnp.float32), 0, keepdims=True)
        for g in range(GROUP)
    ]

    def step(block, carried, masked=False):
        keys = key_ref[block, 0, 0]
        keys_turned = keys.T
        values_turned = value_ref[block, 0, 0].T
        back_key = jnp.zeros(keys.shape, jnp.float32)
        back_value = jnp.zeros(keys.shape, jnp.float32)
        later = []
        for g in range(GROUP):
            scores = dot(keys_turned, queries[g], 1, 0)
            if masked:
                scores = causal(scores)
            weights = jnp.exp(scores - tops[g])
            back_weights = dot(values_turned, backs[g], 1, 0)
            back_scores = (weights * (back_weights - sums[g])).astype(jnp.bfloat16)
            later.append(carried[g] + dot(keys, back_scores, 1, 0))
            back_key += dot(queries[g], back_scores, 1, 1)
            back_value += dot(backs[g], weights.astype(jnp.bfloat16), 1, 1)
        back_keyval_ref[block, 0, 0] = back_key.astype(jnp.bfloat16)
        back_keyval_ref[block, 1, 0] = back_value.astype(jnp.bfloat16)
        return tuple(later)

    start = tuple(jnp.zeros(query_ref.shape[1:], jnp.float32) for g in range(GROUP))
    carried = lax.fori_loop(1, place + 1, step, step(0, start, True))

    def clear(block, unused):
        zero = jnp.zeros(key_ref.shape[3:], jnp.bfloat16)
        back_keyval_ref[block, 0, 0] = zero
        back_keyval_ref[block, 1, 0] = zero
        return unused

    lax.fori_loop(place + 1, blocks, clear, 0)
    cosine = cosine_ref[...]
    sine = sine_ref[...]
    for g in range(GROUP):
        leading = carried[g][:HALF] * SCALE
        trailing = carried[g][HALF:] * SCALE
        back_query_ref[g, :HALF] = (leading * cosine + trailing * sine).astype(jnp.bfloat16)
        back_query_ref[g, HALF:] = (trailing * cosine - leading * sine).astype(jnp.bfloat16)


def attend_backward(query, keyval, back_mixed, mixed, lse, cosine, sine, first, count):
    blocks, token_positions = keyval.shape[0], keyval.shape[-1]
    head_block = (GROUP, HEAD_WIDTH, token_positions)
    key_block = (blocks, 1, 1, HEAD_WIDTH, token_positions)
    area = count * GROUP * token_positions * token_positions * blocks
    heads = pl.BlockSpec(head_block, lambda j: (j + first, 0, 0))
    table = pl.BlockSpec((HALF, token_positions), lambda j: (0, 0))
    return pl.pallas_call(
        backward_kernel,
        grid=(count,),
        in_specs=[
            heads,
            pl.BlockSpec(key_block, lambda j: (0, 0, j + first, 0, 0)),
            pl.BlockSpec(key_block, lambda j: (0, 1, j + first, 0, 0)),
            heads,
            heads,
            pl.BlockSpec((GROUP, 1, token_positions), lambda j: (j + first, 0, 0)),
            table,
            table,
        ],
        out_specs=[
            pl.BlockSpec(head_block, lambda j: (j, 0, 0)),
            pl.BlockSpec((blocks, 2, 1, HEAD_WIDTH, token_positions), lambda j: (0, 0, j, 0, 0)),
        ],
        out_shape=[
            jax.ShapeDtypeStruct((count * GROUP, HEAD_WIDTH, token_positions), jnp.bfloat16),
            jax.ShapeDtypeStruct(
                (blocks, 2, count, HEAD_WIDTH, token_positions), jnp.bfloat16
            ),
        ],
        compiler_params=pltpu.CompilerParams(vmem_limit_bytes=VMEM_LIMIT),
        cost_estimate=pl.CostEstimate(
            flops=40 * HEAD_WIDTH * area, bytes_accessed=10 * query.size, transcendentals=area
        ),
        name="attend_backward",
    )(query, keyval, keyval, back_mixed, mixed, lse, cosine, sine)


def move_along(value, distance):
    blocks = lax.axis_size("ctx")
    pairs = [(i, i + distance) for i in range(blocks) if 0 <= i + distance < blocks]
    return lax.ppermute(value, "ctx", pairs)


def trade(value, axis, step):
    pairs = [(i, i ^ step) for i in range(lax.axis_size(axis))]
    return lax.ppermute(value, axis, pairs)


def add_low(left, right):
    return (left.astype(jnp.float32) + right.astype(jnp.float32)).astype(jnp.bfloat16)


def scatter_sum(value, axis):
    size = lax.axis_size(axis)
    index = lax.axis_index(axis)
    rows = value.shape[0] // size
    step = 1
    while step < size:
        count = value.shape[0] // (2 * rows)
        split = value.reshape(count, 2, rows, value.shape[-1])
        second = (index // step) % 2 == 1
        kept = jnp.where(second, split[:, 1], split[:, 0])
        sent = jnp.where(second, split[:, 0], split[:, 1])
        value = add_low(kept, trade(sent, axis, step)).reshape(count * rows, value.shape[-1])
        step *= 2
    return value


def whole_sum(value, others):
    half_rows = value.shape[0] // 2
    second = lax.axis_index("ctx") % 2 == 1
    upper, lower = value[:half_rows], value[half_rows:]
    received = trade(jnp.where(second, upper, lower), "ctx", 1)
    total = add_low(jnp.where(second, lower, upper), received)
    for axis, first_step in others:
        step = first_step
        while step < lax.axis_size(axis):
            total = add_low(total, trade(total, axis, step))
            step *= 2
    received = trade(total, "ctx", 1)
    return jnp.concatenate(
        [jnp.where(second, received, total), jnp.where(second, total, received)], 0
    ).astype(jnp.float32)


MESH = pl.DeviceIdType.MESH
KERNEL_VMEM = 60 * 1024 * 1024
CHUNK_ROWS = 80


def remote(source, target, send_sem, recv_sem, **place):
    return pltpu.make_async_remote_copy(
        src_ref=source, dst_ref=target, send_sem=send_sem, recv_sem=recv_sem,
        device_id=place, device_id_type=MESH,
    )


def wide(value):
    return value.astype(jnp.float32)


def low(value):
    return value.astype(jnp.bfloat16)


def greet(**place):
    pl.semaphore_signal(
        pltpu.get_barrier_semaphore(), inc=1, device_id=place, device_id_type=MESH
    )


def backward_sum_kernel(
    query_ref, keyval_ref, back_ref, mixed_ref, lse_ref, cosine_ref, sine_ref,
    base_ref, feed_ref, tokens_ref, normed_ref, middle_ref, gains_ref, gain_two_ref,
    full_query, full_keyval, down_ref, gate_ref, up_ref, out_ref,
    share_ref, result_ref, back_tokens_ref, *refs,
):
    chunks_in = 4
    shares, refs = refs[:chunks_in], refs[chunks_in:]
    whole, mate_part, y_part, x_part, z_part = [
        refs[i * chunks_in : (i + 1) * chunks_in] for i in range(5)
    ]
    (
    own, mate_in, y_in, up_in, parts, part_in, back_total, row_sums,
    own_sem, mate_send, mate_recv, y_send, y_recv, up_send, up_recv, down_send, down_recv,
    part_send, part_recv, feed_in, traded, feed_send, feed_recv, trade_send, trade_recv,
    back_query_ref, back_keyval_ref, back_one, token_traded,
    whole_sem, sum_mate_send, sum_mate_recv, sum_y_send, sum_y_recv, sum_x_send, sum_x_recv,
    sum_z_send, sum_z_recv, all_send, all_recv, back_send, back_recv, token_send, token_recv,
    ) = refs[5 * chunks_in :]
    place = lax.axis_index("ctx")
    last = lax.axis_size("ctx") - 1
    blocks = last + 1
    rank = lax.axis_index("fsdp")
    core = rank % 2
    y = rank // 2
    side = lax.axis_index("tp")
    mate = rank + 1 - 2 * core
    across = rank + 2 - 4 * y
    gradients = (down_ref, gate_ref, up_ref)
    rows = share_ref.shape[1]
    per = rows // CHUNK_ROWS
    chunks = len(gradients) * per
    iterations = KEYVAL_HEADS + 2
    early = iterations * blocks // 2 - KEYVAL_HEADS * blocks // 2

    for m, gradient in enumerate(gradients):
        for half in range(2):
            pltpu.make_async_copy(
                gradient.at[2 * half + core], own.at[m, half], own_sem.at[m, half]
            ).start()
    greet(fsdp=mate)
    greet(fsdp=across)
    greet(tp=1 - side)
    for d in range(1, blocks):
        greet(ctx=lax.rem(place + d, blocks))
    filled = out_ref.shape[1]
    tail = whole[0].shape[1] - filled
    for n in range(chunks_in):
        width = whole[n].shape[-1]
        whole[n][:, filled:] = jnp.zeros((whole[n].shape[0], tail, width), jnp.bfloat16)
        mate_part[n][:, filled:] = jnp.zeros((2, tail, width), jnp.bfloat16)
    for f in range(whole[0].shape[0]):
        pltpu.make_async_copy(
            out_ref.at[f], whole[0].at[f, pl.ds(0, filled)], whole_sem.at[f]
        ).start()
    pl.semaphore_wait(pltpu.get_barrier_semaphore(), 3 + last)

    feed_copy = remote(feed_ref, feed_in, feed_send, feed_recv, tp=1 - side)
    trade_copy = remote(traded, result_ref.at[side], trade_send, trade_recv, tp=1 - side)
    feed_copy.start()
    pair_width = traded.shape[-1]
    step_rows = traded.shape[0] // 4

    def finish_result():
        feed_copy.wait_recv()

        def some_rows(i, carry):
            at = pl.ds(pl.multiple_of(i * step_rows, step_rows), step_rows)
            for target, slot in ((result_ref.at[side], side), (traded, 1 - side)):
                columns = pl.ds(pl.multiple_of(slot * pair_width, pair_width), pair_width)
                target[at] = low(base_ref[at, columns] + wide(feed_in[at, columns]))
            return carry

        lax.fori_loop(0, 4, some_rows, 0)
        trade_copy.start()

    half_rows = whole[0].shape[1] // 2
    piece = half_rows // blocks
    kept = 2 * y + core

    def sum_mate(n, half):
        return remote(
            whole[n].at[2 * half + 1 - core, pl.ds(0, filled)],
            mate_part[n].at[half, pl.ds(0, filled)],
            sum_mate_send.at[n, half], sum_mate_recv.at[n, half], fsdp=mate,
        )

    def sum_y(n):
        return remote(
            mate_part[n].at[1 - y], y_part[n], sum_y_send.at[n], sum_y_recv.at[n], fsdp=across
        )

    def sum_x(n):
        other = pl.ds(pl.multiple_of((1 - side) * half_rows, half_rows), half_rows)
        return remote(
            whole[n].at[kept, other], x_part[n], sum_x_send.at[n], sum_x_recv.at[n],
            tp=1 - side,
        )

    def sum_z(n, d):
        target = lax.rem(place + d, blocks)
        at = pl.ds(pl.multiple_of(side * half_rows + target * piece, piece), piece)
        return remote(
            whole[n].at[kept, at], z_part[n].at[d - 1], sum_z_send.at[n, d - 1],
            sum_z_recv.at[n, d - 1], ctx=target,
        )

    def all_copy(n, d, origin):
        spot = shares[n].at[
            pl.ds(pl.multiple_of(side * half_rows + origin * piece, piece), piece)
        ]
        return remote(
            spot, spot, all_send.at[n, d - 1], all_recv.at[n, d - 1],
            ctx=lax.rem(place + d, blocks),
        )

    def back_copy(n, half):
        spot = shares[n].at[pl.ds(pl.multiple_of(half * half_rows, half_rows), half_rows)]
        return remote(spot, spot, back_send.at[n], back_recv.at[n], tp=1 - side)

    def to_mate(n):
        for half in range(2):
            sum_mate(n, half).start()

    def to_y(n):
        for half in range(2):
            sum_mate(n, half).wait_recv()
        quarter = 2 * (1 - y) + core
        mate_part[n][1 - y] = low(wide(whole[n][quarter]) + wide(mate_part[n][1 - y]))
        sum_y(n).start()

    def to_x(n):
        sum_y(n).wait_recv()
        whole[n][kept] = low(
            wide(whole[n][kept]) + wide(mate_part[n][y]) + wide(y_part[n][...])
        )
        sum_x(n).start()

    def to_z(n):
        sum_x(n).wait_recv()
        at = pl.ds(pl.multiple_of(side * half_rows, half_rows), half_rows)
        whole[n][kept, at] = low(wide(whole[n][kept, at]) + wide(x_part[n][...]))
        for d in range(1, blocks):
            sum_z(n, d).start()

    def to_all(n):
        at = pl.ds(pl.multiple_of(side * half_rows + place * piece, piece), piece)
        total = wide(whole[n][kept, at])
        for d in range(1, blocks):
            sum_z(n, d).wait_recv()
            total += wide(z_part[n][d - 1])
        shares[n][at] = low(total)
        for d in range(1, blocks):
            all_copy(n, d, place).start()

    def to_back(n):
        for d in range(1, blocks):
            all_copy(n, d, lax.rem(place + blocks - d, blocks)).wait_recv()
        back_copy(n, side).start()

    def finish_sum(n):
        back_copy(n, 1 - side).wait_recv()
        for half in range(2):
            sum_mate(n, half).wait_send()
        sum_y(n).wait_send()
        sum_x(n).wait_send()
        for d in range(1, blocks):
            sum_z(n, d).wait_send()
            all_copy(n, d, place).wait_send()
        back_copy(n, side).wait_send()

    def weight_gradient(n, back_ref):
        def quarter(f, carry):
            rows_of = normed_ref[pl.ds(pl.multiple_of(f * filled, filled), filled)]
            whole[n][f, :filled] = low(dot(rows_of, back_ref[...], 1, 1))
            return carry

        lax.fori_loop(0, whole[n].shape[0], quarter, 0)

    token_copy = remote(
        token_traded, back_tokens_ref.at[side], token_send, token_recv, tp=1 - side
    )

    def input_gradient():
        tokens = wide(tokens_ref[...])
        inverse = lax.rsqrt(jnp.mean(tokens * tokens, 0, keepdims=True) + EPS)

        def quarter(f, total):
            at = pl.ds(pl.multiple_of(f * filled, filled), filled)
            unit = wide(tokens_ref[at]) * inverse
            back = dot(full_query[at], back_query_ref[...], 1, 0) + dot(
                full_keyval[at], back_keyval_ref[...], 1, 0
            )
            gain_sum = jnp.sum(back * unit, 1, keepdims=True)
            lane = lax.broadcasted_iota(jnp.int32, (filled, whole[3].shape[-1]), 1)
            whole[3][f, :filled] = low(
                jnp.where(lane == 0, gain_sum, jnp.where(lane == 1, gain_two_ref[at], 0.0))
            )
            back = back * wide(gains_ref[at])[:, :1]
            back_one[at] = back
            return total + jnp.sum(back * unit, 0, keepdims=True)

        total = lax.fori_loop(
            0, whole[0].shape[0], quarter, jnp.zeros((1, tokens_ref.shape[-1]), jnp.float32)
        )
        to_mate(3)
        mean = total / tokens_ref.shape[0]

        def rows_back(f, carry):
            at = pl.ds(pl.multiple_of(f * filled, filled), filled)
            unit = wide(tokens_ref[at]) * inverse
            back_one[at] = middle_ref[at] + inverse * (back_one[at] - unit * mean)
            for target, slot in ((back_tokens_ref.at[side], side), (token_traded, 1 - side)):
                columns = pl.ds(pl.multiple_of(slot * pair_width, pair_width), pair_width)
                target[at] = low(back_one[at, columns])
            return carry

        lax.fori_loop(0, whole[0].shape[0], rows_back, 0)
        token_copy.start()

    def chunk_at(ref, m, r, *front):
        return ref.at[(m,) + front + (pl.ds(r * CHUNK_ROWS, CHUNK_ROWS),)]

    def mate_copy(m, r, half):
        gradient = gradients[m]
        return remote(
            gradient.at[2 * half + 1 - core, pl.ds(r * CHUNK_ROWS, CHUNK_ROWS)],
            chunk_at(mate_in, m, r, half),
            mate_send.at[m * per + r, half], mate_recv.at[m * per + r, half], fsdp=mate,
        )

    for m in range(len(gradients)):
        for r in range(per):
            for half in range(2):
                mate_copy(m, r, half).start()
    for f in range(whole[0].shape[0]):
        pltpu.make_async_copy(
            out_ref.at[f], whole[0].at[f, pl.ds(0, filled)], whole_sem.at[f]
        ).wait()
    to_mate(0)
    for m, gradient in enumerate(gradients):
        for half in range(2):
            pltpu.make_async_copy(
                gradient.at[2 * half + core], own.at[m, half], own_sem.at[m, half]
            ).wait()

    def split(k):
        r = lax.rem(k, per)
        return k // per, pl.ds(pl.multiple_of(r * CHUNK_ROWS, CHUNK_ROWS), CHUNK_ROWS)

    def y_copy(k):
        m, at = split(k)
        return remote(
            own.at[m, 1 - y, at], y_in.at[m, at], y_send.at[k], y_recv.at[k], fsdp=across
        )

    def up_copy(k):
        m, at = split(k)
        return remote(
            own.at[m, y, at], up_in.at[m, at], up_send.at[k], up_recv.at[k], ctx=place + 1
        )

    def down_copy(k):
        m, at = split(k)
        return remote(
            share_ref.at[m, at], share_ref.at[m, at], down_send.at[k], down_recv.at[k],
            ctx=place - 1,
        )

    def to_across(k):
        m, at = split(k)
        for half in range(2):
            pltpu.make_async_copy(
                mate_in.at[m, half, at], mate_in.at[m, half, at], mate_recv.at[k, half]
            ).wait()
        own[m, 1 - y, at] = low(wide(own[m, 1 - y, at]) + wide(mate_in[m, 1 - y, at]))
        y_copy(k).start()

    def to_next(k):
        m, at = split(k)
        y_copy(k).wait_recv()
        total = wide(own[m, y, at]) + wide(mate_in[m, y, at]) + wide(y_in[m, at])

        @pl.when(place == 0)
        def _():
            own[m, y, at] = low(total)

        @pl.when(place > 0)
        def _():
            up_copy(k).wait_recv()
            own[m, y, at] = low(total + wide(up_in[m, at]))

        @pl.when(place < last)
        def _():
            up_copy(k).start()

        @pl.when(place == last)
        def _():
            share_ref[m, at] = own[m, y, at]

    def give_back(k):
        @pl.when(place < last)
        def _():
            down_copy(k).wait_recv()

        @pl.when(place > 0)
        def _():
            down_copy(k).start()

    def query_gradient(n):
        weight_gradient(n, back_query_ref)
        to_mate(n)

    def tick(t):
        h = t - last - 2 * (last - place)

        @pl.when((h >= 0) & (h < KEYVAL_HEADS * blocks) & (lax.rem(h, blocks) == 0))
        def _():
            hand_on(h // blocks)

        @pl.when(t < chunks)
        def _():
            to_across(t)

        @pl.when(t == chunks + 1)
        def _():
            finish_result()

        b = t - 4 - 2 * place

        @pl.when((b >= 0) & (b < 2 * chunks) & (lax.rem(b, 2) == 0))
        def _():
            to_next(b // 2)

        c = t - KEYVAL_HEADS * blocks - 2 * (last - place)

        @pl.when((c >= 0) & (c < 2 * chunks) & (lax.rem(c, 2) == 0))
        def _():
            give_back(c // 2)

        for at, stage, n in (
            (4, to_y, 0), (15, to_x, 0), (18, to_z, 0), (20, query_gradient, 1),
            (20, to_all, 0), (21, to_y, 1), (22, to_back, 0), (24, to_x, 1), (26, to_z, 1),
        ):
            @pl.when(t == at)
            def _(stage=stage, n=n):
                stage(n)

    def part_copy(j, s):
        return remote(
            parts.at[j, s], part_in.at[j, s - 1], part_send.at[j, s - 1],
            part_recv.at[j, s - 1], ctx=place - 1,
        )

    def step(j, s, masked):
        keys = keyval_ref[s, j, 0]
        keys_turned = keys.T
        values_turned = keyval_ref[s, j, 1].T
        back_key = jnp.zeros(keys.shape, jnp.float32)
        back_value = jnp.zeros(keys.shape, jnp.float32)
        for g in range(GROUP):
            head = GROUP * j + g
            query = query_ref[head]
            back = back_ref[head]
            if masked:
                row_sums[g] = jnp.sum(wide(back) * wide(mixed_ref[head]), 0, keepdims=True)
            scores = dot(keys_turned, query, 1, 0)
            if masked:
                scores = causal(scores)
            weights = jnp.exp(scores - lse_ref[head])
            back_weights = dot(values_turned, back, 1, 0)
            back_scores = low(weights * (back_weights - row_sums[g]))
            added = dot(keys, back_scores, 1, 0)
            if masked:
                back_total[g] = added
            else:
                back_total[g] += added
            back_key += dot(query, back_scores, 1, 1)
            back_value += dot(back, low(weights), 1, 1)
        parts[j, s, 0] = low(back_key)
        parts[j, s, 1] = low(back_value)
        if not masked:
            @pl.when(place == last)
            def _():
                part_copy(j, s).start()

    def hand_on(j):
        for s in range(blocks):
            @pl.when(s <= place)
            def _(s=s):
                @pl.when(place < last)
                def _():
                    pltpu.make_async_copy(
                        part_in.at[j, s], part_in.at[j, s], part_recv.at[j, s]
                    ).wait()
                    for kind in range(2):
                        total = wide(parts[j, s, kind]) + wide(part_in[j, s, kind])
                        parts[j, s, kind] = low(total)

                if s > 0:
                    @pl.when(place < last)
                    def _():
                        part_copy(j, s).start()
                else:
                    leading = wide(parts[j, 0, 0, :HALF])
                    trailing = wide(parts[j, 0, 0, HALF:])
                    cosine, sine = cosine_ref[...], sine_ref[...]
                    at = j * HEAD_WIDTH
                    back_keyval_ref[pl.ds(pl.multiple_of(at, HALF), HALF)] = low(
                        leading * cosine + trailing * sine
                    )
                    back_keyval_ref[pl.ds(pl.multiple_of(at + HALF, HALF), HALF)] = low(
                        trailing * cosine - leading * sine
                    )
                    at = pl.ds(pl.multiple_of(KEY_WIDTH + at, HEAD_WIDTH), HEAD_WIDTH)
                    back_keyval_ref[at] = low(wide(parts[j, 0, 1]))

    def head_loop(j, carry):
        @pl.when(j < KEYVAL_HEADS)
        def _():
            step(j, 0, True)

        tick(j * blocks)

        def block_loop(s, inner):
            @pl.when((j < KEYVAL_HEADS) & (s <= place))
            def _():
                step(j, s, False)

            tick(j * blocks + s)
            return inner

        lax.fori_loop(1, blocks, block_loop, 0)

        @pl.when(j < KEYVAL_HEADS)
        def _():
            cosine, sine = cosine_ref[...], sine_ref[...]
            for g in range(GROUP):
                leading = back_total[g, :HALF] * SCALE
                trailing = back_total[g, HALF:] * SCALE
                at = (GROUP * j + g) * HEAD_WIDTH
                back_query_ref[pl.ds(pl.multiple_of(at, HALF), HALF)] = low(
                    leading * cosine + trailing * sine
                )
                back_query_ref[pl.ds(pl.multiple_of(at + HALF, HALF), HALF)] = low(
                    trailing * cosine - leading * sine
                )

        return carry

    assert iterations * blocks > 4 + 2 * last + 2 * (chunks - 1)
    lax.fori_loop(0, iterations, head_loop, 0)

    def keyval_gradient(n):
        weight_gradient(n, back_keyval_ref)
        to_mate(n)

    later = (
        ((keyval_gradient, 2), (to_y, 2)), ((to_all, 1),), ((lambda n: input_gradient(), 3),),
        ((to_x, 2), (to_back, 1)), ((to_y, 3),), ((to_z, 2), (to_x, 3)), ((to_all, 2), (to_z, 3)),
        ((to_back, 2), (to_all, 3)), ((to_back, 3),),
    )
    for slot, stages in enumerate(later):
        for stage, n in stages:
            stage(n)
        for index in range(blocks):
            if early + slot - last + index < chunks:
                @pl.when(place == index)
                def _(k=early + slot - last + index):
                    give_back(k)

    assert early >= last and len(later) >= chunks - early + last
    for n in range(chunks_in):
        finish_sum(n)
    token_copy.wait()

    for m in range(len(gradients)):
        for r in range(per):
            for half in range(2):
                mate_copy(m, r, half).wait_send()

    def finish(k, carry):
        y_copy(k).wait_send()

        @pl.when(place < last)
        def _():
            up_copy(k).wait_send()

        @pl.when(place > 0)
        def _():
            down_copy(k).wait_send()

        return carry

    lax.fori_loop(0, chunks, finish, 0)

    def finish_parts(j, carry):
        for s in range(1, blocks):
            @pl.when(s <= place)
            def _(s=s):
                part_copy(j, s).wait_send()
        return carry

    lax.fori_loop(0, KEYVAL_HEADS, finish_parts, 0)
    feed_copy.wait_send()
    trade_copy.wait()


def backward_sum(
    query, keyval, back_mixed, mixed, lse, cosine, sine, base, feed, tokens, normed, middle,
    gains, gain_two, full_query, full_keyval, gradients, gradient_out,
):
    blocks, positions = keyval.shape[0], keyval.shape[-1]
    count, rows, columns = gradients[0].shape
    chunks = len(gradients) * rows // CHUNK_ROWS
    area = QUERY_HEADS * positions * positions * blocks
    vmem = pl.BlockSpec(memory_space=pltpu.VMEM)
    anywhere = pl.BlockSpec(memory_space=pl.ANY)
    dma = pltpu.SemaphoreType.DMA
    share = (len(gradients), rows, columns)
    head = (2, HEAD_WIDTH, positions)
    features = feed.shape[0]
    widths = (QUERY_WIDTH, QUERY_WIDTH, 2 * KEY_WIDTH, gains.shape[-1])
    padded = rows + 16
    half_rows = padded // 2
    low_type = jnp.bfloat16
    scratch = []
    for first in ((count, padded), (2, padded), (padded,), (half_rows,),
                  (blocks - 1, half_rows // blocks)):
        scratch += [pltpu.VMEM(first + (w,), low_type) for w in widths]
    each = len(widths)
    pairs = jax.ShapeDtypeStruct((2, features, positions // 2), low_type)
    return pl.pallas_call(
        backward_sum_kernel,
        in_specs=[vmem] * 16 + [anywhere] * 4,
        out_specs=[vmem] * (3 + each),
        out_shape=[jax.ShapeDtypeStruct(share, low_type), pairs, pairs] + [
            jax.ShapeDtypeStruct((padded, w), low_type) for w in widths
        ],
        scratch_shapes=scratch + [
            pltpu.VMEM((len(gradients), 2, rows, columns), low_type),
            pltpu.VMEM((len(gradients), 2, rows, columns), low_type),
            pltpu.VMEM(share, low_type),
            pltpu.VMEM(share, low_type),
            pltpu.VMEM((KEYVAL_HEADS, blocks) + head, low_type),
            pltpu.VMEM((KEYVAL_HEADS, blocks - 1) + head, low_type),
            pltpu.VMEM((GROUP, HEAD_WIDTH, positions), jnp.float32),
            pltpu.VMEM((GROUP, 1, positions), jnp.float32),
            dma((len(gradients), 2)),
            dma((chunks, 2)), dma((chunks, 2)),
            dma((chunks,)), dma((chunks,)),
            dma((chunks,)), dma((chunks,)),
            dma((chunks,)), dma((chunks,)),
            dma((KEYVAL_HEADS, blocks - 1)), dma((KEYVAL_HEADS, blocks - 1)),
            pltpu.VMEM(feed.shape, low_type),
            pltpu.VMEM((features, positions // 2), low_type),
            dma, dma, dma, dma,
            pltpu.VMEM((QUERY_WIDTH, positions), low_type),
            pltpu.VMEM((2 * KEY_WIDTH, positions), low_type),
            pltpu.VMEM((features, positions), jnp.float32),
            pltpu.VMEM((features, positions // 2), low_type),
            dma((count,)),
            dma((each, 2)), dma((each, 2)),
            dma((each,)), dma((each,)),
            dma((each,)), dma((each,)),
            dma((each, blocks - 1)), dma((each, blocks - 1)),
            dma((each, blocks - 1)), dma((each, blocks - 1)),
            dma((each,)), dma((each,)),
            dma, dma,
        ],
        compiler_params=pltpu.CompilerParams(
            vmem_limit_bytes=KERNEL_VMEM, collective_id=0, has_side_effects=True
        ),
        cost_estimate=pl.CostEstimate(
            flops=40 * HEAD_WIDTH * area, bytes_accessed=10 * query.size, transcendentals=area
        ),
        name="backward_sum",
    )(
        query, keyval, back_mixed, mixed, lse, cosine, sine, base, feed, tokens, normed, middle,
        gains, gain_two, full_query, full_keyval, *gradients, gradient_out,
    )


def front_kernel(
    tokens_ref, cotangent_ref, cosine_ref, sine_ref, *refs
):
    weights, refs = refs[:7], refs[7:]
    (
        tokens_own, cotangent_own, cotangent_other, normed_out, query_out, keyval_ref,
        mixed_out, lse_ref, tokens_other, mixed_other,
    ), refs = refs[:10], refs[10:]
    full, refs = refs[:7], refs[7:]
    (
        raw, tops, totals, sums,
        local_sem, token_send, token_recv, cot_send, cot_recv,
        y_send, y_recv, mate_send, mate_recv, pass_send, pass_recv, key_send, key_recv,
        mixed_send, mixed_recv,
    ) = refs
    place = lax.axis_index("ctx")
    last = lax.axis_size("ctx") - 1
    rank = lax.axis_index("fsdp")
    side = lax.axis_index("tp")
    core = rank % 2
    mate = rank + 1 - 2 * core
    across = rank + 2 - 4 * (rank // 2)
    width = tokens_ref.shape[-1]

    def columns(ref, slot):
        return ref.at[:, pl.ds(pl.multiple_of(slot * width, width), width)]

    local = [
        pltpu.make_async_copy(tokens_ref.at[side], columns(tokens_own, side), local_sem.at[0]),
        pltpu.make_async_copy(
            cotangent_ref.at[side], columns(cotangent_own, side), local_sem.at[1]
        ),
        pltpu.make_async_copy(
            cotangent_ref.at[1 - side], columns(cotangent_other, side), local_sem.at[2]
        ),
        pltpu.make_async_copy(
            tokens_ref.at[1 - side], columns(tokens_other, side), local_sem.at[3]
        ),
    ]
    for w in range(len(weights)):
        local.append(pltpu.make_async_copy(weights[w], full[w].at[rank], local_sem.at[4 + w]))
    for copy in local:
        copy.start()

    greet(fsdp=mate)
    greet(fsdp=across)
    greet(tp=1 - side)

    @pl.when(place > 0)
    def _():
        greet(ctx=place - 1)

    @pl.when(place < last)
    def _():
        greet(ctx=place + 1)

    neighbours = (place + last - 1) // last + (2 * last - place - 1) // last
    pl.semaphore_wait(pltpu.get_barrier_semaphore(), 3 + neighbours)

    token_copy = remote(
        tokens_ref.at[1 - side], columns(tokens_own, side), token_send, token_recv, tp=1 - side
    )
    cot_copies = [
        remote(
            cotangent_ref.at[1 - side], columns(cotangent_own, side), cot_send.at[0],
            cot_recv.at[0], tp=1 - side,
        ),
        remote(
            cotangent_ref.at[side], columns(cotangent_other, side), cot_send.at[1],
            cot_recv.at[1], tp=1 - side,
        ),
        remote(
            tokens_ref.at[side], columns(tokens_other, side), cot_send.at[2], cot_recv.at[2],
            tp=1 - side,
        ),
    ]

    def mixed_copy(j):
        heads = pl.ds(GROUP * j, GROUP)
        return remote(
            mixed_out.at[heads], mixed_other.at[heads], mixed_send.at[j], mixed_recv.at[j],
            tp=1 - side,
        )


    def y_copy(w):
        return remote(
            weights[w], full[w].at[rank], y_send.at[w], y_recv.at[w], fsdp=across
        )

    def mate_copy(w):
        return remote(
            weights[w], full[w].at[rank], mate_send.at[w], mate_recv.at[w], fsdp=mate
        )

    def pass_copy(w):
        return remote(
            full[w].at[across], full[w].at[across], pass_send.at[w], pass_recv.at[w], fsdp=mate
        )

    def arrived(w):
        local[4 + w].wait()
        mate_copy(w).wait_recv()
        pass_copy(w).wait_recv()

    for w in (6, 1):
        y_copy(w).start()
        mate_copy(w).start()
    token_copy.start()
    y_copy(0).start()
    mate_copy(0).start()
    y_copy(6).wait_recv()
    pass_copy(6).start()
    arrived(6)
    gain = wide(full[6][...].reshape(-1, full[6].shape[-1])[:, :1])

    def norm_rows(slot):
        at = pl.ds(pl.multiple_of(slot * width, width), width)
        rows = wide(tokens_own[:, at])
        inverse = lax.rsqrt(jnp.mean(rows * rows, 0, keepdims=True) + EPS)
        normed_out[:, at] = low(rows * inverse * gain)

    local[0].wait()
    norm_rows(side)
    token_copy.wait_recv()
    norm_rows(1 - side)
    for copy in cot_copies:
        copy.start()
    for w in (1, 0):
        y_copy(w).wait_recv()
        pass_copy(w).start()
    for w in range(2, 6):
        y_copy(w).start()
        mate_copy(w).start()
    normed = normed_out[...]
    cosine, sine = cosine_ref[...], sine_ref[...]

    def turned(value, target):
        target[:HALF] = low(value[:HALF] * cosine - value[HALF:] * sine)
        target[HALF:] = low(value[HALF:] * cosine + value[:HALF] * sine)

    def key_copy(s, j):
        return remote(
            keyval_ref.at[s, j], keyval_ref.at[s + 1, j], key_send.at[s, j], key_recv.at[s, j],
            ctx=place + 1,
        )

    arrived(1)
    matrix = full[1][...].reshape(-1, 2 * KEY_WIDTH)
    raw[: 2 * KEY_WIDTH] = dot(matrix, normed, 0, 0)
    for j in range(KEYVAL_HEADS):
        turned(raw[j * HEAD_WIDTH : (j + 1) * HEAD_WIDTH], keyval_ref.at[0, j, 0])
        first = KEY_WIDTH + j * HEAD_WIDTH
        keyval_ref[0, j, 1] = low(raw[first : first + HEAD_WIDTH])

        if j == 0:
            @pl.when(place < last)
            def _():
                key_copy(0, 0).start()

    arrived(0)
    matrix = full[0][...].reshape(-1, QUERY_WIDTH)
    raw[...] = dot(matrix, normed, 0, 0)

    def turn_query(h, carry):
        value = raw[pl.ds(pl.multiple_of(h * HEAD_WIDTH, HEAD_WIDTH), HEAD_WIDTH)]
        first = low(value[:HALF] * cosine - value[HALF:] * sine)
        second = low(value[HALF:] * cosine + value[:HALF] * sine)
        query_out[h, :HALF] = first * jnp.bfloat16(SCALE)
        query_out[h, HALF:] = second * jnp.bfloat16(SCALE)
        return carry

    lax.fori_loop(0, QUERY_HEADS, turn_query, 0)

    def attend(s, j, masked):
        keys_turned = keyval_ref[s, j, 0].T
        values = keyval_ref[s, j, 1]
        for g in range(GROUP):
            head = GROUP * j + g
            scores = dot(keys_turned, query_out[head], 1, 0)
            if masked:
                scores = causal(scores)
                top = jnp.max(scores, 0, keepdims=True)
                lifted = jnp.exp(scores - top)
                tops[head] = top
                totals[head] = jnp.sum(lifted, 0, keepdims=True)
                sums[head] = dot(values, low(lifted), 1, 0)
            else:
                old = tops[head]
                top = jnp.maximum(old, jnp.max(scores, 0, keepdims=True))
                lifted = jnp.exp(scores - top)
                shrink = jnp.exp(old - top)
                tops[head] = top
                totals[head] = totals[head] * shrink + jnp.sum(lifted, 0, keepdims=True)
                sums[head] = sums[head] * shrink + dot(values, low(lifted), 1, 0)

    def hand_on(s, j):
        @pl.when(s < place)
        def _():
            pltpu.make_async_copy(
                keyval_ref.at[s + 1, j], keyval_ref.at[s + 1, j], key_recv.at[s, j]
            ).wait()

            @pl.when(place < last)
            def _():
                key_copy(s + 1, j).start()

    def finish_heads(j):
        for g in range(GROUP):
            head = GROUP * j + g
            total = totals[head]
            mixed_out[head] = low(sums[head] / total)
            lse_ref[head] = tops[head] + jnp.log(total)
        mixed_copy(j).start()

    def one_head(j, carry):
        @pl.when((place < last) & (j + 1 < KEYVAL_HEADS))
        def _():
            key_copy(0, j + 1).start()

        attend(0, j, True)
        hand_on(0, j)

        def later_block(s, inner):
            attend(s, j, False)
            hand_on(s, j)
            return inner

        lax.fori_loop(1, place + 1, later_block, 0)
        finish_heads(j)
        return carry

    lax.fori_loop(0, KEYVAL_HEADS, one_head, 0)
    passed = 2

    for w in range(passed, 6):
        y_copy(w).wait_recv()
        pass_copy(w).start()
    for copy in local[1:4]:
        copy.wait()
    for j in range(KEYVAL_HEADS):
        mixed_copy(j).wait()
    token_copy.wait_send()
    for copy in cot_copies:
        copy.wait()
    for w in range(passed, 6):
        arrived(w)
    for w in range(len(weights)):
        y_copy(w).wait_send()
        mate_copy(w).wait_send()
        pass_copy(w).wait_send()

    @pl.when(place < last)
    def _():
        def sent(i, carry):
            key_copy(i // KEYVAL_HEADS, lax.rem(i, KEYVAL_HEADS)).wait_send()
            return carry

        lax.fori_loop(0, (place + 1) * KEYVAL_HEADS, sent, 0)


def front(tokens, cotangent, cosine, sine, weights):
    blocks = lax.axis_size("ctx")
    parts = lax.axis_size("fsdp")
    positions = cosine.shape[-1]
    vmem = pl.BlockSpec(memory_space=pltpu.VMEM)
    anywhere = pl.BlockSpec(memory_space=pl.ANY)
    dma = pltpu.SemaphoreType.DMA
    shape = lambda *dims: jax.ShapeDtypeStruct(dims, jnp.bfloat16)
    count = len(weights)
    features = tokens.shape[1]
    area = QUERY_HEADS * positions * positions * blocks
    return pl.pallas_call(
        front_kernel,
        in_specs=[vmem] * (4 + count),
        out_specs=[vmem] * 12 + [anywhere] * 4 + [vmem],
        out_shape=[
            shape(features, positions), shape(features, positions), shape(features, positions),
            shape(features, positions),
            shape(QUERY_HEADS, HEAD_WIDTH, positions),
            shape(blocks, KEYVAL_HEADS, 2, HEAD_WIDTH, positions),
            shape(QUERY_HEADS, HEAD_WIDTH, positions),
            jax.ShapeDtypeStruct((QUERY_HEADS, 1, positions), jnp.float32),
            shape(features, positions),
            shape(QUERY_HEADS, HEAD_WIDTH, positions),
        ] + [shape(parts, *w.shape) for w in weights],
        scratch_shapes=[
            pltpu.VMEM((QUERY_WIDTH, positions), jnp.float32),
            pltpu.VMEM((QUERY_HEADS, 1, positions), jnp.float32),
            pltpu.VMEM((QUERY_HEADS, 1, positions), jnp.float32),
            pltpu.VMEM((QUERY_HEADS, HEAD_WIDTH, positions), jnp.float32),
            dma((4 + count,)),
            dma, dma,
            dma((3,)), dma((3,)),
            dma((count,)), dma((count,)),
            dma((count,)), dma((count,)),
            dma((count,)), dma((count,)),
            dma((blocks, KEYVAL_HEADS)), dma((blocks, KEYVAL_HEADS)),
            dma((KEYVAL_HEADS,)), dma((KEYVAL_HEADS,)),
        ],
        compiler_params=pltpu.CompilerParams(
            vmem_limit_bytes=KERNEL_VMEM, collective_id=1, has_side_effects=True
        ),
        cost_estimate=pl.CostEstimate(
            flops=16 * HEAD_WIDTH * area, bytes_accessed=10 * tokens.size, transcendentals=area
        ),
        name="front",
    )(tokens, cotangent, cosine, sine, *weights)


def on_device(
    tokens, cotangent, input_gain, w_query, w_keyval, w_output, middle_gain, w_gate, w_up, w_down
):
    half = lax.axis_index("tp")
    low_half = half == 0
    pair = [(0, 1), (1, 0)]

    def to_partner(value_rows):
        return lax.ppermute(value_rows, "tp", pair)

    def in_order(mine, received):
        return jnp.concatenate(
            [jnp.where(low_half, mine, received), jnp.where(low_half, received, mine)], 0
        )

    def take(value_rows, index):
        return lax.dynamic_index_in_dim(value_rows, index, 0, keepdims=False)

    tokens_own = in_order(take(tokens, half), to_partner(take(tokens, 1 - half)))
    full_gain_one, full_gain_two = (
        lax.all_gather(input_gain, "fsdp", axis=0, tiled=True),
        lax.all_gather(middle_gain, "fsdp", axis=0, tiled=True),
    )
    full_in = lax.all_gather(jnp.concatenate([w_query, w_keyval], 1), "fsdp", axis=0, tiled=True)
    full_output = lax.all_gather(w_output, "fsdp", axis=0, tiled=True)
    full_gate = lax.all_gather(w_gate, "fsdp", axis=0, tiled=True)
    full_up = lax.all_gather(w_up, "fsdp", axis=0, tiled=True)
    full_down = lax.all_gather(w_down, "fsdp", axis=0, tiled=True)
    cotangent_received = to_partner(cotangent)
    cotangent_own = in_order(take(cotangent, half), take(cotangent_received, half))
    cotangent_other = in_order(take(cotangent, 1 - half), take(cotangent_received, 1 - half))

    token_positions = tokens_own.shape[0]
    cosine, sine = rope_tables(token_positions, lax.axis_index("ctx") * token_positions)
    gain_one = full_gain_one.astype(jnp.float32)
    inputs = tokens_own.astype(jnp.float32)
    unit_one, inverse_one = normalize(inputs)
    normed_one = (unit_one * gain_one).astype(jnp.bfloat16)
    keyval_raw = dot(full_in[:, QUERY_WIDTH:], normed_one, 0, 1)
    keyval_low = jnp.concatenate(
        [apply_rotary(keyval_raw[:KEY_WIDTH], cosine, sine), keyval_raw[KEY_WIDTH:]], 0
    ).astype(jnp.bfloat16)
    blocks = lax.axis_size("ctx")
    keyval = jnp.stack([keyval_low] + [move_along(keyval_low, s) for s in range(1, blocks)], 0)
    keyval = keyval.reshape(blocks, 2, KEYVAL_HEADS, HEAD_WIDTH, token_positions)
    query_raw = dot(full_in[:, :QUERY_WIDTH], normed_one, 0, 1)
    query_low = (
        apply_rotary(query_raw, cosine, sine)
        .astype(jnp.bfloat16)
        .reshape(QUERY_HEADS, HEAD_WIDTH, token_positions)
    )
    mixed_heads, lse = attend_forward(query_low, keyval)
    mixed_low = mixed_heads.reshape(QUERY_WIDTH, token_positions)
    middle = inputs + dot(mixed_low, full_output, 0, 0)

    gain_two = full_gain_two.astype(jnp.float32)
    unit_two, inverse_two = normalize(middle)
    normed_two = (unit_two * gain_two).astype(jnp.bfloat16)
    normed_other = to_partner(normed_two)

    def feed(rows, back_rows):
        gate_proj = dot(rows, full_gate, 1, 0)
        up_proj = dot(rows, full_up, 1, 0)
        sigmoid_gate = jax.nn.sigmoid(gate_proj)
        swish_gate = gate_proj * sigmoid_gate
        hidden = (swish_gate * up_proj).astype(jnp.bfloat16)
        back_hidden = dot(back_rows, full_down, 1, 0)
        back_gate = (
            back_hidden * up_proj * sigmoid_gate * (1.0 + gate_proj * (1.0 - sigmoid_gate))
        ).astype(jnp.bfloat16)
        back_up = (back_hidden * swish_gate).astype(jnp.bfloat16)
        return (hidden, back_gate, back_up)

    def feed_input_back(back_gate, back_up):
        return dot(back_gate, full_gate, 1, 1) + dot(back_up, full_up, 1, 1)

    hidden_own, back_gate_own, back_up_own = feed(normed_two, cotangent_own)
    hidden_other, back_gate_other, back_up_other = feed(normed_other, cotangent_other)
    back_two_received = to_partner(
        feed_input_back(back_gate_other, back_up_other).astype(jnp.bfloat16)
    )
    back_two = feed_input_back(back_gate_own, back_up_own) + back_two_received.astype(jnp.float32)
    feed_received = to_partner(dot(hidden_other, full_down, 1, 1).astype(jnp.bfloat16))
    result_own = (
        middle + dot(hidden_own, full_down, 1, 1) + feed_received.astype(jnp.float32)
    ).astype(jnp.bfloat16)

    def feed_gradient(left_own, right_own, left_other, right_other):
        gradient = dot(left_own, right_own, 0, 0) + dot(left_other, right_other, 0, 0)
        shared = scatter_sum(gradient.astype(jnp.bfloat16), "fsdp")
        return whole_sum(shared, (("ctx", 2),))

    share_down = feed_gradient(cotangent_own, hidden_own, cotangent_other, hidden_other)
    share_gate = feed_gradient(normed_two, back_gate_own, normed_other, back_gate_other)
    share_up = feed_gradient(normed_two, back_up_own, normed_other, back_up_other)

    grad_gain_two = jnp.sum(back_two * unit_two, axis=0)
    back_middle = cotangent_own.astype(jnp.float32) + norm_back(
        back_two * gain_two, unit_two, inverse_two
    )
    back_attention = back_middle.astype(jnp.bfloat16)
    back_mixed = dot(full_output, back_attention, 1, 1).astype(jnp.bfloat16)
    back_mixed = back_mixed.reshape(query_low.shape)
    grad_output = dot(mixed_low, back_attention, 1, 0).astype(jnp.bfloat16)
    share_output = whole_sum(scatter_sum(grad_output, "fsdp"), (("tp", 1), ("ctx", 2)))

    back_query = []
    back_key = []
    back_value = []
    for first, count in ((0, 3), (3, 2)):
        part_query, part_keyval = attend_backward(
            query_low, keyval, back_mixed, mixed_heads, lse, cosine, sine, first, count
        )
        part_keyval = part_keyval.reshape(blocks, 2 * count * HEAD_WIDTH, token_positions)
        owned = part_keyval[0].astype(jnp.float32)
        for s in range(1, blocks):
            owned += move_along(part_keyval[s], -s).astype(jnp.float32)
        back_query.append(part_query.reshape(-1, token_positions))
        back_key.append(
            apply_rotary(owned[: count * HEAD_WIDTH], cosine, -sine).astype(jnp.bfloat16)
        )
        back_value.append(owned[count * HEAD_WIDTH :].astype(jnp.bfloat16))
    back_in = jnp.concatenate(back_query + back_key + back_value, 0)
    grad_in = dot(normed_one, back_in, 0, 1)
    back_one = dot(back_in, full_in, 0, 1)
    grad_gain_one = jnp.sum(back_one * unit_one, axis=0)
    back_inputs = back_middle + norm_back(back_one * gain_one, unit_one, inverse_one)

    def to_positions(value_rows):
        split = value_rows.reshape(2, token_positions // 2, value_rows.shape[-1])
        received = to_partner(take(split, 1 - half))
        return in_order(take(split, half)[None], received[None])

    result = to_positions(result_own)
    grad_tokens = to_positions(back_inputs.astype(jnp.bfloat16)).astype(jnp.float32)
    gradients = jnp.concatenate([grad_in, grad_gain_one[:, None], grad_gain_two[:, None]], 1)
    share_in = lax.psum(
        lax.psum_scatter(
            gradients.astype(jnp.bfloat16), "fsdp", scatter_dimension=0, tiled=True
        ),
        ("ctx", "tp"),
    ).astype(jnp.float32)
    width = full_in.shape[1]
    return (
        result,
        grad_tokens,
        share_in[:, width],
        share_in[:, :QUERY_WIDTH],
        share_in[:, QUERY_WIDTH:width],
        share_output,
        share_in[:, width + 1],
        share_gate,
        share_up,
        share_down,
    )


def fast_on_device(
    tokens, cotangent, input_gain, w_query, w_keyval, w_output, middle_gain, w_gate, w_up, w_down
):
    pair = [(0, 1), (1, 0)]

    def to_partner(value_rows):
        return lax.ppermute(value_rows, "tp", pair)

    parts = lax.axis_size("fsdp")
    width_in = tokens.shape[-1]
    rows = width_in // parts
    token_positions = 2 * tokens.shape[1]
    cosine, sine = rope_tables(token_positions, lax.axis_index("ctx") * token_positions)
    gains = jnp.pad(jnp.stack([input_gain, middle_gain], 1), ((0, 0), (0, 126)))
    (
        tokens_own, cotangent_own, cotangent_other, normed_one, query_low, keyval,
        mixed_heads, lse, tokens_other, mixed_other, *full,
    ) = front(
        tokens.swapaxes(1, 2), cotangent.swapaxes(1, 2), cosine, sine,
        (w_query, w_keyval, w_output, w_gate, w_up, w_down, gains),
    )
    full_query, full_keyval, full_output, full_gate, full_up, full_down, gains = [
        w.reshape(width_in, -1) for w in full
    ]
    tokens_own, cotangent_own, cotangent_other, normed_one, tokens_other = [
        v.T for v in (tokens_own, cotangent_own, cotangent_other, normed_one, tokens_other)
    ]
    full_gain_two = gains[:, 1]
    inputs = tokens_own.astype(jnp.float32)
    mixed_low = mixed_heads.reshape(QUERY_WIDTH, token_positions)
    middle = inputs + dot(mixed_low, full_output, 0, 0)

    gain_two = full_gain_two.astype(jnp.float32)
    unit_two, inverse_two = normalize(middle)
    normed_two = (unit_two * gain_two).astype(jnp.bfloat16)
    mixed_other = mixed_other.reshape(QUERY_WIDTH, token_positions)
    middle_other = tokens_other.astype(jnp.float32) + dot(mixed_other, full_output, 0, 0)
    normed_other = (normalize(middle_other)[0] * gain_two).astype(jnp.bfloat16)

    def feed(rows, back_rows):
        gate_proj = dot(rows, full_gate, 1, 0)
        up_proj = dot(rows, full_up, 1, 0)
        sigmoid_gate = jax.nn.sigmoid(gate_proj)
        swish_gate = gate_proj * sigmoid_gate
        hidden = (swish_gate * up_proj).astype(jnp.bfloat16)
        back_hidden = dot(back_rows, full_down, 1, 0)
        back_gate = (
            back_hidden * up_proj * sigmoid_gate * (1.0 + gate_proj * (1.0 - sigmoid_gate))
        ).astype(jnp.bfloat16)
        back_up = (back_hidden * swish_gate).astype(jnp.bfloat16)
        return (hidden, back_gate, back_up)

    def feed_input_back(back_gate, back_up):
        return dot(back_gate, full_gate, 1, 1) + dot(back_up, full_up, 1, 1)

    hidden_other, back_gate_other, back_up_other = feed(normed_other, cotangent_other)
    back_two_received = to_partner(
        feed_input_back(back_gate_other, back_up_other).astype(jnp.bfloat16)
    )
    hidden_own, back_gate_own, back_up_own = feed(normed_two, cotangent_own)
    back_two = feed_input_back(back_gate_own, back_up_own) + back_two_received.astype(jnp.float32)
    feed_other = dot(hidden_other, full_down, 1, 1).astype(jnp.bfloat16)
    base = middle + dot(hidden_own, full_down, 1, 1)

    def feed_gradient(left_own, right_own, left_other, right_other):
        gradient = dot(left_own, right_own, 0, 0) + dot(left_other, right_other, 0, 0)
        return gradient.astype(jnp.bfloat16).reshape(lax.axis_size("fsdp"), -1, gradient.shape[1])

    gradients = (
        feed_gradient(cotangent_own, hidden_own, cotangent_other, hidden_other),
        feed_gradient(normed_two, back_gate_own, normed_other, back_gate_other),
        feed_gradient(normed_two, back_up_own, normed_other, back_up_other),
    )

    grad_gain_two = jnp.sum(back_two * unit_two, axis=0)
    back_middle = cotangent_own.astype(jnp.float32) + norm_back(
        back_two * gain_two, unit_two, inverse_two
    )
    back_attention = back_middle.astype(jnp.bfloat16)
    back_mixed = dot(full_output, back_attention, 1, 1).astype(jnp.bfloat16)
    back_mixed = back_mixed.reshape(query_low.shape)
    grad_output = dot(mixed_low, back_attention, 1, 0).astype(jnp.bfloat16)
    share, result, grad_tokens, share_output, share_query, share_keyval, share_gains = backward_sum(
        query_low, keyval, back_mixed, mixed_heads, lse, cosine, sine, base.T, feed_other.T,
        tokens_own.T, normed_one.T, back_middle.T, gains, grad_gain_two[:, None],
        full_query, full_keyval, gradients, grad_output.reshape(parts, rows, -1),
    )
    return (
        result.swapaxes(1, 2),
        grad_tokens.swapaxes(1, 2).astype(jnp.float32),
        share_gains[:rows, 0].astype(jnp.float32),
        share_query[:rows].astype(jnp.float32),
        share_keyval[:rows].astype(jnp.float32),
        share_output[:rows].astype(jnp.float32),
        share_gains[:rows, 1].astype(jnp.float32),
        share[1].astype(jnp.float32),
        share[2].astype(jnp.float32),
        share[0].astype(jnp.float32),
    )


def solution(mesh):
    rows = P("fsdp", ("ctx", "tp"), None)
    specs = (
        P("fsdp"), P("fsdp", None), P("fsdp", None), P("fsdp", None),
        P("fsdp"), P("fsdp", "tp"), P("fsdp", "tp"), P("fsdp", "tp"),
    )
    kernels = mesh.shape["fsdp"] == 4 and mesh.shape["tp"] == 2 and mesh.shape["ctx"] == 4
    return jax.shard_map(
        fast_on_device if kernels else on_device,
        mesh=mesh,
        in_specs=(rows, rows) + specs,
        out_specs=(rows, rows) + specs,
        check_vma=False,
    )
```

```python
import jax
import jax.numpy as jnp
from jax import lax
from jax.experimental import pallas as pl
from jax.experimental.pallas import tpu as pltpu
from jax.sharding import PartitionSpec as P

QUERY_HEADS = 15
KEYVAL_HEADS = 5
GROUP = QUERY_HEADS // KEYVAL_HEADS
HEAD_WIDTH = 64
HALF = HEAD_WIDTH // 2
KEY_WIDTH = 320
QUERY_WIDTH = QUERY_HEADS * HEAD_WIDTH
SCALE = HEAD_WIDTH ** (-0.5)

EPS = 1e-05
THETA = 10000.0
VMEM_LIMIT = 40 * 1024 * 1024


def dot(left, right, left_dim, right_dim):
    return lax.dot_general(
        left, right, (((left_dim,), (right_dim,)), ((), ())), preferred_element_type=jnp.float32
    )


def rope_tables(token_positions, first_place):
    position = (first_place + lax.iota(jnp.int32, token_positions)).astype(jnp.float32)
    frequency = THETA ** (-(2.0 * lax.iota(jnp.int32, HALF).astype(jnp.float32)) / HEAD_WIDTH)
    angles = frequency[:, None] * position[None, :]
    return (jnp.cos(angles), jnp.sin(angles))


def apply_rotary(rows, cosine, sine):
    shaped = rows.reshape(-1, 2, HALF, rows.shape[-1])
    leading = shaped[:, 0]
    trailing = shaped[:, 1]
    return jnp.stack(
        [leading * cosine - trailing * sine, trailing * cosine + leading * sine], 1
    ).reshape(rows.shape)


def normalize(value_rows):
    inverse_rms = lax.rsqrt(jnp.mean(value_rows * value_rows, -1, keepdims=True) + EPS)
    return (value_rows * inverse_rms, inverse_rms)


def norm_back(back_unit, unit_rows, inverse_rms):
    return inverse_rms * (
        back_unit - unit_rows * jnp.mean(back_unit * unit_rows, -1, keepdims=True)
    )


def causal(scores):
    key_place = lax.broadcasted_iota(jnp.int32, scores.shape, 0)
    query_place = lax.broadcasted_iota(jnp.int32, scores.shape, 1)
    return jnp.where(key_place <= query_place, scores, -jnp.inf)


def forward_kernel(query_ref, key_ref, value_ref, mixed_ref, lse_ref):
    place = lax.axis_index("ctx")
    queries = [query_ref[g] * jnp.bfloat16(SCALE) for g in range(GROUP)]

    def scores_of(keys_turned, g, masked):
        scores = dot(keys_turned, queries[g], 1, 0)
        return causal(scores) if masked else scores

    def first():
        keys_turned = key_ref[0, 0, 0].T
        values = value_ref[0, 0, 0]
        carried = []
        for g in range(GROUP):
            scores = scores_of(keys_turned, g, True)
            top = jnp.max(scores, 0, keepdims=True)
            lifted = jnp.exp(scores - top)
            total = jnp.sum(lifted, 0, keepdims=True)
            carried += [top, total, dot(values, lifted.astype(jnp.bfloat16), 1, 0)]
        return tuple(carried)

    def step(block, carried):
        keys_turned = key_ref[block, 0, 0].T
        values = value_ref[block, 0, 0]
        later = []
        for g in range(GROUP):
            top, total, mixed = carried[3 * g : 3 * g + 3]
            scores = scores_of(keys_turned, g, False)
            new_top = jnp.maximum(top, jnp.max(scores, 0, keepdims=True))
            lifted = jnp.exp(scores - new_top)
            shrink = jnp.exp(top - new_top)
            later += [
                new_top,
                total * shrink + jnp.sum(lifted, 0, keepdims=True),
                mixed * shrink + dot(values, lifted.astype(jnp.bfloat16), 1, 0),
            ]
        return tuple(later)

    carried = lax.fori_loop(1, place + 1, step, first())
    for g in range(GROUP):
        top, total, mixed = carried[3 * g : 3 * g + 3]
        mixed_ref[g] = (mixed / total).astype(jnp.bfloat16)
        lse_ref[g] = top + jnp.log(total)


def attend_forward(query, keyval):
    blocks, token_positions = keyval.shape[0], keyval.shape[-1]
    head_block = (GROUP, HEAD_WIDTH, token_positions)
    key_block = (blocks, 1, 1, HEAD_WIDTH, token_positions)
    area = QUERY_HEADS * token_positions * token_positions * blocks
    return pl.pallas_call(
        forward_kernel,
        grid=(KEYVAL_HEADS,),
        in_specs=[
            pl.BlockSpec(head_block, lambda j: (j, 0, 0)),
            pl.BlockSpec(key_block, lambda j: (0, 0, j, 0, 0)),
            pl.BlockSpec(key_block, lambda j: (0, 1, j, 0, 0)),
        ],
        out_specs=[
            pl.BlockSpec(head_block, lambda j: (j, 0, 0)),
            pl.BlockSpec((GROUP, 1, token_positions), lambda j: (j, 0, 0)),
        ],
        out_shape=[
            jax.ShapeDtypeStruct(query.shape, jnp.bfloat16),
            jax.ShapeDtypeStruct((QUERY_HEADS, 1, token_positions), jnp.float32),
        ],
        compiler_params=pltpu.CompilerParams(vmem_limit_bytes=VMEM_LIMIT),
        cost_estimate=pl.CostEstimate(
            flops=16 * HEAD_WIDTH * area, bytes_accessed=6 * query.size, transcendentals=area
        ),
        name="attend_forward",
    )(query, keyval, keyval)


def backward_kernel(
    query_ref, key_ref, value_ref, back_ref, mixed_ref, lse_ref, cosine_ref, sine_ref,
    back_query_ref, back_keyval_ref,
):
    place = lax.axis_index("ctx")
    blocks = key_ref.shape[0]
    queries = [query_ref[g] * jnp.bfloat16(SCALE) for g in range(GROUP)]
    backs = [back_ref[g] for g in range(GROUP)]
    tops = [lse_ref[g] for g in range(GROUP)]
    sums = [
        jnp.sum(backs[g].astype(jnp.float32) * mixed_ref[g].astype(jnp.float32), 0, keepdims=True)
        for g in range(GROUP)
    ]

    def step(block, carried, masked=False):
        keys = key_ref[block, 0, 0]
        keys_turned = keys.T
        values_turned = value_ref[block, 0, 0].T
        back_key = jnp.zeros(keys.shape, jnp.float32)
        back_value = jnp.zeros(keys.shape, jnp.float32)
        later = []
        for g in range(GROUP):
            scores = dot(keys_turned, queries[g], 1, 0)
            if masked:
                scores = causal(scores)
            weights = jnp.exp(scores - tops[g])
            back_weights = dot(values_turned, backs[g], 1, 0)
            back_scores = (weights * (back_weights - sums[g])).astype(jnp.bfloat16)
            later.append(carried[g] + dot(keys, back_scores, 1, 0))
            back_key += dot(queries[g], back_scores, 1, 1)
            back_value += dot(backs[g], weights.astype(jnp.bfloat16), 1, 1)
        back_keyval_ref[block, 0, 0] = back_key.astype(jnp.bfloat16)
        back_keyval_ref[block, 1, 0] = back_value.astype(jnp.bfloat16)
        return tuple(later)

    start = tuple(jnp.zeros(query_ref.shape[1:], jnp.float32) for g in range(GROUP))
    carried = lax.fori_loop(1, place + 1, step, step(0, start, True))

    def clear(block, unused):
        zero = jnp.zeros(key_ref.shape[3:], jnp.bfloat16)
        back_keyval_ref[block, 0, 0] = zero
        back_keyval_ref[block, 1, 0] = zero
        return unused

    lax.fori_loop(place + 1, blocks, clear, 0)
    cosine = cosine_ref[...]
    sine = sine_ref[...]
    for g in range(GROUP):
        leading = carried[g][:HALF] * SCALE
        trailing = carried[g][HALF:] * SCALE
        back_query_ref[g, :HALF] = (leading * cosine + trailing * sine).astype(jnp.bfloat16)
        back_query_ref[g, HALF:] = (trailing * cosine - leading * sine).astype(jnp.bfloat16)


def attend_backward(query, keyval, back_mixed, mixed, lse, cosine, sine, first, count):
    blocks, token_positions = keyval.shape[0], keyval.shape[-1]
    head_block = (GROUP, HEAD_WIDTH, token_positions)
    key_block = (blocks, 1, 1, HEAD_WIDTH, token_positions)
    area = count * GROUP * token_positions * token_positions * blocks
    heads = pl.BlockSpec(head_block, lambda j: (j + first, 0, 0))
    table = pl.BlockSpec((HALF, token_positions), lambda j: (0, 0))
    return pl.pallas_call(
        backward_kernel,
        grid=(count,),
        in_specs=[
            heads,
            pl.BlockSpec(key_block, lambda j: (0, 0, j + first, 0, 0)),
            pl.BlockSpec(key_block, lambda j: (0, 1, j + first, 0, 0)),
            heads,
            heads,
            pl.BlockSpec((GROUP, 1, token_positions), lambda j: (j + first, 0, 0)),
            table,
            table,
        ],
        out_specs=[
            pl.BlockSpec(head_block, lambda j: (j, 0, 0)),
            pl.BlockSpec((blocks, 2, 1, HEAD_WIDTH, token_positions), lambda j: (0, 0, j, 0, 0)),
        ],
        out_shape=[
            jax.ShapeDtypeStruct((count * GROUP, HEAD_WIDTH, token_positions), jnp.bfloat16),
            jax.ShapeDtypeStruct(
                (blocks, 2, count, HEAD_WIDTH, token_positions), jnp.bfloat16
            ),
        ],
        compiler_params=pltpu.CompilerParams(vmem_limit_bytes=VMEM_LIMIT),
        cost_estimate=pl.CostEstimate(
            flops=40 * HEAD_WIDTH * area, bytes_accessed=10 * query.size, transcendentals=area
        ),
        name="attend_backward",
    )(query, keyval, keyval, back_mixed, mixed, lse, cosine, sine)


def move_along(value, distance):
    blocks = lax.axis_size("ctx")
    pairs = [(i, i + distance) for i in range(blocks) if 0 <= i + distance < blocks]
    return lax.ppermute(value, "ctx", pairs)


def trade(value, axis, step):
    pairs = [(i, i ^ step) for i in range(lax.axis_size(axis))]
    return lax.ppermute(value, axis, pairs)


def add_low(left, right):
    return (left.astype(jnp.float32) + right.astype(jnp.float32)).astype(jnp.bfloat16)


def scatter_sum(value, axis):
    size = lax.axis_size(axis)
    index = lax.axis_index(axis)
    rows = value.shape[0] // size
    step = 1
    while step < size:
        count = value.shape[0] // (2 * rows)
        split = value.reshape(count, 2, rows, value.shape[-1])
        second = (index // step) % 2 == 1
        kept = jnp.where(second, split[:, 1], split[:, 0])
        sent = jnp.where(second, split[:, 0], split[:, 1])
        value = add_low(kept, trade(sent, axis, step)).reshape(count * rows, value.shape[-1])
        step *= 2
    return value


def whole_sum(value, others):
    half_rows = value.shape[0] // 2
    second = lax.axis_index("ctx") % 2 == 1
    upper, lower = value[:half_rows], value[half_rows:]
    received = trade(jnp.where(second, upper, lower), "ctx", 1)
    total = add_low(jnp.where(second, lower, upper), received)
    for axis, first_step in others:
        step = first_step
        while step < lax.axis_size(axis):
            total = add_low(total, trade(total, axis, step))
            step *= 2
    received = trade(total, "ctx", 1)
    return jnp.concatenate(
        [jnp.where(second, received, total), jnp.where(second, total, received)], 0
    ).astype(jnp.float32)


MESH = pl.DeviceIdType.MESH
KERNEL_VMEM = 60 * 1024 * 1024
CHUNK_ROWS = 80


def remote(source, target, send_sem, recv_sem, **place):
    return pltpu.make_async_remote_copy(
        src_ref=source, dst_ref=target, send_sem=send_sem, recv_sem=recv_sem,
        device_id=place, device_id_type=MESH,
    )


def wide(value):
    return value.astype(jnp.float32)


def low(value):
    return value.astype(jnp.bfloat16)


def greet(**place):
    pl.semaphore_signal(
        pltpu.get_barrier_semaphore(), inc=1, device_id=place, device_id_type=MESH
    )


def backward_sum_kernel(
    query_ref, keyval_ref, back_ref, mixed_ref, lse_ref, cosine_ref, sine_ref,
    base_ref, feed_ref, normed_ref, gains_ref, gain_two_ref,
    down_ref, gate_ref, up_ref, out_ref, tokens_far, middle_far, query_far, keyval_far,
    share_ref, result_ref, back_tokens_ref, *refs,
):
    chunks_in = 4
    shares, refs = refs[:chunks_in], refs[chunks_in:]
    whole, mate_part, y_part, x_part, z_part = [
        refs[i * chunks_in : (i + 1) * chunks_in] for i in range(5)
    ]
    (
    own, mate_in, y_in, up_in, parts, part_in, back_total, row_sums,
    own_sem, mate_send, mate_recv, y_send, y_recv, up_send, up_recv, down_send, down_recv,
    part_send, part_recv, feed_in, traded, feed_send, feed_recv, trade_send, trade_recv,
    back_query_ref, back_keyval_ref, back_one, token_traded,
    tokens_ref, middle_ref, full_query, full_keyval, far_sem,
    whole_sem, sum_mate_send, sum_mate_recv, sum_y_send, sum_y_recv, sum_x_send, sum_x_recv,
    sum_z_send, sum_z_recv, all_send, all_recv, back_send, back_recv, token_send, token_recv,
    ) = refs[5 * chunks_in :]
    place = lax.axis_index("ctx")
    last = lax.axis_size("ctx") - 1
    blocks = last + 1
    rank = lax.axis_index("fsdp")
    core = rank % 2
    y = rank // 2
    side = lax.axis_index("tp")
    mate = rank + 1 - 2 * core
    across = rank + 2 - 4 * y
    gradients = (down_ref, gate_ref, up_ref)
    rows = share_ref.shape[1]
    per = rows // CHUNK_ROWS
    chunks = len(gradients) * per
    iterations = KEYVAL_HEADS + 2
    early = iterations * blocks // 2 - KEYVAL_HEADS * blocks // 2

    for m, gradient in enumerate(gradients):
        for half in range(2):
            pltpu.make_async_copy(
                gradient.at[2 * half + core], own.at[m, half], own_sem.at[m, half]
            ).start()
    greet(fsdp=mate)
    greet(fsdp=across)
    greet(tp=1 - side)
    far = [
        pltpu.make_async_copy(source, target, far_sem.at[i])
        for i, (source, target) in enumerate((
            (tokens_far, tokens_ref), (middle_far, middle_ref), (query_far, full_query),
            (keyval_far, full_keyval),
        ))
    ]
    for d in range(1, blocks):
        greet(ctx=lax.rem(place + d, blocks))
    filled = out_ref.shape[1]
    tail = whole[0].shape[1] - filled
    for n in range(chunks_in):
        width = whole[n].shape[-1]
        whole[n][:, filled:] = jnp.zeros((whole[n].shape[0], tail, width), jnp.bfloat16)
        mate_part[n][:, filled:] = jnp.zeros((2, tail, width), jnp.bfloat16)
    for f in range(whole[0].shape[0]):
        pltpu.make_async_copy(
            out_ref.at[f], whole[0].at[f, pl.ds(0, filled)], whole_sem.at[f]
        ).start()
    pl.semaphore_wait(pltpu.get_barrier_semaphore(), 3 + last)

    feed_copy = remote(feed_ref, feed_in, feed_send, feed_recv, tp=1 - side)
    trade_copy = remote(traded, result_ref.at[side], trade_send, trade_recv, tp=1 - side)
    feed_copy.start()
    pair_width = traded.shape[-1]
    step_rows = traded.shape[0] // 4

    def finish_result():
        feed_copy.wait_recv()

        def some_rows(i, carry):
            at = pl.ds(pl.multiple_of(i * step_rows, step_rows), step_rows)
            for target, slot in ((result_ref.at[side], side), (traded, 1 - side)):
                columns = pl.ds(pl.multiple_of(slot * pair_width, pair_width), pair_width)
                target[at] = low(base_ref[at, columns] + wide(feed_in[at, columns]))
            return carry

        lax.fori_loop(0, 4, some_rows, 0)
        trade_copy.start()

    half_rows = whole[0].shape[1] // 2
    piece = half_rows // blocks
    kept = 2 * y + core

    def sum_mate(n, half):
        return remote(
            whole[n].at[2 * half + 1 - core, pl.ds(0, filled)],
            mate_part[n].at[half, pl.ds(0, filled)],
            sum_mate_send.at[n, half], sum_mate_recv.at[n, half], fsdp=mate,
        )

    def sum_y(n):
        return remote(
            mate_part[n].at[1 - y], y_part[n], sum_y_send.at[n], sum_y_recv.at[n], fsdp=across
        )

    def sum_x(n):
        other = pl.ds(pl.multiple_of((1 - side) * half_rows, half_rows), half_rows)
        return remote(
            whole[n].at[kept, other], x_part[n], sum_x_send.at[n], sum_x_recv.at[n],
            tp=1 - side,
        )

    def sum_z(n, d):
        target = lax.rem(place + d, blocks)
        at = pl.ds(pl.multiple_of(side * half_rows + target * piece, piece), piece)
        return remote(
            whole[n].at[kept, at], z_part[n].at[d - 1], sum_z_send.at[n, d - 1],
            sum_z_recv.at[n, d - 1], ctx=target,
        )

    def all_copy(n, d, origin):
        spot = shares[n].at[
            pl.ds(pl.multiple_of(side * half_rows + origin * piece, piece), piece)
        ]
        return remote(
            spot, spot, all_send.at[n, d - 1], all_recv.at[n, d - 1],
            ctx=lax.rem(place + d, blocks),
        )

    def back_copy(n, half):
        spot = shares[n].at[pl.ds(pl.multiple_of(half * half_rows, half_rows), half_rows)]
        return remote(spot, spot, back_send.at[n], back_recv.at[n], tp=1 - side)

    def to_mate(n):
        for half in range(2):
            sum_mate(n, half).start()

    def to_y(n):
        for half in range(2):
            sum_mate(n, half).wait_recv()
        quarter = 2 * (1 - y) + core
        mate_part[n][1 - y] = low(wide(whole[n][quarter]) + wide(mate_part[n][1 - y]))
        sum_y(n).start()

    def to_x(n):
        sum_y(n).wait_recv()
        whole[n][kept] = low(
            wide(whole[n][kept]) + wide(mate_part[n][y]) + wide(y_part[n][...])
        )
        sum_x(n).start()

    def to_z(n):
        sum_x(n).wait_recv()
        at = pl.ds(pl.multiple_of(side * half_rows, half_rows), half_rows)
        whole[n][kept, at] = low(wide(whole[n][kept, at]) + wide(x_part[n][...]))
        for d in range(1, blocks):
            sum_z(n, d).start()

    def to_all(n):
        at = pl.ds(pl.multiple_of(side * half_rows + place * piece, piece), piece)
        total = wide(whole[n][kept, at])
        for d in range(1, blocks):
            sum_z(n, d).wait_recv()
            total += wide(z_part[n][d - 1])
        shares[n][at] = low(total)
        for d in range(1, blocks):
            all_copy(n, d, place).start()

    def to_back(n):
        for d in range(1, blocks):
            all_copy(n, d, lax.rem(place + blocks - d, blocks)).wait_recv()
        back_copy(n, side).start()

    def finish_sum(n):
        back_copy(n, 1 - side).wait_recv()
        for half in range(2):
            sum_mate(n, half).wait_send()
        sum_y(n).wait_send()
        sum_x(n).wait_send()
        for d in range(1, blocks):
            sum_z(n, d).wait_send()
            all_copy(n, d, place).wait_send()
        back_copy(n, side).wait_send()

    def weight_gradient(n, back_ref):
        def quarter(f, carry):
            rows_of = normed_ref[pl.ds(pl.multiple_of(f * filled, filled), filled)]
            whole[n][f, :filled] = low(dot(rows_of, back_ref[...], 1, 1))
            return carry

        lax.fori_loop(0, whole[n].shape[0], quarter, 0)

    token_copy = remote(
        token_traded, back_tokens_ref.at[side], token_send, token_recv, tp=1 - side
    )

    def input_gradient():
        for copy in far:
            copy.wait()
        tokens = wide(tokens_ref[...])
        inverse = lax.rsqrt(jnp.mean(tokens * tokens, 0, keepdims=True) + EPS)

        def quarter(f, total):
            at = pl.ds(pl.multiple_of(f * filled, filled), filled)
            unit = wide(tokens_ref[at]) * inverse
            back = dot(full_query[at], back_query_ref[...], 1, 0) + dot(
                full_keyval[at], back_keyval_ref[...], 1, 0
            )
            gain_sum = jnp.sum(back * unit, 1, keepdims=True)
            lane = lax.broadcasted_iota(jnp.int32, (filled, whole[3].shape[-1]), 1)
            whole[3][f, :filled] = low(
                jnp.where(lane == 0, gain_sum, jnp.where(lane == 1, gain_two_ref[at], 0.0))
            )
            back = back * wide(gains_ref[at])[:, :1]
            back_one[at] = back
            return total + jnp.sum(back * unit, 0, keepdims=True)

        total = lax.fori_loop(
            0, whole[0].shape[0], quarter, jnp.zeros((1, tokens_ref.shape[-1]), jnp.float32)
        )
        to_mate(3)
        mean = total / tokens_ref.shape[0]

        def rows_back(f, carry):
            at = pl.ds(pl.multiple_of(f * filled, filled), filled)
            unit = wide(tokens_ref[at]) * inverse
            back_one[at] = middle_ref[at] + inverse * (back_one[at] - unit * mean)
            for target, slot in ((back_tokens_ref.at[side], side), (token_traded, 1 - side)):
                columns = pl.ds(pl.multiple_of(slot * pair_width, pair_width), pair_width)
                target[at] = low(back_one[at, columns])
            return carry

        lax.fori_loop(0, whole[0].shape[0], rows_back, 0)

    def chunk_at(ref, m, r, *front):
        return ref.at[(m,) + front + (pl.ds(r * CHUNK_ROWS, CHUNK_ROWS),)]

    def mate_copy(m, r, half):
        gradient = gradients[m]
        return remote(
            gradient.at[2 * half + 1 - core, pl.ds(r * CHUNK_ROWS, CHUNK_ROWS)],
            chunk_at(mate_in, m, r, half),
            mate_send.at[m * per + r, half], mate_recv.at[m * per + r, half], fsdp=mate,
        )

    for m in range(len(gradients)):
        for r in range(per):
            for half in range(2):
                mate_copy(m, r, half).start()
    for f in range(whole[0].shape[0]):
        pltpu.make_async_copy(
            out_ref.at[f], whole[0].at[f, pl.ds(0, filled)], whole_sem.at[f]
        ).wait()
    to_mate(0)
    for copy in far:
        copy.start()
    for m, gradient in enumerate(gradients):
        for half in range(2):
            pltpu.make_async_copy(
                gradient.at[2 * half + core], own.at[m, half], own_sem.at[m, half]
            ).wait()

    def split(k):
        r = lax.rem(k, per)
        return k // per, pl.ds(pl.multiple_of(r * CHUNK_ROWS, CHUNK_ROWS), CHUNK_ROWS)

    def y_copy(k):
        m, at = split(k)
        return remote(
            own.at[m, 1 - y, at], y_in.at[m, at], y_send.at[k], y_recv.at[k], fsdp=across
        )

    def up_copy(k):
        m, at = split(k)
        return remote(
            own.at[m, y, at], up_in.at[m, at], up_send.at[k], up_recv.at[k], ctx=place + 1
        )

    def down_copy(k):
        m, at = split(k)
        return remote(
            share_ref.at[m, at], share_ref.at[m, at], down_send.at[k], down_recv.at[k],
            ctx=place - 1,
        )

    def to_across(k):
        m, at = split(k)
        for half in range(2):
            pltpu.make_async_copy(
                mate_in.at[m, half, at], mate_in.at[m, half, at], mate_recv.at[k, half]
            ).wait()
        own[m, 1 - y, at] = low(wide(own[m, 1 - y, at]) + wide(mate_in[m, 1 - y, at]))
        y_copy(k).start()

    def to_next(k):
        m, at = split(k)
        y_copy(k).wait_recv()
        total = wide(own[m, y, at]) + wide(mate_in[m, y, at]) + wide(y_in[m, at])

        @pl.when(place == 0)
        def _():
            own[m, y, at] = low(total)

        @pl.when(place > 0)
        def _():
            up_copy(k).wait_recv()
            own[m, y, at] = low(total + wide(up_in[m, at]))

        @pl.when(place < last)
        def _():
            up_copy(k).start()

        @pl.when(place == last)
        def _():
            share_ref[m, at] = own[m, y, at]

    def give_back(k):
        @pl.when(place < last)
        def _():
            down_copy(k).wait_recv()

        @pl.when(place > 0)
        def _():
            down_copy(k).start()

    def query_gradient(n):
        weight_gradient(n, back_query_ref)
        to_mate(n)

    def tick(t):
        h = t - last - 2 * (last - place)

        @pl.when((h >= 0) & (h < KEYVAL_HEADS * blocks) & (lax.rem(h, blocks) == 0))
        def _():
            hand_on(h // blocks)

        @pl.when(t < chunks)
        def _():
            to_across(t)

        @pl.when(t == chunks + 1)
        def _():
            finish_result()

        b = t - 4 - 2 * place

        @pl.when((b >= 0) & (b < 2 * chunks) & (lax.rem(b, 2) == 0))
        def _():
            to_next(b // 2)

        c = t - KEYVAL_HEADS * blocks - 2 * (last - place)

        @pl.when((c >= 0) & (c < 2 * chunks) & (lax.rem(c, 2) == 0))
        def _():
            give_back(c // 2)

        for at, stage, n in (
            (4, to_y, 0), (15, to_x, 0), (18, to_z, 0), (20, query_gradient, 1),
            (20, to_all, 0), (21, to_y, 1), (22, to_back, 0), (24, to_x, 1), (26, to_z, 1),
        ):
            @pl.when(t == at)
            def _(stage=stage, n=n):
                stage(n)

    def part_copy(j, s):
        return remote(
            parts.at[j, s], part_in.at[j, s - 1], part_send.at[j, s - 1],
            part_recv.at[j, s - 1], ctx=place - 1,
        )

    def step(j, s, masked):
        keys = keyval_ref[s, j, 0]
        keys_turned = keys.T
        values_turned = keyval_ref[s, j, 1].T
        back_key = jnp.zeros(keys.shape, jnp.float32)
        back_value = jnp.zeros(keys.shape, jnp.float32)
        for g in range(GROUP):
            head = GROUP * j + g
            query = query_ref[head]
            back = back_ref[head]
            if masked:
                row_sums[g] = jnp.sum(wide(back) * wide(mixed_ref[head]), 0, keepdims=True)
            scores = dot(keys_turned, query, 1, 0)
            if masked:
                scores = causal(scores)
            weights = jnp.exp(scores - lse_ref[head])
            back_weights = dot(values_turned, back, 1, 0)
            back_scores = low(weights * (back_weights - row_sums[g]))
            added = dot(keys, back_scores, 1, 0)
            if masked:
                back_total[g] = added
            else:
                back_total[g] += added
            back_key += dot(query, back_scores, 1, 1)
            back_value += dot(back, low(weights), 1, 1)
        parts[j, s, 0] = low(back_key)
        parts[j, s, 1] = low(back_value)
        if not masked:
            @pl.when(place == last)
            def _():
                part_copy(j, s).start()

    def hand_on(j):
        for s in range(blocks):
            @pl.when(s <= place)
            def _(s=s):
                @pl.when(place < last)
                def _():
                    pltpu.make_async_copy(
                        part_in.at[j, s], part_in.at[j, s], part_recv.at[j, s]
                    ).wait()
                    for kind in range(2):
                        total = wide(parts[j, s, kind]) + wide(part_in[j, s, kind])
                        parts[j, s, kind] = low(total)

                if s > 0:
                    @pl.when(place < last)
                    def _():
                        part_copy(j, s).start()
                else:
                    leading = wide(parts[j, 0, 0, :HALF])
                    trailing = wide(parts[j, 0, 0, HALF:])
                    cosine, sine = cosine_ref[...], sine_ref[...]
                    at = j * HEAD_WIDTH
                    back_keyval_ref[pl.ds(pl.multiple_of(at, HALF), HALF)] = low(
                        leading * cosine + trailing * sine
                    )
                    back_keyval_ref[pl.ds(pl.multiple_of(at + HALF, HALF), HALF)] = low(
                        trailing * cosine - leading * sine
                    )
                    at = pl.ds(pl.multiple_of(KEY_WIDTH + at, HEAD_WIDTH), HEAD_WIDTH)
                    back_keyval_ref[at] = low(wide(parts[j, 0, 1]))

    def head_loop(j, carry):
        @pl.when(j < KEYVAL_HEADS)
        def _():
            step(j, 0, True)

        tick(j * blocks)

        def block_loop(s, inner):
            @pl.when((j < KEYVAL_HEADS) & (s <= place))
            def _():
                step(j, s, False)

            tick(j * blocks + s)
            return inner

        lax.fori_loop(1, blocks, block_loop, 0)

        @pl.when(j < KEYVAL_HEADS)
        def _():
            cosine, sine = cosine_ref[...], sine_ref[...]
            for g in range(GROUP):
                leading = back_total[g, :HALF] * SCALE
                trailing = back_total[g, HALF:] * SCALE
                at = (GROUP * j + g) * HEAD_WIDTH
                back_query_ref[pl.ds(pl.multiple_of(at, HALF), HALF)] = low(
                    leading * cosine + trailing * sine
                )
                back_query_ref[pl.ds(pl.multiple_of(at + HALF, HALF), HALF)] = low(
                    trailing * cosine - leading * sine
                )

        return carry

    assert iterations * blocks > 4 + 2 * last + 2 * (chunks - 1)
    lax.fori_loop(0, iterations, head_loop, 0)

    def start_tokens(n):
        token_copy.start()

    def keyval_gradient(n):
        weight_gradient(n, back_keyval_ref)
        to_mate(n)

    later = (
        ((keyval_gradient, 2), (to_y, 2)), ((to_all, 1),), ((lambda n: input_gradient(), 3),),
        ((to_y, 3), (to_x, 2), (to_back, 1)), ((to_x, 3), (to_z, 2), (start_tokens, 3)),
        ((to_all, 2), (to_z, 3)), ((to_back, 2), (to_all, 3)), ((to_back, 3),),
    )
    for slot, stages in enumerate(later):
        for stage, n in stages:
            stage(n)
        for index in range(blocks):
            if early + slot - last + index < chunks:
                @pl.when(place == index)
                def _(k=early + slot - last + index):
                    give_back(k)

    assert early >= last and len(later) >= chunks - early + last
    for n in range(chunks_in):
        finish_sum(n)
    token_copy.wait()

    for m in range(len(gradients)):
        for r in range(per):
            for half in range(2):
                mate_copy(m, r, half).wait_send()

    def finish(k, carry):
        y_copy(k).wait_send()

        @pl.when(place < last)
        def _():
            up_copy(k).wait_send()

        @pl.when(place > 0)
        def _():
            down_copy(k).wait_send()

        return carry

    lax.fori_loop(0, chunks, finish, 0)

    def finish_parts(j, carry):
        for s in range(1, blocks):
            @pl.when(s <= place)
            def _(s=s):
                part_copy(j, s).wait_send()
        return carry

    lax.fori_loop(0, KEYVAL_HEADS, finish_parts, 0)
    feed_copy.wait_send()
    trade_copy.wait()


def backward_sum(
    query, keyval, back_mixed, mixed, lse, cosine, sine, base, feed, tokens, normed, middle,
    gains, gain_two, full_query, full_keyval, gradients, gradient_out,
):
    blocks, positions = keyval.shape[0], keyval.shape[-1]
    count, rows, columns = gradients[0].shape
    chunks = len(gradients) * rows // CHUNK_ROWS
    area = QUERY_HEADS * positions * positions * blocks
    vmem = pl.BlockSpec(memory_space=pltpu.VMEM)
    anywhere = pl.BlockSpec(memory_space=pl.ANY)
    dma = pltpu.SemaphoreType.DMA
    share = (len(gradients), rows, columns)
    head = (2, HEAD_WIDTH, positions)
    features = feed.shape[0]
    widths = (QUERY_WIDTH, QUERY_WIDTH, 2 * KEY_WIDTH, gains.shape[-1])
    padded = rows + 16
    half_rows = padded // 2
    low_type = jnp.bfloat16
    scratch = []
    for first in ((count, padded), (2, padded), (padded,), (half_rows,),
                  (blocks - 1, half_rows // blocks)):
        scratch += [pltpu.VMEM(first + (w,), low_type) for w in widths]
    each = len(widths)
    pairs = jax.ShapeDtypeStruct((2, features, positions // 2), low_type)
    return pl.pallas_call(
        backward_sum_kernel,
        in_specs=[vmem] * 12 + [anywhere] * 8,
        out_specs=[vmem] * (3 + each),
        out_shape=[jax.ShapeDtypeStruct(share, low_type), pairs, pairs] + [
            jax.ShapeDtypeStruct((padded, w), low_type) for w in widths
        ],
        scratch_shapes=scratch + [
            pltpu.VMEM((len(gradients), 2, rows, columns), low_type),
            pltpu.VMEM((len(gradients), 2, rows, columns), low_type),
            pltpu.VMEM(share, low_type),
            pltpu.VMEM(share, low_type),
            pltpu.VMEM((KEYVAL_HEADS, blocks) + head, low_type),
            pltpu.VMEM((KEYVAL_HEADS, blocks - 1) + head, low_type),
            pltpu.VMEM((GROUP, HEAD_WIDTH, positions), jnp.float32),
            pltpu.VMEM((GROUP, 1, positions), jnp.float32),
            dma((len(gradients), 2)),
            dma((chunks, 2)), dma((chunks, 2)),
            dma((chunks,)), dma((chunks,)),
            dma((chunks,)), dma((chunks,)),
            dma((chunks,)), dma((chunks,)),
            dma((KEYVAL_HEADS, blocks - 1)), dma((KEYVAL_HEADS, blocks - 1)),
            pltpu.VMEM(feed.shape, low_type),
            pltpu.VMEM((features, positions // 2), low_type),
            dma, dma, dma, dma,
            pltpu.VMEM((QUERY_WIDTH, positions), low_type),
            pltpu.VMEM((2 * KEY_WIDTH, positions), low_type),
            pltpu.VMEM((features, positions), jnp.float32),
            pltpu.VMEM((features, positions // 2), low_type),
            pltpu.VMEM(tokens.shape, low_type),
            pltpu.VMEM(middle.shape, jnp.float32),
            pltpu.VMEM(full_query.shape, low_type),
            pltpu.VMEM(full_keyval.shape, low_type),
            dma((4,)),
            dma((count,)),
            dma((each, 2)), dma((each, 2)),
            dma((each,)), dma((each,)),
            dma((each,)), dma((each,)),
            dma((each, blocks - 1)), dma((each, blocks - 1)),
            dma((each, blocks - 1)), dma((each, blocks - 1)),
            dma((each,)), dma((each,)),
            dma, dma,
        ],
        compiler_params=pltpu.CompilerParams(
            vmem_limit_bytes=KERNEL_VMEM, collective_id=0, has_side_effects=True
        ),
        cost_estimate=pl.CostEstimate(
            flops=40 * HEAD_WIDTH * area, bytes_accessed=10 * query.size, transcendentals=area
        ),
        name="backward_sum",
    )(
        query, keyval, back_mixed, mixed, lse, cosine, sine, base, feed, normed, gains, gain_two,
        *gradients, gradient_out, tokens, middle, full_query, full_keyval,
    )


def front_kernel(
    tokens_ref, cotangent_ref, cosine_ref, sine_ref, *refs
):
    weights, refs = refs[:7], refs[7:]
    (
        tokens_own, cotangent_own, cotangent_other, normed_out, query_out, keyval_ref,
        mixed_out, lse_ref, tokens_other, mixed_other,
    ), refs = refs[:10], refs[10:]
    full, refs = refs[:7], refs[7:]
    (
        raw, tops, totals, sums,
        local_sem, token_send, token_recv, cot_send, cot_recv,
        y_send, y_recv, mate_send, mate_recv, pass_send, pass_recv, key_send, key_recv,
        mixed_send, mixed_recv,
    ) = refs
    place = lax.axis_index("ctx")
    last = lax.axis_size("ctx") - 1
    rank = lax.axis_index("fsdp")
    side = lax.axis_index("tp")
    core = rank % 2
    mate = rank + 1 - 2 * core
    across = rank + 2 - 4 * (rank // 2)
    width = tokens_ref.shape[-1]

    def columns(ref, slot):
        return ref.at[:, pl.ds(pl.multiple_of(slot * width, width), width)]

    local = [
        pltpu.make_async_copy(tokens_ref.at[side], columns(tokens_own, side), local_sem.at[0]),
        pltpu.make_async_copy(
            cotangent_ref.at[side], columns(cotangent_own, side), local_sem.at[1]
        ),
        pltpu.make_async_copy(
            cotangent_ref.at[1 - side], columns(cotangent_other, side), local_sem.at[2]
        ),
        pltpu.make_async_copy(
            tokens_ref.at[1 - side], columns(tokens_other, side), local_sem.at[3]
        ),
    ]
    for w in range(len(weights)):
        local.append(pltpu.make_async_copy(weights[w], full[w].at[rank], local_sem.at[4 + w]))
    for copy in local:
        copy.start()

    greet(fsdp=mate)
    greet(fsdp=across)
    greet(tp=1 - side)

    @pl.when(place > 0)
    def _():
        greet(ctx=place - 1)

    @pl.when(place < last)
    def _():
        greet(ctx=place + 1)

    neighbours = (place + last - 1) // last + (2 * last - place - 1) // last
    pl.semaphore_wait(pltpu.get_barrier_semaphore(), 3 + neighbours)

    token_copy = remote(
        tokens_ref.at[1 - side], columns(tokens_own, side), token_send, token_recv, tp=1 - side
    )
    cot_copies = [
        remote(
            cotangent_ref.at[1 - side], columns(cotangent_own, side), cot_send.at[0],
            cot_recv.at[0], tp=1 - side,
        ),
        remote(
            cotangent_ref.at[side], columns(cotangent_other, side), cot_send.at[1],
            cot_recv.at[1], tp=1 - side,
        ),
        remote(
            tokens_ref.at[side], columns(tokens_other, side), cot_send.at[2], cot_recv.at[2],
            tp=1 - side,
        ),
    ]

    def mixed_copy(j):
        heads = pl.ds(GROUP * j, GROUP)
        return remote(
            mixed_out.at[heads], mixed_other.at[heads], mixed_send.at[j], mixed_recv.at[j],
            tp=1 - side,
        )


    def y_copy(w):
        return remote(
            weights[w], full[w].at[rank], y_send.at[w], y_recv.at[w], fsdp=across
        )

    def mate_copy(w):
        return remote(
            weights[w], full[w].at[rank], mate_send.at[w], mate_recv.at[w], fsdp=mate
        )

    def pass_copy(w):
        return remote(
            full[w].at[across], full[w].at[across], pass_send.at[w], pass_recv.at[w], fsdp=mate
        )

    def arrived(w):
        local[4 + w].wait()
        mate_copy(w).wait_recv()
        pass_copy(w).wait_recv()

    for w in (6, 1):
        y_copy(w).start()
        mate_copy(w).start()
    token_copy.start()
    for w in (0, 2, 3, 4, 5):
        y_copy(w).start()
        mate_copy(w).start()
    y_copy(6).wait_recv()
    pass_copy(6).start()
    arrived(6)
    gain = wide(full[6][...].reshape(-1, full[6].shape[-1])[:, :1])

    def norm_rows(slot):
        at = pl.ds(pl.multiple_of(slot * width, width), width)
        rows = wide(tokens_own[:, at])
        inverse = lax.rsqrt(jnp.mean(rows * rows, 0, keepdims=True) + EPS)
        normed_out[:, at] = low(rows * inverse * gain)

    local[0].wait()
    norm_rows(side)
    token_copy.wait_recv()
    norm_rows(1 - side)
    for copy in cot_copies:
        copy.start()
    for w in (1, 0):
        y_copy(w).wait_recv()
        pass_copy(w).start()
    normed = normed_out[...]
    cosine, sine = cosine_ref[...], sine_ref[...]

    def turned(value, target):
        target[:HALF] = low(value[:HALF] * cosine - value[HALF:] * sine)
        target[HALF:] = low(value[HALF:] * cosine + value[:HALF] * sine)

    def key_copy(s, j):
        return remote(
            keyval_ref.at[s, j], keyval_ref.at[s + 1, j], key_send.at[s, j], key_recv.at[s, j],
            ctx=place + 1,
        )

    arrived(1)
    matrix = full[1][...].reshape(-1, 2 * KEY_WIDTH)
    raw[: 2 * KEY_WIDTH] = dot(matrix, normed, 0, 0)
    for j in range(KEYVAL_HEADS):
        turned(raw[j * HEAD_WIDTH : (j + 1) * HEAD_WIDTH], keyval_ref.at[0, j, 0])
        first = KEY_WIDTH + j * HEAD_WIDTH
        keyval_ref[0, j, 1] = low(raw[first : first + HEAD_WIDTH])

        if j == 0:
            @pl.when(place < last)
            def _():
                key_copy(0, 0).start()

    arrived(0)
    matrix = full[0][...].reshape(-1, QUERY_WIDTH)
    raw[...] = dot(matrix, normed, 0, 0)

    def turn_query(h, carry):
        value = raw[pl.ds(pl.multiple_of(h * HEAD_WIDTH, HEAD_WIDTH), HEAD_WIDTH)]
        first = low(value[:HALF] * cosine - value[HALF:] * sine)
        second = low(value[HALF:] * cosine + value[:HALF] * sine)
        query_out[h, :HALF] = first * jnp.bfloat16(SCALE)
        query_out[h, HALF:] = second * jnp.bfloat16(SCALE)
        return carry

    lax.fori_loop(0, QUERY_HEADS, turn_query, 0)

    def attend(s, j, masked):
        keys_turned = keyval_ref[s, j, 0].T
        values = keyval_ref[s, j, 1]
        for g in range(GROUP):
            head = GROUP * j + g
            scores = dot(keys_turned, query_out[head], 1, 0)
            if masked:
                scores = causal(scores)
                top = jnp.max(scores, 0, keepdims=True)
                lifted = jnp.exp(scores - top)
                tops[head] = top
                totals[head] = jnp.sum(lifted, 0, keepdims=True)
                sums[head] = dot(values, low(lifted), 1, 0)
            else:
                old = tops[head]
                top = jnp.maximum(old, jnp.max(scores, 0, keepdims=True))
                lifted = jnp.exp(scores - top)
                shrink = jnp.exp(old - top)
                tops[head] = top
                totals[head] = totals[head] * shrink + jnp.sum(lifted, 0, keepdims=True)
                sums[head] = sums[head] * shrink + dot(values, low(lifted), 1, 0)

    def hand_on(s, j):
        @pl.when(s < place)
        def _():
            pltpu.make_async_copy(
                keyval_ref.at[s + 1, j], keyval_ref.at[s + 1, j], key_recv.at[s, j]
            ).wait()

            @pl.when(place < last)
            def _():
                key_copy(s + 1, j).start()

    def finish_heads(j):
        for g in range(GROUP):
            head = GROUP * j + g
            total = totals[head]
            mixed_out[head] = low(sums[head] / total)
            lse_ref[head] = tops[head] + jnp.log(total)
        mixed_copy(j).start()

    def one_head(j, carry):
        @pl.when((place < last) & (j + 1 < KEYVAL_HEADS))
        def _():
            key_copy(0, j + 1).start()

        attend(0, j, True)
        hand_on(0, j)

        def later_block(s, inner):
            attend(s, j, False)
            hand_on(s, j)
            return inner

        lax.fori_loop(1, place + 1, later_block, 0)
        finish_heads(j)
        return carry

    lax.fori_loop(0, KEYVAL_HEADS, one_head, 0)
    passed = 2

    for w in range(passed, 6):
        y_copy(w).wait_recv()
        pass_copy(w).start()
    for copy in local[1:4]:
        copy.wait()
    for j in range(KEYVAL_HEADS):
        mixed_copy(j).wait()
    token_copy.wait_send()
    for copy in cot_copies:
        copy.wait()
    for w in range(passed, 6):
        arrived(w)
    for w in range(len(weights)):
        y_copy(w).wait_send()
        mate_copy(w).wait_send()
        pass_copy(w).wait_send()

    @pl.when(place < last)
    def _():
        def sent(i, carry):
            key_copy(i // KEYVAL_HEADS, lax.rem(i, KEYVAL_HEADS)).wait_send()
            return carry

        lax.fori_loop(0, (place + 1) * KEYVAL_HEADS, sent, 0)


def front(tokens, cotangent, cosine, sine, weights):
    blocks = lax.axis_size("ctx")
    parts = lax.axis_size("fsdp")
    positions = cosine.shape[-1]
    vmem = pl.BlockSpec(memory_space=pltpu.VMEM)
    anywhere = pl.BlockSpec(memory_space=pl.ANY)
    dma = pltpu.SemaphoreType.DMA
    shape = lambda *dims: jax.ShapeDtypeStruct(dims, jnp.bfloat16)
    count = len(weights)
    features = tokens.shape[1]
    area = QUERY_HEADS * positions * positions * blocks
    return pl.pallas_call(
        front_kernel,
        in_specs=[vmem] * (4 + count),
        out_specs=[vmem] * 12 + [anywhere] * 4 + [vmem],
        out_shape=[
            shape(features, positions), shape(features, positions), shape(features, positions),
            shape(features, positions),
            shape(QUERY_HEADS, HEAD_WIDTH, positions),
            shape(blocks, KEYVAL_HEADS, 2, HEAD_WIDTH, positions),
            shape(QUERY_HEADS, HEAD_WIDTH, positions),
            jax.ShapeDtypeStruct((QUERY_HEADS, 1, positions), jnp.float32),
            shape(features, positions),
            shape(QUERY_HEADS, HEAD_WIDTH, positions),
        ] + [shape(parts, *w.shape) for w in weights],
        scratch_shapes=[
            pltpu.VMEM((QUERY_WIDTH, positions), jnp.float32),
            pltpu.VMEM((QUERY_HEADS, 1, positions), jnp.float32),
            pltpu.VMEM((QUERY_HEADS, 1, positions), jnp.float32),
            pltpu.VMEM((QUERY_HEADS, HEAD_WIDTH, positions), jnp.float32),
            dma((4 + count,)),
            dma, dma,
            dma((3,)), dma((3,)),
            dma((count,)), dma((count,)),
            dma((count,)), dma((count,)),
            dma((count,)), dma((count,)),
            dma((blocks, KEYVAL_HEADS)), dma((blocks, KEYVAL_HEADS)),
            dma((KEYVAL_HEADS,)), dma((KEYVAL_HEADS,)),
        ],
        compiler_params=pltpu.CompilerParams(
            vmem_limit_bytes=KERNEL_VMEM, collective_id=1, has_side_effects=True
        ),
        cost_estimate=pl.CostEstimate(
            flops=16 * HEAD_WIDTH * area, bytes_accessed=10 * tokens.size, transcendentals=area
        ),
        name="front",
    )(tokens, cotangent, cosine, sine, *weights)


def on_device(
    tokens, cotangent, input_gain, w_query, w_keyval, w_output, middle_gain, w_gate, w_up, w_down
):
    half = lax.axis_index("tp")
    low_half = half == 0
    pair = [(0, 1), (1, 0)]

    def to_partner(value_rows):
        return lax.ppermute(value_rows, "tp", pair)

    def in_order(mine, received):
        return jnp.concatenate(
            [jnp.where(low_half, mine, received), jnp.where(low_half, received, mine)], 0
        )

    def take(value_rows, index):
        return lax.dynamic_index_in_dim(value_rows, index, 0, keepdims=False)

    tokens_own = in_order(take(tokens, half), to_partner(take(tokens, 1 - half)))
    full_gain_one, full_gain_two = (
        lax.all_gather(input_gain, "fsdp", axis=0, tiled=True),
        lax.all_gather(middle_gain, "fsdp", axis=0, tiled=True),
    )
    full_in = lax.all_gather(jnp.concatenate([w_query, w_keyval], 1), "fsdp", axis=0, tiled=True)
    full_output = lax.all_gather(w_output, "fsdp", axis=0, tiled=True)
    full_gate = lax.all_gather(w_gate, "fsdp", axis=0, tiled=True)
    full_up = lax.all_gather(w_up, "fsdp", axis=0, tiled=True)
    full_down = lax.all_gather(w_down, "fsdp", axis=0, tiled=True)
    cotangent_received = to_partner(cotangent)
    cotangent_own = in_order(take(cotangent, half), take(cotangent_received, half))
    cotangent_other = in_order(take(cotangent, 1 - half), take(cotangent_received, 1 - half))

    token_positions = tokens_own.shape[0]
    cosine, sine = rope_tables(token_positions, lax.axis_index("ctx") * token_positions)
    gain_one = full_gain_one.astype(jnp.float32)
    inputs = tokens_own.astype(jnp.float32)
    unit_one, inverse_one = normalize(inputs)
    normed_one = (unit_one * gain_one).astype(jnp.bfloat16)
    keyval_raw = dot(full_in[:, QUERY_WIDTH:], normed_one, 0, 1)
    keyval_low = jnp.concatenate(
        [apply_rotary(keyval_raw[:KEY_WIDTH], cosine, sine), keyval_raw[KEY_WIDTH:]], 0
    ).astype(jnp.bfloat16)
    blocks = lax.axis_size("ctx")
    keyval = jnp.stack([keyval_low] + [move_along(keyval_low, s) for s in range(1, blocks)], 0)
    keyval = keyval.reshape(blocks, 2, KEYVAL_HEADS, HEAD_WIDTH, token_positions)
    query_raw = dot(full_in[:, :QUERY_WIDTH], normed_one, 0, 1)
    query_low = (
        apply_rotary(query_raw, cosine, sine)
        .astype(jnp.bfloat16)
        .reshape(QUERY_HEADS, HEAD_WIDTH, token_positions)
    )
    mixed_heads, lse = attend_forward(query_low, keyval)
    mixed_low = mixed_heads.reshape(QUERY_WIDTH, token_positions)
    middle = inputs + dot(mixed_low, full_output, 0, 0)

    gain_two = full_gain_two.astype(jnp.float32)
    unit_two, inverse_two = normalize(middle)
    normed_two = (unit_two * gain_two).astype(jnp.bfloat16)
    normed_other = to_partner(normed_two)

    def feed(rows, back_rows):
        gate_proj = dot(rows, full_gate, 1, 0)
        up_proj = dot(rows, full_up, 1, 0)
        sigmoid_gate = jax.nn.sigmoid(gate_proj)
        swish_gate = gate_proj * sigmoid_gate
        hidden = (swish_gate * up_proj).astype(jnp.bfloat16)
        back_hidden = dot(back_rows, full_down, 1, 0)
        back_gate = (
            back_hidden * up_proj * sigmoid_gate * (1.0 + gate_proj * (1.0 - sigmoid_gate))
        ).astype(jnp.bfloat16)
        back_up = (back_hidden * swish_gate).astype(jnp.bfloat16)
        return (hidden, back_gate, back_up)

    def feed_input_back(back_gate, back_up):
        return dot(back_gate, full_gate, 1, 1) + dot(back_up, full_up, 1, 1)

    hidden_own, back_gate_own, back_up_own = feed(normed_two, cotangent_own)
    hidden_other, back_gate_other, back_up_other = feed(normed_other, cotangent_other)
    back_two_received = to_partner(
        feed_input_back(back_gate_other, back_up_other).astype(jnp.bfloat16)
    )
    back_two = feed_input_back(back_gate_own, back_up_own) + back_two_received.astype(jnp.float32)
    feed_received = to_partner(dot(hidden_other, full_down, 1, 1).astype(jnp.bfloat16))
    result_own = (
        middle + dot(hidden_own, full_down, 1, 1) + feed_received.astype(jnp.float32)
    ).astype(jnp.bfloat16)

    def feed_gradient(left_own, right_own, left_other, right_other):
        gradient = dot(left_own, right_own, 0, 0) + dot(left_other, right_other, 0, 0)
        shared = scatter_sum(gradient.astype(jnp.bfloat16), "fsdp")
        return whole_sum(shared, (("ctx", 2),))

    share_down = feed_gradient(cotangent_own, hidden_own, cotangent_other, hidden_other)
    share_gate = feed_gradient(normed_two, back_gate_own, normed_other, back_gate_other)
    share_up = feed_gradient(normed_two, back_up_own, normed_other, back_up_other)

    grad_gain_two = jnp.sum(back_two * unit_two, axis=0)
    back_middle = cotangent_own.astype(jnp.float32) + norm_back(
        back_two * gain_two, unit_two, inverse_two
    )
    back_attention = back_middle.astype(jnp.bfloat16)
    back_mixed = dot(full_output, back_attention, 1, 1).astype(jnp.bfloat16)
    back_mixed = back_mixed.reshape(query_low.shape)
    grad_output = dot(mixed_low, back_attention, 1, 0).astype(jnp.bfloat16)
    share_output = whole_sum(scatter_sum(grad_output, "fsdp"), (("tp", 1), ("ctx", 2)))

    back_query = []
    back_key = []
    back_value = []
    for first, count in ((0, 3), (3, 2)):
        part_query, part_keyval = attend_backward(
            query_low, keyval, back_mixed, mixed_heads, lse, cosine, sine, first, count
        )
        part_keyval = part_keyval.reshape(blocks, 2 * count * HEAD_WIDTH, token_positions)
        owned = part_keyval[0].astype(jnp.float32)
        for s in range(1, blocks):
            owned += move_along(part_keyval[s], -s).astype(jnp.float32)
        back_query.append(part_query.reshape(-1, token_positions))
        back_key.append(
            apply_rotary(owned[: count * HEAD_WIDTH], cosine, -sine).astype(jnp.bfloat16)
        )
        back_value.append(owned[count * HEAD_WIDTH :].astype(jnp.bfloat16))
    back_in = jnp.concatenate(back_query + back_key + back_value, 0)
    grad_in = dot(normed_one, back_in, 0, 1)
    back_one = dot(back_in, full_in, 0, 1)
    grad_gain_one = jnp.sum(back_one * unit_one, axis=0)
    back_inputs = back_middle + norm_back(back_one * gain_one, unit_one, inverse_one)

    def to_positions(value_rows):
        split = value_rows.reshape(2, token_positions // 2, value_rows.shape[-1])
        received = to_partner(take(split, 1 - half))
        return in_order(take(split, half)[None], received[None])

    result = to_positions(result_own)
    grad_tokens = to_positions(back_inputs.astype(jnp.bfloat16)).astype(jnp.float32)
    gradients = jnp.concatenate([grad_in, grad_gain_one[:, None], grad_gain_two[:, None]], 1)
    share_in = lax.psum(
        lax.psum_scatter(
            gradients.astype(jnp.bfloat16), "fsdp", scatter_dimension=0, tiled=True
        ),
        ("ctx", "tp"),
    ).astype(jnp.float32)
    width = full_in.shape[1]
    return (
        result,
        grad_tokens,
        share_in[:, width],
        share_in[:, :QUERY_WIDTH],
        share_in[:, QUERY_WIDTH:width],
        share_output,
        share_in[:, width + 1],
        share_gate,
        share_up,
        share_down,
    )


def fast_on_device(
    tokens, cotangent, input_gain, w_query, w_keyval, w_output, middle_gain, w_gate, w_up, w_down
):
    pair = [(0, 1), (1, 0)]

    def to_partner(value_rows):
        return lax.ppermute(value_rows, "tp", pair)

    parts = lax.axis_size("fsdp")
    width_in = tokens.shape[-1]
    rows = width_in // parts
    token_positions = 2 * tokens.shape[1]
    cosine, sine = rope_tables(token_positions, lax.axis_index("ctx") * token_positions)
    gains = jnp.pad(jnp.stack([input_gain, middle_gain], 1), ((0, 0), (0, 126)))
    (
        tokens_own, cotangent_own, cotangent_other, normed_one, query_low, keyval,
        mixed_heads, lse, tokens_other, mixed_other, *full,
    ) = front(
        tokens.swapaxes(1, 2), cotangent.swapaxes(1, 2), cosine, sine,
        (w_query, w_keyval, w_output, w_gate, w_up, w_down, gains),
    )
    full_query, full_keyval, full_output, full_gate, full_up, full_down, gains = [
        w.reshape(width_in, -1) for w in full
    ]
    tokens_own, cotangent_own, cotangent_other, normed_one, tokens_other = [
        v.T for v in (tokens_own, cotangent_own, cotangent_other, normed_one, tokens_other)
    ]
    full_gain_two = gains[:, 1]
    inputs = tokens_own.astype(jnp.float32)
    mixed_low = mixed_heads.reshape(QUERY_WIDTH, token_positions)
    middle = inputs + dot(mixed_low, full_output, 0, 0)

    gain_two = full_gain_two.astype(jnp.float32)
    unit_two, inverse_two = normalize(middle)
    normed_two = (unit_two * gain_two).astype(jnp.bfloat16)
    mixed_other = mixed_other.reshape(QUERY_WIDTH, token_positions)
    middle_other = tokens_other.astype(jnp.float32) + dot(mixed_other, full_output, 0, 0)
    normed_other = (normalize(middle_other)[0] * gain_two).astype(jnp.bfloat16)

    def feed(rows, back_rows):
        gate_proj = dot(rows, full_gate, 1, 0)
        up_proj = dot(rows, full_up, 1, 0)
        sigmoid_gate = jax.nn.sigmoid(gate_proj)
        swish_gate = gate_proj * sigmoid_gate
        hidden = (swish_gate * up_proj).astype(jnp.bfloat16)
        back_hidden = dot(back_rows, full_down, 1, 0)
        back_gate = (
            back_hidden * up_proj * sigmoid_gate * (1.0 + gate_proj * (1.0 - sigmoid_gate))
        ).astype(jnp.bfloat16)
        back_up = (back_hidden * swish_gate).astype(jnp.bfloat16)
        return (hidden, back_gate, back_up)

    def feed_input_back(back_gate, back_up):
        return dot(back_gate, full_gate, 1, 1) + dot(back_up, full_up, 1, 1)

    hidden_other, back_gate_other, back_up_other = feed(normed_other, cotangent_other)
    back_two_received = to_partner(
        feed_input_back(back_gate_other, back_up_other).astype(jnp.bfloat16)
    )
    hidden_own, back_gate_own, back_up_own = feed(normed_two, cotangent_own)
    back_two = feed_input_back(back_gate_own, back_up_own) + back_two_received.astype(jnp.float32)
    feed_other = dot(hidden_other, full_down, 1, 1).astype(jnp.bfloat16)
    base = middle + dot(hidden_own, full_down, 1, 1)

    def feed_gradient(left_own, right_own, left_other, right_other):
        gradient = dot(left_own, right_own, 0, 0) + dot(left_other, right_other, 0, 0)
        return gradient.astype(jnp.bfloat16).reshape(lax.axis_size("fsdp"), -1, gradient.shape[1])

    gradients = (
        feed_gradient(cotangent_own, hidden_own, cotangent_other, hidden_other),
        feed_gradient(normed_two, back_gate_own, normed_other, back_gate_other),
        feed_gradient(normed_two, back_up_own, normed_other, back_up_other),
    )

    grad_gain_two = jnp.sum(back_two * unit_two, axis=0)
    back_middle = cotangent_own.astype(jnp.float32) + norm_back(
        back_two * gain_two, unit_two, inverse_two
    )
    back_attention = back_middle.astype(jnp.bfloat16)
    back_mixed = dot(full_output, back_attention, 1, 1).astype(jnp.bfloat16)
    back_mixed = back_mixed.reshape(query_low.shape)
    grad_output = dot(mixed_low, back_attention, 1, 0).astype(jnp.bfloat16)
    share, result, grad_tokens, share_output, share_query, share_keyval, share_gains = backward_sum(
        query_low, keyval, back_mixed, mixed_heads, lse, cosine, sine, base.T, feed_other.T,
        tokens_own.T, normed_one.T, back_middle.T, gains, grad_gain_two[:, None],
        full_query, full_keyval, gradients, grad_output.reshape(parts, rows, -1),
    )
    return (
        result.swapaxes(1, 2),
        grad_tokens.swapaxes(1, 2).astype(jnp.float32),
        share_gains[:rows, 0].astype(jnp.float32),
        share_query[:rows].astype(jnp.float32),
        share_keyval[:rows].astype(jnp.float32),
        share_output[:rows].astype(jnp.float32),
        share_gains[:rows, 1].astype(jnp.float32),
        share[1].astype(jnp.float32),
        share[2].astype(jnp.float32),
        share[0].astype(jnp.float32),
    )


def solution(mesh):
    rows = P("fsdp", ("ctx", "tp"), None)
    specs = (
        P("fsdp"), P("fsdp", None), P("fsdp", None), P("fsdp", None),
        P("fsdp"), P("fsdp", "tp"), P("fsdp", "tp"), P("fsdp", "tp"),
    )
    kernels = mesh.shape["fsdp"] == 4 and mesh.shape["tp"] == 2 and mesh.shape["ctx"] == 4
    return jax.shard_map(
        fast_on_device if kernels else on_device,
        mesh=mesh,
        in_specs=(rows, rows) + specs,
        out_specs=(rows, rows) + specs,
        check_vma=False,
    )
```

```python
import jax
import jax.numpy as jnp
from jax import lax
from jax.experimental import pallas as pl
from jax.experimental.pallas import tpu as pltpu
from jax.sharding import PartitionSpec as P

QUERY_HEADS = 15
KEYVAL_HEADS = 5
GROUP = QUERY_HEADS // KEYVAL_HEADS
HEAD_WIDTH = 64
HALF = HEAD_WIDTH // 2
KEY_WIDTH = 320
QUERY_WIDTH = QUERY_HEADS * HEAD_WIDTH
SCALE = HEAD_WIDTH ** (-0.5)

EPS = 1e-05
THETA = 10000.0
VMEM_LIMIT = 40 * 1024 * 1024


def dot(left, right, left_dim, right_dim):
    return lax.dot_general(
        left, right, (((left_dim,), (right_dim,)), ((), ())), preferred_element_type=jnp.float32
    )


def rope_tables(token_positions, first_place):
    position = (first_place + lax.iota(jnp.int32, token_positions)).astype(jnp.float32)
    frequency = THETA ** (-(2.0 * lax.iota(jnp.int32, HALF).astype(jnp.float32)) / HEAD_WIDTH)
    angles = frequency[:, None] * position[None, :]
    return (jnp.cos(angles), jnp.sin(angles))


def apply_rotary(rows, cosine, sine):
    shaped = rows.reshape(-1, 2, HALF, rows.shape[-1])
    leading = shaped[:, 0]
    trailing = shaped[:, 1]
    return jnp.stack(
        [leading * cosine - trailing * sine, trailing * cosine + leading * sine], 1
    ).reshape(rows.shape)


def normalize(value_rows):
    inverse_rms = lax.rsqrt(jnp.mean(value_rows * value_rows, -1, keepdims=True) + EPS)
    return (value_rows * inverse_rms, inverse_rms)


def norm_back(back_unit, unit_rows, inverse_rms):
    return inverse_rms * (
        back_unit - unit_rows * jnp.mean(back_unit * unit_rows, -1, keepdims=True)
    )


def causal(scores):
    key_place = lax.broadcasted_iota(jnp.int32, scores.shape, 0)
    query_place = lax.broadcasted_iota(jnp.int32, scores.shape, 1)
    return jnp.where(key_place <= query_place, scores, -jnp.inf)


def forward_kernel(query_ref, key_ref, value_ref, mixed_ref, lse_ref):
    place = lax.axis_index("ctx")
    queries = [query_ref[g] * jnp.bfloat16(SCALE) for g in range(GROUP)]

    def scores_of(keys_turned, g, masked):
        scores = dot(keys_turned, queries[g], 1, 0)
        return causal(scores) if masked else scores

    def first():
        keys_turned = key_ref[0, 0, 0].T
        values = value_ref[0, 0, 0]
        carried = []
        for g in range(GROUP):
            scores = scores_of(keys_turned, g, True)
            top = jnp.max(scores, 0, keepdims=True)
            lifted = jnp.exp(scores - top)
            total = jnp.sum(lifted, 0, keepdims=True)
            carried += [top, total, dot(values, lifted.astype(jnp.bfloat16), 1, 0)]
        return tuple(carried)

    def step(block, carried):
        keys_turned = key_ref[block, 0, 0].T
        values = value_ref[block, 0, 0]
        later = []
        for g in range(GROUP):
            top, total, mixed = carried[3 * g : 3 * g + 3]
            scores = scores_of(keys_turned, g, False)
            new_top = jnp.maximum(top, jnp.max(scores, 0, keepdims=True))
            lifted = jnp.exp(scores - new_top)
            shrink = jnp.exp(top - new_top)
            later += [
                new_top,
                total * shrink + jnp.sum(lifted, 0, keepdims=True),
                mixed * shrink + dot(values, lifted.astype(jnp.bfloat16), 1, 0),
            ]
        return tuple(later)

    carried = lax.fori_loop(1, place + 1, step, first())
    for g in range(GROUP):
        top, total, mixed = carried[3 * g : 3 * g + 3]
        mixed_ref[g] = (mixed / total).astype(jnp.bfloat16)
        lse_ref[g] = top + jnp.log(total)


def attend_forward(query, keyval):
    blocks, token_positions = keyval.shape[0], keyval.shape[-1]
    head_block = (GROUP, HEAD_WIDTH, token_positions)
    key_block = (blocks, 1, 1, HEAD_WIDTH, token_positions)
    area = QUERY_HEADS * token_positions * token_positions * blocks
    return pl.pallas_call(
        forward_kernel,
        grid=(KEYVAL_HEADS,),
        in_specs=[
            pl.BlockSpec(head_block, lambda j: (j, 0, 0)),
            pl.BlockSpec(key_block, lambda j: (0, 0, j, 0, 0)),
            pl.BlockSpec(key_block, lambda j: (0, 1, j, 0, 0)),
        ],
        out_specs=[
            pl.BlockSpec(head_block, lambda j: (j, 0, 0)),
            pl.BlockSpec((GROUP, 1, token_positions), lambda j: (j, 0, 0)),
        ],
        out_shape=[
            jax.ShapeDtypeStruct(query.shape, jnp.bfloat16),
            jax.ShapeDtypeStruct((QUERY_HEADS, 1, token_positions), jnp.float32),
        ],
        compiler_params=pltpu.CompilerParams(vmem_limit_bytes=VMEM_LIMIT),
        cost_estimate=pl.CostEstimate(
            flops=16 * HEAD_WIDTH * area, bytes_accessed=6 * query.size, transcendentals=area
        ),
        name="attend_forward",
    )(query, keyval, keyval)


def backward_kernel(
    query_ref, key_ref, value_ref, back_ref, mixed_ref, lse_ref, cosine_ref, sine_ref,
    back_query_ref, back_keyval_ref,
):
    place = lax.axis_index("ctx")
    blocks = key_ref.shape[0]
    queries = [query_ref[g] * jnp.bfloat16(SCALE) for g in range(GROUP)]
    backs = [back_ref[g] for g in range(GROUP)]
    tops = [lse_ref[g] for g in range(GROUP)]
    sums = [
        jnp.sum(backs[g].astype(jnp.float32) * mixed_ref[g].astype(jnp.float32), 0, keepdims=True)
        for g in range(GROUP)
    ]

    def step(block, carried, masked=False):
        keys = key_ref[block, 0, 0]
        keys_turned = keys.T
        values_turned = value_ref[block, 0, 0].T
        back_key = jnp.zeros(keys.shape, jnp.float32)
        back_value = jnp.zeros(keys.shape, jnp.float32)
        later = []
        for g in range(GROUP):
            scores = dot(keys_turned, queries[g], 1, 0)
            if masked:
                scores = causal(scores)
            weights = jnp.exp(scores - tops[g])
            back_weights = dot(values_turned, backs[g], 1, 0)
            back_scores = (weights * (back_weights - sums[g])).astype(jnp.bfloat16)
            later.append(carried[g] + dot(keys, back_scores, 1, 0))
            back_key += dot(queries[g], back_scores, 1, 1)
            back_value += dot(backs[g], weights.astype(jnp.bfloat16), 1, 1)
        back_keyval_ref[block, 0, 0] = back_key.astype(jnp.bfloat16)
        back_keyval_ref[block, 1, 0] = back_value.astype(jnp.bfloat16)
        return tuple(later)

    start = tuple(jnp.zeros(query_ref.shape[1:], jnp.float32) for g in range(GROUP))
    carried = lax.fori_loop(1, place + 1, step, step(0, start, True))

    def clear(block, unused):
        zero = jnp.zeros(key_ref.shape[3:], jnp.bfloat16)
        back_keyval_ref[block, 0, 0] = zero
        back_keyval_ref[block, 1, 0] = zero
        return unused

    lax.fori_loop(place + 1, blocks, clear, 0)
    cosine = cosine_ref[...]
    sine = sine_ref[...]
    for g in range(GROUP):
        leading = carried[g][:HALF] * SCALE
        trailing = carried[g][HALF:] * SCALE
        back_query_ref[g, :HALF] = (leading * cosine + trailing * sine).astype(jnp.bfloat16)
        back_query_ref[g, HALF:] = (trailing * cosine - leading * sine).astype(jnp.bfloat16)


def attend_backward(query, keyval, back_mixed, mixed, lse, cosine, sine, first, count):
    blocks, token_positions = keyval.shape[0], keyval.shape[-1]
    head_block = (GROUP, HEAD_WIDTH, token_positions)
    key_block = (blocks, 1, 1, HEAD_WIDTH, token_positions)
    area = count * GROUP * token_positions * token_positions * blocks
    heads = pl.BlockSpec(head_block, lambda j: (j + first, 0, 0))
    table = pl.BlockSpec((HALF, token_positions), lambda j: (0, 0))
    return pl.pallas_call(
        backward_kernel,
        grid=(count,),
        in_specs=[
            heads,
            pl.BlockSpec(key_block, lambda j: (0, 0, j + first, 0, 0)),
            pl.BlockSpec(key_block, lambda j: (0, 1, j + first, 0, 0)),
            heads,
            heads,
            pl.BlockSpec((GROUP, 1, token_positions), lambda j: (j + first, 0, 0)),
            table,
            table,
        ],
        out_specs=[
            pl.BlockSpec(head_block, lambda j: (j, 0, 0)),
            pl.BlockSpec((blocks, 2, 1, HEAD_WIDTH, token_positions), lambda j: (0, 0, j, 0, 0)),
        ],
        out_shape=[
            jax.ShapeDtypeStruct((count * GROUP, HEAD_WIDTH, token_positions), jnp.bfloat16),
            jax.ShapeDtypeStruct(
                (blocks, 2, count, HEAD_WIDTH, token_positions), jnp.bfloat16
            ),
        ],
        compiler_params=pltpu.CompilerParams(vmem_limit_bytes=VMEM_LIMIT),
        cost_estimate=pl.CostEstimate(
            flops=40 * HEAD_WIDTH * area, bytes_accessed=10 * query.size, transcendentals=area
        ),
        name="attend_backward",
    )(query, keyval, keyval, back_mixed, mixed, lse, cosine, sine)


def move_along(value, distance):
    blocks = lax.axis_size("ctx")
    pairs = [(i, i + distance) for i in range(blocks) if 0 <= i + distance < blocks]
    return lax.ppermute(value, "ctx", pairs)


def trade(value, axis, step):
    pairs = [(i, i ^ step) for i in range(lax.axis_size(axis))]
    return lax.ppermute(value, axis, pairs)


def add_low(left, right):
    return (left.astype(jnp.float32) + right.astype(jnp.float32)).astype(jnp.bfloat16)


def scatter_sum(value, axis):
    size = lax.axis_size(axis)
    index = lax.axis_index(axis)
    rows = value.shape[0] // size
    step = 1
    while step < size:
        count = value.shape[0] // (2 * rows)
        split = value.reshape(count, 2, rows, value.shape[-1])
        second = (index // step) % 2 == 1
        kept = jnp.where(second, split[:, 1], split[:, 0])
        sent = jnp.where(second, split[:, 0], split[:, 1])
        value = add_low(kept, trade(sent, axis, step)).reshape(count * rows, value.shape[-1])
        step *= 2
    return value


def whole_sum(value, others):
    half_rows = value.shape[0] // 2
    second = lax.axis_index("ctx") % 2 == 1
    upper, lower = value[:half_rows], value[half_rows:]
    received = trade(jnp.where(second, upper, lower), "ctx", 1)
    total = add_low(jnp.where(second, lower, upper), received)
    for axis, first_step in others:
        step = first_step
        while step < lax.axis_size(axis):
            total = add_low(total, trade(total, axis, step))
            step *= 2
    received = trade(total, "ctx", 1)
    return jnp.concatenate(
        [jnp.where(second, received, total), jnp.where(second, total, received)], 0
    ).astype(jnp.float32)


MESH = pl.DeviceIdType.MESH
KERNEL_VMEM = 60 * 1024 * 1024
CHUNK_ROWS = 80


def remote(source, target, send_sem, recv_sem, **place):
    return pltpu.make_async_remote_copy(
        src_ref=source, dst_ref=target, send_sem=send_sem, recv_sem=recv_sem,
        device_id=place, device_id_type=MESH,
    )


def wide(value):
    return value.astype(jnp.float32)


def low(value):
    return value.astype(jnp.bfloat16)


def greet(**place):
    pl.semaphore_signal(
        pltpu.get_barrier_semaphore(), inc=1, device_id=place, device_id_type=MESH
    )


def backward_sum_kernel(
    query_ref, keyval_ref, back_ref, mixed_ref, lse_ref, cosine_ref, sine_ref,
    base_ref, feed_ref, normed_ref, gains_ref, gain_two_ref,
    down_ref, gate_ref, up_ref, out_ref, tokens_far, middle_far, query_far, keyval_far,
    share_ref, result_ref, back_tokens_ref, *refs,
):
    chunks_in = 4
    shares, refs = refs[:chunks_in], refs[chunks_in:]
    whole, mate_part, y_part, x_part, z_part = [
        refs[i * chunks_in : (i + 1) * chunks_in] for i in range(5)
    ]
    (
    own, mate_in, y_in, up_in, parts, part_in, back_total, row_sums,
    own_sem, mate_send, mate_recv, y_send, y_recv, up_send, up_recv, down_send, down_recv,
    part_send, part_recv, feed_in, traded, feed_send, feed_recv, trade_send, trade_recv,
    back_query_ref, back_keyval_ref, back_one, token_traded,
    tokens_ref, middle_ref, full_query, full_keyval, far_sem,
    whole_sem, sum_mate_send, sum_mate_recv, sum_y_send, sum_y_recv, sum_x_send, sum_x_recv,
    sum_z_send, sum_z_recv, all_send, all_recv, back_send, back_recv, token_send, token_recv,
    ) = refs[5 * chunks_in :]
    place = lax.axis_index("ctx")
    last = lax.axis_size("ctx") - 1
    blocks = last + 1
    rank = lax.axis_index("fsdp")
    core = rank % 2
    y = rank // 2
    side = lax.axis_index("tp")
    mate = rank + 1 - 2 * core
    across = rank + 2 - 4 * y
    gradients = (down_ref, gate_ref, up_ref)
    rows = share_ref.shape[1]
    per = rows // CHUNK_ROWS
    chunks = len(gradients) * per
    iterations = KEYVAL_HEADS + 2
    early = (iterations - KEYVAL_HEADS) * blocks

    for m, gradient in enumerate(gradients):
        for half in range(2):
            pltpu.make_async_copy(
                gradient.at[2 * half + core], own.at[m, half], own_sem.at[m, half]
            ).start()
    greet(fsdp=mate)
    greet(fsdp=across)
    greet(tp=1 - side)
    far = [
        pltpu.make_async_copy(source, target, far_sem.at[i])
        for i, (source, target) in enumerate((
            (tokens_far, tokens_ref), (middle_far, middle_ref), (query_far, full_query),
            (keyval_far, full_keyval),
        ))
    ]
    for d in range(1, blocks):
        greet(ctx=lax.rem(place + d, blocks))
    filled = out_ref.shape[1]
    tail = whole[0].shape[1] - filled
    for n in range(chunks_in):
        width = whole[n].shape[-1]
        whole[n][:, filled:] = jnp.zeros((whole[n].shape[0], tail, width), jnp.bfloat16)
        mate_part[n][:, filled:] = jnp.zeros((2, tail, width), jnp.bfloat16)
    for f in range(whole[0].shape[0]):
        pltpu.make_async_copy(
            out_ref.at[f], whole[0].at[f, pl.ds(0, filled)], whole_sem.at[f]
        ).start()
    pl.semaphore_wait(pltpu.get_barrier_semaphore(), 3 + last)

    feed_copy = remote(feed_ref, feed_in, feed_send, feed_recv, tp=1 - side)
    trade_copy = remote(traded, result_ref.at[side], trade_send, trade_recv, tp=1 - side)
    feed_copy.start()
    pair_width = traded.shape[-1]
    step_rows = traded.shape[0] // 4

    def finish_result():
        feed_copy.wait_recv()

        def some_rows(i, carry):
            at = pl.ds(pl.multiple_of(i * step_rows, step_rows), step_rows)
            for target, slot in ((result_ref.at[side], side), (traded, 1 - side)):
                columns = pl.ds(pl.multiple_of(slot * pair_width, pair_width), pair_width)
                target[at] = low(base_ref[at, columns] + wide(feed_in[at, columns]))
            return carry

        lax.fori_loop(0, 4, some_rows, 0)
        trade_copy.start()

    half_rows = whole[0].shape[1] // 2
    piece = half_rows // blocks
    kept = 2 * y + core

    def sum_mate(n, half):
        return remote(
            whole[n].at[2 * half + 1 - core, pl.ds(0, filled)],
            mate_part[n].at[half, pl.ds(0, filled)],
            sum_mate_send.at[n, half], sum_mate_recv.at[n, half], fsdp=mate,
        )

    def sum_y(n):
        return remote(
            mate_part[n].at[1 - y], y_part[n], sum_y_send.at[n], sum_y_recv.at[n], fsdp=across
        )

    def sum_x(n):
        other = pl.ds(pl.multiple_of((1 - side) * half_rows, half_rows), half_rows)
        return remote(
            whole[n].at[kept, other], x_part[n], sum_x_send.at[n], sum_x_recv.at[n],
            tp=1 - side,
        )

    def sum_z(n, d):
        target = lax.rem(place + d, blocks)
        at = pl.ds(pl.multiple_of(side * half_rows + target * piece, piece), piece)
        return remote(
            whole[n].at[kept, at], z_part[n].at[d - 1], sum_z_send.at[n, d - 1],
            sum_z_recv.at[n, d - 1], ctx=target,
        )

    def all_copy(n, d, origin):
        spot = shares[n].at[
            pl.ds(pl.multiple_of(side * half_rows + origin * piece, piece), piece)
        ]
        return remote(
            spot, spot, all_send.at[n, d - 1], all_recv.at[n, d - 1],
            ctx=lax.rem(place + d, blocks),
        )

    def back_copy(n, half):
        spot = shares[n].at[pl.ds(pl.multiple_of(half * half_rows, half_rows), half_rows)]
        return remote(spot, spot, back_send.at[n], back_recv.at[n], tp=1 - side)

    def to_mate(n):
        for half in range(2):
            sum_mate(n, half).start()

    def to_y(n):
        for half in range(2):
            sum_mate(n, half).wait_recv()
        quarter = 2 * (1 - y) + core
        mate_part[n][1 - y] = low(wide(whole[n][quarter]) + wide(mate_part[n][1 - y]))
        sum_y(n).start()

    def to_x(n):
        sum_y(n).wait_recv()
        whole[n][kept] = low(
            wide(whole[n][kept]) + wide(mate_part[n][y]) + wide(y_part[n][...])
        )
        sum_x(n).start()

    def to_z(n):
        sum_x(n).wait_recv()
        at = pl.ds(pl.multiple_of(side * half_rows, half_rows), half_rows)
        whole[n][kept, at] = low(wide(whole[n][kept, at]) + wide(x_part[n][...]))
        for d in range(1, blocks):
            sum_z(n, d).start()

    def to_all(n):
        at = pl.ds(pl.multiple_of(side * half_rows + place * piece, piece), piece)
        total = wide(whole[n][kept, at])
        for d in range(1, blocks):
            sum_z(n, d).wait_recv()
            total += wide(z_part[n][d - 1])
        shares[n][at] = low(total)
        for d in range(1, blocks):
            all_copy(n, d, place).start()

    def to_back(n):
        for d in range(1, blocks):
            all_copy(n, d, lax.rem(place + blocks - d, blocks)).wait_recv()
        back_copy(n, side).start()

    def finish_sum(n):
        back_copy(n, 1 - side).wait_recv()
        for half in range(2):
            sum_mate(n, half).wait_send()
        sum_y(n).wait_send()
        sum_x(n).wait_send()
        for d in range(1, blocks):
            sum_z(n, d).wait_send()
            all_copy(n, d, place).wait_send()
        back_copy(n, side).wait_send()

    def weight_gradient(n, back_ref):
        def quarter(f, carry):
            rows_of = normed_ref[pl.ds(pl.multiple_of(f * filled, filled), filled)]
            whole[n][f, :filled] = low(dot(rows_of, back_ref[...], 1, 1))
            return carry

        lax.fori_loop(0, whole[n].shape[0], quarter, 0)

    token_copy = remote(
        token_traded, back_tokens_ref.at[side], token_send, token_recv, tp=1 - side
    )

    def input_gradient():
        for copy in far:
            copy.wait()
        tokens = wide(tokens_ref[...])
        inverse = lax.rsqrt(jnp.mean(tokens * tokens, 0, keepdims=True) + EPS)

        def quarter(f, total):
            at = pl.ds(pl.multiple_of(f * filled, filled), filled)
            unit = wide(tokens_ref[at]) * inverse
            back = dot(full_query[at], back_query_ref[...], 1, 0) + dot(
                full_keyval[at], back_keyval_ref[...], 1, 0
            )
            gain_sum = jnp.sum(back * unit, 1, keepdims=True)
            lane = lax.broadcasted_iota(jnp.int32, (filled, whole[3].shape[-1]), 1)
            whole[3][f, :filled] = low(
                jnp.where(lane == 0, gain_sum, jnp.where(lane == 1, gain_two_ref[at], 0.0))
            )
            back = back * wide(gains_ref[at])[:, :1]
            back_one[at] = back
            return total + jnp.sum(back * unit, 0, keepdims=True)

        total = lax.fori_loop(
            0, whole[0].shape[0], quarter, jnp.zeros((1, tokens_ref.shape[-1]), jnp.float32)
        )
        to_mate(3)
        mean = total / tokens_ref.shape[0]

        def rows_back(f, carry):
            at = pl.ds(pl.multiple_of(f * filled, filled), filled)
            unit = wide(tokens_ref[at]) * inverse
            back_one[at] = middle_ref[at] + inverse * (back_one[at] - unit * mean)
            for target, slot in ((back_tokens_ref.at[side], side), (token_traded, 1 - side)):
                columns = pl.ds(pl.multiple_of(slot * pair_width, pair_width), pair_width)
                target[at] = low(back_one[at, columns])
            return carry

        lax.fori_loop(0, whole[0].shape[0], rows_back, 0)

    def chunk_at(ref, m, r, *front):
        return ref.at[(m,) + front + (pl.ds(r * CHUNK_ROWS, CHUNK_ROWS),)]

    def mate_copy(m, r, half):
        gradient = gradients[m]
        return remote(
            gradient.at[2 * half + 1 - core, pl.ds(r * CHUNK_ROWS, CHUNK_ROWS)],
            chunk_at(mate_in, m, r, half),
            mate_send.at[m * per + r, half], mate_recv.at[m * per + r, half], fsdp=mate,
        )

    for m in range(len(gradients)):
        for r in range(per):
            for half in range(2):
                mate_copy(m, r, half).start()
    for f in range(whole[0].shape[0]):
        pltpu.make_async_copy(
            out_ref.at[f], whole[0].at[f, pl.ds(0, filled)], whole_sem.at[f]
        ).wait()
    to_mate(0)
    for copy in far:
        copy.start()
    for m, gradient in enumerate(gradients):
        for half in range(2):
            pltpu.make_async_copy(
                gradient.at[2 * half + core], own.at[m, half], own_sem.at[m, half]
            ).wait()

    def split(k):
        r = lax.rem(k, per)
        return k // per, pl.ds(pl.multiple_of(r * CHUNK_ROWS, CHUNK_ROWS), CHUNK_ROWS)

    def y_copy(k):
        m, at = split(k)
        return remote(
            own.at[m, 1 - y, at], y_in.at[m, at], y_send.at[k], y_recv.at[k], fsdp=across
        )

    def up_copy(k):
        m, at = split(k)
        return remote(
            own.at[m, y, at], up_in.at[m, at], up_send.at[k], up_recv.at[k], ctx=place + 1
        )

    def down_copy(k):
        m, at = split(k)
        return remote(
            share_ref.at[m, at], share_ref.at[m, at], down_send.at[k], down_recv.at[k],
            ctx=place - 1,
        )

    def to_across(k):
        m, at = split(k)
        for half in range(2):
            pltpu.make_async_copy(
                mate_in.at[m, half, at], mate_in.at[m, half, at], mate_recv.at[k, half]
            ).wait()
        own[m, 1 - y, at] = low(wide(own[m, 1 - y, at]) + wide(mate_in[m, 1 - y, at]))
        y_copy(k).start()

    def to_next(k):
        m, at = split(k)
        y_copy(k).wait_recv()
        total = wide(own[m, y, at]) + wide(mate_in[m, y, at]) + wide(y_in[m, at])

        @pl.when(place == 0)
        def _():
            own[m, y, at] = low(total)

        @pl.when(place > 0)
        def _():
            up_copy(k).wait_recv()
            own[m, y, at] = low(total + wide(up_in[m, at]))

        @pl.when(place < last)
        def _():
            up_copy(k).start()

        @pl.when(place == last)
        def _():
            share_ref[m, at] = own[m, y, at]

    def give_back(k):
        @pl.when(place < last)
        def _():
            down_copy(k).wait_recv()

        @pl.when(place > 0)
        def _():
            down_copy(k).start()

    def query_gradient(n):
        weight_gradient(n, back_query_ref)
        to_mate(n)

    def tick(t):
        h = t - last - 2 * (last - place)

        @pl.when((h >= 0) & (h < KEYVAL_HEADS * blocks) & (lax.rem(h, blocks) == 0))
        def _():
            hand_on(h // blocks)

        @pl.when(t < chunks)
        def _():
            to_across(t)

        @pl.when(t == chunks + 1)
        def _():
            finish_result()

        b = t - 4 - 2 * place

        @pl.when((b >= 0) & (b < 2 * chunks) & (lax.rem(b, 2) == 0))
        def _():
            to_next(b // 2)

        c = t - KEYVAL_HEADS * blocks - 2 * (last - place)

        @pl.when((c >= 0) & (c < chunks))
        def _():
            give_back(c)

        for at, stage, n in (
            (4, to_y, 0), (15, to_x, 0), (18, to_z, 0), (20, query_gradient, 1),
            (20, to_all, 0), (21, to_y, 1), (22, to_back, 0), (24, to_x, 1), (26, to_z, 1),
        ):
            @pl.when(t == at)
            def _(stage=stage, n=n):
                stage(n)

    def part_copy(j, s):
        return remote(
            parts.at[j, s], part_in.at[j, s - 1], part_send.at[j, s - 1],
            part_recv.at[j, s - 1], ctx=place - 1,
        )

    def step(j, s, masked):
        keys = keyval_ref[s, j, 0]
        keys_turned = keys.T
        values_turned = keyval_ref[s, j, 1].T
        back_key = jnp.zeros(keys.shape, jnp.float32)
        back_value = jnp.zeros(keys.shape, jnp.float32)
        for g in range(GROUP):
            head = GROUP * j + g
            query = query_ref[head]
            back = back_ref[head]
            if masked:
                row_sums[g] = jnp.sum(wide(back) * wide(mixed_ref[head]), 0, keepdims=True)
            scores = dot(keys_turned, query, 1, 0)
            if masked:
                scores = causal(scores)
            weights = jnp.exp(scores - lse_ref[head])
            back_weights = dot(values_turned, back, 1, 0)
            back_scores = low(weights * (back_weights - row_sums[g]))
            added = dot(keys, back_scores, 1, 0)
            if masked:
                back_total[g] = added
            else:
                back_total[g] += added
            back_key += dot(query, back_scores, 1, 1)
            back_value += dot(back, low(weights), 1, 1)
        parts[j, s, 0] = low(back_key)
        parts[j, s, 1] = low(back_value)
        if not masked:
            @pl.when(place == last)
            def _():
                part_copy(j, s).start()

    def hand_on(j):
        for s in range(blocks):
            @pl.when(s <= place)
            def _(s=s):
                @pl.when(place < last)
                def _():
                    pltpu.make_async_copy(
                        part_in.at[j, s], part_in.at[j, s], part_recv.at[j, s]
                    ).wait()
                    for kind in range(2):
                        total = wide(parts[j, s, kind]) + wide(part_in[j, s, kind])
                        parts[j, s, kind] = low(total)

                if s > 0:
                    @pl.when(place < last)
                    def _():
                        part_copy(j, s).start()
                else:
                    leading = wide(parts[j, 0, 0, :HALF])
                    trailing = wide(parts[j, 0, 0, HALF:])
                    cosine, sine = cosine_ref[...], sine_ref[...]
                    at = j * HEAD_WIDTH
                    back_keyval_ref[pl.ds(pl.multiple_of(at, HALF), HALF)] = low(
                        leading * cosine + trailing * sine
                    )
                    back_keyval_ref[pl.ds(pl.multiple_of(at + HALF, HALF), HALF)] = low(
                        trailing * cosine - leading * sine
                    )
                    at = pl.ds(pl.multiple_of(KEY_WIDTH + at, HEAD_WIDTH), HEAD_WIDTH)
                    back_keyval_ref[at] = low(wide(parts[j, 0, 1]))

    def head_loop(j, carry):
        @pl.when(j < KEYVAL_HEADS)
        def _():
            step(j, 0, True)

        tick(j * blocks)

        def block_loop(s, inner):
            @pl.when((j < KEYVAL_HEADS) & (s <= place))
            def _():
                step(j, s, False)

            tick(j * blocks + s)
            return inner

        lax.fori_loop(1, blocks, block_loop, 0)

        @pl.when(j < KEYVAL_HEADS)
        def _():
            cosine, sine = cosine_ref[...], sine_ref[...]
            for g in range(GROUP):
                leading = back_total[g, :HALF] * SCALE
                trailing = back_total[g, HALF:] * SCALE
                at = (GROUP * j + g) * HEAD_WIDTH
                back_query_ref[pl.ds(pl.multiple_of(at, HALF), HALF)] = low(
                    leading * cosine + trailing * sine
                )
                back_query_ref[pl.ds(pl.multiple_of(at + HALF, HALF), HALF)] = low(
                    trailing * cosine - leading * sine
                )

        return carry

    assert iterations * blocks > 4 + 2 * last + 2 * (chunks - 1)
    lax.fori_loop(0, iterations, head_loop, 0)

    def start_tokens(n):
        token_copy.start()

    def keyval_gradient(n):
        weight_gradient(n, back_keyval_ref)
        to_mate(n)

    later = (
        ((keyval_gradient, 2), (to_y, 2)), ((lambda n: input_gradient(), 3),),
        ((to_y, 3), (to_x, 2), (to_all, 1)), ((to_x, 3), (to_z, 2), (start_tokens, 3)),
        ((to_all, 2), (to_z, 3), (to_back, 1)), ((to_back, 2), (to_all, 3)), ((to_back, 3),),
    )
    for slot, stages in enumerate(later):
        for stage, n in stages:
            stage(n)
        for index in range(blocks):
            if early + slot - 2 * (last - index) < chunks:
                @pl.when(place == index)
                def _(k=early + slot - 2 * (last - index)):
                    give_back(k)

    assert early >= 2 * last and len(later) >= chunks - early + 2 * last
    for n in range(chunks_in):
        finish_sum(n)
    token_copy.wait()

    for m in range(len(gradients)):
        for r in range(per):
            for half in range(2):
                mate_copy(m, r, half).wait_send()

    def finish(k, carry):
        y_copy(k).wait_send()

        @pl.when(place < last)
        def _():
            up_copy(k).wait_send()

        @pl.when(place > 0)
        def _():
            down_copy(k).wait_send()

        return carry

    lax.fori_loop(0, chunks, finish, 0)

    def finish_parts(j, carry):
        for s in range(1, blocks):
            @pl.when(s <= place)
            def _(s=s):
                part_copy(j, s).wait_send()
        return carry

    lax.fori_loop(0, KEYVAL_HEADS, finish_parts, 0)
    feed_copy.wait_send()
    trade_copy.wait()


def backward_sum(
    query, keyval, back_mixed, mixed, lse, cosine, sine, base, feed, tokens, normed, middle,
    gains, gain_two, full_query, full_keyval, gradients, gradient_out,
):
    blocks, positions = keyval.shape[0], keyval.shape[-1]
    count, rows, columns = gradients[0].shape
    chunks = len(gradients) * rows // CHUNK_ROWS
    area = QUERY_HEADS * positions * positions * blocks
    vmem = pl.BlockSpec(memory_space=pltpu.VMEM)
    anywhere = pl.BlockSpec(memory_space=pl.ANY)
    dma = pltpu.SemaphoreType.DMA
    share = (len(gradients), rows, columns)
    head = (2, HEAD_WIDTH, positions)
    features = feed.shape[0]
    widths = (QUERY_WIDTH, QUERY_WIDTH, 2 * KEY_WIDTH, gains.shape[-1])
    padded = rows + 16
    half_rows = padded // 2
    low_type = jnp.bfloat16
    scratch = []
    for first in ((count, padded), (2, padded), (padded,), (half_rows,),
                  (blocks - 1, half_rows // blocks)):
        scratch += [pltpu.VMEM(first + (w,), low_type) for w in widths]
    each = len(widths)
    pairs = jax.ShapeDtypeStruct((2, features, positions // 2), low_type)
    return pl.pallas_call(
        backward_sum_kernel,
        in_specs=[vmem] * 12 + [anywhere] * 8,
        out_specs=[vmem] * (3 + each),
        out_shape=[jax.ShapeDtypeStruct(share, low_type), pairs, pairs] + [
            jax.ShapeDtypeStruct((padded, w), low_type) for w in widths
        ],
        scratch_shapes=scratch + [
            pltpu.VMEM((len(gradients), 2, rows, columns), low_type),
            pltpu.VMEM((len(gradients), 2, rows, columns), low_type),
            pltpu.VMEM(share, low_type),
            pltpu.VMEM(share, low_type),
            pltpu.VMEM((KEYVAL_HEADS, blocks) + head, low_type),
            pltpu.VMEM((KEYVAL_HEADS, blocks - 1) + head, low_type),
            pltpu.VMEM((GROUP, HEAD_WIDTH, positions), jnp.float32),
            pltpu.VMEM((GROUP, 1, positions), jnp.float32),
            dma((len(gradients), 2)),
            dma((chunks, 2)), dma((chunks, 2)),
            dma((chunks,)), dma((chunks,)),
            dma((chunks,)), dma((chunks,)),
            dma((chunks,)), dma((chunks,)),
            dma((KEYVAL_HEADS, blocks - 1)), dma((KEYVAL_HEADS, blocks - 1)),
            pltpu.VMEM(feed.shape, low_type),
            pltpu.VMEM((features, positions // 2), low_type),
            dma, dma, dma, dma,
            pltpu.VMEM((QUERY_WIDTH, positions), low_type),
            pltpu.VMEM((2 * KEY_WIDTH, positions), low_type),
            pltpu.VMEM((features, positions), jnp.float32),
            pltpu.VMEM((features, positions // 2), low_type),
            pltpu.VMEM(tokens.shape, low_type),
            pltpu.VMEM(middle.shape, jnp.float32),
            pltpu.VMEM(full_query.shape, low_type),
            pltpu.VMEM(full_keyval.shape, low_type),
            dma((4,)),
            dma((count,)),
            dma((each, 2)), dma((each, 2)),
            dma((each,)), dma((each,)),
            dma((each,)), dma((each,)),
            dma((each, blocks - 1)), dma((each, blocks - 1)),
            dma((each, blocks - 1)), dma((each, blocks - 1)),
            dma((each,)), dma((each,)),
            dma, dma,
        ],
        compiler_params=pltpu.CompilerParams(
            vmem_limit_bytes=KERNEL_VMEM, collective_id=0, has_side_effects=True
        ),
        cost_estimate=pl.CostEstimate(
            flops=40 * HEAD_WIDTH * area, bytes_accessed=10 * query.size, transcendentals=area
        ),
        name="backward_sum",
    )(
        query, keyval, back_mixed, mixed, lse, cosine, sine, base, feed, normed, gains, gain_two,
        *gradients, gradient_out, tokens, middle, full_query, full_keyval,
    )


def front_kernel(
    tokens_ref, cotangent_ref, cosine_ref, sine_ref, *refs
):
    weights, refs = refs[:7], refs[7:]
    (
        tokens_own, cotangent_own, cotangent_other, normed_out, query_out, keyval_ref,
        mixed_out, lse_ref, tokens_other, mixed_other,
    ), refs = refs[:10], refs[10:]
    full, refs = refs[:7], refs[7:]
    (
        raw, tops, totals, sums,
        local_sem, token_send, token_recv, cot_send, cot_recv,
        y_send, y_recv, mate_send, mate_recv, pass_send, pass_recv, key_send, key_recv,
        mixed_send, mixed_recv,
    ) = refs
    place = lax.axis_index("ctx")
    last = lax.axis_size("ctx") - 1
    rank = lax.axis_index("fsdp")
    side = lax.axis_index("tp")
    core = rank % 2
    mate = rank + 1 - 2 * core
    across = rank + 2 - 4 * (rank // 2)
    width = tokens_ref.shape[-1]

    def columns(ref, slot):
        return ref.at[:, pl.ds(pl.multiple_of(slot * width, width), width)]

    local = [
        pltpu.make_async_copy(tokens_ref.at[side], columns(tokens_own, side), local_sem.at[0]),
        pltpu.make_async_copy(
            cotangent_ref.at[side], columns(cotangent_own, side), local_sem.at[1]
        ),
        pltpu.make_async_copy(
            cotangent_ref.at[1 - side], columns(cotangent_other, side), local_sem.at[2]
        ),
        pltpu.make_async_copy(
            tokens_ref.at[1 - side], columns(tokens_other, side), local_sem.at[3]
        ),
    ]
    for w in range(len(weights)):
        local.append(pltpu.make_async_copy(weights[w], full[w].at[rank], local_sem.at[4 + w]))
    for copy in local:
        copy.start()

    greet(fsdp=mate)
    greet(fsdp=across)
    greet(tp=1 - side)

    @pl.when(place > 0)
    def _():
        greet(ctx=place - 1)

    @pl.when(place < last)
    def _():
        greet(ctx=place + 1)

    neighbours = (place + last - 1) // last + (2 * last - place - 1) // last
    pl.semaphore_wait(pltpu.get_barrier_semaphore(), 3 + neighbours)

    token_copy = remote(
        tokens_ref.at[1 - side], columns(tokens_own, side), token_send, token_recv, tp=1 - side
    )
    cot_copies = [
        remote(
            cotangent_ref.at[1 - side], columns(cotangent_own, side), cot_send.at[0],
            cot_recv.at[0], tp=1 - side,
        ),
        remote(
            cotangent_ref.at[side], columns(cotangent_other, side), cot_send.at[1],
            cot_recv.at[1], tp=1 - side,
        ),
        remote(
            tokens_ref.at[side], columns(tokens_other, side), cot_send.at[2], cot_recv.at[2],
            tp=1 - side,
        ),
    ]

    def mixed_copy(j):
        heads = pl.ds(GROUP * j, GROUP)
        return remote(
            mixed_out.at[heads], mixed_other.at[heads], mixed_send.at[j], mixed_recv.at[j],
            tp=1 - side,
        )


    def y_copy(w):
        return remote(
            weights[w], full[w].at[rank], y_send.at[w], y_recv.at[w], fsdp=across
        )

    def mate_copy(w):
        return remote(
            weights[w], full[w].at[rank], mate_send.at[w], mate_recv.at[w], fsdp=mate
        )

    def pass_copy(w):
        return remote(
            full[w].at[across], full[w].at[across], pass_send.at[w], pass_recv.at[w], fsdp=mate
        )

    def arrived(w):
        local[4 + w].wait()
        mate_copy(w).wait_recv()
        pass_copy(w).wait_recv()

    for w in (6, 1):
        y_copy(w).start()
        mate_copy(w).start()
    token_copy.start()
    for w in (0, 2, 3, 4, 5):
        y_copy(w).start()
        mate_copy(w).start()
    y_copy(6).wait_recv()
    pass_copy(6).start()
    arrived(6)
    gain = wide(full[6][...].reshape(-1, full[6].shape[-1])[:, :1])

    def norm_rows(slot):
        at = pl.ds(pl.multiple_of(slot * width, width), width)
        rows = wide(tokens_own[:, at])
        inverse = lax.rsqrt(jnp.mean(rows * rows, 0, keepdims=True) + EPS)
        normed_out[:, at] = low(rows * inverse * gain)

    local[0].wait()
    norm_rows(side)
    token_copy.wait_recv()
    norm_rows(1 - side)
    for copy in cot_copies:
        copy.start()
    for w in (1, 0):
        y_copy(w).wait_recv()
        pass_copy(w).start()
    normed = normed_out[...]
    cosine, sine = cosine_ref[...], sine_ref[...]

    def turned(value, target):
        target[:HALF] = low(value[:HALF] * cosine - value[HALF:] * sine)
        target[HALF:] = low(value[HALF:] * cosine + value[:HALF] * sine)

    def key_copy(s, j):
        return remote(
            keyval_ref.at[s, j], keyval_ref.at[s + 1, j], key_send.at[s, j], key_recv.at[s, j],
            ctx=place + 1,
        )

    arrived(1)
    matrix = full[1][...].reshape(-1, 2 * KEY_WIDTH)
    raw[: 2 * KEY_WIDTH] = dot(matrix, normed, 0, 0)
    for j in range(KEYVAL_HEADS):
        turned(raw[j * HEAD_WIDTH : (j + 1) * HEAD_WIDTH], keyval_ref.at[0, j, 0])
        first = KEY_WIDTH + j * HEAD_WIDTH
        keyval_ref[0, j, 1] = low(raw[first : first + HEAD_WIDTH])

        if j == 0:
            @pl.when(place < last)
            def _():
                key_copy(0, 0).start()

    arrived(0)
    matrix = full[0][...].reshape(-1, QUERY_WIDTH)
    raw[...] = dot(matrix, normed, 0, 0)

    def turn_query(h, carry):
        value = raw[pl.ds(pl.multiple_of(h * HEAD_WIDTH, HEAD_WIDTH), HEAD_WIDTH)]
        first = low(value[:HALF] * cosine - value[HALF:] * sine)
        second = low(value[HALF:] * cosine + value[:HALF] * sine)
        query_out[h, :HALF] = first * jnp.bfloat16(SCALE)
        query_out[h, HALF:] = second * jnp.bfloat16(SCALE)
        return carry

    lax.fori_loop(0, QUERY_HEADS, turn_query, 0)

    def attend(s, j, masked):
        keys_turned = keyval_ref[s, j, 0].T
        values = keyval_ref[s, j, 1]
        for g in range(GROUP):
            head = GROUP * j + g
            scores = dot(keys_turned, query_out[head], 1, 0)
            if masked:
                scores = causal(scores)
                top = jnp.max(scores, 0, keepdims=True)
                lifted = jnp.exp(scores - top)
                tops[head] = top
                totals[head] = jnp.sum(lifted, 0, keepdims=True)
                sums[head] = dot(values, low(lifted), 1, 0)
            else:
                old = tops[head]
                top = jnp.maximum(old, jnp.max(scores, 0, keepdims=True))
                lifted = jnp.exp(scores - top)
                shrink = jnp.exp(old - top)
                tops[head] = top
                totals[head] = totals[head] * shrink + jnp.sum(lifted, 0, keepdims=True)
                sums[head] = sums[head] * shrink + dot(values, low(lifted), 1, 0)

    def hand_on(s, j):
        @pl.when(s < place)
        def _():
            pltpu.make_async_copy(
                keyval_ref.at[s + 1, j], keyval_ref.at[s + 1, j], key_recv.at[s, j]
            ).wait()

            @pl.when(place < last)
            def _():
                key_copy(s + 1, j).start()

    def finish_heads(j):
        for g in range(GROUP):
            head = GROUP * j + g
            total = totals[head]
            mixed_out[head] = low(sums[head] / total)
            lse_ref[head] = tops[head] + jnp.log(total)
        mixed_copy(j).start()

    def one_head(j, carry):
        @pl.when((place < last) & (j + 1 < KEYVAL_HEADS))
        def _():
            key_copy(0, j + 1).start()

        attend(0, j, True)
        hand_on(0, j)

        def later_block(s, inner):
            attend(s, j, False)
            hand_on(s, j)
            return inner

        lax.fori_loop(1, place + 1, later_block, 0)
        finish_heads(j)
        return carry

    lax.fori_loop(0, KEYVAL_HEADS, one_head, 0)
    passed = 2

    for w in range(passed, 6):
        y_copy(w).wait_recv()
        pass_copy(w).start()
    for copy in local[1:4]:
        copy.wait()
    for j in range(KEYVAL_HEADS):
        mixed_copy(j).wait()
    token_copy.wait_send()
    for copy in cot_copies:
        copy.wait()
    for w in range(passed, 6):
        arrived(w)
    for w in range(len(weights)):
        y_copy(w).wait_send()
        mate_copy(w).wait_send()
        pass_copy(w).wait_send()

    @pl.when(place < last)
    def _():
        def sent(i, carry):
            key_copy(i // KEYVAL_HEADS, lax.rem(i, KEYVAL_HEADS)).wait_send()
            return carry

        lax.fori_loop(0, (place + 1) * KEYVAL_HEADS, sent, 0)


def front(tokens, cotangent, cosine, sine, weights):
    blocks = lax.axis_size("ctx")
    parts = lax.axis_size("fsdp")
    positions = cosine.shape[-1]
    vmem = pl.BlockSpec(memory_space=pltpu.VMEM)
    anywhere = pl.BlockSpec(memory_space=pl.ANY)
    dma = pltpu.SemaphoreType.DMA
    shape = lambda *dims: jax.ShapeDtypeStruct(dims, jnp.bfloat16)
    count = len(weights)
    features = tokens.shape[1]
    area = QUERY_HEADS * positions * positions * blocks
    return pl.pallas_call(
        front_kernel,
        in_specs=[vmem] * (4 + count),
        out_specs=[vmem] * 12 + [anywhere] * 4 + [vmem],
        out_shape=[
            shape(features, positions), shape(features, positions), shape(features, positions),
            shape(features, positions),
            shape(QUERY_HEADS, HEAD_WIDTH, positions),
            shape(blocks, KEYVAL_HEADS, 2, HEAD_WIDTH, positions),
            shape(QUERY_HEADS, HEAD_WIDTH, positions),
            jax.ShapeDtypeStruct((QUERY_HEADS, 1, positions), jnp.float32),
            shape(features, positions),
            shape(QUERY_HEADS, HEAD_WIDTH, positions),
        ] + [shape(parts, *w.shape) for w in weights],
        scratch_shapes=[
            pltpu.VMEM((QUERY_WIDTH, positions), jnp.float32),
            pltpu.VMEM((QUERY_HEADS, 1, positions), jnp.float32),
            pltpu.VMEM((QUERY_HEADS, 1, positions), jnp.float32),
            pltpu.VMEM((QUERY_HEADS, HEAD_WIDTH, positions), jnp.float32),
            dma((4 + count,)),
            dma, dma,
            dma((3,)), dma((3,)),
            dma((count,)), dma((count,)),
            dma((count,)), dma((count,)),
            dma((count,)), dma((count,)),
            dma((blocks, KEYVAL_HEADS)), dma((blocks, KEYVAL_HEADS)),
            dma((KEYVAL_HEADS,)), dma((KEYVAL_HEADS,)),
        ],
        compiler_params=pltpu.CompilerParams(
            vmem_limit_bytes=KERNEL_VMEM, collective_id=1, has_side_effects=True
        ),
        cost_estimate=pl.CostEstimate(
            flops=16 * HEAD_WIDTH * area, bytes_accessed=10 * tokens.size, transcendentals=area
        ),
        name="front",
    )(tokens, cotangent, cosine, sine, *weights)


def on_device(
    tokens, cotangent, input_gain, w_query, w_keyval, w_output, middle_gain, w_gate, w_up, w_down
):
    half = lax.axis_index("tp")
    low_half = half == 0
    pair = [(0, 1), (1, 0)]

    def to_partner(value_rows):
        return lax.ppermute(value_rows, "tp", pair)

    def in_order(mine, received):
        return jnp.concatenate(
            [jnp.where(low_half, mine, received), jnp.where(low_half, received, mine)], 0
        )

    def take(value_rows, index):
        return lax.dynamic_index_in_dim(value_rows, index, 0, keepdims=False)

    tokens_own = in_order(take(tokens, half), to_partner(take(tokens, 1 - half)))
    full_gain_one, full_gain_two = (
        lax.all_gather(input_gain, "fsdp", axis=0, tiled=True),
        lax.all_gather(middle_gain, "fsdp", axis=0, tiled=True),
    )
    full_in = lax.all_gather(jnp.concatenate([w_query, w_keyval], 1), "fsdp", axis=0, tiled=True)
    full_output = lax.all_gather(w_output, "fsdp", axis=0, tiled=True)
    full_gate = lax.all_gather(w_gate, "fsdp", axis=0, tiled=True)
    full_up = lax.all_gather(w_up, "fsdp", axis=0, tiled=True)
    full_down = lax.all_gather(w_down, "fsdp", axis=0, tiled=True)
    cotangent_received = to_partner(cotangent)
    cotangent_own = in_order(take(cotangent, half), take(cotangent_received, half))
    cotangent_other = in_order(take(cotangent, 1 - half), take(cotangent_received, 1 - half))

    token_positions = tokens_own.shape[0]
    cosine, sine = rope_tables(token_positions, lax.axis_index("ctx") * token_positions)
    gain_one = full_gain_one.astype(jnp.float32)
    inputs = tokens_own.astype(jnp.float32)
    unit_one, inverse_one = normalize(inputs)
    normed_one = (unit_one * gain_one).astype(jnp.bfloat16)
    keyval_raw = dot(full_in[:, QUERY_WIDTH:], normed_one, 0, 1)
    keyval_low = jnp.concatenate(
        [apply_rotary(keyval_raw[:KEY_WIDTH], cosine, sine), keyval_raw[KEY_WIDTH:]], 0
    ).astype(jnp.bfloat16)
    blocks = lax.axis_size("ctx")
    keyval = jnp.stack([keyval_low] + [move_along(keyval_low, s) for s in range(1, blocks)], 0)
    keyval = keyval.reshape(blocks, 2, KEYVAL_HEADS, HEAD_WIDTH, token_positions)
    query_raw = dot(full_in[:, :QUERY_WIDTH], normed_one, 0, 1)
    query_low = (
        apply_rotary(query_raw, cosine, sine)
        .astype(jnp.bfloat16)
        .reshape(QUERY_HEADS, HEAD_WIDTH, token_positions)
    )
    mixed_heads, lse = attend_forward(query_low, keyval)
    mixed_low = mixed_heads.reshape(QUERY_WIDTH, token_positions)
    middle = inputs + dot(mixed_low, full_output, 0, 0)

    gain_two = full_gain_two.astype(jnp.float32)
    unit_two, inverse_two = normalize(middle)
    normed_two = (unit_two * gain_two).astype(jnp.bfloat16)
    normed_other = to_partner(normed_two)

    def feed(rows, back_rows):
        gate_proj = dot(rows, full_gate, 1, 0)
        up_proj = dot(rows, full_up, 1, 0)
        sigmoid_gate = jax.nn.sigmoid(gate_proj)
        swish_gate = gate_proj * sigmoid_gate
        hidden = (swish_gate * up_proj).astype(jnp.bfloat16)
        back_hidden = dot(back_rows, full_down, 1, 0)
        back_gate = (
            back_hidden * up_proj * sigmoid_gate * (1.0 + gate_proj * (1.0 - sigmoid_gate))
        ).astype(jnp.bfloat16)
        back_up = (back_hidden * swish_gate).astype(jnp.bfloat16)
        return (hidden, back_gate, back_up)

    def feed_input_back(back_gate, back_up):
        return dot(back_gate, full_gate, 1, 1) + dot(back_up, full_up, 1, 1)

    hidden_own, back_gate_own, back_up_own = feed(normed_two, cotangent_own)
    hidden_other, back_gate_other, back_up_other = feed(normed_other, cotangent_other)
    back_two_received = to_partner(
        feed_input_back(back_gate_other, back_up_other).astype(jnp.bfloat16)
    )
    back_two = feed_input_back(back_gate_own, back_up_own) + back_two_received.astype(jnp.float32)
    feed_received = to_partner(dot(hidden_other, full_down, 1, 1).astype(jnp.bfloat16))
    result_own = (
        middle + dot(hidden_own, full_down, 1, 1) + feed_received.astype(jnp.float32)
    ).astype(jnp.bfloat16)

    def feed_gradient(left_own, right_own, left_other, right_other):
        gradient = dot(left_own, right_own, 0, 0) + dot(left_other, right_other, 0, 0)
        shared = scatter_sum(gradient.astype(jnp.bfloat16), "fsdp")
        return whole_sum(shared, (("ctx", 2),))

    share_down = feed_gradient(cotangent_own, hidden_own, cotangent_other, hidden_other)
    share_gate = feed_gradient(normed_two, back_gate_own, normed_other, back_gate_other)
    share_up = feed_gradient(normed_two, back_up_own, normed_other, back_up_other)

    grad_gain_two = jnp.sum(back_two * unit_two, axis=0)
    back_middle = cotangent_own.astype(jnp.float32) + norm_back(
        back_two * gain_two, unit_two, inverse_two
    )
    back_attention = back_middle.astype(jnp.bfloat16)
    back_mixed = dot(full_output, back_attention, 1, 1).astype(jnp.bfloat16)
    back_mixed = back_mixed.reshape(query_low.shape)
    grad_output = dot(mixed_low, back_attention, 1, 0).astype(jnp.bfloat16)
    share_output = whole_sum(scatter_sum(grad_output, "fsdp"), (("tp", 1), ("ctx", 2)))

    back_query = []
    back_key = []
    back_value = []
    for first, count in ((0, 3), (3, 2)):
        part_query, part_keyval = attend_backward(
            query_low, keyval, back_mixed, mixed_heads, lse, cosine, sine, first, count
        )
        part_keyval = part_keyval.reshape(blocks, 2 * count * HEAD_WIDTH, token_positions)
        owned = part_keyval[0].astype(jnp.float32)
        for s in range(1, blocks):
            owned += move_along(part_keyval[s], -s).astype(jnp.float32)
        back_query.append(part_query.reshape(-1, token_positions))
        back_key.append(
            apply_rotary(owned[: count * HEAD_WIDTH], cosine, -sine).astype(jnp.bfloat16)
        )
        back_value.append(owned[count * HEAD_WIDTH :].astype(jnp.bfloat16))
    back_in = jnp.concatenate(back_query + back_key + back_value, 0)
    grad_in = dot(normed_one, back_in, 0, 1)
    back_one = dot(back_in, full_in, 0, 1)
    grad_gain_one = jnp.sum(back_one * unit_one, axis=0)
    back_inputs = back_middle + norm_back(back_one * gain_one, unit_one, inverse_one)

    def to_positions(value_rows):
        split = value_rows.reshape(2, token_positions // 2, value_rows.shape[-1])
        received = to_partner(take(split, 1 - half))
        return in_order(take(split, half)[None], received[None])

    result = to_positions(result_own)
    grad_tokens = to_positions(back_inputs.astype(jnp.bfloat16)).astype(jnp.float32)
    gradients = jnp.concatenate([grad_in, grad_gain_one[:, None], grad_gain_two[:, None]], 1)
    share_in = lax.psum(
        lax.psum_scatter(
            gradients.astype(jnp.bfloat16), "fsdp", scatter_dimension=0, tiled=True
        ),
        ("ctx", "tp"),
    ).astype(jnp.float32)
    width = full_in.shape[1]
    return (
        result,
        grad_tokens,
        share_in[:, width],
        share_in[:, :QUERY_WIDTH],
        share_in[:, QUERY_WIDTH:width],
        share_output,
        share_in[:, width + 1],
        share_gate,
        share_up,
        share_down,
    )


def fast_on_device(
    tokens, cotangent, input_gain, w_query, w_keyval, w_output, middle_gain, w_gate, w_up, w_down
):
    pair = [(0, 1), (1, 0)]

    def to_partner(value_rows):
        return lax.ppermute(value_rows, "tp", pair)

    parts = lax.axis_size("fsdp")
    width_in = tokens.shape[-1]
    rows = width_in // parts
    token_positions = 2 * tokens.shape[1]
    cosine, sine = rope_tables(token_positions, lax.axis_index("ctx") * token_positions)
    gains = jnp.pad(jnp.stack([input_gain, middle_gain], 1), ((0, 0), (0, 126)))
    (
        tokens_own, cotangent_own, cotangent_other, normed_one, query_low, keyval,
        mixed_heads, lse, tokens_other, mixed_other, *full,
    ) = front(
        tokens.swapaxes(1, 2), cotangent.swapaxes(1, 2), cosine, sine,
        (w_query, w_keyval, w_output, w_gate, w_up, w_down, gains),
    )
    full_query, full_keyval, full_output, full_gate, full_up, full_down, gains = [
        w.reshape(width_in, -1) for w in full
    ]
    tokens_own, cotangent_own, cotangent_other, normed_one, tokens_other = [
        v.T for v in (tokens_own, cotangent_own, cotangent_other, normed_one, tokens_other)
    ]
    full_gain_two = gains[:, 1]
    inputs = tokens_own.astype(jnp.float32)
    mixed_low = mixed_heads.reshape(QUERY_WIDTH, token_positions)
    middle = inputs + dot(mixed_low, full_output, 0, 0)

    gain_two = full_gain_two.astype(jnp.float32)
    unit_two, inverse_two = normalize(middle)
    normed_two = (unit_two * gain_two).astype(jnp.bfloat16)
    mixed_other = mixed_other.reshape(QUERY_WIDTH, token_positions)
    middle_other = tokens_other.astype(jnp.float32) + dot(mixed_other, full_output, 0, 0)
    normed_other = (normalize(middle_other)[0] * gain_two).astype(jnp.bfloat16)

    def feed(rows, back_rows):
        gate_proj = dot(rows, full_gate, 1, 0)
        up_proj = dot(rows, full_up, 1, 0)
        sigmoid_gate = jax.nn.sigmoid(gate_proj)
        swish_gate = gate_proj * sigmoid_gate
        hidden = (swish_gate * up_proj).astype(jnp.bfloat16)
        back_hidden = dot(back_rows, full_down, 1, 0)
        back_gate = (
            back_hidden * up_proj * sigmoid_gate * (1.0 + gate_proj * (1.0 - sigmoid_gate))
        ).astype(jnp.bfloat16)
        back_up = (back_hidden * swish_gate).astype(jnp.bfloat16)
        return (hidden, back_gate, back_up)

    def feed_input_back(back_gate, back_up):
        return dot(back_gate, full_gate, 1, 1) + dot(back_up, full_up, 1, 1)

    hidden_other, back_gate_other, back_up_other = feed(normed_other, cotangent_other)
    back_two_received = to_partner(
        feed_input_back(back_gate_other, back_up_other).astype(jnp.bfloat16)
    )
    hidden_own, back_gate_own, back_up_own = feed(normed_two, cotangent_own)
    back_two = feed_input_back(back_gate_own, back_up_own) + back_two_received.astype(jnp.float32)
    feed_other = dot(hidden_other, full_down, 1, 1).astype(jnp.bfloat16)
    base = middle + dot(hidden_own, full_down, 1, 1)

    def feed_gradient(left_own, right_own, left_other, right_other):
        gradient = dot(left_own, right_own, 0, 0) + dot(left_other, right_other, 0, 0)
        return gradient.astype(jnp.bfloat16).reshape(lax.axis_size("fsdp"), -1, gradient.shape[1])

    gradients = (
        feed_gradient(cotangent_own, hidden_own, cotangent_other, hidden_other),
        feed_gradient(normed_two, back_gate_own, normed_other, back_gate_other),
        feed_gradient(normed_two, back_up_own, normed_other, back_up_other),
    )

    grad_gain_two = jnp.sum(back_two * unit_two, axis=0)
    back_middle = cotangent_own.astype(jnp.float32) + norm_back(
        back_two * gain_two, unit_two, inverse_two
    )
    back_attention = back_middle.astype(jnp.bfloat16)
    back_mixed = dot(full_output, back_attention, 1, 1).astype(jnp.bfloat16)
    back_mixed = back_mixed.reshape(query_low.shape)
    grad_output = dot(mixed_low, back_attention, 1, 0).astype(jnp.bfloat16)
    share, result, grad_tokens, share_output, share_query, share_keyval, share_gains = backward_sum(
        query_low, keyval, back_mixed, mixed_heads, lse, cosine, sine, base.T, feed_other.T,
        tokens_own.T, normed_one.T, back_middle.T, gains, grad_gain_two[:, None],
        full_query, full_keyval, gradients, grad_output.reshape(parts, rows, -1),
    )
    return (
        result.swapaxes(1, 2),
        grad_tokens.swapaxes(1, 2).astype(jnp.float32),
        share_gains[:rows, 0].astype(jnp.float32),
        share_query[:rows].astype(jnp.float32),
        share_keyval[:rows].astype(jnp.float32),
        share_output[:rows].astype(jnp.float32),
        share_gains[:rows, 1].astype(jnp.float32),
        share[1].astype(jnp.float32),
        share[2].astype(jnp.float32),
        share[0].astype(jnp.float32),
    )


def solution(mesh):
    rows = P("fsdp", ("ctx", "tp"), None)
    specs = (
        P("fsdp"), P("fsdp", None), P("fsdp", None), P("fsdp", None),
        P("fsdp"), P("fsdp", "tp"), P("fsdp", "tp"), P("fsdp", "tp"),
    )
    kernels = mesh.shape["fsdp"] == 4 and mesh.shape["tp"] == 2 and mesh.shape["ctx"] == 4
    return jax.shard_map(
        fast_on_device if kernels else on_device,
        mesh=mesh,
        in_specs=(rows, rows) + specs,
        out_specs=(rows, rows) + specs,
        check_vma=False,
    )
```
